32 devices in a mesh: dp: 4 (over z), ctx: 4 (over y, x), tp: 2 (over core).
Axes of the slice: x: 2, y: 2, z: 4, core: 2. Of those that a mesh axis runs over, the one named last changes fastest.
Arguments:
- tokens: float32 [32, 580, 384], P('dp', 'ctx'), may hold values from -6 to 6
- valid_mask: int32 [32, 580], P('dp', 'ctx'), may hold values from 0 to 1, as said below
- cotangent: float32 [32, 580, 384], P('dp', 'ctx'), may hold values from -6 to 6
- w_query: bfloat16 [384, 384], P('dp', 'tp'), may hold values from -0.3125 to 0.3125
- w_key: bfloat16 [384, 384], P('dp', 'tp'), may hold values from -0.3125 to 0.3125
- w_value: bfloat16 [384, 384], P('dp', 'tp'), may hold values from -0.3125 to 0.3125
- query_bias: bfloat16 [384], P('tp'), may hold values from -3 to 3
- value_bias: bfloat16 [384], P('tp'), may hold values from -3 to 3
- w_out: bfloat16 [384, 384], P('tp', 'dp'), may hold values from -1.25 to 1.25
- w_up: bfloat16 [384, 1536], P('dp', 'tp'), may hold values from -0.3125 to 0.3125
- up_bias: bfloat16 [1536], P('tp'), may hold values from -3 to 3
- w_down: bfloat16 [1536, 384], P('tp', 'dp'), may hold values from -0.15625 to 0.15625
- norm1_gain: bfloat16 [384], P('dp'), may hold values from 0.25 to 1.75
- norm1_shift: bfloat16 [384], P('dp'), may hold values from -2 to 2
- norm2_gain: bfloat16 [384], P('dp'), may hold values from 0.25 to 1.75
- norm2_shift: bfloat16 [384], P('dp'), may hold values from -2 to 2
- out_bias: bfloat16 [384], P('dp'), may hold values from -2 to 2
- down_bias: bfloat16 [384], P('dp'), may hold values from -2 to 2
Outputs:
- block_out: float32 [32, 580, 384], P('dp', 'ctx')
- input_grad: float32 [32, 580, 384], P('dp', 'ctx')
- grad_query: float32 [384, 384], P('dp', 'tp')
- grad_key: float32 [384, 384], P('dp', 'tp')
- grad_value: float32 [384, 384], P('dp', 'tp')
- grad_query_bias: float32 [384], P('tp')
- grad_value_bias: float32 [384], P('tp')
- grad_out: float32 [384, 384], P('tp', 'dp')
- grad_up: float32 [384, 1536], P('dp', 'tp')
- grad_up_bias: float32 [1536], P('tp')
- grad_down: float32 [1536, 384], P('tp', 'dp')
- grad_norm1_gain: float32 [384], P('dp')
- grad_norm1_shift: float32 [384], P('dp')
- grad_norm2_gain: float32 [384], P('dp')
- grad_norm2_shift: float32 [384], P('dp')
- grad_out_bias: float32 [384], P('dp')
- grad_down_bias: float32 [384], P('dp')
The draws below stay inside these ranges and needn't reach their ends.
Inputs may be any that keep to these rules, and one draw needn't show every extreme that they name: `valid_mask`: in every image each block of 145 slots (slots c * 145 to (c + 1) * 145 - 1) has its first 144 slots valid; in exactly one block of each image, the last slot is valid too; all other slots are 0.
All inputs are finite; a program needn't handle non-finite values.
Results may differ from the reference program's by a relative error of at most 0.018.
Values may be sent and summed in bfloat16 or wider, within the bound.
No kernel may reach another device: no remote copies, remote signals or barrier semaphores. Data moves between devices by JAX's collectives and lax.ppermute only.
A program may use at most 128 MiB of HBM per device.

```python
import jax
import jax.numpy as jnp
from jax import lax

D = 384
HEADS = 6
HD = 64
FF = 1536
BLK = 145
IMAGES = 32
SEQ = 580


def draw_valid_mask(key, part):
    key = jax.random.fold_in(key, 7)
    block_count = SEQ // BLK
    full_block = jax.random.randint(key, (IMAGES, 1), 0, block_count)
    slot_index = jnp.arange(SEQ, dtype=jnp.int32)[None, :]
    inside = slot_index % BLK
    owner = slot_index // BLK
    return jnp.where((inside < BLK - 1) | (owner == full_block), 1, 0).astype(jnp.int32)


def raised(entries, rng, source, target, parts, factor):
    owner, partner = [(jnp.arange(entries.shape[dim]) // (entries.shape[dim] // parts)).reshape([-1 if axis == dim else 1 for axis in range(entries.ndim)]) for dim in (source, target)]
    chosen = jax.random.permutation(rng, parts)[partner]
    strong = (owner == chosen) | (owner == (partner + parts // 2) % parts)
    return jnp.where(strong, factor * entries, entries)


def block_scale(key, dims, shards, least, high):
    def one(position, shards_of):
        heights = jax.random.uniform(jax.random.fold_in(jax.random.fold_in(key, 6), position), (shards_of,), jnp.float32, least / len(shards), high / len(shards))
        return jnp.repeat(jnp.exp(heights), dims[position] // shards_of).reshape((-1,) + (1,) * (len(dims) - position - 1))

    loudness = one(*shards[0])
    for cut in shards[1:]:
        loudness = loudness * one(*cut)
    return loudness


def noise(own_key, shape, scale, reach, shards=(), held_as=jnp.bfloat16):
    factor_of = block_scale(own_key, shape, shards, -0.22, 0.18) if shards else 1.0
    values = jax.random.normal(own_key, shape, jnp.float32) * scale * factor_of
    return jnp.minimum(jnp.maximum(values, -reach), reach).astype(held_as)


def bell_draw_with(own_key, extent, scale, most, split, heavy, held_as=jnp.bfloat16):
    values = scale * jax.random.normal(own_key, extent, jnp.float32)
    if split:
        values = values * block_scale(own_key, extent, split, -0.22, 0.18)
    return jnp.clip(raised(values, jax.random.fold_in(own_key, 3), *heavy), -most, most).astype(held_as)


def setup_inputs(seed: int = 0) -> dict:
    keys = jax.random.split(jax.random.key(seed), 19)
    tokens = noise(keys[0], (IMAGES, SEQ, D), 1.0, 6.0, ((0, 4), (1, 4)), jnp.float32)
    valid_mask = draw_valid_mask(jax.random.fold_in(keys[18], 71), 0)
    cotangent = bell_draw_with(keys[2], (IMAGES, SEQ, D), 1.0, 6.0, ((0, 4), (1, 4)), (0, 2, 4, 2.0), jnp.float32)
    w_query = noise(keys[3], (D, D), D ** -0.5, 0.3125, ((0, 4), (1, 2)))
    w_key = noise(keys[4], (D, D), D ** -0.5, 0.3125, ((0, 4), (1, 2)))
    w_value = noise(keys[5], (D, D), D ** -0.5, 0.3125, ((0, 4), (1, 2)))
    query_bias = noise(keys[6], (D,), 0.5, 3.0, ((0, 2),))
    value_bias = noise(keys[7], (D,), 0.5, 3.0, ((0, 2),))
    w_out = noise(keys[8], (D, D), (D // 16) ** -0.5, 1.25, ((0, 2), (1, 4)))
    w_up = noise(keys[9], (D, FF), D ** -0.5, 0.3125, ((0, 4), (1, 2)))
    up_bias = noise(keys[10], (FF,), 0.5, 3.0, ((0, 2),))
    w_down = noise(keys[11], (FF, D), FF ** -0.5, 0.15625, ((0, 2), (1, 4)))
    norm1_gain = jnp.clip(1.0 + 0.15 * jax.random.normal(keys[12], (D,), jnp.float32), 0.25, 1.75).astype(jnp.bfloat16)
    norm1_shift = noise(keys[13], (D,), 0.3, 2.0, ((0, 4),))
    norm2_gain = jnp.clip(1.0 + 0.15 * jax.random.normal(keys[14], (D,), jnp.float32), 0.25, 1.75).astype(jnp.bfloat16)
    norm2_shift = noise(keys[15], (D,), 0.3, 2.0, ((0, 4),))
    out_bias = noise(keys[16], (D,), 0.3, 2.0, ((0, 4),))
    down_bias = noise(keys[17], (D,), 0.3, 2.0, ((0, 4),))
    return dict(tokens=tokens, valid_mask=valid_mask, cotangent=cotangent, w_query=w_query, w_key=w_key, w_value=w_value, query_bias=query_bias, value_bias=value_bias, w_out=w_out, w_up=w_up, up_bias=up_bias, w_down=w_down, norm1_gain=norm1_gain, norm1_shift=norm1_shift, norm2_gain=norm2_gain, norm2_shift=norm2_shift, out_bias=out_bias, down_bias=down_bias)


@jax.custom_vjp
def low(v):
    return lax.optimization_barrier(v.astype(jnp.bfloat16)).astype(jnp.float32)

@jax.custom_vjp
def low_back(v):
    return v

def low_keep(v):
    return (low(v), None)

def low_pass(kept, grad):
    return (grad,)

def back_keep(v):
    return (v, None)

def back_low(kept, grad):
    return (low(grad),)
low.defvjp(low_keep, low_pass)
low_back.defvjp(back_keep, back_low)
EPS = 1e-06
SCALE = 0.125
FLOOR = -1e+30
HIGH = lax.Precision.HIGHEST

def layer_norm(values, gain_vec, shift_vec):
    row_mean = lax.optimization_barrier(jnp.mean(values, axis=-1, keepdims=True))
    centered = values - row_mean
    spread = lax.optimization_barrier(jnp.mean(centered * centered, axis=-1, keepdims=True))
    return centered * lax.rsqrt(spread + EPS) * gain_vec + shift_vec

def matmul(left, right):
    return jnp.dot(left, right, precision=HIGH)

def block_image(tokens, mask_rows, params):
    w_query, w_key, w_value, query_bias, value_bias, w_out, w_up, up_bias, w_down, norm1_gain, norm1_shift, norm2_gain, norm2_shift, out_bias, down_bias = params
    slots = tokens.shape[0]
    row_gate = mask_rows[:, None]
    normed_one = low(layer_norm(tokens, norm1_gain, norm1_shift))
    queries = low_back(low(matmul(normed_one, w_query) + query_bias)).reshape(slots, HEADS, HD)
    keys_all = low_back(low(matmul(normed_one, w_key))).reshape(slots, HEADS, HD)
    values = low_back(low(matmul(normed_one, w_value) + value_bias)).reshape(slots, HEADS, HD)
    scores = low_back(jnp.einsum('qhd,khd->hqk', queries, keys_all, precision=HIGH) * SCALE)
    scores = jnp.where(mask_rows[None, None, :] > 0, scores, FLOOR)
    log_total = jax.nn.logsumexp(scores, axis=-1, keepdims=True)
    weights = low(jnp.exp(scores - log_total))
    context = jnp.einsum('hqk,khd->qhd', weights, values, precision=HIGH)
    context = low_back(low(context)).reshape(slots, HEADS * HD)
    attended = low_back(matmul(context, w_out) + out_bias)
    middle = tokens + row_gate * attended
    normed_two = low(layer_norm(middle, norm2_gain, norm2_shift))
    hidden_pre = low_back(matmul(normed_two, w_up) + up_bias)
    hidden = low(jax.nn.gelu(hidden_pre, approximate=False))
    mlp_out = low_back(matmul(hidden, w_down) + down_bias)
    return middle + row_gate * mlp_out

def reference(tokens, valid_mask, cotangent, w_query, w_key, w_value, query_bias, value_bias, w_out, w_up, up_bias, w_down, norm1_gain, norm1_shift, norm2_gain, norm2_shift, out_bias, down_bias):
    params = tuple((item.astype(jnp.float32) for item in (w_query, w_key, w_value, query_bias, value_bias, w_out, w_up, up_bias, w_down, norm1_gain, norm1_shift, norm2_gain, norm2_shift, out_bias, down_bias)))

    def image_step(totals, sliced):
        image_tokens, image_mask, image_cot = sliced
        mask_rows = image_mask.astype(jnp.float32)

        def forward(inputs, *weights_in):
            return block_image(inputs, mask_rows, weights_in)
        result, pullback = jax.vjp(forward, image_tokens, *params)
        grads = pullback(image_cot)
        summed = tuple((left + right for left, right in zip(totals, grads[1:])))
        return (summed, (result, grads[0]))
    zeros_init = tuple((jnp.zeros(item.shape, jnp.float32) for item in params))
    totals, (block_out, input_grad) = lax.scan(image_step, zeros_init, (tokens, valid_mask, cotangent))
    return (block_out, input_grad, totals[0], totals[1], totals[2], totals[3], totals[4], totals[5], totals[6], totals[7], totals[8], totals[9], totals[10], totals[11], totals[12], totals[13], totals[14])
```

```python
import functools

import jax
import jax.numpy as jnp
from jax import lax
from jax.experimental import pallas as pl
from jax.experimental.pallas import tpu as pltpu
from jax.sharding import PartitionSpec as P

HD = 64
EPS = 1e-06
SCALE = 0.125
FLOOR = -1e30
BF = jnp.bfloat16
F32 = jnp.float32
TILE = 128
EXTRA = 16
VMEM_LIMIT = 56 * 1024 * 1024


def call(kernel, out_shape, scratch=(), flops=0, smem=()):
    def run(*args):
        specs = [
            pl.BlockSpec(memory_space=pltpu.SMEM if i in smem else pltpu.VMEM)
            for i in range(len(args))
        ]
        return pl.pallas_call(
            kernel,
            out_shape=out_shape,
            in_specs=specs,
            out_specs=jax.tree.map(lambda _: pl.BlockSpec(memory_space=pltpu.VMEM), out_shape),
            scratch_shapes=list(scratch),
            compiler_params=pltpu.CompilerParams(vmem_limit_bytes=VMEM_LIMIT),
            cost_estimate=pl.CostEstimate(flops=flops, bytes_accessed=1 << 20, transcendentals=0),
        )(*args)

    return run


def sds(shape, dtype):
    return jax.ShapeDtypeStruct(shape, dtype)


def nn(a, b):
    return lax.dot_general(a, b, (((1,), (0,)), ((), ())), preferred_element_type=F32)


def nt(a, b):
    return lax.dot_general(a, b, (((1,), (1,)), ((), ())), preferred_element_type=F32)


def tn(a, b):
    return lax.dot_general(a, b, (((0,), (0,)), ((), ())), preferred_element_type=F32)


def swap(v):
    return pltpu.roll(v, HD, axis=1)


def low_lanes(shape):
    return lax.broadcasted_iota(jnp.int32, shape, 1) < HD


def row_is(shape, row):
    return lax.broadcasted_iota(jnp.int32, shape, 0) == row


def tile(v, i):
    return v[:, i * TILE : (i + 1) * TILE]


def assemble(own, oth):
    low = low_lanes((own.shape[0], TILE))
    own_qk, own_vo, oth_qk, oth_vo = tile(own, 4), tile(own, 5), tile(oth, 4), tile(oth, 5)
    qkv = [
        tile(own, 0), tile(oth, 0), jnp.where(low, own_qk, swap(oth_qk)),
        tile(own, 1), tile(oth, 1), jnp.where(low, swap(own_qk), oth_qk),
        tile(own, 2), tile(oth, 2), jnp.where(low, own_vo, swap(oth_vo)),
    ]
    out = [tile(own, 3), tile(oth, 3), jnp.where(low, swap(own_vo), oth_vo)]
    return qkv, out


def disassemble(qkv, out):
    low = low_lanes(qkv[0].shape)
    own = [qkv[0], qkv[3], qkv[6], out[0], jnp.where(low, qkv[2], swap(qkv[5])), jnp.where(low, qkv[8], swap(out[2]))]
    oth = [qkv[1], qkv[4], qkv[7], out[1], jnp.where(low, swap(qkv[2]), qkv[5]), jnp.where(low, swap(qkv[8]), out[2])]
    return own, oth


def norm_stats(v):
    mean = jnp.mean(v, axis=-1, keepdims=True)
    centered = v - mean
    r = lax.rsqrt(jnp.mean(centered * centered, axis=-1, keepdims=True) + EPS)
    return centered * r, r


def norm_back(e, xhat, r):
    return r * (
        e
        - jnp.mean(e, axis=-1, keepdims=True)
        - xhat * jnp.mean(e * xhat, axis=-1, keepdims=True)
    )


def gelu_pair(v):
    a = jnp.abs(v)
    t = 1.0 / (1.0 + (0.3275911 * 0.7071067811865476) * a)
    g = jnp.exp(-0.5 * v * v)
    poly = t * (
        0.254829592 + t * (-0.284496736 + t * (1.421413741 + t * (-1.453152027 + t * 1.061405429)))
    )
    tail = 0.5 * poly * g
    phi = jnp.where(v < 0, tail, 1.0 - tail)
    return v * phi, phi + v * (0.3989422804014327 * g)


def pack_kernel(sizes, tok, cot, mask, wq, wk, wv, wo, wu, wd, qb, vb, ub, *rest):
    nctx, ntp, ndp, main, width, rows, padded = sizes
    vecs, outs = rest[:6], rest[6:]
    t_out, c_out, (p1, p2, tex, cex) = outs[:nctx], outs[nctx : 2 * nctx], outs[2 * nctx :]
    me_c, me_t, me_d = lax.axis_index("ctx"), lax.axis_index("tp"), lax.axis_index("dp")
    for k in range(nctx):
        img = (me_c ^ k) * ntp + me_t
        t_out[k][0:main, :] = tok[img, 0:main, :].astype(BF)
        c_out[k][...] = cot[img, 0:main, :].astype(BF)
        gate = mask[img, main].astype(F32)
        te = tok[img, main : main + 1, :] * gate
        ce = cot[img, main : main + 1, :] * gate
        shape = (EXTRA, width)
        t_out[k][main : main + EXTRA, :] = jnp.where(
            row_is(shape, 0), te, jnp.where(row_is(shape, 1), ce, 0.0)
        ).astype(BF)
    for i in range(nctx * ntp):
        tex[i : i + 1, :] = tok[i, main : main + 1, :]
        cex[i : i + 1, :] = cot[i, main : main + 1, :]

    def put(ref, lo, value):
        ref[0:rows, lo : lo + value.shape[1]] = value.astype(BF)

    if padded > rows:
        p1[0:padded, :] = jnp.zeros((padded, p1.shape[1]), BF)
        for j in range(4):
            p2[j] = jnp.zeros(p2.shape[1:], BF)
    fq, fk, fv = wq[...].astype(F32), wk[...].astype(F32), wv[...].astype(F32)
    fo = jnp.transpose(wo[...].astype(F32))
    for i, w in enumerate((fq, fk, fv, fo)):
        put(p1, i * TILE, tile(w, 0))
    put(p1, 4 * TILE, jnp.concatenate([fq[:, TILE:], fk[:, TILE:]], axis=1))
    put(p1, 5 * TILE, jnp.concatenate([fv[:, TILE:], fo[:, TILE:]], axis=1))
    fd = jnp.transpose(wd[...].astype(F32))
    half = fd.shape[1] // 2
    for j in range(2):
        p2[j, 0:rows, :] = wu[:, j * half : (j + 1) * half]
        p2[2 + j, 0:rows, :] = fd[:, j * half : (j + 1) * half].astype(BF)
    cols = p1.shape[1]
    fqb, fvb = qb[...].astype(F32)[None, :], vb[...].astype(F32)[None, :]
    none = jnp.zeros((1, TILE), F32)
    short = jnp.zeros((1, HD), F32)
    bias = jnp.concatenate(
        [fqb[:, :TILE], none, fvb[:, :TILE], none, fqb[:, TILE:], short, fvb[:, TILE:], short], axis=1
    )
    spread = lax.broadcasted_iota(jnp.int32, (rows, width), 1) == (
        lax.broadcasted_iota(jnp.int32, (rows, width), 0) + rows * me_d
    )
    spread = spread.astype(F32).astype(BF)
    block = jnp.where(row_is((EXTRA, cols), 0), bias, 0.0)
    block = jnp.where(row_is((EXTRA, cols), 7), ub[...].astype(F32)[None, :], block)
    lanes = jnp.zeros((EXTRA, width), F32)
    for i in range(6):
        one = nn(jnp.broadcast_to(vecs[i][...].astype(F32)[None, :], (8, rows)).astype(BF), spread)
        lanes = jnp.where(row_is((EXTRA, width), 1 + i), one[0:1, :], lanes)
    p1[padded : padded + EXTRA, :] = block.astype(BF)
    mixed = jnp.where(
        (lax.broadcasted_iota(jnp.int32, (EXTRA, width), 0) - 1).astype(jnp.uint32) < 6,
        lanes,
        block[:, :width],
    )
    p1[padded : padded + EXTRA, 0:width] = mixed.astype(BF)


def attention_kernel(sizes, *refs):
    nctx, ntp, ndp, main, width, rows, padded = sizes
    t_in, refs = refs[:nctx], refs[nctx:]
    own_in, refs = refs[:ndp], refs[ndp:]
    oth_in, refs = refs[:ndp], refs[ndp:]
    x_out, mid_out, n1_out, n2_out, qkv, ctx, lse, wqkv, wot, vec, ub, cex = refs[:12]
    wf = refs[12]
    me_d = lax.axis_index("dp")
    body = nctx * main
    total = body + EXTRA
    vec_sum = jnp.zeros((EXTRA, width), F32)
    for k in range(ndp):
        own, oth = own_in[k][...].astype(F32), oth_in[k][...].astype(F32)
        tiles, outs = assemble(own[:rows], oth[:rows])
        at = pl.ds(pl.multiple_of((me_d ^ k) * rows, 8), rows)
        for i, v in enumerate(tiles + outs):
            wf[at, i * TILE : (i + 1) * TILE] = v
        vec_sum += own[padded:, :width]
        if k == 0:
            tiles, _ = assemble(own[padded:], oth[padded:])
            bias = jnp.concatenate(tiles, axis=1)[0:1, :]
            ub[...] = jnp.broadcast_to(
                jnp.concatenate([own[padded + 7 : padded + 8], oth[padded + 7 : padded + 8]], axis=1),
                ub.shape,
            )
    vec[...] = vec_sum
    wqkv[...] = wf[:, 0 : 9 * TILE].astype(BF)
    wot[...] = wf[:, 9 * TILE :].astype(BF)
    extra = jnp.zeros((EXTRA, width), F32)
    for k in range(nctx):
        x_out[k * main : (k + 1) * main, :] = t_in[k][0:main, :].astype(F32)
        extra += t_in[k][main:, :].astype(F32)
    x_out[body:, :] = jnp.where(row_is((EXTRA, width), 0), extra, 0.0)
    cex[...] = jnp.where(row_is((EXTRA, width), 0), extra[1:2, :], 0.0).astype(BF)
    x = x_out[...]
    xhat, _ = norm_stats(x)
    n1 = (xhat * vec_sum[1:2, :] + vec_sum[2:3, :]).astype(BF)
    n1_out[...] = n1
    proj = nn(n1, wqkv[...]) + bias
    qkv[0:total, 0:width] = (proj[:, 0:width].astype(BF).astype(F32) * SCALE).astype(BF)
    qkv[0:total, width:] = proj[:, width:].astype(BF)
    keys = qkv.shape[0]
    qkv[total:, :] = jnp.zeros((keys - total, qkv.shape[1]), BF)
    off = jnp.where(lax.broadcasted_iota(jnp.int32, (1, keys), 1) > body, FLOOR, 0.0)
    low = low_lanes((total, TILE))
    lane = lax.broadcasted_iota(jnp.int32, (total, TILE), 1)
    all_lse = jnp.zeros((total, TILE), F32)
    for p in range(3):
        qp = qkv[0:total, p * TILE : (p + 1) * TILE]
        kp = qkv[:, width + p * TILE : width + (p + 1) * TILE]
        vp = qkv[:, 2 * width + p * TILE : 2 * width + (p + 1) * TILE]
        parts = []
        for a in range(2):
            qa = jnp.where(low if a == 0 else ~low, qp, jnp.zeros_like(qp))
            s = nt(qa, kp) + off
            m = jnp.max(s, axis=-1, keepdims=True)
            e = jnp.exp(s - m)
            l = jnp.sum(e, axis=-1, keepdims=True)
            w = (e * (1.0 / l)).astype(BF)
            parts.append(nn(w, vp))
            all_lse = jnp.where(lane == 2 * p + a, m + jnp.log(l), all_lse)
        ctx[:, p * TILE : (p + 1) * TILE] = jnp.where(low, parts[0], parts[1]).astype(BF)
    lse[...] = all_lse
    attended = nt(ctx[...], wot[...]) + vec_sum[5:6, :]
    valid = lax.broadcasted_iota(jnp.int32, (total, 1), 0) <= body
    middle = x_out[...] + jnp.where(valid, attended, 0.0)
    mid_out[...] = middle
    xhat2, _ = norm_stats(middle)
    n2_out[...] = (xhat2 * vec_sum[3:4, :] + vec_sum[4:5, :]).astype(BF)


def mlp_kernel(sizes, *refs):
    nctx, ntp, ndp, main, width, rows, padded = sizes
    c_in, refs = refs[:nctx], refs[nctx:]
    own_in, refs = refs[:ndp], refs[ndp:]
    oth_in, refs = refs[:ndp], refs[ndp:]
    mid, n2, ctx, wot, vec, ub, cex = refs[:7]
    refs = refs[7:]
    bo, refs = refs[:nctx], refs[nctx:]
    dmid, dctx, g_own, g_oth, g_out, vgrad, ubgrad = refs[:7]
    wf, cot, hid, hgr = refs[7:]
    me_d = lax.axis_index("dp")
    body = nctx * main
    total = body + EXTRA
    ff = wf.shape[2]
    quarter = ff // 4
    for k in range(ndp):
        at = pl.ds(pl.multiple_of((me_d ^ k) * rows, 8), rows)
        for j in range(4):
            part, lo = j // 2, (j % 2) * quarter
            wf[part, at, lo : lo + quarter] = own_in[k][j].astype(F32)[:rows]
            wf[part, at, 2 * quarter + lo : 3 * quarter + lo] = oth_in[k][j].astype(F32)[:rows]
    wu, wd = wf[0].astype(BF), wf[1].astype(BF)
    for k in range(nctx):
        cot[k * main : (k + 1) * main, :] = c_in[k][...]
    cot[body:, :] = cex[...]
    dcot = cot[...]
    n2v = n2[...]
    for j in range(ff // 256):
        sl = slice(j * 256, (j + 1) * 256)
        pre = nn(n2v, wu[:, sl]) + ub[0:1, sl]
        hc = nn(dcot, wd[:, sl])
        act, slope = gelu_pair(pre)
        h = act.astype(BF)
        hg = (hc * slope).astype(BF)
        hid[:, sl] = h
        hgr[:, sl] = hg
        ubgrad[:, sl] = jnp.broadcast_to(jnp.sum(hg.astype(F32), axis=0, keepdims=True), (8, 256))
        gu, gd = tn(n2v, hg).astype(BF), tn(dcot, h).astype(BF)
        to = g_own if j * 256 < ff // 2 else g_oth
        lo = (j * 256) % (ff // 2)
        for part, g in ((0, gu), (1, gd)):
            for d in range(ndp):
                for c in range(2):
                    col = lo + c * 128
                    to[2 * part + col // quarter, d, 0:rows, col % quarter : col % quarter + 128] = (
                        g[d * rows : (d + 1) * rows, c * 128 : (c + 1) * 128]
                    )
    middle = mid[...]
    valid = lax.broadcasted_iota(jnp.int32, (total, 1), 0) <= body
    mlp_out = nt(hid[...], wd) + vec[6:7, :]
    out = (middle + jnp.where(valid, mlp_out, 0.0)).astype(BF)
    for k in range(nctx):
        bo[k][0:main, :] = out[k * main : (k + 1) * main]
        bo[k][main:, :] = out[body:]
    n2g = nt(hgr[...], wu)
    xhat, r = norm_stats(middle)
    back = norm_back(n2g * vec[3:4, :], xhat, r)
    middle_grad = dcot.astype(F32) + back
    dmid[...] = middle_grad
    agrad = jnp.where(valid, middle_grad, 0.0).astype(BF)
    dctx[...] = nn(agrad, wot[...]).astype(BF)
    g_out[...] = tn(agrad, ctx[...])
    shape = vgrad.shape
    v = jnp.where(row_is(shape, 2), jnp.sum(n2g * xhat, axis=0, keepdims=True), 0.0)
    v = jnp.where(row_is(shape, 3), jnp.sum(n2g, axis=0, keepdims=True), v)
    v = jnp.where(row_is(shape, 4), jnp.sum(agrad.astype(F32), axis=0, keepdims=True), v)
    v = jnp.where(row_is(shape, 5), jnp.sum(dcot.astype(F32), axis=0, keepdims=True), v)
    vgrad[...] = v


def attention_back_kernel(sizes, *refs):
    nctx, ntp, ndp, main, width, rows, padded = sizes
    qkv, dctx, lse, n1, x_in, dmid, wqkv, vec, g_out, vgrad, ubgrad = refs[:11]
    refs = refs[11:]
    ig, refs = refs[:nctx], refs[nctx:]
    g_own, g_oth = refs[:2]
    dqkv = refs[2]
    body = nctx * main
    total = body + EXTRA
    keys = qkv.shape[0]
    off = jnp.where(lax.broadcasted_iota(jnp.int32, (1, keys), 1) > body, FLOOR, 0.0)
    low = low_lanes((total, TILE))
    for p in range(3):
        qp = qkv[0:total, p * TILE : (p + 1) * TILE]
        kp = qkv[:, width + p * TILE : width + (p + 1) * TILE]
        vp = qkv[:, 2 * width + p * TILE : 2 * width + (p + 1) * TILE]
        dp = dctx[:, p * TILE : (p + 1) * TILE]
        dq, dk, dv = [], 0.0, 0.0
        for a in range(2):
            sel = low if a == 0 else ~low
            qa = jnp.where(sel, qp, jnp.zeros_like(qp))
            da = jnp.where(sel, dp, jnp.zeros_like(dp))
            prob = jnp.exp(nt(qa, kp) + off - lse[:, 2 * p + a : 2 * p + a + 1])
            wg = nt(da, vp)
            inner = jnp.sum(prob * wg, axis=-1, keepdims=True)
            ds = (prob * (wg - inner)).astype(BF)
            w = prob.astype(BF)
            dq.append(nn(ds, kp))
            dk = dk + tn(ds, qa)
            dv = dv + tn(w, da)
        dqkv[:, p * TILE : (p + 1) * TILE] = (jnp.where(low, dq[0], dq[1]) * SCALE).astype(BF)
        dqkv[:, width + p * TILE : width + (p + 1) * TILE] = dk[0:total].astype(BF)
        dqkv[:, 2 * width + p * TILE : 2 * width + (p + 1) * TILE] = dv[0:total].astype(BF)
    d = dqkv[...]
    bias = jnp.sum(d.astype(F32), axis=0, keepdims=True)
    g = tn(n1[...], d)
    go = g_out[...]
    own, oth = disassemble([tile(g, i) for i in range(9)], [tile(go, i) for i in range(3)])
    for to, tiles in ((g_own, own), (g_oth, oth)):
        for j in range(6):
            for e in range(ndp):
                to[j // 2, e, 0:rows, (j % 2) * TILE : (j % 2 + 1) * TILE] = (
                    tiles[j][e * rows : (e + 1) * rows].astype(BF)
                )
    dn1 = nt(d, wqkv[...])
    xhat, r = norm_stats(x_in[...])
    grad = dmid[...] + norm_back(dn1 * vec[1:2, :], xhat, r)
    out = grad.astype(BF)
    for k in range(nctx):
        ig[k][0:main, :] = out[k * main : (k + 1) * main]
        ig[k][main:, :] = out[body:]
    gains = jnp.sum(dn1 * xhat, axis=0, keepdims=True)
    shifts = jnp.sum(dn1, axis=0, keepdims=True)
    vecs = [gains, shifts] + [vgrad[i : i + 1, :] for i in range(2, 6)]
    zero = [jnp.zeros((1, TILE), F32)] * 3
    bias_own, bias_oth = disassemble([tile(bias, i) for i in range(9)], zero)
    half = ubgrad.shape[1] // 2
    for to, tiles, lo in ((g_own, bias_own, 0), (g_oth, bias_oth, half)):
        rows_ = [tile(v, i) for v in vecs for i in range(3)] + tiles
        rows_ += [ubgrad[0:1, lo + i * TILE : lo + (i + 1) * TILE] for i in range(6)]
        for side in range(2):
            block = jnp.zeros((EXTRA, TILE), F32)
            for i, v in enumerate(rows_[side * EXTRA : (side + 1) * EXTRA]):
                block = jnp.where(row_is(block.shape, i), v, block)
            for e in range(ndp):
                to[3, e, 0:EXTRA, side * TILE : (side + 1) * TILE] = block.astype(BF)
                if padded > EXTRA:
                    to[3, e, EXTRA:padded, side * TILE : (side + 1) * TILE] = jnp.zeros(
                        (padded - EXTRA, TILE), BF
                    )


def sum_core_kernel(n, own, oth, *outs):
    me = lax.axis_index("ctx")
    for k in range(n):
        outs[k][...] = (own[me ^ k].astype(F32) + oth[me ^ k].astype(F32)).astype(BF)


def sum_ctx_kernel(n, ndp, *refs):
    me = lax.axis_index("dp")
    for part in range(len(refs) // (n + ndp)):
        base = part * n
        outs = refs[(len(refs) // (n + ndp)) * n + part * ndp :]
        for k in range(ndp):
            v = refs[base][me ^ k].astype(F32)
            for i in range(1, n):
                v = v + refs[base + i][me ^ k].astype(F32)
            outs[k][...] = v.astype(BF)


def sum_dp_kernel(ndp, *refs):
    parts = len(refs) // (ndp + 1)
    for part in range(parts):
        v = refs[part * ndp][...].astype(F32)
        for i in range(1, ndp):
            v = v + refs[part * ndp + i][...].astype(F32)
        refs[parts * ndp + part][...] = v.astype(BF)


def grads_kernel(sizes, *refs):
    nctx, ntp, ndp, main, width, rows, padded = sizes
    in1, in2, refs = refs[:nctx], refs[nctx : 2 * nctx], refs[2 * nctx :]
    gq, gk, gv, gqb, gvb, go, gu, gub, gd = refs[:9]
    gvec = refs[9:15]
    f1, f2 = refs[15:]
    me, me_d = lax.axis_index("ctx"), lax.axis_index("dp")
    for k in range(nctx):
        f1[me ^ k] = in1[k][...].astype(F32)
        f2[me ^ k] = in2[k][...].astype(F32)
    q01, k01 = f1[0, 0:rows, 0:TILE], f1[0, 0:rows, TILE:]
    v01, o01 = f1[1, 0:rows, 0:TILE], f1[1, 0:rows, TILE:]
    qk2, vo2 = f1[2, 0:rows, 0:TILE], f1[2, 0:rows, TILE:]
    gq[:, 0:TILE] = q01
    gq[:, TILE:] = qk2[:, 0:HD]
    gk[:, 0:TILE] = k01
    gk[:, TILE:] = swap(qk2)[:, 0:HD]
    gv[:, 0:TILE] = v01
    gv[:, TILE:] = vo2[:, 0:HD]
    go[0:TILE, :] = jnp.transpose(o01)
    go[TILE:, :] = jnp.transpose(vo2)[HD:, :]
    half = f2.shape[2]
    for j in range(2):
        gu[:, j * half : (j + 1) * half] = f2[j, 0:rows, :]
        gd[j * half : (j + 1) * half, :] = jnp.transpose(f2[2 + j, 0:rows, :])
    ex = [f1[3, 0:EXTRA, 0:TILE], f1[3, 0:EXTRA, TILE:]]

    def line(i):
        return ex[i // EXTRA][i % EXTRA : i % EXTRA + 1, :]

    for i in range(6):
        v = jnp.concatenate([line(3 * i), line(3 * i + 1), line(3 * i + 2)], axis=1)
        v = jnp.broadcast_to(v, (8, width))
        v = pltpu.roll(v, lax.rem(width - me_d * rows, width), axis=1)
        gvec[i][...] = v[0, 0:rows]
    b = [line(18 + i) for i in range(6)]
    gqb[...] = jnp.concatenate([b[0], b[4][:, 0:HD]], axis=1)[0]
    gvb[...] = jnp.concatenate([b[2], b[5][:, 0:HD]], axis=1)[0]
    gub[...] = jnp.concatenate([line(24 + i) for i in range(6)], axis=1)[0]


def unpack_kernel(sizes, *refs):
    nctx, ntp, ndp, main, width, rows, padded = sizes
    own, oth, (extra, mask, out) = refs[:nctx], refs[nctx : 2 * nctx], refs[2 * nctx :]
    me_c, me_t = lax.axis_index("ctx"), lax.axis_index("tp")
    for k in range(nctx):
        for src, t in ((own[k], me_t), (oth[k], 1 - me_t)):
            img = (me_c ^ k) * ntp + t
            out[img, 0:main, :] = src[0:main, :].astype(F32)
            got = src[main:, :].astype(F32)[0:1, :]
            out[img, main : main + 1, :] = jnp.where(
                mask[img, main] > 0, got, extra[pl.ds(img, 1), :]
            )


def xor(n, k):
    return [(i, i ^ k) for i in range(n)]


def over(axis, n, items):
    return [items[0]] + [lax.ppermute(items[k], axis, xor(n, k)) for k in range(1, n)]


def body(nctx, ntp, ndp, *args):
    (tokens, valid_mask, cotangent, w_query, w_key, w_value, query_bias, value_bias, w_out, w_up, up_bias, w_down) = args[:12]
    vecs = args[12:]
    images, slots, width = tokens.shape
    main = slots - 1
    rows = w_query.shape[0]
    padded = -(-rows // EXTRA) * EXTRA
    ff = w_up.shape[1]
    heads_cols = w_query.shape[1]
    p1_cols = 4 * heads_cols
    quarter = ff // 2
    sizes = (nctx, ntp, ndp, main, width, rows, padded)
    total = nctx * main + EXTRA
    keys = -(-total // TILE) * TILE
    one = lambda f: functools.partial(f, sizes)
    packed = call(
        one(pack_kernel),
        [sds((main + EXTRA, width), BF)] * nctx
        + [sds((main, width), BF)] * nctx
        + [sds((padded + EXTRA, p1_cols), BF), sds((4, padded, quarter), BF)]
        + [sds((images, width), F32)] * 2,
        smem=(2,),
    )(tokens, cotangent, valid_mask, w_query, w_key, w_value, w_out, w_up, w_down, query_bias, value_bias, up_bias, *vecs)
    t_send, c_send = packed[:nctx], packed[nctx : 2 * nctx]
    p1, p2, tex, cex = packed[2 * nctx :]
    flip = xor(ntp, 1)
    t_in = over("ctx", nctx, t_send)
    w1_own = over("dp", ndp, [p1] * ndp)
    c_in = over("ctx", nctx, c_send)
    w2_own = over("dp", ndp, [p2] * ndp)
    w1_oth = [lax.ppermute(v, "tp", flip) for v in w1_own]
    w2_oth = [lax.ppermute(v, "tp", flip) for v in w2_own]
    x, mid, n1, n2, qkv, ctx, lse, wqkv, wot, vec, ub, cex_in = call(
        one(attention_kernel),
        [
            sds((total, width), F32), sds((total, width), F32), sds((total, width), BF), sds((total, width), BF),
            sds((keys, 3 * width), BF), sds((total, width), BF), sds((total, TILE), F32),
            sds((width, 3 * width), BF), sds((width, width), BF), sds((EXTRA, width), F32), sds((8, 2 * ff), F32),
            sds((EXTRA, width), BF),
        ],
        scratch=[pltpu.VMEM((width, 4 * width), F32)],
        flops=2 * 10**9,
    )(*t_in, *w1_own, *w1_oth)
    out = call(
        one(mlp_kernel),
        [sds((main + EXTRA, width), BF)] * nctx
        + [sds((total, width), F32), sds((total, width), BF)]
        + [sds((4, ndp, padded, quarter), BF)] * 2
        + [sds((width, width), F32), sds((EXTRA, width), F32), sds((8, 2 * ff), F32)],
        scratch=[
            pltpu.VMEM((2, width, 2 * ff), F32),
            pltpu.VMEM((total, width), BF),
            pltpu.VMEM((total, 2 * ff), BF),
            pltpu.VMEM((total, 2 * ff), BF),
        ],
        flops=4 * 10**9,
    )(*c_in, *w2_own, *w2_oth, mid, n2, ctx, wot, vec, ub, cex_in)
    bo, (dmid, dctx, g2_own, g2_oth, g_out, vgrad, ubgrad) = out[:nctx], out[nctx:]
    quarter_sums = lambda own, oth: call(
        functools.partial(sum_core_kernel, nctx), [sds(own.shape[1:], BF)] * nctx
    )(own, oth)
    s2 = quarter_sums(g2_own, lax.ppermute(g2_oth, "tp", flip))
    s2 = over("ctx", nctx, s2)
    bo_own = over("ctx", nctx, bo)
    out = call(
        one(attention_back_kernel),
        [sds((main + EXTRA, width), BF)] * nctx + [sds((4, ndp, padded, 2 * TILE), BF)] * 2,
        scratch=[pltpu.VMEM((total, 3 * width), BF)],
        flops=4 * 10**9,
    )(qkv, dctx, lse, n1, x, dmid, wqkv, vec, g_out, vgrad, ubgrad)
    ig, (g1_own, g1_oth) = out[:nctx], out[nctx:]
    s1 = quarter_sums(g1_own, lax.ppermute(g1_oth, "tp", flip))
    s1 = over("ctx", nctx, s1)
    ig_own = over("ctx", nctx, ig)
    parts = call(
        functools.partial(sum_ctx_kernel, nctx, ndp),
        [sds(s1[0].shape[1:], BF)] * ndp + [sds(s2[0].shape[1:], BF)] * ndp,
    )(*s1, *s2)
    u1, u2 = over("dp", ndp, parts[:ndp]), over("dp", ndp, parts[ndp:])
    v1, v2 = call(
        functools.partial(sum_dp_kernel, ndp), [sds(u1[0].shape, BF), sds(u2[0].shape, BF)]
    )(*u1, *u2)
    f1, f2 = over("ctx", nctx, [v1] * nctx), over("ctx", nctx, [v2] * nctx)
    gq, gk, gv, gqb, gvb, go, gu, gub, gd, *gvec = call(
        one(grads_kernel),
        [
            sds(w_query.shape, F32), sds(w_key.shape, F32), sds(w_value.shape, F32),
            sds(query_bias.shape, F32), sds(value_bias.shape, F32), sds(w_out.shape, F32),
            sds(w_up.shape, F32), sds(up_bias.shape, F32), sds(w_down.shape, F32),
        ]
        + [sds((rows,), F32)] * 6,
        scratch=[pltpu.VMEM((4,) + v1.shape, F32), pltpu.VMEM((4,) + v2.shape, F32)],
    )(*f1, *f2)
    results = []
    for own, extra in ((bo_own, tex), (ig_own, cex)):
        oth = [lax.ppermute(v, "tp", flip) for v in own]
        results.append(
            call(one(unpack_kernel), sds(tokens.shape, F32), smem=(2 * nctx + 1,))(
                *own, *oth, extra, valid_mask
            )
        )
    return (*results, gq, gk, gv, gqb, gvb, go, gu, gub, gd, *gvec)


def solution(mesh):
    rows, cols, tp, dp = P("dp", "tp"), P("tp", "dp"), P("tp"), P("dp")
    act = P("dp", "ctx", None)
    return jax.shard_map(
        functools.partial(body, mesh.shape["ctx"], mesh.shape["tp"], mesh.shape["dp"]),
        mesh=mesh,
        in_specs=(act, P("dp", "ctx"), act, rows, rows, rows, tp, tp, cols, rows, tp, cols) + (dp,) * 6,
        out_specs=(act, act, rows, rows, rows, tp, tp, cols, rows, tp, cols) + (dp,) * 6,
        check_vma=False,
    )
```

```python
import functools

import jax
import jax.numpy as jnp
from jax import lax
from jax.experimental import pallas as pl
from jax.experimental.pallas import tpu as pltpu
from jax.sharding import PartitionSpec as P

HD = 64
EPS = 1e-06
SCALE = 0.125
FLOOR = -1e30
BF = jnp.bfloat16
F32 = jnp.float32
TILE = 128
TIMES = {
    "pack_weights": 2.0, "pack_slots": 3.0, "pack_cotangent": 2.0, "attention": 6.0, "mlp_own": 4.0, "mlp_oth": 4.0, "mlp_sums": 2.0, "attention_back": 11.0,
    "place_grads": 1.0, "place_slots": 2.3,
}
EXTRA = 16


def call(name, kernel, out_shape, scratch=(), mib=8, after=(), raw=(), raw_out=False):
    after = list(after)

    def ordered(*refs):
        kernel(*refs[len(after) :])

    def run(*args):
        specs = [pl.BlockSpec(memory_space=pl.ANY)] * len(after) + [
            pl.BlockSpec(memory_space=pltpu.HBM if i in raw else pltpu.VMEM)
            for i in range(len(args))
        ]
        return pl.pallas_call(
            ordered,
            name=name,
            out_shape=out_shape,
            in_specs=specs,
            out_specs=jax.tree.map(
                lambda _: pl.BlockSpec(memory_space=pltpu.HBM if raw_out else pltpu.VMEM), out_shape
            ),
            scratch_shapes=list(scratch),
            compiler_params=pltpu.CompilerParams(vmem_limit_bytes=mib << 20),
            cost_estimate=pl.CostEstimate(
                flops=int(TIMES.get(name, 0.2) * 1.15e9), bytes_accessed=1, transcendentals=0
            ),
        )(*after, *args)

    return run


def sds(shape, dtype):
    return jax.ShapeDtypeStruct(shape, dtype)


def nn(a, b):
    return lax.dot_general(a, b, (((1,), (0,)), ((), ())), preferred_element_type=F32)


def nt(a, b):
    return lax.dot_general(a, b, (((1,), (1,)), ((), ())), preferred_element_type=F32)


def tn(a, b):
    return lax.dot_general(a, b, (((0,), (0,)), ((), ())), preferred_element_type=F32)


def swap(v):
    return pltpu.roll(v, HD, axis=1)


def low_lanes(shape):
    return lax.broadcasted_iota(jnp.int32, shape, 1) < HD


def row_is(shape, row):
    return lax.broadcasted_iota(jnp.int32, shape, 0) == row


def tile(v, i):
    return v[:, i * TILE : (i + 1) * TILE]


def assemble(own, oth):
    low = low_lanes((own.shape[0], TILE))
    own_qk, own_vo, oth_qk, oth_vo = tile(own, 4), tile(own, 5), tile(oth, 4), tile(oth, 5)
    qkv = [
        tile(own, 0), tile(oth, 0), jnp.where(low, own_qk, swap(oth_qk)),
        tile(own, 1), tile(oth, 1), jnp.where(low, swap(own_qk), oth_qk),
        tile(own, 2), tile(oth, 2), jnp.where(low, own_vo, swap(oth_vo)),
    ]
    out = [tile(own, 3), tile(oth, 3), jnp.where(low, swap(own_vo), oth_vo)]
    return qkv, out


def disassemble(qkv, out):
    low = low_lanes(qkv[0].shape)
    own = [qkv[0], qkv[3], qkv[6], out[0], jnp.where(low, qkv[2], swap(qkv[5])), jnp.where(low, qkv[8], swap(out[2]))]
    oth = [qkv[1], qkv[4], qkv[7], out[1], jnp.where(low, swap(qkv[2]), qkv[5]), jnp.where(low, swap(qkv[8]), out[2])]
    return own, oth


def norm_stats(v):
    mean = jnp.mean(v, axis=-1, keepdims=True)
    centered = v - mean
    r = lax.rsqrt(jnp.mean(centered * centered, axis=-1, keepdims=True) + EPS)
    return centered * r, r


def norm_back(e, xhat, r):
    return r * (
        e
        - jnp.mean(e, axis=-1, keepdims=True)
        - xhat * jnp.mean(e * xhat, axis=-1, keepdims=True)
    )


def gelu_pair(v):
    a = jnp.abs(v)
    t = 1.0 / (1.0 + (0.3275911 * 0.7071067811865476) * a)
    g = jnp.exp(-0.5 * v * v)
    poly = t * (
        0.254829592 + t * (-0.284496736 + t * (1.421413741 + t * (-1.453152027 + t * 1.061405429)))
    )
    tail = 0.5 * poly * g
    phi = jnp.where(v < 0, tail, 1.0 - tail)
    return v * phi, phi + v * (0.3989422804014327 * g)


BLOCK = 16


def one_hot(shape, hit):
    r, c = (lax.broadcasted_iota(jnp.int32, shape, i) for i in range(2))
    return hit(r, c).astype(F32).astype(BF)


def picker(wanted, images):
    def hit(r, c):
        img = wanted[-1]
        for k in range(len(wanted) - 1):
            img = jnp.where(r // BLOCK == k, wanted[k], img)
        return c == (r % BLOCK) * images + img

    return one_hot((len(wanted) * BLOCK, images * BLOCK), hit)


def take_images(ref, outs, at, pick, images, count):
    for b in range(count // BLOCK):
        got = nn(pick, ref[b * BLOCK * images : (b + 1) * BLOCK * images, :].astype(BF)).astype(BF)
        for k in range(len(outs)):
            outs[k][at + b * BLOCK : at + (b + 1) * BLOCK, :] = got[k * BLOCK : (k + 1) * BLOCK]


def fetch(sources, held, sem):
    copies = [pltpu.make_async_copy(sources[i], held[i], sem.at[i]) for i in range(len(sources))]
    for c in copies:
        c.start()
    return copies


def pack_weights_kernel(sizes, count, *refs):
    nctx, ntp, ndp, main, width, rows, padded = sizes
    sources, (p1, p2q), refs = refs[:count], refs[count : count + 2], refs[count + 2 :]
    held, sem = refs[:count], refs[count]
    copies = fetch(sources, held, sem)
    wq, wk, wv, wo, wu, wd, qb, vb, ub = held[:9]
    vecs = held[9:]
    me_c, me_d = lax.axis_index("ctx"), lax.axis_index("dp")
    for c in copies:
        c.wait()
    if padded > rows:
        p1[0:padded, :] = jnp.zeros((padded, p1.shape[1]), BF)
        p2q[...] = jnp.zeros(p2q.shape, BF)
    quarter = p2q.shape[1]
    for j in range(nctx):
        src = (wu, wd)[j // 2][:, (j % 2) * quarter : (j % 2 + 1) * quarter]

        @pl.when(me_c == j)
        def _(src=src):
            p2q[0:rows, :] = src

    def put(lo, value):
        p1[0:rows, lo : lo + value.shape[1]] = value.astype(BF)

    fq, fk, fv = wq[...].astype(F32), wk[...].astype(F32), wv[...].astype(F32)
    fo = jnp.transpose(wo[...].astype(F32))
    for i, w in enumerate((fq, fk, fv, fo)):
        put(i * TILE, tile(w, 0))
    put(4 * TILE, jnp.concatenate([fq[:, TILE:], fk[:, TILE:]], axis=1))
    put(5 * TILE, jnp.concatenate([fv[:, TILE:], fo[:, TILE:]], axis=1))
    cols = p1.shape[1]
    fqb, fvb = qb[...].astype(F32)[None, :], vb[...].astype(F32)[None, :]
    none = jnp.zeros((1, TILE), F32)
    short = jnp.zeros((1, HD), F32)
    bias = jnp.concatenate(
        [fqb[:, :TILE], none, fvb[:, :TILE], none, fqb[:, TILE:], short, fvb[:, TILE:], short], axis=1
    )
    spread = one_hot((rows, width), lambda r, c: c == r + rows * me_d)
    block = jnp.where(row_is((EXTRA, cols), 0), bias, 0.0)
    block = jnp.where(row_is((EXTRA, cols), 7), ub[...].astype(F32)[None, :], block)
    lanes = jnp.zeros((EXTRA, rows), F32)
    for i in range(6):
        lanes = jnp.where(row_is((EXTRA, rows), 1 + i), vecs[i][...].astype(F32)[None, :], lanes)
    lanes = nn(lanes.astype(BF), spread)
    p1[padded : padded + EXTRA, :] = block.astype(BF)
    mixed = jnp.where(
        (lax.broadcasted_iota(jnp.int32, (EXTRA, width), 0) - 1).astype(jnp.uint32) < 6,
        lanes,
        block[:, :width],
    )
    p1[padded : padded + EXTRA, 0:width] = mixed.astype(BF)


def pack_slots_kernel(sizes, *refs):
    nctx, ntp, ndp, main, width, rows, padded = sizes
    count = len(refs) - nctx
    count = count // 2
    sources, sent, refs = refs[:count], refs[count : count + nctx], refs[count + nctx :]
    held, sem = refs[:count], refs[count]
    images = nctx * ntp
    last = pl.ds(main * images, images)
    copies = [pltpu.make_async_copy(sources[0], held[0], sem.at[0])]
    if count > 1:
        copies.append(pltpu.make_async_copy(sources[1].at[last, :], held[1], sem.at[1]))
        copies.append(pltpu.make_async_copy(sources[2], held[2], sem.at[2]))
    for c in copies:
        c.start()
    me_c, me_t = lax.axis_index("ctx"), lax.axis_index("tp")
    wanted = [(me_c ^ k) * ntp + me_t for k in range(nctx)]
    pick = picker(wanted, images)
    for c in copies:
        c.wait()
    take_images(held[0], sent, 0, pick, images, main)
    if count > 1:
        tok, cot, mask = held
        for k in range(nctx):
            gate = mask[wanted[k], main].astype(F32)
            te = tok[pl.ds(main * images + wanted[k], 1), :] * gate
            ce = cot[pl.ds(wanted[k], 1), :] * gate
            shape = (EXTRA, width)
            sent[k][main : main + EXTRA, :] = jnp.where(
                row_is(shape, 0), te, jnp.where(row_is(shape, 1), ce, 0.0)
            ).astype(BF)


def join_kernel(axis, stride, own, got, out):
    bit = lax.rem(lax.div(lax.axis_index(axis), stride), 2)
    for i in range(own.shape[0]):
        out[2 * i + bit] = own[i]
        out[2 * i + 1 - bit] = got[i]


def place_rows(out, own, got, rows, stage):
    bit = lax.rem(lax.axis_index("dp"), 2)
    for i in range(own.shape[0]):
        for piece, last in ((own[i], bit), (got[i], 1 - bit)):
            at = pl.ds(pl.multiple_of((2 * i + last) * rows, 16 if rows % 16 == 0 else 8), rows)
            stage[at, :] = piece.astype(stage.dtype)[:rows]
    out[0 : stage.shape[0], :] = stage[...].astype(BF)


def merge_quarter_kernel(sizes, own, got, out, stage):
    place_rows(out, own, got, sizes[5], stage)


def merge_attn_kernel(sizes, own, got, out, stage):
    nctx, ntp, ndp, main, width, rows, padded = sizes
    place_rows(out, own, got, rows, stage)
    extra = own[0, padded:, :].astype(F32)
    for more in [own[i] for i in range(1, own.shape[0])] + [got[i] for i in range(own.shape[0])]:
        more = more[padded:, :].astype(F32)
        row = lax.broadcasted_iota(jnp.int32, more.shape, 0)
        extra += jnp.where((row > 0) & (row < 7), more, 0.0)
    out[width:, :] = extra.astype(BF)


def merge_ff_kernel(nctx, *refs):
    out = refs[nctx]
    me_c = lax.axis_index("ctx")
    for k in range(nctx):
        quarter = refs[k].shape[1]
        out[:, pl.ds(pl.multiple_of((me_c ^ k) * quarter, quarter), quarter)] = refs[k][...]


def attention_kernel(sizes, *refs):
    nctx, ntp, ndp, main, width, rows, padded = sizes
    t_in, c_in, refs = refs[:nctx], refs[nctx : 2 * nctx], refs[2 * nctx :]
    (own_in, oth_in), refs = refs[:2], refs[2:]
    x_out, mid_out, n1_out, n2_out, qkv, ctx, lse, wqkv, wot, vec, ub, cot = refs
    body = nctx * main
    total = body + EXTRA
    own, oth = own_in[...].astype(F32), oth_in[...].astype(F32)
    tiles, outs = assemble(own, oth)
    for i, v in enumerate(tiles):
        wqkv[:, i * TILE : (i + 1) * TILE] = v[:width].astype(BF)
    for i, v in enumerate(outs):
        wot[:, i * TILE : (i + 1) * TILE] = v[:width].astype(BF)
    bias = jnp.concatenate([v[width : width + 1] for v in tiles], axis=1)
    vec_sum = own[width:, :width]
    vec[...] = vec_sum
    ub[...] = jnp.broadcast_to(
        jnp.concatenate([own[width + 7 : width + 8], oth[width + 7 : width + 8]], axis=1), ub.shape
    )
    extra = jnp.zeros((EXTRA, width), F32)
    for k in range(nctx):
        x_out[k * main : (k + 1) * main, :] = t_in[k][0:main, :].astype(F32)
        cot[k * main : (k + 1) * main, :] = c_in[k][...]
        extra += t_in[k][main : main + EXTRA, :].astype(F32)
    x_out[body:, :] = jnp.where(row_is((EXTRA, width), 0), extra, 0.0)
    cot[body:, :] = jnp.where(row_is((EXTRA, width), 0), extra[1:2, :], 0.0).astype(BF)
    x = x_out[...]
    xhat, _ = norm_stats(x)
    n1 = (xhat * vec_sum[1:2, :] + vec_sum[2:3, :]).astype(BF)
    n1_out[...] = n1
    proj = nn(n1, wqkv[...]) + bias
    qkv[0:total, 0:width] = (proj[:, 0:width].astype(BF).astype(F32) * SCALE).astype(BF)
    qkv[0:total, width:] = proj[:, width:].astype(BF)
    keys = qkv.shape[0]
    qkv[total:, :] = jnp.zeros((keys - total, qkv.shape[1]), BF)
    off = jnp.where(lax.broadcasted_iota(jnp.int32, (1, keys), 1) > body, FLOOR, 0.0)
    low = low_lanes((total, TILE))
    lane = lax.broadcasted_iota(jnp.int32, (total, TILE), 1)
    all_lse = jnp.zeros((total, TILE), F32)
    for p in range(3):
        qp = qkv[0:total, p * TILE : (p + 1) * TILE]
        kp = qkv[:, width + p * TILE : width + (p + 1) * TILE]
        vp = qkv[:, 2 * width + p * TILE : 2 * width + (p + 1) * TILE]
        parts = []
        for a in range(2):
            qa = jnp.where(low if a == 0 else ~low, qp, jnp.zeros_like(qp))
            s = nt(qa, kp) + off
            m = jnp.max(s, axis=-1, keepdims=True)
            e = jnp.exp(s - m)
            l = jnp.sum(e, axis=-1, keepdims=True)
            w = (e * (1.0 / l)).astype(BF)
            parts.append(nn(w, vp))
            all_lse = jnp.where(lane == 2 * p + a, m + jnp.log(l), all_lse)
        ctx[:, p * TILE : (p + 1) * TILE] = jnp.where(low, parts[0], parts[1]).astype(BF)
    lse[...] = all_lse
    attended = nt(ctx[...], wot[...]) + vec_sum[5:6, :]
    valid = lax.broadcasted_iota(jnp.int32, (total, 1), 0) <= body
    middle = x_out[...] + jnp.where(valid, attended, 0.0)
    mid_out[...] = middle
    xhat2, _ = norm_stats(middle)
    n2_out[...] = (xhat2 * vec_sum[3:4, :] + vec_sum[4:5, :]).astype(BF)


def ff_half(n2v, dcot, w, ub, hid, hgr, ubgrad, grads, ndp, rows):
    half = w.shape[1] // 2
    quarter = half // 2
    for lo in range(0, half, 256):
        sl = slice(lo, lo + 256)
        pre = nn(n2v, w[:, sl]) + ub[0:1, sl]
        hc = nn(dcot, w[:, half + lo : half + lo + 256])
        act, slope = gelu_pair(pre)
        h = act.astype(BF)
        hg = (hc * slope).astype(BF)
        hid[:, sl] = h
        hgr[:, sl] = hg
        ubgrad[:, sl] = jnp.broadcast_to(jnp.sum(hg.astype(F32), axis=0, keepdims=True), (8, 256))
        for part, g in ((0, tn(n2v, hg).astype(BF)), (1, tn(dcot, h).astype(BF))):
            for d in range(ndp):
                for c in range(2):
                    col = lo + c * TILE
                    at = slice(col % quarter, col % quarter + TILE)
                    grads[2 * part + col // quarter, d, 0:rows, at] = (
                        g[d * rows : (d + 1) * rows, c * TILE : (c + 1) * TILE]
                    )


def mlp_half_kernel(sizes, side, n2, cot, w, ub, hid, hgr, ubgrad, grads):
    half = w.shape[1] // 2
    ff_half(
        n2[...], cot[...], w[...], ub[:, side * half : (side + 1) * half], hid, hgr, ubgrad, grads, sizes[2], sizes[5]
    )


def mlp_sums_kernel(sizes, mid, ctx, wot, vec, cot, w_own, w_oth, hid_own, hid_oth, hgr_own, hgr_oth, bo, dmid, dctx, g_out, vgrad):
    nctx, ntp, ndp, main, width, rows, padded = sizes
    body = nctx * main
    total = body + EXTRA
    half = w_own.shape[1] // 2
    dcot = cot[...]
    middle = mid[...]
    valid = lax.broadcasted_iota(jnp.int32, (total, 1), 0) <= body
    n2g = nt(hgr_own[...], w_own[:, :half]) + nt(hgr_oth[...], w_oth[:, :half])
    xhat, r = norm_stats(middle)
    back = norm_back(n2g * vec[3:4, :], xhat, r)
    middle_grad = dcot.astype(F32) + back
    dmid[...] = middle_grad
    agrad = jnp.where(valid, middle_grad, 0.0).astype(BF)
    dctx[...] = nn(agrad, wot[...]).astype(BF)
    g_out[...] = tn(agrad, ctx[...])
    mlp_out = nt(hid_own[...], w_own[:, half:]) + nt(hid_oth[...], w_oth[:, half:]) + vec[6:7, :]
    bo[...] = (middle + jnp.where(valid, mlp_out, 0.0)).astype(BF)
    shape = vgrad.shape
    v = jnp.where(row_is(shape, 2), jnp.sum(n2g * xhat, axis=0, keepdims=True), 0.0)
    v = jnp.where(row_is(shape, 3), jnp.sum(n2g, axis=0, keepdims=True), v)
    v = jnp.where(row_is(shape, 4), jnp.sum(agrad.astype(F32), axis=0, keepdims=True), v)
    v = jnp.where(row_is(shape, 5), jnp.sum(dcot.astype(F32), axis=0, keepdims=True), v)
    vgrad[...] = v


def pair_back(p, width, total, body, qkv, dctx, lse):
    keys = qkv.shape[0]
    off = jnp.where(lax.broadcasted_iota(jnp.int32, (1, keys), 1) > body, FLOOR, 0.0)
    low = low_lanes((total, TILE))
    qp = qkv[0:total, p * TILE : (p + 1) * TILE]
    kp = qkv[:, width + p * TILE : width + (p + 1) * TILE]
    vp = qkv[:, 2 * width + p * TILE : 2 * width + (p + 1) * TILE]
    dp = dctx[:, p * TILE : (p + 1) * TILE]
    dq, dk, dv = [], 0.0, 0.0
    for a in range(2):
        sel = low if a == 0 else ~low
        qa = jnp.where(sel, qp, jnp.zeros_like(qp))
        da = jnp.where(sel, dp, jnp.zeros_like(dp))
        prob = jnp.exp(nt(qa, kp) + off - lse[:, 2 * p + a : 2 * p + a + 1])
        wg = nt(da, vp)
        inner = jnp.sum(prob * wg, axis=-1, keepdims=True)
        ds = (prob * (wg - inner)).astype(BF)
        w = prob.astype(BF)
        dq.append(nn(ds, kp))
        dk = dk + tn(ds, qa)
        dv = dv + tn(w, da)
    dq = jnp.where(low, dq[0], dq[1]) * SCALE
    return dq.astype(BF), dk[0:total].astype(BF), dv[0:total].astype(BF)


def attention_back_kernel(sizes, *refs):
    nctx, ntp, ndp, main, width, rows, padded = sizes
    qkv, dctx, lse, n1, x_in, dmid, wqkv, vec, g_out, vgrad, ub_own, ub_oth = refs[:12]
    ig, g_own, g_oth, dqkv = refs[12:]
    body = nctx * main
    total = body + EXTRA
    for p in range(3):
        for i, v in enumerate(pair_back(p, width, total, body, qkv, dctx, lse)):
            dqkv[:, i * width + p * TILE : i * width + (p + 1) * TILE] = v
    d = dqkv[...]
    bias = jnp.sum(d.astype(F32), axis=0, keepdims=True)
    g = tn(n1[...], d)
    go = g_out[...]
    own, oth = disassemble([tile(g, i) for i in range(9)], [tile(go, i) for i in range(3)])
    for to, tiles in ((g_own, own), (g_oth, oth)):
        for j in range(6):
            for e in range(ndp):
                to[j // 2, e, 0:rows, (j % 2) * TILE : (j % 2 + 1) * TILE] = (
                    tiles[j][e * rows : (e + 1) * rows].astype(BF)
                )
    dn1 = nt(d, wqkv[...])
    xhat, r = norm_stats(x_in[...])
    grad = dmid[...] + norm_back(dn1 * vec[1:2, :], xhat, r)
    ig[...] = grad.astype(BF)
    gains = jnp.sum(dn1 * xhat, axis=0, keepdims=True)
    shifts = jnp.sum(dn1, axis=0, keepdims=True)
    vecs = [gains, shifts] + [vgrad[i : i + 1, :] for i in range(2, 6)]
    zero = [jnp.zeros((1, TILE), F32)] * 3
    bias_own, bias_oth = disassemble([tile(bias, i) for i in range(9)], zero)
    for to, tiles, ub in ((g_own, bias_own, ub_own), (g_oth, bias_oth, ub_oth)):
        rows_ = [tile(v, i) for v in vecs for i in range(3)] + tiles
        rows_ += [ub[0:1, i * TILE : (i + 1) * TILE] for i in range(6)]
        for side in range(2):
            block = jnp.zeros((EXTRA, TILE), F32)
            for i, v in enumerate(rows_[side * EXTRA : (side + 1) * EXTRA]):
                block = jnp.where(row_is(block.shape, i), v, block)
            for e in range(ndp):
                to[3, e, 0:EXTRA, side * TILE : (side + 1) * TILE] = block.astype(BF)
                if padded > EXTRA:
                    to[3, e, EXTRA:padded, side * TILE : (side + 1) * TILE] = jnp.zeros(
                        (padded - EXTRA, TILE), BF
                    )


def sum_core_kernel(n, own, oth, *outs):
    me = lax.axis_index("ctx")
    for k in range(n):
        outs[k][...] = (own[me ^ k].astype(F32) + oth[me ^ k].astype(F32)).astype(BF)


def sum_ctx_kernel(n, ndp, *refs):
    me = lax.axis_index("dp")
    if len(refs) > n + ndp:
        refs[-1][...] = refs[n][...]
        refs = refs[:n] + refs[n + 1 : -1]
    for k in range(ndp):
        v = refs[0][me ^ k].astype(F32)
        for i in range(1, n):
            v = v + refs[i][me ^ k].astype(F32)
        refs[n + k][...] = v.astype(BF)


def sum_dp(refs):
    v = refs[0][...].astype(F32)
    for r in refs[1:]:
        v = v + r[...].astype(F32)
    return v.astype(BF)


def sum_dp_kernel(n, *refs):
    out = refs[2 * n]
    cols = refs[0].shape[1]
    out[:, :cols] = sum_dp(refs[:n])
    out[:, cols:] = sum_dp(refs[n : 2 * n])


def returns_kernel(sizes, bo, ig, *outs):
    nctx, ntp, ndp, main, width, rows, padded = sizes
    span = main + EXTRA
    for k in range(nctx):
        at = slice(k * main, (k + 1) * main)
        for i, src in enumerate((bo, ig)):
            outs[k][i * span : i * span + main, :] = src[at, :]
            outs[k][i * span + main : (i + 1) * span, :] = src[nctx * main :, :]


def stack_kernel(*refs):
    out = refs[-1]
    for i, r in enumerate(refs[:-1]):
        out[i] = r[...]


def grads_kernel(sizes, *refs):
    nctx, ntp, ndp, main, width, rows, padded = sizes
    parts, refs = refs[:nctx], refs[nctx:]
    gq, gk, gv, gqb, gvb, go, gu, gub, gd = refs[:9]
    gvec, f, f2 = refs[9:15], refs[15], refs[16]
    me, me_d = lax.axis_index("ctx"), lax.axis_index("dp")
    half = f2.shape[2]
    for k in range(nctx):
        f2[me ^ k] = parts[k][:, :half].astype(F32)
        f[me ^ k] = parts[k][:, half:].astype(F32)
    for j in range(2):
        gu[:, j * half : (j + 1) * half] = f2[j, 0:rows, :]
        gd[:, j * half : (j + 1) * half] = f2[2 + j, 0:rows, :]
    q01, k01 = f[0, 0:rows, 0:TILE], f[0, 0:rows, TILE:]
    v01, o01 = f[1, 0:rows, 0:TILE], f[1, 0:rows, TILE:]
    qk2, vo2 = f[2, 0:rows, 0:TILE], f[2, 0:rows, TILE:]
    gq[:, 0:TILE] = q01
    gq[:, TILE:] = qk2[:, 0:HD]
    gk[:, 0:TILE] = k01
    gk[:, TILE:] = swap(qk2)[:, 0:HD]
    gv[:, 0:TILE] = v01
    gv[:, TILE:] = vo2[:, 0:HD]
    go[0:TILE, :] = jnp.transpose(o01)
    go[TILE:, :] = jnp.transpose(vo2)[HD:, :]
    ex = [f[3, 0:EXTRA, 0:TILE], f[3, 0:EXTRA, TILE:]]

    def line(i):
        return ex[i // EXTRA][i % EXTRA : i % EXTRA + 1, :]

    for i in range(6):
        v = jnp.concatenate([line(3 * i), line(3 * i + 1), line(3 * i + 2)], axis=1)
        v = jnp.broadcast_to(v, (8, width))
        v = pltpu.roll(v, lax.rem(width - me_d * rows, width), axis=1)
        gvec[i][...] = v[0, 0:rows]
    b = [line(18 + i) for i in range(6)]
    gqb[...] = jnp.concatenate([b[0], b[4][:, 0:HD]], axis=1)[0]
    gvb[...] = jnp.concatenate([b[2], b[5][:, 0:HD]], axis=1)[0]
    gub[...] = jnp.concatenate([line(24 + i) for i in range(6)], axis=1)[0]


def unpack_kernel(sizes, *refs):
    nctx, ntp, ndp, main, width, rows, padded = sizes
    own, oth, refs = refs[:nctx], refs[nctx], refs[nctx + 1 :]
    kept, mask, outs, refs = refs[:2], refs[2], refs[3:5], refs[5:]
    stage, tail, valid, sem = refs
    images = nctx * ntp
    me_c, me_t = lax.axis_index("ctx"), lax.axis_index("tp")
    where = [(me_c ^ k) * ntp + t for t in (me_t, 1 - me_t) for k in range(nctx)]
    sources = [own[k] for k in range(nctx)] + [oth.at[k] for k in range(nctx)]
    blocks = main // BLOCK
    span = main + EXTRA
    last = pl.ds(main * images, images)
    gets = [pltpu.make_async_copy(kept[i].at[last, :], tail.at[i], sem.at[2, i]) for i in range(2)]
    gets.append(pltpu.make_async_copy(mask, valid, sem.at[2, 2]))
    for c in gets:
        c.start()

    def hit(r, c):
        img = where[-1]
        for j in range(images - 1):
            img = jnp.where(c // BLOCK == j, where[j], img)
        return r == (c % BLOCK) * images + img

    put = one_hot((images * BLOCK, images * BLOCK), hit)
    copies = []
    for i in range(2):
        for b in range(blocks):
            lo = i * span + b * BLOCK
            got = jnp.concatenate([src[lo : lo + BLOCK, :] for src in sources], axis=0)
            at = pl.ds(b * BLOCK * images, BLOCK * images)
            stage[i, at, :] = nn(put, got)
            copies.append(pltpu.make_async_copy(stage.at[i, at, :], outs[i].at[at, :], sem.at[i, b]))
            copies[-1].start()
    for c in gets:
        c.wait()
    for i in range(2):
        for src, img in zip(sources, where):
            got = src[i * span + main : (i + 1) * span, :].astype(F32)[0:1, :]
            stage[i, pl.ds(main * images + img, 1), :] = jnp.where(
                valid[img, main] > 0, got, tail[i, pl.ds(img, 1), :]
            )
        copies.append(pltpu.make_async_copy(stage.at[i, last, :], outs[i].at[last, :], sem.at[i, blocks]))
        copies[-1].start()
    for c in copies:
        c.wait()


def xor(n, k):
    return [(i, i ^ k) for i in range(n)]


def over(axis, n, items):
    return [items[0]] + [lax.ppermute(items[k], axis, xor(n, k)) for k in range(1, n)]


def body(nctx, ntp, ndp, *args):
    (tokens, valid_mask, cotangent, w_query, w_key, w_value, query_bias, value_bias, w_out, w_up, up_bias, w_down) = args[:12]
    vecs = args[12:]
    images, slots, width = tokens.shape
    main = slots - 1
    rows = w_query.shape[0]
    padded = -(-rows // EXTRA) * EXTRA
    ff = w_up.shape[1]
    p1_cols = 4 * w_query.shape[1]
    sizes = (nctx, ntp, ndp, main, width, rows, padded)
    total = nctx * main + EXTRA
    keys = -(-total // TILE) * TILE
    stage = BF if rows % 16 == 0 else F32
    flip = xor(ntp, 1)
    tok = jnp.transpose(tokens, (1, 0, 2)).reshape(slots * images, width)
    cot = jnp.transpose(cotangent, (1, 0, 2)).reshape(slots * images, width)

    def one(f):
        return functools.partial(f, sizes)

    def other(v):
        return lax.ppermute(v, "tp", flip)

    def held(arrays):
        return [
            (pltpu.SMEM if v.dtype == jnp.int32 else pltpu.VMEM)(v.shape, v.dtype) for v in arrays
        ] + [pltpu.SemaphoreType.DMA((len(arrays),))]

    def gather_dp(name, piece, after):
        v = piece[None]
        stride = ndp // 2
        while stride > 1:
            v = call(
                name,
                functools.partial(join_kernel, "dp", stride),
                sds((2 * v.shape[0],) + v.shape[1:], v.dtype),
                after=after,
            )(v, lax.ppermute(v, "dp", xor(ndp, stride)))
            stride //= 2
        return v, lax.ppermute(v, "dp", xor(ndp, 1))

    sources = [w_query, w_key, w_value, w_out, w_up, jnp.transpose(w_down), query_bias, value_bias, up_bias, *vecs]
    p1, p2q = call(
        "pack_weights",
        functools.partial(pack_weights_kernel, sizes, len(sources)),
        [sds((padded + EXTRA, p1_cols), BF), sds((padded, ff // 2), BF)],
        scratch=held(sources),
        mib=60,
        raw=range(len(sources)),
    )(*sources)
    sources = [tok, cot, valid_mask]
    scratch = held(sources)
    scratch[1] = pltpu.VMEM((images, width), F32)
    sent = call(
        "pack_slots",
        one(pack_slots_kernel),
        [sds((main + EXTRA, width), BF)] * nctx,
        scratch=scratch,
        mib=60,
        raw=range(3),
        after=[p1],
    )(*sources)
    t_in = over("ctx", nctx, sent)
    w2q = gather_dp("join_quarter", p2q, [sent[0]])
    sent = call(
        "pack_cotangent",
        one(pack_slots_kernel),
        [sds((main, width), BF)] * nctx,
        scratch=held([cot]),
        mib=60,
        raw=range(1),
        after=[w2q[0]],
    )(cot)
    w1 = gather_dp("join_attn", p1, [w2q[0], sent[0], *t_in[1:]])
    c_in = over("ctx", nctx, sent)
    w2q = call(
        "merge_quarter",
        one(merge_quarter_kernel),
        sds((width, ff // 2), BF),
        scratch=[pltpu.VMEM((width, ff // 2), stage)],
        after=[w1[0], *c_in[1:]],
    )(*w2q)
    w1_own = call(
        "merge_attn",
        one(merge_attn_kernel),
        sds((width + EXTRA, p1_cols), BF),
        scratch=[pltpu.VMEM((width, p1_cols), stage)],
        after=[w2q],
    )(*w1)
    w2q = over("ctx", nctx, [w2q] * nctx)
    x, mid, n1, n2, qkv, ctx, lse, wqkv, wot, vec, ub, cot_in = call(
        "attention",
        one(attention_kernel),
        [
            sds((total, width), F32), sds((total, width), F32), sds((total, width), BF), sds((total, width), BF),
            sds((keys, 3 * width), BF), sds((total, width), BF), sds((total, TILE), F32),
            sds((width, 3 * width), BF), sds((width, width), BF), sds((EXTRA, width), F32), sds((8, 2 * ff), F32),
            sds((total, width), BF),
        ],
        mib=32,
    )(*t_in, *c_in, w1_own, other(w1_own))
    w2_own = call(
        "merge_ff", functools.partial(merge_ff_kernel, nctx), sds((width, 2 * ff), BF), after=[vec]
    )(*w2q)
    w2_oth = other(w2_own)
    ff_grads = sds((4, ndp, padded, ff // 2), BF)

    def mlp_half(name, side, w, after=()):
        return call(
            name,
            functools.partial(mlp_half_kernel, sizes, side),
            [sds((total, ff), BF), sds((total, ff), BF), sds((8, ff), F32), ff_grads],
            mib=32,
            after=after,
        )(n2, cot_in, w, ub)

    hid_own, hgr_own, ub_own, g2_own = mlp_half("mlp_own", 0, w2_own)
    hid_oth, hgr_oth, ub_oth, g2_oth = mlp_half("mlp_oth", 1, w2_oth, [ub_own])
    bo, dmid, dctx, g_out, vgrad = call(
        "mlp_sums",
        one(mlp_sums_kernel),
        [
            sds((total, width), BF), sds((total, width), F32), sds((total, width), BF), sds((width, width), F32),
            sds((EXTRA, width), F32),
        ],
        mib=32,
    )(mid, ctx, wot, vec, cot_in, w2_own, w2_oth, hid_own, hid_oth, hgr_own, hgr_oth)

    def core_sums(name, own, oth, after=()):
        outs = [sds(own.shape[1:], BF)] * nctx
        return call(name, functools.partial(sum_core_kernel, nctx), outs, after=after)(own, other(oth))

    def ctx_sums(name, s, through=(), after=()):
        outs = [sds(s[0].shape[1:], BF)] * ndp + [sds(v.shape, v.dtype) for v in through]
        return call(name, functools.partial(sum_ctx_kernel, nctx, ndp), outs, after=after)(*s, *through)

    def by_image(v):
        return jnp.transpose(v.reshape(slots, images, width), (1, 0, 2))

    s2_send = core_sums("sum_core_ff", g2_own, g2_oth, after=[vgrad])
    s2 = over("ctx", nctx, s2_send)
    ig, g1_own, g1_oth = call(
        "attention_back",
        one(attention_back_kernel),
        [sds((total, width), BF)] + [sds((4, ndp, padded, 2 * TILE), BF)] * 2,
        scratch=[pltpu.VMEM((total, 3 * width), BF)],
        mib=32,
        after=[s2_send[0]],
    )(qkv, dctx, lse, n1, x, dmid, wqkv, vec, g_out, vgrad, ub_own, ub_oth)
    *u2_send, g1_oth = ctx_sums("sum_ctx_ff", s2, through=[g1_oth], after=[g1_own])
    s1_send = core_sums("sum_core_attn", g1_own, g1_oth)
    s1 = over("ctx", nctx, s1_send)
    u2 = over("dp", ndp, u2_send)
    back = call(
        "returns",
        one(returns_kernel),
        [sds((2 * (main + EXTRA), width), BF)] * nctx,
        after=[s1_send[0]],
    )(bo, ig)
    back = over("ctx", nctx, back)
    u1_send = ctx_sums("sum_ctx_attn", s1, after=[back[0]])
    u1 = over("dp", ndp, u1_send)
    summed = call(
        "sum_dp",
        functools.partial(sum_dp_kernel, ndp),
        sds((padded, ff // 2 + 2 * TILE), BF),
    )(*u2, *u1)
    shares = over("ctx", nctx, [summed] * nctx)
    stacked = call("stack", stack_kernel, sds((nctx,) + back[0].shape, BF), after=[summed])(*back)
    block_out, input_grad = call(
        "place_slots",
        one(unpack_kernel),
        [sds(tok.shape, F32)] * 2,
        scratch=[
            pltpu.VMEM((2,) + tok.shape, F32),
            pltpu.VMEM((2, images, width), F32),
            pltpu.SMEM(valid_mask.shape, valid_mask.dtype),
            pltpu.SemaphoreType.DMA((3, max(main // BLOCK + 1, 3))),
        ],
        raw=range(nctx + 1, nctx + 4),
        raw_out=True,
    )(*back, other(stacked), tok, cot, valid_mask)
    gq, gk, gv, gqb, gvb, go, gu, gub, gd, *gvec = call(
        "place_grads",
        one(grads_kernel),
        [
            sds(w_query.shape, F32), sds(w_key.shape, F32), sds(w_value.shape, F32),
            sds(query_bias.shape, F32), sds(value_bias.shape, F32), sds(w_out.shape, F32),
            sds(w_up.shape, F32), sds(up_bias.shape, F32), sds((rows, ff), F32),
        ]
        + [sds((rows,), F32)] * 6,
        scratch=[
            pltpu.VMEM((nctx, padded, 2 * TILE), F32),
            pltpu.VMEM((nctx, padded, ff // 2), F32),
        ],
    )(*shares)
    return (by_image(block_out), by_image(input_grad), gq, gk, gv, gqb, gvb, go, gu, gub, jnp.transpose(gd), *gvec)


def solution(mesh):
    rows, cols, tp, dp = P("dp", "tp"), P("tp", "dp"), P("tp"), P("dp")
    act = P("dp", "ctx", None)
    return jax.shard_map(
        functools.partial(body, mesh.shape["ctx"], mesh.shape["tp"], mesh.shape["dp"]),
        mesh=mesh,
        in_specs=(act, P("dp", "ctx"), act, rows, rows, rows, tp, tp, cols, rows, tp, cols) + (dp,) * 6,
        out_specs=(act, act, rows, rows, rows, tp, tp, cols, rows, tp, cols) + (dp,) * 6,
        check_vma=False,
    )
```

```python
import functools

import jax
import jax.numpy as jnp
from jax import lax
from jax.experimental import pallas as pl
from jax.experimental.pallas import tpu as pltpu
from jax.sharding import PartitionSpec as P

HD = 64
EPS = 1e-06
SCALE = 0.125
FLOOR = -1e30
BF = jnp.bfloat16
F32 = jnp.float32
TILE = 128
TIMES = {
    "pack_weights": 2.0, "pack_slots": 3.0, "pack_cotangent": 2.0, "attention": 0.0, "mlp_own": 4.0, "mlp_oth": 4.0, "mlp_sums": 2.0, "attention_back": 11.0,
    "place_grads": 1.0, "place_slots": 2.3, "join_quarter": 20.0, "sum_ctx_attn": 50.0, "sum_ctx_ff": 50.0,
}
EXTRA = 16


def call(name, kernel, out_shape, scratch=(), mib=8, after=(), raw=()):
    after = list(after)

    def ordered(*refs):
        kernel(*refs[len(after) :])

    def run(*args):
        specs = [pl.BlockSpec(memory_space=pl.ANY)] * len(after) + [
            pl.BlockSpec(memory_space=pltpu.HBM if i in raw else pltpu.VMEM)
            for i in range(len(args))
        ]
        return pl.pallas_call(
            ordered,
            name=name,
            out_shape=out_shape,
            in_specs=specs,
            out_specs=jax.tree.map(lambda _: pl.BlockSpec(memory_space=pltpu.VMEM), out_shape),
            scratch_shapes=list(scratch),
            compiler_params=pltpu.CompilerParams(vmem_limit_bytes=mib << 20),
            cost_estimate=pl.CostEstimate(
                flops=int(TIMES.get(name, 0.2) * 1.15e9), bytes_accessed=1, transcendentals=0
            ),
        )(*after, *args)

    return run


def sds(shape, dtype):
    return jax.ShapeDtypeStruct(shape, dtype)


def nn(a, b):
    return lax.dot_general(a, b, (((1,), (0,)), ((), ())), preferred_element_type=F32)


def nt(a, b):
    return lax.dot_general(a, b, (((1,), (1,)), ((), ())), preferred_element_type=F32)


def tn(a, b):
    return lax.dot_general(a, b, (((0,), (0,)), ((), ())), preferred_element_type=F32)


def swap(v):
    return pltpu.roll(v, HD, axis=1)


def low_lanes(shape):
    return lax.broadcasted_iota(jnp.int32, shape, 1) < HD


def row_is(shape, row):
    return lax.broadcasted_iota(jnp.int32, shape, 0) == row


def tile(v, i):
    return v[:, i * TILE : (i + 1) * TILE]


def assemble(own, oth):
    low = low_lanes((own.shape[0], TILE))
    own_qk, own_vo, oth_qk, oth_vo = tile(own, 4), tile(own, 5), tile(oth, 4), tile(oth, 5)
    qkv = [
        tile(own, 0), tile(oth, 0), jnp.where(low, own_qk, swap(oth_qk)),
        tile(own, 1), tile(oth, 1), jnp.where(low, swap(own_qk), oth_qk),
        tile(own, 2), tile(oth, 2), jnp.where(low, own_vo, swap(oth_vo)),
    ]
    out = [tile(own, 3), tile(oth, 3), jnp.where(low, swap(own_vo), oth_vo)]
    return qkv, out


def disassemble(qkv, out):
    low = low_lanes(qkv[0].shape)
    own = [qkv[0], qkv[3], qkv[6], out[0], jnp.where(low, qkv[2], swap(qkv[5])), jnp.where(low, qkv[8], swap(out[2]))]
    oth = [qkv[1], qkv[4], qkv[7], out[1], jnp.where(low, swap(qkv[2]), qkv[5]), jnp.where(low, swap(qkv[8]), out[2])]
    return own, oth


def norm_stats(v):
    mean = jnp.mean(v, axis=-1, keepdims=True)
    centered = v - mean
    r = lax.rsqrt(jnp.mean(centered * centered, axis=-1, keepdims=True) + EPS)
    return centered * r, r


def norm_back(e, xhat, r):
    return r * (
        e
        - jnp.mean(e, axis=-1, keepdims=True)
        - xhat * jnp.mean(e * xhat, axis=-1, keepdims=True)
    )


def gelu_pair(v):
    a = jnp.abs(v)
    t = 1.0 / (1.0 + (0.3275911 * 0.7071067811865476) * a)
    g = jnp.exp(-0.5 * v * v)
    poly = t * (
        0.254829592 + t * (-0.284496736 + t * (1.421413741 + t * (-1.453152027 + t * 1.061405429)))
    )
    tail = 0.5 * poly * g
    phi = jnp.where(v < 0, tail, 1.0 - tail)
    return v * phi, phi + v * (0.3989422804014327 * g)


BLOCK = 16


def one_hot(shape, hit):
    r, c = (lax.broadcasted_iota(jnp.int32, shape, i) for i in range(2))
    return hit(r, c).astype(F32).astype(BF)


def picker(wanted, images):
    def hit(r, c):
        img = wanted[-1]
        for k in range(len(wanted) - 1):
            img = jnp.where(r // BLOCK == k, wanted[k], img)
        return c == (r % BLOCK) * images + img

    return one_hot((len(wanted) * BLOCK, images * BLOCK), hit)


def take_images(ref, outs, at, pick, images, count):
    for b in range(count // BLOCK):
        got = nn(pick, ref[b * BLOCK * images : (b + 1) * BLOCK * images, :].astype(BF)).astype(BF)
        for k in range(len(outs)):
            outs[k][at + b * BLOCK : at + (b + 1) * BLOCK, :] = got[k * BLOCK : (k + 1) * BLOCK]


def fetch(sources, held, sem):
    copies = [pltpu.make_async_copy(sources[i], held[i], sem.at[i]) for i in range(len(sources))]
    for c in copies:
        c.start()
    return copies


def pack_weights_kernel(sizes, count, *refs):
    nctx, ntp, ndp, main, width, rows, padded = sizes
    sources, (p1, p2q), refs = refs[:count], refs[count : count + 2], refs[count + 2 :]
    held, sem = refs[:count], refs[count]
    copies = fetch(sources, held, sem)
    wq, wk, wv, wo, wu, wd, qb, vb, ub = held[:9]
    vecs = held[9:]
    me_c, me_d = lax.axis_index("ctx"), lax.axis_index("dp")
    for c in copies:
        c.wait()
    if padded > rows:
        p1[0:padded, :] = jnp.zeros((padded, p1.shape[1]), BF)
        p2q[...] = jnp.zeros(p2q.shape, BF)
    quarter = p2q.shape[1]
    for j in range(nctx):
        src = (wu, wd)[j // 2][:, (j % 2) * quarter : (j % 2 + 1) * quarter]

        @pl.when(me_c == j)
        def _(src=src):
            p2q[0:rows, :] = src

    def put(lo, value):
        p1[0:rows, lo : lo + value.shape[1]] = value.astype(BF)

    fq, fk, fv = wq[...].astype(F32), wk[...].astype(F32), wv[...].astype(F32)
    fo = jnp.transpose(wo[...].astype(F32))
    for i, w in enumerate((fq, fk, fv, fo)):
        put(i * TILE, tile(w, 0))
    put(4 * TILE, jnp.concatenate([fq[:, TILE:], fk[:, TILE:]], axis=1))
    put(5 * TILE, jnp.concatenate([fv[:, TILE:], fo[:, TILE:]], axis=1))
    cols = p1.shape[1]
    fqb, fvb = qb[...].astype(F32)[None, :], vb[...].astype(F32)[None, :]
    none = jnp.zeros((1, TILE), F32)
    short = jnp.zeros((1, HD), F32)
    bias = jnp.concatenate(
        [fqb[:, :TILE], none, fvb[:, :TILE], none, fqb[:, TILE:], short, fvb[:, TILE:], short], axis=1
    )
    spread = one_hot((rows, width), lambda r, c: c == r + rows * me_d)
    block = jnp.where(row_is((EXTRA, cols), 0), bias, 0.0)
    block = jnp.where(row_is((EXTRA, cols), 7), ub[...].astype(F32)[None, :], block)
    lanes = jnp.zeros((EXTRA, rows), F32)
    for i in range(6):
        lanes = jnp.where(row_is((EXTRA, rows), 1 + i), vecs[i][...].astype(F32)[None, :], lanes)
    lanes = nn(lanes.astype(BF), spread)
    p1[padded : padded + EXTRA, :] = block.astype(BF)
    mixed = jnp.where(
        (lax.broadcasted_iota(jnp.int32, (EXTRA, width), 0) - 1).astype(jnp.uint32) < 6,
        lanes,
        block[:, :width],
    )
    p1[padded : padded + EXTRA, 0:width] = mixed.astype(BF)


def pack_slots_kernel(sizes, *refs):
    nctx, ntp, ndp, main, width, rows, padded = sizes
    sources, sent, tails, refs = refs[:3], refs[3 : 3 + nctx], refs[3 + nctx], refs[4 + nctx :]
    held, sem = refs[:3], refs[3]
    copies = fetch(sources, held, sem)
    tok, cot, mask = held
    images = nctx * ntp
    me_c, me_t = lax.axis_index("ctx"), lax.axis_index("tp")
    wanted = [(me_c ^ k) * ntp + me_t for k in range(nctx)]
    pick = picker(wanted, images)
    for i in range(2):
        copies[i].wait()
        take_images(held[i], sent, i * (main + EXTRA), pick, images, main)
        tails[i] = held[i][main * images :, :]
    copies[2].wait()
    for k in range(nctx):
        gate = mask[wanted[k], main].astype(F32)
        te = tok[pl.ds(main * images + wanted[k], 1), :] * gate
        ce = cot[pl.ds(main * images + wanted[k], 1), :] * gate
        shape = (EXTRA, width)
        sent[k][main : main + EXTRA, :] = jnp.where(
            row_is(shape, 0), te, jnp.where(row_is(shape, 1), ce, 0.0)
        ).astype(BF)


def join_kernel(axis, stride, own, got, out):
    bit = lax.rem(lax.div(lax.axis_index(axis), stride), 2)
    for i in range(own.shape[0]):
        out[2 * i + bit] = own[i]
        out[2 * i + 1 - bit] = got[i]


def place_rows(outs, own, got, rows, stage):
    bit = lax.rem(lax.axis_index("dp"), 2)
    for i in range(own.shape[0]):
        for piece, last in ((own[i], bit), (got[i], 1 - bit)):
            at = pl.ds(pl.multiple_of((2 * i + last) * rows, 16 if rows % 16 == 0 else 8), rows)
            stage[at, :] = piece.astype(stage.dtype)[:rows]
    cols = outs[0].shape[1]
    for i, out in enumerate(outs):
        out[0 : stage.shape[0], :] = stage[:, i * cols : (i + 1) * cols].astype(BF)


def merge_quarter_kernel(sizes, own, got, out, stage):
    place_rows([out], own, got, sizes[5], stage)


def merge_attn_kernel(sizes, own, got, *refs):
    nctx, ntp, ndp, main, width, rows, padded = sizes
    outs, stage = refs[:-1], refs[-1]
    place_rows(outs, own, got, rows, stage)
    extra = own[0, padded:, :].astype(F32)
    for more in [own[i] for i in range(1, own.shape[0])] + [got[i] for i in range(own.shape[0])]:
        more = more[padded:, :].astype(F32)
        row = lax.broadcasted_iota(jnp.int32, more.shape, 0)
        extra += jnp.where((row > 0) & (row < 7), more, 0.0)
    for i, out in enumerate(outs):
        out[width:, :] = extra[:, 2 * i * TILE : 2 * (i + 1) * TILE].astype(BF)


def merge_ff_kernel(nctx, *refs):
    out = refs[nctx]
    me_c = lax.axis_index("ctx")
    for k in range(nctx):
        quarter = refs[k].shape[1]
        out[:, pl.ds(pl.multiple_of((me_c ^ k) * quarter, quarter), quarter)] = refs[k][...]


def attention_kernel(sizes, *refs):
    nctx, ntp, ndp, main, width, rows, padded = sizes
    t_in, own_in, oth_in, refs = refs[:nctx], refs[nctx : nctx + 3], refs[nctx + 3 : nctx + 6], refs[nctx + 6 :]
    x_out, mid_out, n1_out, n2_out, qkv, ctx, lse, wqkv, wot, vec, ub, cot = refs
    body = nctx * main
    total = body + EXTRA
    own, oth = (jnp.concatenate([v[...] for v in part], axis=1).astype(F32) for part in (own_in, oth_in))
    tiles, outs = assemble(own, oth)
    for i, v in enumerate(tiles):
        wqkv[:, i * TILE : (i + 1) * TILE] = v[:width].astype(BF)
    for i, v in enumerate(outs):
        wot[:, i * TILE : (i + 1) * TILE] = v[:width].astype(BF)
    bias = jnp.concatenate([v[width : width + 1] for v in tiles], axis=1)
    vec_sum = own[width:, :width]
    vec[...] = vec_sum
    ub[...] = jnp.broadcast_to(
        jnp.concatenate([own[width + 7 : width + 8], oth[width + 7 : width + 8]], axis=1), ub.shape
    )
    extra = jnp.zeros((EXTRA, width), F32)
    for k in range(nctx):
        x_out[k * main : (k + 1) * main, :] = t_in[k][0:main, :].astype(F32)
        cot[k * main : (k + 1) * main, :] = t_in[k][main + EXTRA :, :]
        extra += t_in[k][main : main + EXTRA, :].astype(F32)
    x_out[body:, :] = jnp.where(row_is((EXTRA, width), 0), extra, 0.0)
    cot[body:, :] = jnp.where(row_is((EXTRA, width), 0), extra[1:2, :], 0.0).astype(BF)
    x = x_out[...]
    xhat, _ = norm_stats(x)
    n1 = (xhat * vec_sum[1:2, :] + vec_sum[2:3, :]).astype(BF)
    n1_out[...] = n1
    proj = nn(n1, wqkv[...]) + bias
    qkv[0:total, 0:width] = (proj[:, 0:width].astype(BF).astype(F32) * SCALE).astype(BF)
    qkv[0:total, width:] = proj[:, width:].astype(BF)
    keys = qkv.shape[0]
    qkv[total:, :] = jnp.zeros((keys - total, qkv.shape[1]), BF)
    off = jnp.where(lax.broadcasted_iota(jnp.int32, (1, keys), 1) > body, FLOOR, 0.0)
    low = low_lanes((total, TILE))
    lane = lax.broadcasted_iota(jnp.int32, (total, TILE), 1)
    all_lse = jnp.zeros((total, TILE), F32)
    for p in range(3):
        qp = qkv[0:total, p * TILE : (p + 1) * TILE]
        kp = qkv[:, width + p * TILE : width + (p + 1) * TILE]
        vp = qkv[:, 2 * width + p * TILE : 2 * width + (p + 1) * TILE]
        parts = []
        for a in range(2):
            qa = jnp.where(low if a == 0 else ~low, qp, jnp.zeros_like(qp))
            s = nt(qa, kp) + off
            m = jnp.max(s, axis=-1, keepdims=True)
            e = jnp.exp(s - m)
            l = jnp.sum(e, axis=-1, keepdims=True)
            w = (e * (1.0 / l)).astype(BF)
            parts.append(nn(w, vp))
            all_lse = jnp.where(lane == 2 * p + a, m + jnp.log(l), all_lse)
        ctx[:, p * TILE : (p + 1) * TILE] = jnp.where(low, parts[0], parts[1]).astype(BF)
    lse[...] = all_lse
    attended = nt(ctx[...], wot[...]) + vec_sum[5:6, :]
    valid = lax.broadcasted_iota(jnp.int32, (total, 1), 0) <= body
    middle = x_out[...] + jnp.where(valid, attended, 0.0)
    mid_out[...] = middle
    xhat2, _ = norm_stats(middle)
    n2_out[...] = (xhat2 * vec_sum[3:4, :] + vec_sum[4:5, :]).astype(BF)


def ff_half(n2v, dcot, w, ub, hid, hgr, ubgrad, grads, ndp, rows):
    half = w.shape[1] // 2
    quarter = half // 2
    for lo in range(0, half, 256):
        sl = slice(lo, lo + 256)
        pre = nn(n2v, w[:, sl]) + ub[0:1, sl]
        hc = nn(dcot, w[:, half + lo : half + lo + 256])
        act, slope = gelu_pair(pre)
        h = act.astype(BF)
        hg = (hc * slope).astype(BF)
        hid[:, sl] = h
        hgr[:, sl] = hg
        ubgrad[:, sl] = jnp.broadcast_to(jnp.sum(hg.astype(F32), axis=0, keepdims=True), (8, 256))
        for part, g in ((0, tn(n2v, hg).astype(BF)), (1, tn(dcot, h).astype(BF))):
            for d in range(ndp):
                for c in range(2):
                    col = lo + c * TILE
                    at = slice(col % quarter, col % quarter + TILE)
                    grads[2 * part + col // quarter, d, 0:rows, at] = (
                        g[d * rows : (d + 1) * rows, c * TILE : (c + 1) * TILE]
                    )


def mlp_half_kernel(sizes, side, n2, cot, w, ub, hid, hgr, ubgrad, grads):
    half = w.shape[1] // 2
    ff_half(
        n2[...], cot[...], w[...], ub[:, side * half : (side + 1) * half], hid, hgr, ubgrad, grads, sizes[2], sizes[5]
    )


def mlp_sums_kernel(sizes, mid, ctx, wot, vec, cot, w_own, w_oth, hid_own, hid_oth, hgr_own, hgr_oth, bo, dmid, dctx, g_out, vgrad):
    nctx, ntp, ndp, main, width, rows, padded = sizes
    body = nctx * main
    total = body + EXTRA
    half = w_own.shape[1] // 2
    dcot = cot[...]
    middle = mid[...]
    valid = lax.broadcasted_iota(jnp.int32, (total, 1), 0) <= body
    n2g = nt(hgr_own[...], w_own[:, :half]) + nt(hgr_oth[...], w_oth[:, :half])
    xhat, r = norm_stats(middle)
    back = norm_back(n2g * vec[3:4, :], xhat, r)
    middle_grad = dcot.astype(F32) + back
    dmid[...] = middle_grad
    agrad = jnp.where(valid, middle_grad, 0.0).astype(BF)
    dctx[...] = nn(agrad, wot[...]).astype(BF)
    g_out[...] = tn(agrad, ctx[...])
    mlp_out = nt(hid_own[...], w_own[:, half:]) + nt(hid_oth[...], w_oth[:, half:]) + vec[6:7, :]
    bo[...] = (middle + jnp.where(valid, mlp_out, 0.0)).astype(BF)
    shape = vgrad.shape
    v = jnp.where(row_is(shape, 2), jnp.sum(n2g * xhat, axis=0, keepdims=True), 0.0)
    v = jnp.where(row_is(shape, 3), jnp.sum(n2g, axis=0, keepdims=True), v)
    v = jnp.where(row_is(shape, 4), jnp.sum(agrad.astype(F32), axis=0, keepdims=True), v)
    v = jnp.where(row_is(shape, 5), jnp.sum(dcot.astype(F32), axis=0, keepdims=True), v)
    vgrad[...] = v


def pair_back(p, width, total, body, qkv, dctx, lse):
    keys = qkv.shape[0]
    off = jnp.where(lax.broadcasted_iota(jnp.int32, (1, keys), 1) > body, FLOOR, 0.0)
    low = low_lanes((total, TILE))
    qp = qkv[0:total, p * TILE : (p + 1) * TILE]
    kp = qkv[:, width + p * TILE : width + (p + 1) * TILE]
    vp = qkv[:, 2 * width + p * TILE : 2 * width + (p + 1) * TILE]
    dp = dctx[:, p * TILE : (p + 1) * TILE]
    dq, dk, dv = [], 0.0, 0.0
    for a in range(2):
        sel = low if a == 0 else ~low
        qa = jnp.where(sel, qp, jnp.zeros_like(qp))
        da = jnp.where(sel, dp, jnp.zeros_like(dp))
        prob = jnp.exp(nt(qa, kp) + off - lse[:, 2 * p + a : 2 * p + a + 1])
        wg = nt(da, vp)
        inner = jnp.sum(prob * wg, axis=-1, keepdims=True)
        ds = (prob * (wg - inner)).astype(BF)
        w = prob.astype(BF)
        dq.append(nn(ds, kp))
        dk = dk + tn(ds, qa)
        dv = dv + tn(w, da)
    dq = jnp.where(low, dq[0], dq[1]) * SCALE
    return dq.astype(BF), dk[0:total].astype(BF), dv[0:total].astype(BF)


def attention_back_kernel(sizes, *refs):
    nctx, ntp, ndp, main, width, rows, padded = sizes
    qkv, dctx, lse, n1, x_in, dmid, wqkv, vec, g_out, vgrad, ub_own, ub_oth = refs[:12]
    ig, g_own, g_oth, dqkv = refs[12:]
    body = nctx * main
    total = body + EXTRA
    for p in range(3):
        for i, v in enumerate(pair_back(p, width, total, body, qkv, dctx, lse)):
            dqkv[:, i * width + p * TILE : i * width + (p + 1) * TILE] = v
    d = dqkv[...]
    bias = jnp.sum(d.astype(F32), axis=0, keepdims=True)
    g = tn(n1[...], d)
    go = g_out[...]
    own, oth = disassemble([tile(g, i) for i in range(9)], [tile(go, i) for i in range(3)])
    for to, tiles in ((g_own, own), (g_oth, oth)):
        for j in range(6):
            for e in range(ndp):
                to[j // 2, e, 0:rows, (j % 2) * TILE : (j % 2 + 1) * TILE] = (
                    tiles[j][e * rows : (e + 1) * rows].astype(BF)
                )
    dn1 = nt(d, wqkv[...])
    xhat, r = norm_stats(x_in[...])
    grad = dmid[...] + norm_back(dn1 * vec[1:2, :], xhat, r)
    ig[...] = grad.astype(BF)
    gains = jnp.sum(dn1 * xhat, axis=0, keepdims=True)
    shifts = jnp.sum(dn1, axis=0, keepdims=True)
    vecs = [gains, shifts] + [vgrad[i : i + 1, :] for i in range(2, 6)]
    zero = [jnp.zeros((1, TILE), F32)] * 3
    bias_own, bias_oth = disassemble([tile(bias, i) for i in range(9)], zero)
    for to, tiles, ub in ((g_own, bias_own, ub_own), (g_oth, bias_oth, ub_oth)):
        rows_ = [tile(v, i) for v in vecs for i in range(3)] + tiles
        rows_ += [ub[0:1, i * TILE : (i + 1) * TILE] for i in range(6)]
        for side in range(2):
            block = jnp.zeros((EXTRA, TILE), F32)
            for i, v in enumerate(rows_[side * EXTRA : (side + 1) * EXTRA]):
                block = jnp.where(row_is(block.shape, i), v, block)
            for e in range(ndp):
                to[3, e, 0:EXTRA, side * TILE : (side + 1) * TILE] = block.astype(BF)
                if padded > EXTRA:
                    to[3, e, EXTRA:padded, side * TILE : (side + 1) * TILE] = jnp.zeros(
                        (padded - EXTRA, TILE), BF
                    )


def sum_core_kernel(n, own, oth, *outs):
    me = lax.axis_index("ctx")
    for k in range(n):
        outs[k][...] = (own[me ^ k].astype(F32) + oth[me ^ k].astype(F32)).astype(BF)


def sum_ctx_kernel(n, ndp, *refs):
    me = lax.axis_index("dp")
    for k in range(ndp):
        v = refs[0][me ^ k].astype(F32)
        for i in range(1, n):
            v = v + refs[i][me ^ k].astype(F32)
        refs[n + k][...] = v.astype(BF)


def halve(axis, stride, item, keep, send):
    bit = lax.rem(lax.div(lax.axis_index(axis), stride), 2)
    for j in range(keep.shape[0]):
        keep[j] = item(2 * j + bit).astype(BF)
        send[j] = item(2 * j + 1 - bit).astype(BF)


def sum_ctx_halves_kernel(n, *refs):
    terms, (keep, send) = refs[:n], refs[n:]

    def item(i):
        v = terms[0][i].astype(F32)
        for t in terms[1:]:
            v = v + t[i].astype(F32)
        return v

    halve("dp", 1, item, keep, send)


def add_halves_kernel(stride, own, got, keep, send):
    halve("dp", stride, lambda i: own[i].astype(F32) + got[i].astype(F32), keep, send)


def sum_dp_kernel(n, own, got, *refs):
    out = refs[n]
    cols = own.shape[2]
    out[:, :cols] = (own[0].astype(F32) + got[0].astype(F32)).astype(BF)
    v = refs[0][...].astype(F32)
    for r in refs[1:n]:
        v = v + r[...].astype(F32)
    out[:, cols:] = v.astype(BF)


def returns_kernel(sizes, bo, ig, out):
    nctx, ntp, ndp, main, width, rows, padded = sizes
    me = lax.axis_index("ctx")
    span = main + EXTRA
    for k in range(nctx):
        at = slice(k * main, (k + 1) * main)
        for i, src in enumerate((bo, ig)):
            out[me ^ k, i * span : i * span + main, :] = src[at, :]
            out[me ^ k, i * span + main : (i + 1) * span, :] = src[nctx * main :, :]


def hand_on_kernel(held, out):
    out[...] = held[...]


def grads_kernel(sizes, *refs):
    nctx, ntp, ndp, main, width, rows, padded = sizes
    parts, refs = refs[:nctx], refs[nctx:]
    gq, gk, gv, gqb, gvb, go, gu, gub, gd = refs[:9]
    gvec, f, f2 = refs[9:15], refs[15], refs[16]
    me, me_d = lax.axis_index("ctx"), lax.axis_index("dp")
    half = f2.shape[2]
    for k in range(nctx):
        f2[me ^ k] = parts[k][:, :half].astype(F32)
        f[me ^ k] = parts[k][:, half:].astype(F32)
    for j in range(2):
        gu[:, j * half : (j + 1) * half] = f2[j, 0:rows, :]
        gd[:, j * half : (j + 1) * half] = f2[2 + j, 0:rows, :]
    q01, k01 = f[0, 0:rows, 0:TILE], f[0, 0:rows, TILE:]
    v01, o01 = f[1, 0:rows, 0:TILE], f[1, 0:rows, TILE:]
    qk2, vo2 = f[2, 0:rows, 0:TILE], f[2, 0:rows, TILE:]
    gq[:, 0:TILE] = q01
    gq[:, TILE:] = qk2[:, 0:HD]
    gk[:, 0:TILE] = k01
    gk[:, TILE:] = swap(qk2)[:, 0:HD]
    gv[:, 0:TILE] = v01
    gv[:, TILE:] = vo2[:, 0:HD]
    go[0:TILE, :] = jnp.transpose(o01)
    go[TILE:, :] = jnp.transpose(vo2)[HD:, :]
    ex = [f[3, 0:EXTRA, 0:TILE], f[3, 0:EXTRA, TILE:]]

    def line(i):
        return ex[i // EXTRA][i % EXTRA : i % EXTRA + 1, :]

    for i in range(6):
        v = jnp.concatenate([line(3 * i), line(3 * i + 1), line(3 * i + 2)], axis=1)
        v = jnp.broadcast_to(v, (8, width))
        v = pltpu.roll(v, lax.rem(width - me_d * rows, width), axis=1)
        gvec[i][...] = v[0, 0:rows]
    b = [line(18 + i) for i in range(6)]
    gqb[...] = jnp.concatenate([b[0], b[4][:, 0:HD]], axis=1)[0]
    gvb[...] = jnp.concatenate([b[2], b[5][:, 0:HD]], axis=1)[0]
    gub[...] = jnp.concatenate([line(24 + i) for i in range(6)], axis=1)[0]


def unpack_kernel(sizes, own, oth, tails, mask, *refs):
    nctx, ntp, ndp, main, width, rows, padded = sizes
    outs, done, valid, sem = refs[:2], refs[2], refs[3], refs[4]
    images = nctx * ntp
    me_t = lax.axis_index("tp")
    where = [j * ntp + t for t in (me_t, 1 - me_t) for j in range(nctx)]
    sources = [v.at[j] for v in (own, oth) for j in range(nctx)]
    span = main + EXTRA
    get_valid = pltpu.make_async_copy(mask, valid, sem.at[0])
    get_valid.start()

    def hit(r, c):
        img = where[-1]
        for j in range(images - 1):
            img = jnp.where(c // BLOCK == j, where[j], img)
        return r == (c % BLOCK) * images + img

    put = one_hot((images * BLOCK, images * BLOCK), hit)
    for i in range(2):
        for b in range(main // BLOCK):
            lo = i * span + b * BLOCK
            got = jnp.concatenate([src[lo : lo + BLOCK, :] for src in sources], axis=0)
            outs[i][b * BLOCK * images : (b + 1) * BLOCK * images, :] = nn(put, got)
    get_valid.wait()
    for i in range(2):
        for src, img in zip(sources, where):
            got = src[i * span + main : (i + 1) * span, :].astype(F32)[0:1, :]
            outs[i][pl.ds(main * images + img, 1), :] = jnp.where(
                valid[img, main] > 0, got, tails[i, pl.ds(img, 1), :]
            )
    done[...] = jnp.zeros_like(done)


def xor(n, k):
    return [(i, i ^ k) for i in range(n)]


def over(axis, n, items):
    return [items[0]] + [lax.ppermute(items[k], axis, xor(n, k)) for k in range(1, n)]


def body(nctx, ntp, ndp, *args):
    (tokens, valid_mask, cotangent, w_query, w_key, w_value, query_bias, value_bias, w_out, w_up, up_bias, w_down) = args[:12]
    vecs = args[12:]
    images, slots, width = tokens.shape
    main = slots - 1
    rows = w_query.shape[0]
    padded = -(-rows // EXTRA) * EXTRA
    ff = w_up.shape[1]
    p1_cols = 4 * w_query.shape[1]
    sizes = (nctx, ntp, ndp, main, width, rows, padded)
    total = nctx * main + EXTRA
    keys = -(-total // TILE) * TILE
    stage = BF if rows % 16 == 0 else F32
    flip = xor(ntp, 1)
    tok = jnp.transpose(tokens, (1, 0, 2)).reshape(slots * images, width)
    cot = jnp.transpose(cotangent, (1, 0, 2)).reshape(slots * images, width)

    def one(f):
        return functools.partial(f, sizes)

    def other(v):
        return lax.ppermute(v, "tp", flip)

    def held(arrays):
        return [
            (pltpu.SMEM if v.dtype == jnp.int32 else pltpu.VMEM)(v.shape, v.dtype) for v in arrays
        ] + [pltpu.SemaphoreType.DMA((len(arrays),))]

    def gather_dp(name, piece, after):
        v = piece[None]
        stride = ndp // 2
        while stride > 1:
            v = call(
                name,
                functools.partial(join_kernel, "dp", stride),
                sds((2 * v.shape[0],) + v.shape[1:], v.dtype),
                after=after,
            )(v, lax.ppermute(v, "dp", xor(ndp, stride)))
            stride //= 2
        return v, lax.ppermute(v, "dp", xor(ndp, 1))

    sources = [w_query, w_key, w_value, w_out, w_up, jnp.transpose(w_down), query_bias, value_bias, up_bias, *vecs]
    p1, p2q = call(
        "pack_weights",
        functools.partial(pack_weights_kernel, sizes, len(sources)),
        [sds((padded + EXTRA, p1_cols), BF), sds((padded, ff // 2), BF)],
        scratch=held(sources),
        mib=60,
        raw=range(len(sources)),
    )(*sources)
    sources = [tok, cot, valid_mask]
    *sent, tails = call(
        "pack_slots",
        one(pack_slots_kernel),
        [sds((2 * main + EXTRA, width), BF)] * nctx + [sds((2, images, width), F32)],
        scratch=held(sources),
        mib=60,
        raw=range(3),
        after=[p1],
    )(*sources)
    t_in = over("ctx", nctx, sent)
    w2q = call(
        "merge_quarter",
        one(merge_quarter_kernel),
        sds((width, ff // 2), BF),
        scratch=[pltpu.VMEM((width, ff // 2), stage)],
        after=t_in[1:],
    )(*gather_dp("join_quarter", p2q, [sent[0]]))
    w1 = gather_dp("join_attn", p1, [sent[0]])
    w2q = over("ctx", nctx, [w2q] * nctx)
    w1_own = call(
        "merge_attn",
        one(merge_attn_kernel),
        [sds((width + EXTRA, 2 * TILE), BF)] * (p1_cols // (2 * TILE)),
        scratch=[pltpu.VMEM((width, p1_cols), stage)],
        after=w2q[1:-1],
    )(*w1)
    x, mid, n1, n2, qkv, ctx, lse, wqkv, wot, vec, ub, cot_in = call(
        "attention",
        one(attention_kernel),
        [
            sds((total, width), F32), sds((total, width), F32), sds((total, width), BF), sds((total, width), BF),
            sds((keys, 3 * width), BF), sds((total, width), BF), sds((total, TILE), F32),
            sds((width, 3 * width), BF), sds((width, width), BF), sds((EXTRA, width), F32), sds((8, 2 * ff), F32),
            sds((total, width), BF),
        ],
        mib=32,
    )(*t_in, *w1_own, *[other(v) for v in w1_own])
    w2_own = call(
        "merge_ff", functools.partial(merge_ff_kernel, nctx), sds((width, 2 * ff), BF), after=[vec]
    )(*w2q)
    w2_oth = other(w2_own)
    ff_grads = sds((4, ndp, padded, ff // 2), BF)

    def mlp_half(name, side, w, after=()):
        return call(
            name,
            functools.partial(mlp_half_kernel, sizes, side),
            [sds((total, ff), BF), sds((total, ff), BF), sds((8, ff), F32), ff_grads],
            mib=32,
            after=after,
        )(n2, cot_in, w, ub)

    hid_own, hgr_own, ub_own, g2_own = mlp_half("mlp_own", 0, w2_own)
    hid_oth, hgr_oth, ub_oth, g2_oth = mlp_half("mlp_oth", 1, w2_oth, [ub_own])
    bo, dmid, dctx, g_out, vgrad = call(
        "mlp_sums",
        one(mlp_sums_kernel),
        [
            sds((total, width), BF), sds((total, width), F32), sds((total, width), BF), sds((width, width), F32),
            sds((EXTRA, width), F32),
        ],
        mib=32,
    )(mid, ctx, wot, vec, cot_in, w2_own, w2_oth, hid_own, hid_oth, hgr_own, hgr_oth)

    def core_sums(name, own, oth, after=()):
        outs = [sds(own.shape[1:], BF)] * nctx
        return call(name, functools.partial(sum_core_kernel, nctx), outs, after=after)(own, other(oth))

    def by_image(v):
        return jnp.transpose(v.reshape(slots, images, width), (1, 0, 2))

    s2_send = core_sums("sum_core_ff", g2_own, g2_oth, after=[vgrad])
    s2 = over("ctx", nctx, s2_send)
    ig, g1_own, g1_oth = call(
        "attention_back",
        one(attention_back_kernel),
        [sds((total, width), BF)] + [sds((4, ndp, padded, 2 * TILE), BF)] * 2,
        scratch=[pltpu.VMEM((total, 3 * width), BF)],
        mib=32,
        after=[s2_send[0]],
    )(qkv, dctx, lse, n1, x, dmid, wqkv, vec, g_out, vgrad, ub_own, ub_oth)
    half = sds((ndp // 2,) + s2[0].shape[1:], BF)
    keep, send = call(
        "sum_ctx_ff", functools.partial(sum_ctx_halves_kernel, nctx), [half, half], after=[g1_own]
    )(*s2)
    s1_send = core_sums("sum_core_attn", g1_own, g1_oth, after=[keep])
    s1 = over("ctx", nctx, s1_send)
    back = call(
        "returns",
        one(returns_kernel),
        sds((nctx, 2 * (main + EXTRA), width), BF),
        after=[s1[1]],
    )(bo, ig)
    returned = lax.all_to_all(back, "ctx", 0, 0)
    u1_send = call(
        "sum_ctx_attn",
        functools.partial(sum_ctx_kernel, nctx, ndp),
        [sds(s1[0].shape[1:], BF)] * ndp,
        after=[back],
    )(*s1)
    u1 = over("dp", ndp, u1_send)
    stride = 2
    while stride < ndp:
        half = sds((keep.shape[0] // 2,) + keep.shape[1:], BF)
        keep, send = call(
            "add_dp_ff", functools.partial(add_halves_kernel, stride), [half, half], after=[u1_send[0]]
        )(keep, lax.ppermute(send, "dp", xor(ndp, stride // 2)))
        stride *= 2
    summed = call(
        "sum_dp", functools.partial(sum_dp_kernel, ndp), sds((padded, ff // 2 + 2 * TILE), BF)
    )(keep, lax.ppermute(send, "dp", xor(ndp, ndp // 2)), *u1)
    shares = over("ctx", nctx, [summed] * nctx)
    back = call("hand_on", hand_on_kernel, sds(returned.shape, BF), after=[summed])(returned)
    block_out, input_grad, placed = call(
        "place_slots",
        one(unpack_kernel),
        [sds(tok.shape, F32)] * 2 + [sds((8, TILE), F32)],
        scratch=[pltpu.SMEM(valid_mask.shape, valid_mask.dtype), pltpu.SemaphoreType.DMA((1,))],
        raw=(3,),
        mib=16,
    )(back, other(back), tails, valid_mask)
    gq, gk, gv, gqb, gvb, go, gu, gub, gd, *gvec = call(
        "place_grads",
        one(grads_kernel),
        [
            sds(w_query.shape, F32), sds(w_key.shape, F32), sds(w_value.shape, F32),
            sds(query_bias.shape, F32), sds(value_bias.shape, F32), sds(w_out.shape, F32),
            sds(w_up.shape, F32), sds(up_bias.shape, F32), sds((rows, ff), F32),
        ]
        + [sds((rows,), F32)] * 6,
        scratch=[
            pltpu.VMEM((nctx, padded, 2 * TILE), F32),
            pltpu.VMEM((nctx, padded, ff // 2), F32),
        ],
        after=[placed],
    )(*shares)
    return (by_image(block_out), by_image(input_grad), gq, gk, gv, gqb, gvb, go, gu, gub, jnp.transpose(gd), *gvec)


def solution(mesh):
    rows, cols, tp, dp = P("dp", "tp"), P("tp", "dp"), P("tp"), P("dp")
    act = P("dp", "ctx", None)
    return jax.shard_map(
        functools.partial(body, mesh.shape["ctx"], mesh.shape["tp"], mesh.shape["dp"]),
        mesh=mesh,
        in_specs=(act, P("dp", "ctx"), act, rows, rows, rows, tp, tp, cols, rows, tp, cols) + (dp,) * 6,
        out_specs=(act, act, rows, rows, rows, tp, tp, cols, rows, tp, cols) + (dp,) * 6,
        check_vma=False,
    )
```

```python
import functools

import jax
import jax.numpy as jnp
from jax import lax
from jax.experimental import pallas as pl
from jax.experimental.pallas import tpu as pltpu
from jax.sharding import PartitionSpec as P

HD = 64
EPS = 1e-06
SCALE = 0.125
FLOOR = -1e30
BF = jnp.bfloat16
F32 = jnp.float32
TILE = 128
TIMES = {
    "pack_weights": 2.0, "pack_slots": 3.0, "pack_cotangent": 2.0, "attention": 0.0, "mlp_own": 4.0, "mlp_oth": 4.0, "mlp_sums": 2.0, "attention_back": 11.0,
    "place_grads": 1.0, "place_slots": 2.3, "join_quarter": 20.0, "sum_ctx_attn": 50.0, "sum_ctx_ff": 50.0,
}
EXTRA = 16


def call(name, kernel, out_shape, scratch=(), mib=8, after=(), raw=()):
    after = list(after)

    def ordered(*refs):
        kernel(*refs[len(after) :])

    def run(*args):
        specs = [pl.BlockSpec(memory_space=pl.ANY)] * len(after) + [
            pl.BlockSpec(memory_space=pltpu.HBM if i in raw else pltpu.VMEM)
            for i in range(len(args))
        ]
        return pl.pallas_call(
            ordered,
            name=name,
            out_shape=out_shape,
            in_specs=specs,
            out_specs=jax.tree.map(lambda _: pl.BlockSpec(memory_space=pltpu.VMEM), out_shape),
            scratch_shapes=list(scratch),
            compiler_params=pltpu.CompilerParams(vmem_limit_bytes=mib << 20),
            cost_estimate=pl.CostEstimate(
                flops=int(TIMES.get(name, 0.2) * 1.15e9), bytes_accessed=1, transcendentals=0
            ),
        )(*after, *args)

    return run


def sds(shape, dtype):
    return jax.ShapeDtypeStruct(shape, dtype)


def nn(a, b):
    return lax.dot_general(a, b, (((1,), (0,)), ((), ())), preferred_element_type=F32)


def nt(a, b):
    return lax.dot_general(a, b, (((1,), (1,)), ((), ())), preferred_element_type=F32)


def tn(a, b):
    return lax.dot_general(a, b, (((0,), (0,)), ((), ())), preferred_element_type=F32)


def swap(v):
    return pltpu.roll(v, HD, axis=1)


def low_lanes(shape):
    return lax.broadcasted_iota(jnp.int32, shape, 1) < HD


def row_is(shape, row):
    return lax.broadcasted_iota(jnp.int32, shape, 0) == row


def tile(v, i):
    return v[:, i * TILE : (i + 1) * TILE]


def assemble(own, oth):
    low = low_lanes((own.shape[0], TILE))
    own_qk, own_vo, oth_qk, oth_vo = tile(own, 4), tile(own, 5), tile(oth, 4), tile(oth, 5)
    qkv = [
        tile(own, 0), tile(oth, 0), jnp.where(low, own_qk, swap(oth_qk)),
        tile(own, 1), tile(oth, 1), jnp.where(low, swap(own_qk), oth_qk),
        tile(own, 2), tile(oth, 2), jnp.where(low, own_vo, swap(oth_vo)),
    ]
    out = [tile(own, 3), tile(oth, 3), jnp.where(low, swap(own_vo), oth_vo)]
    return qkv, out


def disassemble(qkv, out):
    low = low_lanes(qkv[0].shape)
    own = [qkv[0], qkv[3], qkv[6], out[0], jnp.where(low, qkv[2], swap(qkv[5])), jnp.where(low, qkv[8], swap(out[2]))]
    oth = [qkv[1], qkv[4], qkv[7], out[1], jnp.where(low, swap(qkv[2]), qkv[5]), jnp.where(low, swap(qkv[8]), out[2])]
    return own, oth


def norm_stats(v):
    mean = jnp.mean(v, axis=-1, keepdims=True)
    centered = v - mean
    r = lax.rsqrt(jnp.mean(centered * centered, axis=-1, keepdims=True) + EPS)
    return centered * r, r


def norm_back(e, xhat, r):
    return r * (
        e
        - jnp.mean(e, axis=-1, keepdims=True)
        - xhat * jnp.mean(e * xhat, axis=-1, keepdims=True)
    )


def gelu_pair(v):
    phi = 0.5 + 0.5 * lax.erf(v * 0.7071067811865476)
    return v * phi, phi + (0.3989422804014327 * v) * jnp.exp(-0.5 * v * v)


BLOCK = 16


def one_hot(shape, hit):
    r, c = (lax.broadcasted_iota(jnp.int32, shape, i) for i in range(2))
    return hit(r, c).astype(F32).astype(BF)


def picker(wanted, images):
    def hit(r, c):
        img = wanted[-1]
        for k in range(len(wanted) - 1):
            img = jnp.where(r // BLOCK == k, wanted[k], img)
        return c == (r % BLOCK) * images + img

    return one_hot((len(wanted) * BLOCK, images * BLOCK), hit)


def take_images(ref, outs, at, pick, images, count):
    for b in range(count // BLOCK):
        got = nn(pick, ref[b * BLOCK * images : (b + 1) * BLOCK * images, :].astype(BF)).astype(BF)
        for k in range(len(outs)):
            outs[k][at + b * BLOCK : at + (b + 1) * BLOCK, :] = got[k * BLOCK : (k + 1) * BLOCK]


def fetch(sources, held, sem):
    copies = [pltpu.make_async_copy(sources[i], held[i], sem.at[i]) for i in range(len(sources))]
    for c in copies:
        c.start()
    return copies


def pack_weights_kernel(sizes, count, *refs):
    nctx, ntp, ndp, main, width, rows, padded = sizes
    sources, (p1, p2q), refs = refs[:count], refs[count : count + 2], refs[count + 2 :]
    held, sem = refs[:count], refs[count]
    copies = fetch(sources, held, sem)
    wq, wk, wv, wo, wu, wd, qb, vb, ub = held[:9]
    vecs = held[9:]
    me_c, me_d = lax.axis_index("ctx"), lax.axis_index("dp")
    for c in copies:
        c.wait()
    if padded > rows:
        p1[0:padded, :] = jnp.zeros((padded, p1.shape[1]), BF)
        p2q[...] = jnp.zeros(p2q.shape, BF)
    quarter = p2q.shape[1]
    for j in range(nctx):
        src = (wu, wd)[j // 2][:, (j % 2) * quarter : (j % 2 + 1) * quarter]

        @pl.when(me_c == j)
        def _(src=src):
            p2q[0:rows, :] = src

    def put(lo, value):
        p1[0:rows, lo : lo + value.shape[1]] = value.astype(BF)

    fq, fk, fv = wq[...].astype(F32), wk[...].astype(F32), wv[...].astype(F32)
    fo = jnp.transpose(wo[...].astype(F32))
    for i, w in enumerate((fq, fk, fv, fo)):
        put(i * TILE, tile(w, 0))
    put(4 * TILE, jnp.concatenate([fq[:, TILE:], fk[:, TILE:]], axis=1))
    put(5 * TILE, jnp.concatenate([fv[:, TILE:], fo[:, TILE:]], axis=1))
    cols = p1.shape[1]
    fqb, fvb = qb[...].astype(F32)[None, :], vb[...].astype(F32)[None, :]
    none = jnp.zeros((1, TILE), F32)
    short = jnp.zeros((1, HD), F32)
    bias = jnp.concatenate(
        [fqb[:, :TILE], none, fvb[:, :TILE], none, fqb[:, TILE:], short, fvb[:, TILE:], short], axis=1
    )
    spread = one_hot((rows, width), lambda r, c: c == r + rows * me_d)
    block = jnp.where(row_is((EXTRA, cols), 0), bias, 0.0)
    block = jnp.where(row_is((EXTRA, cols), 7), ub[...].astype(F32)[None, :], block)
    lanes = jnp.zeros((EXTRA, rows), F32)
    for i in range(6):
        lanes = jnp.where(row_is((EXTRA, rows), 1 + i), vecs[i][...].astype(F32)[None, :], lanes)
    lanes = nn(lanes.astype(BF), spread)
    p1[padded : padded + EXTRA, :] = block.astype(BF)
    mixed = jnp.where(
        (lax.broadcasted_iota(jnp.int32, (EXTRA, width), 0) - 1).astype(jnp.uint32) < 6,
        lanes,
        block[:, :width],
    )
    p1[padded : padded + EXTRA, 0:width] = mixed.astype(BF)


def pack_slots_kernel(sizes, *refs):
    nctx, ntp, ndp, main, width, rows, padded = sizes
    sources, sent, tails, refs = refs[:3], refs[3 : 3 + nctx], refs[3 + nctx], refs[4 + nctx :]
    held, sem = refs[:3], refs[3]
    copies = fetch(sources, held, sem)
    tok, cot, mask = held
    images = nctx * ntp
    me_c, me_t = lax.axis_index("ctx"), lax.axis_index("tp")
    wanted = [(me_c ^ k) * ntp + me_t for k in range(nctx)]
    pick = picker(wanted, images)
    for i in range(2):
        copies[i].wait()
        take_images(held[i], sent, i * (main + EXTRA), pick, images, main)
        tails[i] = held[i][main * images :, :]
    copies[2].wait()
    for k in range(nctx):
        gate = mask[wanted[k], main].astype(F32)
        te = tok[pl.ds(main * images + wanted[k], 1), :] * gate
        ce = cot[pl.ds(main * images + wanted[k], 1), :] * gate
        shape = (EXTRA, width)
        sent[k][main : main + EXTRA, :] = jnp.where(
            row_is(shape, 0), te, jnp.where(row_is(shape, 1), ce, 0.0)
        ).astype(BF)


def join_kernel(axis, stride, own, got, out):
    bit = lax.rem(lax.div(lax.axis_index(axis), stride), 2)
    for i in range(own.shape[0]):
        out[2 * i + bit] = own[i]
        out[2 * i + 1 - bit] = got[i]


def place_rows(stage, own, got, rows):
    bit = lax.rem(lax.axis_index("dp"), 2)
    for i in range(own.shape[0]):
        for piece, last in ((own, bit), (got, 1 - bit)):
            at = pl.ds(pl.multiple_of((2 * i + last) * rows, 16 if rows % 16 == 0 else 8), rows)
            stage[at, :] = piece[i].astype(stage.dtype)[:rows]


def merge_quarter_kernel(sizes, attn, own, got, out, attn_out, stage):
    place_rows(stage, own, got, sizes[5])
    out[...] = stage[...].astype(BF)
    attn_out[...] = attn[...]


def split_kernel(got, *outs):
    for i, out in enumerate(outs):
        cols = out.shape[2]
        out[...] = got[:, :, i * cols : (i + 1) * cols]


def merge_ff_kernel(nctx, *refs):
    out = refs[nctx]
    me_c = lax.axis_index("ctx")
    for k in range(nctx):
        quarter = refs[k].shape[1]
        out[:, pl.ds(pl.multiple_of((me_c ^ k) * quarter, quarter), quarter)] = refs[k][...]


def attention_kernel(sizes, *refs):
    nctx, ntp, ndp, main, width, rows, padded = sizes
    t_in, (own, got, own_oth, got_oth_a, got_oth_b), refs = refs[:nctx], refs[nctx : nctx + 5], refs[nctx + 5 :]
    x_out, mid_out, n1_out, n2_out, qkv, ctx, lse, wqkv, wot, vec, ub, cot, stage, stage_oth = refs
    body = nctx * main
    total = body + EXTRA
    half = got_oth_a.shape[2]
    place_rows(stage, own, got, rows)
    place_rows(stage_oth.at[:, :half], own_oth.at[:, :, :half], got_oth_a, rows)
    place_rows(stage_oth.at[:, half:], own_oth.at[:, :, half:], got_oth_b, rows)
    tiles, outs = assemble(stage[...].astype(F32), stage_oth[...].astype(F32))
    for i, v in enumerate(tiles):
        wqkv[:, i * TILE : (i + 1) * TILE] = v.astype(BF)
    for i, v in enumerate(outs):
        wot[:, i * TILE : (i + 1) * TILE] = v.astype(BF)
    extra = own[0, padded:, :].astype(F32)
    extra_oth = own_oth[0, padded:, :].astype(F32)
    tiles, _ = assemble(extra, extra_oth)
    bias = jnp.concatenate([v[0:1] for v in tiles], axis=1)
    vec_sum = jnp.zeros((EXTRA, width), F32)
    for i in range(own.shape[0]):
        vec_sum += own[i, padded:, :width].astype(F32) + got[i, padded:, :width].astype(F32)
    vec[...] = vec_sum
    ub[...] = jnp.broadcast_to(jnp.concatenate([extra[7:8], extra_oth[7:8]], axis=1), ub.shape)
    extra = jnp.zeros((EXTRA, width), F32)
    for k in range(nctx):
        x_out[k * main : (k + 1) * main, :] = t_in[k][0:main, :].astype(F32)
        cot[k * main : (k + 1) * main, :] = t_in[k][main + EXTRA :, :]
        extra += t_in[k][main : main + EXTRA, :].astype(F32)
    x_out[body:, :] = jnp.where(row_is((EXTRA, width), 0), extra, 0.0)
    cot[body:, :] = jnp.where(row_is((EXTRA, width), 0), extra[1:2, :], 0.0).astype(BF)
    x = x_out[...]
    xhat, _ = norm_stats(x)
    n1 = (xhat * vec_sum[1:2, :] + vec_sum[2:3, :]).astype(BF)
    n1_out[...] = n1
    proj = nn(n1, wqkv[...]) + bias
    qkv[0:total, 0:width] = (proj[:, 0:width].astype(BF).astype(F32) * SCALE).astype(BF)
    qkv[0:total, width:] = proj[:, width:].astype(BF)
    keys = qkv.shape[0]
    qkv[total:, :] = jnp.zeros((keys - total, qkv.shape[1]), BF)
    off = jnp.where(lax.broadcasted_iota(jnp.int32, (1, keys), 1) > body, FLOOR, 0.0)
    low = low_lanes((total, TILE))
    lane = lax.broadcasted_iota(jnp.int32, (total, TILE), 1)
    all_lse = jnp.zeros((total, TILE), F32)
    for p in range(3):
        qp = qkv[0:total, p * TILE : (p + 1) * TILE]
        kp = qkv[:, width + p * TILE : width + (p + 1) * TILE]
        vp = qkv[:, 2 * width + p * TILE : 2 * width + (p + 1) * TILE]
        parts = []
        for a in range(2):
            qa = jnp.where(low if a == 0 else ~low, qp, jnp.zeros_like(qp))
            s = nt(qa, kp) + off
            m = jnp.max(s, axis=-1, keepdims=True)
            e = jnp.exp(s - m)
            l = jnp.sum(e, axis=-1, keepdims=True)
            parts.append(nn(e.astype(BF), vp) * (1.0 / l))
            all_lse = jnp.where(lane == 2 * p + a, m + jnp.log(l), all_lse)
        ctx[:, p * TILE : (p + 1) * TILE] = jnp.where(low, parts[0], parts[1]).astype(BF)
    lse[...] = all_lse
    attended = nt(ctx[...], wot[...]) + vec_sum[5:6, :]
    valid = lax.broadcasted_iota(jnp.int32, (total, 1), 0) <= body
    middle = x_out[...] + jnp.where(valid, attended, 0.0)
    mid_out[...] = middle
    xhat2, _ = norm_stats(middle)
    n2_out[...] = (xhat2 * vec_sum[3:4, :] + vec_sum[4:5, :]).astype(BF)


def ff_half(n2v, dcot, w, ub, hid, hgr, ubgrad, grads, ndp, rows):
    half = w.shape[1] // 2
    quarter = half // 2
    for lo in range(0, half, 256):
        sl = slice(lo, lo + 256)
        pre = nn(n2v, w[:, sl]) + ub[0:1, sl]
        hc = nn(dcot, w[:, half + lo : half + lo + 256])
        act, slope = gelu_pair(pre)
        h = act.astype(BF)
        hg = (hc * slope).astype(BF)
        hid[:, sl] = h
        hgr[:, sl] = hg
        ubgrad[:, sl] = jnp.broadcast_to(jnp.sum(hg.astype(F32), axis=0, keepdims=True), (8, 256))
        for part, g in ((0, tn(n2v, hg).astype(BF)), (1, tn(dcot, h).astype(BF))):
            for d in range(ndp):
                for c in range(2):
                    col = lo + c * TILE
                    at = slice(col % quarter, col % quarter + TILE)
                    grads[2 * part + col // quarter, d, 0:rows, at] = (
                        g[d * rows : (d + 1) * rows, c * TILE : (c + 1) * TILE]
                    )


def mlp_half_kernel(sizes, side, n2, cot, w, ub, hid, hgr, ubgrad, grads):
    half = w.shape[1] // 2
    ff_half(
        n2[...], cot[...], w[...], ub[:, side * half : (side + 1) * half], hid, hgr, ubgrad, grads, sizes[2], sizes[5]
    )


def mlp_sums_kernel(sizes, mid, ctx, wot, vec, cot, w_own, w_oth, hid_own, hid_oth, hgr_own, hgr_oth, bo, dmid, dctx, g_out, vgrad):
    nctx, ntp, ndp, main, width, rows, padded = sizes
    body = nctx * main
    total = body + EXTRA
    half = w_own.shape[1] // 2
    dcot = cot[...]
    middle = mid[...]
    valid = lax.broadcasted_iota(jnp.int32, (total, 1), 0) <= body
    n2g = nt(hgr_own[...], w_own[:, :half]) + nt(hgr_oth[...], w_oth[:, :half])
    xhat, r = norm_stats(middle)
    back = norm_back(n2g * vec[3:4, :], xhat, r)
    middle_grad = dcot.astype(F32) + back
    dmid[...] = middle_grad
    agrad = jnp.where(valid, middle_grad, 0.0).astype(BF)
    dctx[...] = nn(agrad, wot[...]).astype(BF)
    g_out[...] = tn(agrad, ctx[...])
    mlp_out = nt(hid_own[...], w_own[:, half:]) + nt(hid_oth[...], w_oth[:, half:]) + vec[6:7, :]
    bo[...] = (middle + jnp.where(valid, mlp_out, 0.0)).astype(BF)
    shape = vgrad.shape
    v = jnp.where(row_is(shape, 2), jnp.sum(n2g * xhat, axis=0, keepdims=True), 0.0)
    v = jnp.where(row_is(shape, 3), jnp.sum(n2g, axis=0, keepdims=True), v)
    v = jnp.where(row_is(shape, 4), jnp.sum(agrad.astype(F32), axis=0, keepdims=True), v)
    v = jnp.where(row_is(shape, 5), jnp.sum(dcot.astype(F32), axis=0, keepdims=True), v)
    vgrad[...] = v


def pair_back(p, width, total, body, qkv, dctx, lse, ctx):
    keys = qkv.shape[0]
    off = jnp.where(lax.broadcasted_iota(jnp.int32, (1, keys), 1) > body, FLOOR, 0.0)
    low = low_lanes((total, TILE))
    at = slice(p * TILE, (p + 1) * TILE)
    qp = qkv[0:total, at]
    kp = qkv[:, width + p * TILE : width + (p + 1) * TILE]
    vp = qkv[:, 2 * width + p * TILE : 2 * width + (p + 1) * TILE]
    dp = dctx[:, at]
    both = dp.astype(F32) * ctx[:, at].astype(F32)
    qt = jnp.transpose(qp.astype(F32)).astype(BF)
    dt = jnp.transpose(dp.astype(F32)).astype(BF)
    dq, dk, dv = [], [], []
    for a in range(2):
        sel = low if a == 0 else ~low
        qa = jnp.where(sel, qp, jnp.zeros_like(qp))
        da = jnp.where(sel, dp, jnp.zeros_like(dp))
        inner = jnp.sum(jnp.where(sel, both, 0.0), axis=-1, keepdims=True)
        prob = jnp.exp(nt(qa, kp) + off - lse[:, 2 * p + a : 2 * p + a + 1])
        ds = (prob * (nt(da, vp) - inner)).astype(BF)
        dq.append(nn(ds, kp))
        dk.append(nn(qt[a * HD : (a + 1) * HD], ds))
        dv.append(nn(dt[a * HD : (a + 1) * HD], prob.astype(BF)))
    dq = jnp.where(low, dq[0], dq[1]) * SCALE
    dk, dv = (jnp.transpose(jnp.concatenate(v, axis=0))[0:total] for v in (dk, dv))
    return dq.astype(BF), dk.astype(BF), dv.astype(BF)


def attention_back_kernel(sizes, *refs):
    nctx, ntp, ndp, main, width, rows, padded = sizes
    qkv, dctx, lse, ctx, n1, x_in, dmid, wqkv, vec, g_out, vgrad, ub_own, ub_oth = refs[:13]
    ig, g_own, g_oth, dqkv = refs[13:]
    body = nctx * main
    total = body + EXTRA
    for p in range(3):
        for i, v in enumerate(pair_back(p, width, total, body, qkv, dctx, lse, ctx)):
            dqkv[:, i * width + p * TILE : i * width + (p + 1) * TILE] = v
    d = dqkv[...]
    bias = jnp.sum(d.astype(F32), axis=0, keepdims=True)
    g = tn(n1[...], d)
    go = g_out[...]
    own, oth = disassemble([tile(g, i) for i in range(9)], [tile(go, i) for i in range(3)])
    for to, tiles in ((g_own, own), (g_oth, oth)):
        for j in range(6):
            for e in range(ndp):
                to[j // 2, e, 0:rows, (j % 2) * TILE : (j % 2 + 1) * TILE] = (
                    tiles[j][e * rows : (e + 1) * rows].astype(BF)
                )
    dn1 = nt(d, wqkv[...])
    xhat, r = norm_stats(x_in[...])
    grad = dmid[...] + norm_back(dn1 * vec[1:2, :], xhat, r)
    ig[...] = grad.astype(BF)
    gains = jnp.sum(dn1 * xhat, axis=0, keepdims=True)
    shifts = jnp.sum(dn1, axis=0, keepdims=True)
    vecs = [gains, shifts] + [vgrad[i : i + 1, :] for i in range(2, 6)]
    zero = [jnp.zeros((1, TILE), F32)] * 3
    bias_own, bias_oth = disassemble([tile(bias, i) for i in range(9)], zero)
    for to, tiles, ub in ((g_own, bias_own, ub_own), (g_oth, bias_oth, ub_oth)):
        rows_ = [tile(v, i) for v in vecs for i in range(3)] + tiles
        rows_ += [ub[0:1, i * TILE : (i + 1) * TILE] for i in range(6)]
        for side in range(2):
            block = jnp.zeros((EXTRA, TILE), F32)
            for i, v in enumerate(rows_[side * EXTRA : (side + 1) * EXTRA]):
                block = jnp.where(row_is(block.shape, i), v, block)
            for e in range(ndp):
                to[3, e, 0:EXTRA, side * TILE : (side + 1) * TILE] = block.astype(BF)
                if padded > EXTRA:
                    to[3, e, EXTRA:padded, side * TILE : (side + 1) * TILE] = jnp.zeros(
                        (padded - EXTRA, TILE), BF
                    )


def sum_core_kernel(n, own, oth, *outs):
    me = lax.axis_index("ctx")
    for k in range(n):
        outs[k][...] = (own[me ^ k].astype(F32) + oth[me ^ k].astype(F32)).astype(BF)


def sum_ctx_kernel(n, ndp, *refs):
    me = lax.axis_index("dp")
    for k in range(ndp):
        v = refs[0][me ^ k].astype(F32)
        for i in range(1, n):
            v = v + refs[i][me ^ k].astype(F32)
        refs[n + k][...] = v.astype(BF)


def halve(axis, stride, item, keep, send):
    bit = lax.rem(lax.div(lax.axis_index(axis), stride), 2)
    for j in range(keep.shape[0]):
        keep[j] = item(2 * j + bit).astype(BF)
        send[j] = item(2 * j + 1 - bit).astype(BF)


def sum_ctx_halves_kernel(n, *refs):
    terms, (keep, send) = refs[:n], refs[n:]

    def item(i):
        v = terms[0][i].astype(F32)
        for t in terms[1:]:
            v = v + t[i].astype(F32)
        return v

    halve("dp", 1, item, keep, send)


def add_halves_kernel(stride, own, got, keep, send):
    halve("dp", stride, lambda i: own[i].astype(F32) + got[i].astype(F32), keep, send)


def sum_dp_kernel(n, own, got, *refs):
    out = refs[n]
    cols = own.shape[2]
    out[:, :cols] = (own[0].astype(F32) + got[0].astype(F32)).astype(BF)
    v = refs[0][...].astype(F32)
    for r in refs[1:n]:
        v = v + r[...].astype(F32)
    out[:, cols:] = v.astype(BF)


def returns_kernel(sizes, bo, ig, out):
    nctx, ntp, ndp, main, width, rows, padded = sizes
    me = lax.axis_index("ctx")
    span = main + EXTRA
    for k in range(nctx):
        at = slice(k * main, (k + 1) * main)
        for i, src in enumerate((bo, ig)):
            out[me ^ k, i * span : i * span + main, :] = src[at, :]
            out[me ^ k, i * span + main : (i + 1) * span, :] = src[nctx * main :, :]


def hand_on_kernel(held, out):
    out[...] = held[...]


def grads_kernel(sizes, *refs):
    nctx, ntp, ndp, main, width, rows, padded = sizes
    parts, refs = refs[:nctx], refs[nctx:]
    gq, gk, gv, gqb, gvb, go, gu, gub, gd = refs[:9]
    gvec, f, f2 = refs[9:15], refs[15], refs[16]
    me, me_d = lax.axis_index("ctx"), lax.axis_index("dp")
    half = f2.shape[2]
    for k in range(nctx):
        f2[me ^ k] = parts[k][:, :half].astype(F32)
        f[me ^ k] = parts[k][:, half:].astype(F32)
    for j in range(2):
        gu[:, j * half : (j + 1) * half] = f2[j, 0:rows, :]
        gd[:, j * half : (j + 1) * half] = f2[2 + j, 0:rows, :]
    q01, k01 = f[0, 0:rows, 0:TILE], f[0, 0:rows, TILE:]
    v01, o01 = f[1, 0:rows, 0:TILE], f[1, 0:rows, TILE:]
    qk2, vo2 = f[2, 0:rows, 0:TILE], f[2, 0:rows, TILE:]
    gq[:, 0:TILE] = q01
    gq[:, TILE:] = qk2[:, 0:HD]
    gk[:, 0:TILE] = k01
    gk[:, TILE:] = swap(qk2)[:, 0:HD]
    gv[:, 0:TILE] = v01
    gv[:, TILE:] = vo2[:, 0:HD]
    go[0:TILE, :] = jnp.transpose(o01)
    go[TILE:, :] = jnp.transpose(vo2)[HD:, :]
    ex = [f[3, 0:EXTRA, 0:TILE], f[3, 0:EXTRA, TILE:]]

    def line(i):
        return ex[i // EXTRA][i % EXTRA : i % EXTRA + 1, :]

    for i in range(6):
        v = jnp.concatenate([line(3 * i), line(3 * i + 1), line(3 * i + 2)], axis=1)
        v = jnp.broadcast_to(v, (8, width))
        v = pltpu.roll(v, lax.rem(width - me_d * rows, width), axis=1)
        gvec[i][...] = v[0, 0:rows]
    b = [line(18 + i) for i in range(6)]
    gqb[...] = jnp.concatenate([b[0], b[4][:, 0:HD]], axis=1)[0]
    gvb[...] = jnp.concatenate([b[2], b[5][:, 0:HD]], axis=1)[0]
    gub[...] = jnp.concatenate([line(24 + i) for i in range(6)], axis=1)[0]


def unpack_kernel(sizes, own, oth, tails, mask, *refs):
    nctx, ntp, ndp, main, width, rows, padded = sizes
    outs, done, valid, sem = refs[:2], refs[2], refs[3], refs[4]
    images = nctx * ntp
    me_t = lax.axis_index("tp")
    where = [j * ntp + t for t in (me_t, 1 - me_t) for j in range(nctx)]
    sources = [v.at[j] for v in (own, oth) for j in range(nctx)]
    span = main + EXTRA
    get_valid = pltpu.make_async_copy(mask, valid, sem.at[0])
    get_valid.start()

    def hit(r, c):
        img = where[-1]
        for j in range(images - 1):
            img = jnp.where(c // BLOCK == j, where[j], img)
        return r == (c % BLOCK) * images + img

    put = one_hot((images * BLOCK, images * BLOCK), hit)
    for i in range(2):
        for b in range(main // BLOCK):
            lo = i * span + b * BLOCK
            got = jnp.concatenate([src[lo : lo + BLOCK, :] for src in sources], axis=0)
            outs[i][b * BLOCK * images : (b + 1) * BLOCK * images, :] = nn(put, got)
    get_valid.wait()
    for i in range(2):
        for src, img in zip(sources, where):
            got = src[i * span + main : (i + 1) * span, :].astype(F32)[0:1, :]
            outs[i][pl.ds(main * images + img, 1), :] = jnp.where(
                valid[img, main] > 0, got, tails[i, pl.ds(img, 1), :]
            )
    done[...] = jnp.zeros_like(done)


def xor(n, k):
    return [(i, i ^ k) for i in range(n)]


def over(axis, n, items):
    return [items[0]] + [lax.ppermute(items[k], axis, xor(n, k)) for k in range(1, n)]


def body(nctx, ntp, ndp, *args):
    (tokens, valid_mask, cotangent, w_query, w_key, w_value, query_bias, value_bias, w_out, w_up, up_bias, w_down) = args[:12]
    vecs = args[12:]
    images, slots, width = tokens.shape
    main = slots - 1
    rows = w_query.shape[0]
    padded = -(-rows // EXTRA) * EXTRA
    ff = w_up.shape[1]
    p1_cols = 4 * w_query.shape[1]
    sizes = (nctx, ntp, ndp, main, width, rows, padded)
    total = nctx * main + EXTRA
    keys = -(-total // TILE) * TILE
    stage = BF if rows % 16 == 0 else F32
    flip = xor(ntp, 1)
    tok = jnp.transpose(tokens, (1, 0, 2)).reshape(slots * images, width)
    cot = jnp.transpose(cotangent, (1, 0, 2)).reshape(slots * images, width)

    def one(f):
        return functools.partial(f, sizes)

    def other(v):
        return lax.ppermute(v, "tp", flip)

    def held(arrays):
        return [
            (pltpu.SMEM if v.dtype == jnp.int32 else pltpu.VMEM)(v.shape, v.dtype) for v in arrays
        ] + [pltpu.SemaphoreType.DMA((len(arrays),))]

    def gather_dp(name, piece, after):
        v = piece[None]
        stride = ndp // 2
        while stride > 1:
            v = call(
                name,
                functools.partial(join_kernel, "dp", stride),
                sds((2 * v.shape[0],) + v.shape[1:], v.dtype),
                after=after,
            )(v, lax.ppermute(v, "dp", xor(ndp, stride)))
            stride //= 2
        return v, lax.ppermute(v, "dp", xor(ndp, 1))

    sources = [w_query, w_key, w_value, w_out, w_up, jnp.transpose(w_down), query_bias, value_bias, up_bias, *vecs]
    p1, p2q = call(
        "pack_weights",
        functools.partial(pack_weights_kernel, sizes, len(sources)),
        [sds((padded + EXTRA, p1_cols), BF), sds((padded, ff // 2), BF)],
        scratch=held(sources),
        mib=60,
        raw=range(len(sources)),
    )(*sources)
    sources = [tok, cot, valid_mask]
    *sent, tails = call(
        "pack_slots",
        one(pack_slots_kernel),
        [sds((2 * main + EXTRA, width), BF)] * nctx + [sds((2, images, width), F32)],
        scratch=held(sources),
        mib=60,
        raw=range(3),
        after=[p1],
    )(*sources)
    t_in = over("ctx", nctx, sent)
    w2q = gather_dp("join_quarter", p2q, [sent[0]])
    w1, w1_got = gather_dp("join_attn", p1, [sent[0]])
    w2q, w1_early = call(
        "merge_quarter",
        one(merge_quarter_kernel),
        [sds((width, ff // 2), BF), sds(w1.shape, BF)],
        scratch=[pltpu.VMEM((width, ff // 2), stage)],
        after=t_in[1:],
    )(w1, *w2q)
    w1_oth = other(w1_early)
    w2q = over("ctx", nctx, [w2q] * nctx)
    late = call(
        "split_attn",
        split_kernel,
        [sds(w1.shape[:2] + (p1_cols // 2,), BF)] * 2,
        after=[w1_oth, w2q[0]],
    )(w1_got)
    w1 = [w1, w1_got, w1_oth, *[other(v) for v in late]]
    x, mid, n1, n2, qkv, ctx, lse, wqkv, wot, vec, ub, cot_in = call(
        "attention",
        one(attention_kernel),
        [
            sds((total, width), F32), sds((total, width), F32), sds((total, width), BF), sds((total, width), BF),
            sds((keys, 3 * width), BF), sds((total, width), BF), sds((total, TILE), F32),
            sds((width, 3 * width), BF), sds((width, width), BF), sds((EXTRA, width), F32), sds((8, 2 * ff), F32),
            sds((total, width), BF),
        ],
        scratch=[pltpu.VMEM((width, p1_cols), stage)] * 2,
        mib=32,
    )(*t_in, *w1)
    w2_own = call(
        "merge_ff", functools.partial(merge_ff_kernel, nctx), sds((width, 2 * ff), BF), after=[vec]
    )(*w2q)
    w2_oth = other(w2_own)
    ff_grads = sds((4, ndp, padded, ff // 2), BF)

    def mlp_half(name, side, w, after=()):
        return call(
            name,
            functools.partial(mlp_half_kernel, sizes, side),
            [sds((total, ff), BF), sds((total, ff), BF), sds((8, ff), F32), ff_grads],
            mib=32,
            after=after,
        )(n2, cot_in, w, ub)

    hid_own, hgr_own, ub_own, g2_own = mlp_half("mlp_own", 0, w2_own)
    hid_oth, hgr_oth, ub_oth, g2_oth = mlp_half("mlp_oth", 1, w2_oth, [ub_own])
    bo, dmid, dctx, g_out, vgrad = call(
        "mlp_sums",
        one(mlp_sums_kernel),
        [
            sds((total, width), BF), sds((total, width), F32), sds((total, width), BF), sds((width, width), F32),
            sds((EXTRA, width), F32),
        ],
        mib=32,
    )(mid, ctx, wot, vec, cot_in, w2_own, w2_oth, hid_own, hid_oth, hgr_own, hgr_oth)

    def core_sums(name, own, oth, after=()):
        outs = [sds(own.shape[1:], BF)] * nctx
        return call(name, functools.partial(sum_core_kernel, nctx), outs, after=after)(own, other(oth))

    def by_image(v):
        return jnp.transpose(v.reshape(slots, images, width), (1, 0, 2))

    s2_send = core_sums("sum_core_ff", g2_own, g2_oth, after=[vgrad])
    s2 = over("ctx", nctx, s2_send)
    ig, g1_own, g1_oth = call(
        "attention_back",
        one(attention_back_kernel),
        [sds((total, width), BF)] + [sds((4, ndp, padded, 2 * TILE), BF)] * 2,
        scratch=[pltpu.VMEM((total, 3 * width), BF)],
        mib=32,
        after=[s2_send[0]],
    )(qkv, dctx, lse, ctx, n1, x, dmid, wqkv, vec, g_out, vgrad, ub_own, ub_oth)
    half = sds((ndp // 2,) + s2[0].shape[1:], BF)
    keep, send = call(
        "sum_ctx_ff", functools.partial(sum_ctx_halves_kernel, nctx), [half, half], after=[g1_own]
    )(*s2)
    s1_send = core_sums("sum_core_attn", g1_own, g1_oth, after=[keep])
    s1 = over("ctx", nctx, s1_send)
    back = call(
        "returns",
        one(returns_kernel),
        sds((nctx, 2 * (main + EXTRA), width), BF),
        after=[s1[1]],
    )(bo, ig)
    returned = lax.all_to_all(back, "ctx", 0, 0)
    u1_send = call(
        "sum_ctx_attn",
        functools.partial(sum_ctx_kernel, nctx, ndp),
        [sds(s1[0].shape[1:], BF)] * ndp,
        after=[back],
    )(*s1)
    u1 = over("dp", ndp, u1_send)
    stride = 2
    while stride < ndp:
        half = sds((keep.shape[0] // 2,) + keep.shape[1:], BF)
        keep, send = call(
            "add_dp_ff", functools.partial(add_halves_kernel, stride), [half, half], after=[u1_send[0]]
        )(keep, lax.ppermute(send, "dp", xor(ndp, stride // 2)))
        stride *= 2
    summed = call(
        "sum_dp", functools.partial(sum_dp_kernel, ndp), sds((padded, ff // 2 + 2 * TILE), BF)
    )(keep, lax.ppermute(send, "dp", xor(ndp, ndp // 2)), *u1)
    shares = over("ctx", nctx, [summed] * nctx)
    back = call("hand_on", hand_on_kernel, sds(returned.shape, BF), after=[summed])(returned)
    block_out, input_grad, placed = call(
        "place_slots",
        one(unpack_kernel),
        [sds(tok.shape, F32)] * 2 + [sds((8, TILE), F32)],
        scratch=[pltpu.SMEM(valid_mask.shape, valid_mask.dtype), pltpu.SemaphoreType.DMA((1,))],
        raw=(3,),
        mib=16,
    )(back, other(back), tails, valid_mask)
    gq, gk, gv, gqb, gvb, go, gu, gub, gd, *gvec = call(
        "place_grads",
        one(grads_kernel),
        [
            sds(w_query.shape, F32), sds(w_key.shape, F32), sds(w_value.shape, F32),
            sds(query_bias.shape, F32), sds(value_bias.shape, F32), sds(w_out.shape, F32),
            sds(w_up.shape, F32), sds(up_bias.shape, F32), sds((rows, ff), F32),
        ]
        + [sds((rows,), F32)] * 6,
        scratch=[
            pltpu.VMEM((nctx, padded, 2 * TILE), F32),
            pltpu.VMEM((nctx, padded, ff // 2), F32),
        ],
        after=[placed],
    )(*shares)
    return (by_image(block_out), by_image(input_grad), gq, gk, gv, gqb, gvb, go, gu, gub, jnp.transpose(gd), *gvec)


def solution(mesh):
    rows, cols, tp, dp = P("dp", "tp"), P("tp", "dp"), P("tp"), P("dp")
    act = P("dp", "ctx", None)
    return jax.shard_map(
        functools.partial(body, mesh.shape["ctx"], mesh.shape["tp"], mesh.shape["dp"]),
        mesh=mesh,
        in_specs=(act, P("dp", "ctx"), act, rows, rows, rows, tp, tp, cols, rows, tp, cols) + (dp,) * 6,
        out_specs=(act, act, rows, rows, rows, tp, tp, cols, rows, tp, cols) + (dp,) * 6,
        check_vma=False,
    )
```

```python
import functools

import jax
import jax.numpy as jnp
from jax import lax
from jax.experimental import pallas as pl
from jax.experimental.pallas import tpu as pltpu
from jax.sharding import PartitionSpec as P

HD = 64
EPS = 1e-06
SCALE = 0.125
FLOOR = -1e30
BF = jnp.bfloat16
F32 = jnp.float32
TILE = 128
TIMES = {
    "pack_weights": 2.0, "pack_slots": 3.0, "pack_cotangent": 2.0, "attention": 0.0, "mlp_own": 4.0, "mlp_oth": 4.0, "mlp_sums": 2.0, "attention_back": 11.0,
    "place_grads": 1.0, "place_slots": 2.3, "join_quarter": 20.0, "sum_ctx_attn": 50.0, "sum_ctx_ff": 50.0,
}
EXTRA = 16


def call(name, kernel, out_shape, scratch=(), mib=8, after=(), raw=()):
    after = list(after)

    def ordered(*refs):
        kernel(*refs[len(after) :])

    def run(*args):
        specs = [pl.BlockSpec(memory_space=pl.ANY)] * len(after) + [
            pl.BlockSpec(memory_space=pltpu.HBM if i in raw else pltpu.VMEM)
            for i in range(len(args))
        ]
        return pl.pallas_call(
            ordered,
            name=name,
            out_shape=out_shape,
            in_specs=specs,
            out_specs=jax.tree.map(lambda _: pl.BlockSpec(memory_space=pltpu.VMEM), out_shape),
            scratch_shapes=list(scratch),
            compiler_params=pltpu.CompilerParams(vmem_limit_bytes=mib << 20),
            cost_estimate=pl.CostEstimate(
                flops=int(TIMES.get(name, 0.2) * 1.15e9), bytes_accessed=1, transcendentals=0
            ),
        )(*after, *args)

    return run


def sds(shape, dtype):
    return jax.ShapeDtypeStruct(shape, dtype)


def nn(a, b):
    return lax.dot_general(a, b, (((1,), (0,)), ((), ())), preferred_element_type=F32)


def nt(a, b):
    return lax.dot_general(a, b, (((1,), (1,)), ((), ())), preferred_element_type=F32)


def tn(a, b):
    return lax.dot_general(a, b, (((0,), (0,)), ((), ())), preferred_element_type=F32)


def swap(v):
    return pltpu.roll(v, HD, axis=1)


def low_lanes(shape):
    return lax.broadcasted_iota(jnp.int32, shape, 1) < HD


def row_is(shape, row):
    return lax.broadcasted_iota(jnp.int32, shape, 0) == row


def tile(v, i):
    return v[:, i * TILE : (i + 1) * TILE]


def assemble(own, oth):
    low = low_lanes((own.shape[0], TILE))
    own_qk, own_vo, oth_qk, oth_vo = tile(own, 4), tile(own, 5), tile(oth, 4), tile(oth, 5)
    qkv = [
        tile(own, 0), tile(oth, 0), jnp.where(low, own_qk, swap(oth_qk)),
        tile(own, 1), tile(oth, 1), jnp.where(low, swap(own_qk), oth_qk),
        tile(own, 2), tile(oth, 2), jnp.where(low, own_vo, swap(oth_vo)),
    ]
    out = [tile(own, 3), tile(oth, 3), jnp.where(low, swap(own_vo), oth_vo)]
    return qkv, out


def disassemble(qkv, out):
    low = low_lanes(qkv[0].shape)
    own = [qkv[0], qkv[3], qkv[6], out[0], jnp.where(low, qkv[2], swap(qkv[5])), jnp.where(low, qkv[8], swap(out[2]))]
    oth = [qkv[1], qkv[4], qkv[7], out[1], jnp.where(low, swap(qkv[2]), qkv[5]), jnp.where(low, swap(qkv[8]), out[2])]
    return own, oth


def norm_stats(v):
    mean = jnp.mean(v, axis=-1, keepdims=True)
    centered = v - mean
    r = lax.rsqrt(jnp.mean(centered * centered, axis=-1, keepdims=True) + EPS)
    return centered * r, r


def norm_back(e, xhat, r):
    return r * (
        e
        - jnp.mean(e, axis=-1, keepdims=True)
        - xhat * jnp.mean(e * xhat, axis=-1, keepdims=True)
    )


def gelu_pair(v):
    phi = 0.5 + 0.5 * lax.erf(v * 0.7071067811865476)
    return v * phi, phi + (0.3989422804014327 * v) * jnp.exp(-0.5 * v * v)


BLOCK = 16


def one_hot(shape, hit):
    r, c = (lax.broadcasted_iota(jnp.int32, shape, i) for i in range(2))
    return hit(r, c).astype(F32).astype(BF)


def picker(wanted, images):
    def hit(r, c):
        img = wanted[-1]
        for k in range(len(wanted) - 1):
            img = jnp.where(r // BLOCK == k, wanted[k], img)
        return c == (r % BLOCK) * images + img

    return one_hot((len(wanted) * BLOCK, images * BLOCK), hit)


def take_images(ref, outs, at, pick, images, count):
    for b in range(count // BLOCK):
        got = nn(pick, ref[b * BLOCK * images : (b + 1) * BLOCK * images, :].astype(BF)).astype(BF)
        for k in range(len(outs)):
            outs[k][at + b * BLOCK : at + (b + 1) * BLOCK, :] = got[k * BLOCK : (k + 1) * BLOCK]


def fetch(sources, held, sem):
    copies = [pltpu.make_async_copy(sources[i], held[i], sem.at[i]) for i in range(len(sources))]
    for c in copies:
        c.start()
    return copies


def pack_weights_kernel(sizes, count, *refs):
    nctx, ntp, ndp, main, width, rows, padded = sizes
    sources, (p1, p2q, done), refs = refs[:count], refs[count : count + 3], refs[count + 3 :]
    held, sem = refs[:count], refs[count]
    copies = fetch(sources, held, sem)
    wq, wk, wv, wo, wu, wd, qb, vb, ub = held[:9]
    vecs = held[9:]
    me_c, me_d = lax.axis_index("ctx"), lax.axis_index("dp")
    for c in copies:
        c.wait()
    if padded > rows:
        p1[0:padded, :] = jnp.zeros((padded, p1.shape[1]), BF)
        p2q[...] = jnp.zeros(p2q.shape, BF)
    quarter = p2q.shape[1]
    for j in range(nctx):
        src = (wu, wd)[j // 2][:, (j % 2) * quarter : (j % 2 + 1) * quarter]

        @pl.when(me_c == j)
        def _(src=src):
            p2q[0:rows, :] = src

    def put(lo, value):
        p1[0:rows, lo : lo + value.shape[1]] = value.astype(BF)

    fq, fk, fv = wq[...].astype(F32), wk[...].astype(F32), wv[...].astype(F32)
    fo = jnp.transpose(wo[...].astype(F32))
    for i, w in enumerate((fq, fk, fv, fo)):
        put(i * TILE, tile(w, 0))
    put(4 * TILE, jnp.concatenate([fq[:, TILE:], fk[:, TILE:]], axis=1))
    put(5 * TILE, jnp.concatenate([fv[:, TILE:], fo[:, TILE:]], axis=1))
    cols = p1.shape[1]
    fqb, fvb = qb[...].astype(F32)[None, :], vb[...].astype(F32)[None, :]
    none = jnp.zeros((1, TILE), F32)
    short = jnp.zeros((1, HD), F32)
    bias = jnp.concatenate(
        [fqb[:, :TILE], none, fvb[:, :TILE], none, fqb[:, TILE:], short, fvb[:, TILE:], short], axis=1
    )
    spread = one_hot((rows, width), lambda r, c: c == r + rows * me_d)
    block = jnp.where(row_is((EXTRA, cols), 0), bias, 0.0)
    block = jnp.where(row_is((EXTRA, cols), 7), ub[...].astype(F32)[None, :], block)
    lanes = jnp.zeros((EXTRA, rows), F32)
    for i in range(6):
        lanes = jnp.where(row_is((EXTRA, rows), 1 + i), vecs[i][...].astype(F32)[None, :], lanes)
    lanes = nn(lanes.astype(BF), spread)
    p1[padded : padded + EXTRA, :] = block.astype(BF)
    mixed = jnp.where(
        (lax.broadcasted_iota(jnp.int32, (EXTRA, width), 0) - 1).astype(jnp.uint32) < 6,
        lanes,
        block[:, :width],
    )
    p1[padded : padded + EXTRA, 0:width] = mixed.astype(BF)
    done[...] = jnp.zeros_like(done)


def pack_slots_kernel(sizes, *refs):
    nctx, ntp, ndp, main, width, rows, padded = sizes
    sources, sent, tails, refs = refs[:3], refs[3 : 3 + nctx], refs[3 + nctx], refs[4 + nctx :]
    held, sem = refs[:3], refs[3]
    copies = fetch(sources, held, sem)
    tok, cot, mask = held
    images = nctx * ntp
    me_c, me_t = lax.axis_index("ctx"), lax.axis_index("tp")
    wanted = [(me_c ^ k) * ntp + me_t for k in range(nctx)]
    pick = picker(wanted, images)
    for i in range(2):
        copies[i].wait()
        take_images(held[i], sent, i * (main + EXTRA), pick, images, main)
        tails[i] = held[i][main * images :, :]
    copies[2].wait()
    for k in range(nctx):
        gate = mask[wanted[k], main].astype(F32)
        te = tok[pl.ds(main * images + wanted[k], 1), :] * gate
        ce = cot[pl.ds(main * images + wanted[k], 1), :] * gate
        shape = (EXTRA, width)
        sent[k][main : main + EXTRA, :] = jnp.where(
            row_is(shape, 0), te, jnp.where(row_is(shape, 1), ce, 0.0)
        ).astype(BF)


def join_kernel(axis, stride, own, got, out):
    bit = lax.rem(lax.div(lax.axis_index(axis), stride), 2)
    for i in range(own.shape[0]):
        out[2 * i + bit] = own[i]
        out[2 * i + 1 - bit] = got[i]


def place_rows(stage, own, got, rows):
    bit = lax.rem(lax.axis_index("dp"), 2)
    for i in range(own.shape[0]):
        for piece, last in ((own, bit), (got, 1 - bit)):
            at = pl.ds(pl.multiple_of((2 * i + last) * rows, 16 if rows % 16 == 0 else 8), rows)
            stage[at, :] = piece[i].astype(stage.dtype)[:rows]


def merge_quarter_kernel(sizes, attn, own, got, out, attn_out, stage):
    place_rows(stage, own, got, sizes[5])
    out[...] = stage[...].astype(BF)
    attn_out[...] = attn[...]


def split_kernel(got, *outs):
    for i, out in enumerate(outs):
        cols = out.shape[2]
        out[...] = got[:, :, i * cols : (i + 1) * cols]


def merge_ff_kernel(nctx, *refs):
    out = refs[nctx]
    me_c = lax.axis_index("ctx")
    for k in range(nctx):
        quarter = refs[k].shape[1]
        out[:, pl.ds(pl.multiple_of((me_c ^ k) * quarter, quarter), quarter)] = refs[k][...]


def attention_kernel(sizes, *refs):
    nctx, ntp, ndp, main, width, rows, padded = sizes
    t_in, (own, got, own_oth, got_oth_a, got_oth_b), refs = refs[:nctx], refs[nctx : nctx + 5], refs[nctx + 5 :]
    x_out, mid_out, n1_out, n2_out, qkv, ctx, ctx_full, lse, wqkv, wot, vec, ub, cot, stage, stage_oth = refs
    body = nctx * main
    total = body + EXTRA
    half = got_oth_a.shape[2]
    place_rows(stage, own, got, rows)
    place_rows(stage_oth.at[:, :half], own_oth.at[:, :, :half], got_oth_a, rows)
    place_rows(stage_oth.at[:, half:], own_oth.at[:, :, half:], got_oth_b, rows)
    tiles, outs = assemble(stage[...].astype(F32), stage_oth[...].astype(F32))
    for i, v in enumerate(tiles):
        wqkv[:, i * TILE : (i + 1) * TILE] = v.astype(BF)
    for i, v in enumerate(outs):
        wot[:, i * TILE : (i + 1) * TILE] = v.astype(BF)
    extra = own[0, padded:, :].astype(F32)
    extra_oth = own_oth[0, padded:, :].astype(F32)
    tiles, _ = assemble(extra, extra_oth)
    bias = jnp.concatenate([v[0:1] for v in tiles], axis=1)
    vec_sum = jnp.zeros((EXTRA, width), F32)
    for i in range(own.shape[0]):
        vec_sum += own[i, padded:, :width].astype(F32) + got[i, padded:, :width].astype(F32)
    vec[...] = vec_sum
    ub[...] = jnp.broadcast_to(jnp.concatenate([extra[7:8], extra_oth[7:8]], axis=1), ub.shape)
    extra = jnp.zeros((EXTRA, width), F32)
    for k in range(nctx):
        x_out[k * main : (k + 1) * main, :] = t_in[k][0:main, :].astype(F32)
        cot[k * main : (k + 1) * main, :] = t_in[k][main + EXTRA :, :]
        extra += t_in[k][main : main + EXTRA, :].astype(F32)
    x_out[body:, :] = jnp.where(row_is((EXTRA, width), 0), extra, 0.0)
    cot[body:, :] = jnp.where(row_is((EXTRA, width), 0), extra[1:2, :], 0.0).astype(BF)
    x = x_out[...]
    xhat, _ = norm_stats(x)
    n1 = (xhat * vec_sum[1:2, :] + vec_sum[2:3, :]).astype(BF)
    n1_out[...] = n1
    proj = nn(n1, wqkv[...]) + bias
    qkv[0:total, 0:width] = (proj[:, 0:width].astype(BF).astype(F32) * SCALE).astype(BF)
    qkv[0:total, width:] = proj[:, width:].astype(BF)
    keys = qkv.shape[0]
    qkv[total:, :] = jnp.zeros((keys - total, qkv.shape[1]), BF)
    off = jnp.where(lax.broadcasted_iota(jnp.int32, (1, keys), 1) > body, FLOOR, 0.0)
    low = low_lanes((total, TILE))
    lane = lax.broadcasted_iota(jnp.int32, (total, TILE), 1)
    all_lse = jnp.zeros((total, TILE), F32)
    for p in range(3):
        qp = qkv[0:total, p * TILE : (p + 1) * TILE]
        kp = qkv[:, width + p * TILE : width + (p + 1) * TILE]
        vp = qkv[:, 2 * width + p * TILE : 2 * width + (p + 1) * TILE]
        parts = []
        for a in range(2):
            qa = jnp.where(low if a == 0 else ~low, qp, jnp.zeros_like(qp))
            s = nt(qa, kp) + off
            m = jnp.max(s, axis=-1, keepdims=True)
            e = jnp.exp(s - m)
            l = jnp.sum(e, axis=-1, keepdims=True)
            parts.append(nn(e.astype(BF), vp) * (1.0 / l))
            all_lse = jnp.where(lane == 2 * p + a, m + jnp.log(l), all_lse)
        ctx_full[:, p * TILE : (p + 1) * TILE] = jnp.where(low, parts[0], parts[1])
    ctx[...] = ctx_full[...].astype(BF)
    lse[...] = all_lse
    attended = nt(ctx[...], wot[...]) + vec_sum[5:6, :]
    valid = lax.broadcasted_iota(jnp.int32, (total, 1), 0) <= body
    middle = x_out[...] + jnp.where(valid, attended, 0.0)
    mid_out[...] = middle
    xhat2, _ = norm_stats(middle)
    n2_out[...] = (xhat2 * vec_sum[3:4, :] + vec_sum[4:5, :]).astype(BF)


def ff_half(n2v, dcot, w, ub, hid, hgr, ubgrad, grads, ndp, rows):
    half = w.shape[1] // 2
    quarter = half // 2
    for lo in range(0, half, 256):
        sl = slice(lo, lo + 256)
        pre = nn(n2v, w[:, sl]) + ub[0:1, sl]
        hc = nn(dcot, w[:, half + lo : half + lo + 256])
        act, slope = gelu_pair(pre)
        h = act.astype(BF)
        hg = (hc * slope).astype(BF)
        hid[:, sl] = h
        hgr[:, sl] = hg
        ubgrad[:, sl] = jnp.broadcast_to(jnp.sum(hg.astype(F32), axis=0, keepdims=True), (8, 256))
        for part, g in ((0, tn(n2v, hg).astype(BF)), (1, tn(dcot, h).astype(BF))):
            for d in range(ndp):
                for c in range(2):
                    col = lo + c * TILE
                    at = slice(col % quarter, col % quarter + TILE)
                    grads[2 * part + col // quarter, d, 0:rows, at] = (
                        g[d * rows : (d + 1) * rows, c * TILE : (c + 1) * TILE]
                    )


def mlp_half_kernel(sizes, side, n2, cot, w, ub, hid, hgr, ubgrad, grads):
    half = w.shape[1] // 2
    ff_half(
        n2[...], cot[...], w[...], ub[:, side * half : (side + 1) * half], hid, hgr, ubgrad, grads, sizes[2], sizes[5]
    )


def mlp_sums_kernel(sizes, mid, ctx, wot, vec, cot, w_own, w_oth, hid_own, hid_oth, hgr_own, hgr_oth, bo, dmid, dctx, g_out, vgrad):
    nctx, ntp, ndp, main, width, rows, padded = sizes
    body = nctx * main
    total = body + EXTRA
    half = w_own.shape[1] // 2
    dcot = cot[...]
    middle = mid[...]
    valid = lax.broadcasted_iota(jnp.int32, (total, 1), 0) <= body
    n2g = nt(hgr_own[...], w_own[:, :half]) + nt(hgr_oth[...], w_oth[:, :half])
    xhat, r = norm_stats(middle)
    back = norm_back(n2g * vec[3:4, :], xhat, r)
    middle_grad = dcot.astype(F32) + back
    dmid[...] = middle_grad
    agrad = jnp.where(valid, middle_grad, 0.0).astype(BF)
    dctx[...] = nn(agrad, wot[...]).astype(BF)
    g_out[...] = tn(agrad, ctx[...])
    mlp_out = nt(hid_own[...], w_own[:, half:]) + nt(hid_oth[...], w_oth[:, half:]) + vec[6:7, :]
    bo[...] = (middle + jnp.where(valid, mlp_out, 0.0)).astype(BF)
    shape = vgrad.shape
    v = jnp.where(row_is(shape, 2), jnp.sum(n2g * xhat, axis=0, keepdims=True), 0.0)
    v = jnp.where(row_is(shape, 3), jnp.sum(n2g, axis=0, keepdims=True), v)
    v = jnp.where(row_is(shape, 4), jnp.sum(agrad.astype(F32), axis=0, keepdims=True), v)
    v = jnp.where(row_is(shape, 5), jnp.sum(dcot.astype(F32), axis=0, keepdims=True), v)
    vgrad[...] = v


def pair_back(p, width, total, body, qkv, dctx, lse, ctx):
    keys = qkv.shape[0]
    off = jnp.where(lax.broadcasted_iota(jnp.int32, (1, keys), 1) > body, FLOOR, 0.0)
    low = low_lanes((total, TILE))
    at = slice(p * TILE, (p + 1) * TILE)
    qp = qkv[0:total, at]
    kp = qkv[:, width + p * TILE : width + (p + 1) * TILE]
    vp = qkv[:, 2 * width + p * TILE : 2 * width + (p + 1) * TILE]
    dp = dctx[:, at]
    both = dp.astype(F32) * ctx[:, at]
    qt = jnp.transpose(qp.astype(F32)).astype(BF)
    dt = jnp.transpose(dp.astype(F32)).astype(BF)
    dq, dk, dv = [], [], []
    for a in range(2):
        sel = low if a == 0 else ~low
        qa = jnp.where(sel, qp, jnp.zeros_like(qp))
        da = jnp.where(sel, dp, jnp.zeros_like(dp))
        inner = jnp.sum(jnp.where(sel, both, 0.0), axis=-1, keepdims=True)
        prob = jnp.exp(nt(qa, kp) + off - lse[:, 2 * p + a : 2 * p + a + 1])
        ds = (prob * (nt(da, vp) - inner)).astype(BF)
        dq.append(nn(ds, kp))
        dk.append(nn(qt[a * HD : (a + 1) * HD], ds))
        dv.append(nn(dt[a * HD : (a + 1) * HD], prob.astype(BF)))
    dq = jnp.where(low, dq[0], dq[1]) * SCALE
    dk, dv = (jnp.transpose(jnp.concatenate(v, axis=0))[0:total] for v in (dk, dv))
    return dq.astype(BF), dk.astype(BF), dv.astype(BF)


def attention_back_kernel(sizes, *refs):
    nctx, ntp, ndp, main, width, rows, padded = sizes
    qkv, dctx, lse, ctx, n1, x_in, dmid, wqkv, vec, g_out, vgrad, ub_own, ub_oth = refs[:13]
    ig, g_own, g_oth, dqkv = refs[13:]
    body = nctx * main
    total = body + EXTRA
    for p in range(3):
        for i, v in enumerate(pair_back(p, width, total, body, qkv, dctx, lse, ctx)):
            dqkv[:, i * width + p * TILE : i * width + (p + 1) * TILE] = v
    d = dqkv[...]
    bias = jnp.sum(d.astype(F32), axis=0, keepdims=True)
    g = tn(n1[...], d)
    go = g_out[...]
    own, oth = disassemble([tile(g, i) for i in range(9)], [tile(go, i) for i in range(3)])
    half = padded // 2
    for to, tiles in ((g_own, own), (g_oth, oth)):
        for j in range(4):
            lo = j % 2 * half
            for e in range(ndp):
                to[j, e, 0:rows, :] = tiles[j][e * rows : (e + 1) * rows].astype(BF)
                shared = tiles[4 + j // 2][e * rows + lo : e * rows + min(rows, lo + half)]
                to[j, e, padded : padded + shared.shape[0], :] = shared.astype(BF)
    dn1 = nt(d, wqkv[...])
    xhat, r = norm_stats(x_in[...])
    grad = dmid[...] + norm_back(dn1 * vec[1:2, :], xhat, r)
    ig[...] = grad.astype(BF)
    gains = jnp.sum(dn1 * xhat, axis=0, keepdims=True)
    shifts = jnp.sum(dn1, axis=0, keepdims=True)
    vecs = [gains, shifts] + [vgrad[i : i + 1, :] for i in range(2, 6)]
    zero = [jnp.zeros((1, TILE), F32)] * 3
    bias_own, bias_oth = disassemble([tile(bias, i) for i in range(9)], zero)
    for to, tiles, ub in ((g_own, bias_own, ub_own), (g_oth, bias_oth, ub_oth)):
        rows_ = [tile(v, i) for v in vecs for i in range(3)] + tiles
        rows_ += [ub[0:1, i * TILE : (i + 1) * TILE] for i in range(6)]
        for j in range(4):
            block = jnp.zeros((EXTRA, TILE), F32)
            for i, v in enumerate(rows_[8 * j : 8 * (j + 1)]):
                block = jnp.where(row_is(block.shape, i), v, block)
            for e in range(ndp):
                to[j, e, padded + half :, :] = block.astype(BF)


def sum_core_kernel(n, own, oth, *outs):
    me = lax.axis_index("ctx")
    for k in range(n):
        outs[k][...] = (own[me ^ k].astype(F32) + oth[me ^ k].astype(F32)).astype(BF)


def sum_ctx_kernel(n, ndp, *refs):
    me = lax.axis_index("dp")
    for k in range(ndp):
        v = refs[0][me ^ k].astype(F32)
        for i in range(1, n):
            v = v + refs[i][me ^ k].astype(F32)
        refs[n + k][...] = v.astype(BF)


def halve(axis, stride, item, keep, send):
    bit = lax.rem(lax.div(lax.axis_index(axis), stride), 2)
    for j in range(keep.shape[0]):
        keep[j] = item(2 * j + bit).astype(BF)
        send[j] = item(2 * j + 1 - bit).astype(BF)


def sum_ctx_halves_kernel(n, *refs):
    terms, (keep, send) = refs[:n], refs[n:]

    def item(i):
        v = terms[0][i].astype(F32)
        for t in terms[1:]:
            v = v + t[i].astype(F32)
        return v

    halve("dp", 1, item, keep, send)


def add_halves_kernel(stride, own, got, keep, send):
    halve("dp", stride, lambda i: own[i].astype(F32) + got[i].astype(F32), keep, send)


def sum_dp_kernel(n, own, got, *refs):
    out = refs[n]
    rows = own.shape[1]
    out[:rows, :] = (own[0].astype(F32) + got[0, 0:rows, :].astype(F32)).astype(BF)
    v = refs[0][...].astype(F32)
    for r in refs[1:n]:
        v = v + r[...].astype(F32)
    span = out.shape[0] - rows
    out[rows:, :] = jnp.zeros((span, out.shape[1]), BF)
    for i in range(out.shape[1] // TILE):
        part = v[i * span : (i + 1) * span].astype(BF)
        if part.shape[0]:
            out[rows : rows + part.shape[0], i * TILE : (i + 1) * TILE] = part


def returns_kernel(sizes, bo, ig, out):
    nctx, ntp, ndp, main, width, rows, padded = sizes
    me = lax.axis_index("ctx")
    body = nctx * main
    shape = (EXTRA, width)
    extra = jnp.where(
        row_is(shape, 0),
        bo[body:, :].astype(F32),
        jnp.where(row_is(shape, 1), ig[body:, :].astype(F32)[0:1, :], 0.0),
    ).astype(BF)
    for k in range(nctx):
        at = slice(k * main, (k + 1) * main)
        out[me ^ k, 0:main, :] = bo[at, :]
        out[me ^ k, main : main + EXTRA, :] = extra
        out[me ^ k, main + EXTRA :, :] = ig[at, :]


def hand_on_kernel(held, out):
    out[...] = held[...]


def grads_kernel(sizes, *refs):
    nctx, ntp, ndp, main, width, rows, padded = sizes
    parts, refs = refs[:nctx], refs[nctx:]
    gq, gk, gv, gqb, gvb, go, gu, gub, gd = refs[:9]
    gvec, f, f2 = refs[9:15], refs[15], refs[16]
    me, me_d = lax.axis_index("ctx"), lax.axis_index("dp")
    span = parts[0].shape[0] - padded
    for k in range(nctx):
        f2[me ^ k] = parts[k][0:padded, :].astype(F32)
        for i in range(f2.shape[2] // TILE):
            n = min(span, f.shape[1] - i * span)
            if n > 0:
                f[me ^ k, i * span : i * span + n, :] = parts[k][
                    padded : padded + n, i * TILE : (i + 1) * TILE
                ].astype(F32)
    half = f2.shape[2]
    for j in range(2):
        gu[:, j * half : (j + 1) * half] = f2[j, 0:rows, :]
        gd[:, j * half : (j + 1) * half] = f2[2 + j, 0:rows, :]
    q01, k01, v01, o01 = (f[j, 0:rows, :] for j in range(4))
    low, high = slice(padded, padded + padded // 2), slice(padded, padded + rows - padded // 2)
    qk2 = jnp.concatenate([f[0, low, :], f[1, high, :]], axis=0)
    vo2 = jnp.concatenate([f[2, low, :], f[3, high, :]], axis=0)
    gq[:, 0:TILE] = q01
    gq[:, TILE:] = qk2[:, 0:HD]
    gk[:, 0:TILE] = k01
    gk[:, TILE:] = swap(qk2)[:, 0:HD]
    gv[:, 0:TILE] = v01
    gv[:, TILE:] = vo2[:, 0:HD]
    go[0:TILE, :] = jnp.transpose(o01)
    go[TILE:, :] = jnp.transpose(vo2)[HD:, :]

    def line(i):
        at = padded + padded // 2 + i % 8
        return f[i // 8, at : at + 1, :]

    for i in range(6):
        v = jnp.concatenate([line(3 * i), line(3 * i + 1), line(3 * i + 2)], axis=1)
        v = jnp.broadcast_to(v, (8, width))
        v = pltpu.roll(v, lax.rem(width - me_d * rows, width), axis=1)
        gvec[i][...] = v[0, 0:rows]
    b = [line(18 + i) for i in range(6)]
    gqb[...] = jnp.concatenate([b[0], b[4][:, 0:HD]], axis=1)[0]
    gvb[...] = jnp.concatenate([b[2], b[5][:, 0:HD]], axis=1)[0]
    gub[...] = jnp.concatenate([line(24 + i) for i in range(6)], axis=1)[0]


def unpack_kernel(sizes, own, oth, tails, mask, *refs):
    nctx, ntp, ndp, main, width, rows, padded = sizes
    outs, done, valid, sem = refs[:2], refs[2], refs[3], refs[4]
    images = nctx * ntp
    me_t = lax.axis_index("tp")
    where = [j * ntp + t for t in (me_t, 1 - me_t) for j in range(nctx)]
    sources = [v.at[j] for v in (own, oth) for j in range(nctx)]
    get_valid = pltpu.make_async_copy(mask, valid, sem.at[0])
    get_valid.start()

    def hit(r, c):
        img = where[-1]
        for j in range(images - 1):
            img = jnp.where(c // BLOCK == j, where[j], img)
        return r == (c % BLOCK) * images + img

    put = one_hot((images * BLOCK, images * BLOCK), hit)
    for i in range(2):
        for b in range(main // BLOCK):
            lo = i * (main + EXTRA) + b * BLOCK
            got = jnp.concatenate([src[lo : lo + BLOCK, :] for src in sources], axis=0)
            outs[i][b * BLOCK * images : (b + 1) * BLOCK * images, :] = nn(put, got)
    get_valid.wait()
    for i in range(2):
        for src, img in zip(sources, where):
            got = src[main : main + EXTRA, :].astype(F32)[i : i + 1, :]
            outs[i][pl.ds(main * images + img, 1), :] = jnp.where(
                valid[img, main] > 0, got, tails[i, pl.ds(img, 1), :]
            )
    done[...] = jnp.zeros_like(done)


def xor(n, k):
    return [(i, i ^ k) for i in range(n)]


def over(axis, n, items):
    return [items[0]] + [lax.ppermute(items[k], axis, xor(n, k)) for k in range(1, n)]


def body(nctx, ntp, ndp, *args):
    (tokens, valid_mask, cotangent, w_query, w_key, w_value, query_bias, value_bias, w_out, w_up, up_bias, w_down) = args[:12]
    vecs = args[12:]
    images, slots, width = tokens.shape
    main = slots - 1
    rows = w_query.shape[0]
    padded = -(-rows // EXTRA) * EXTRA
    ff = w_up.shape[1]
    p1_cols = 4 * w_query.shape[1]
    sizes = (nctx, ntp, ndp, main, width, rows, padded)
    total = nctx * main + EXTRA
    keys = -(-total // TILE) * TILE
    stage = BF if rows % 16 == 0 else F32
    flip = xor(ntp, 1)
    tok = jnp.transpose(tokens, (1, 0, 2)).reshape(slots * images, width)
    cot = jnp.transpose(cotangent, (1, 0, 2)).reshape(slots * images, width)

    def one(f):
        return functools.partial(f, sizes)

    def other(v):
        return lax.ppermute(v, "tp", flip)

    def held(arrays):
        return [
            (pltpu.SMEM if v.dtype == jnp.int32 else pltpu.VMEM)(v.shape, v.dtype) for v in arrays
        ] + [pltpu.SemaphoreType.DMA((len(arrays),))]

    def gather_dp(name, piece, after):
        v = piece[None]
        stride = ndp // 2
        while stride > 1:
            v = call(
                name,
                functools.partial(join_kernel, "dp", stride),
                sds((2 * v.shape[0],) + v.shape[1:], v.dtype),
                after=after,
            )(v, lax.ppermute(v, "dp", xor(ndp, stride)))
            stride //= 2
        return v, lax.ppermute(v, "dp", xor(ndp, 1))

    sources = [w_query, w_key, w_value, w_out, w_up, jnp.transpose(w_down), query_bias, value_bias, up_bias, *vecs]
    p1, p2q, packed = call(
        "pack_weights",
        functools.partial(pack_weights_kernel, sizes, len(sources)),
        [sds((padded + EXTRA, p1_cols), BF), sds((padded, ff // 2), BF), sds((8, TILE), F32)],
        scratch=held(sources),
        mib=56,
        raw=range(len(sources)),
    )(*sources)
    sources = [tok, cot, valid_mask]
    *sent, tails = call(
        "pack_slots",
        one(pack_slots_kernel),
        [sds((2 * main + EXTRA, width), BF)] * nctx + [sds((2, images, width), F32)],
        scratch=held(sources),
        mib=48,
        raw=range(3),
    )(*sources)
    t_in = over("ctx", nctx, sent)
    w2q = gather_dp("join_quarter", p2q, [])
    w1, w1_got = gather_dp("join_attn", p1, [])
    w2q, w1_early = call(
        "merge_quarter",
        one(merge_quarter_kernel),
        [sds((width, ff // 2), BF), sds(w1.shape, BF)],
        scratch=[pltpu.VMEM((width, ff // 2), stage)],
        after=t_in[1:],
    )(w1, *w2q)
    w1_oth = other(w1_early)
    w2q = over("ctx", nctx, [w2q] * nctx)
    late = call(
        "split_attn",
        split_kernel,
        [sds(w1.shape[:2] + (p1_cols // 2,), BF)] * 2,
        after=[w1_oth, w2q[0]],
    )(w1_got)
    w1 = [w1, w1_got, w1_oth, *[other(v) for v in late]]
    x, mid, n1, n2, qkv, ctx, ctx_full, lse, wqkv, wot, vec, ub, cot_in = call(
        "attention",
        one(attention_kernel),
        [
            sds((total, width), F32), sds((total, width), F32), sds((total, width), BF), sds((total, width), BF),
            sds((keys, 3 * width), BF), sds((total, width), BF), sds((total, width), F32), sds((total, TILE), F32),
            sds((width, 3 * width), BF), sds((width, width), BF), sds((EXTRA, width), F32), sds((8, 2 * ff), F32),
            sds((total, width), BF),
        ],
        scratch=[pltpu.VMEM((width, p1_cols), stage)] * 2,
        mib=32,
    )(*t_in, *w1)
    w2_own = call(
        "merge_ff", functools.partial(merge_ff_kernel, nctx), sds((width, 2 * ff), BF), after=[vec]
    )(*w2q)
    w2_oth = other(w2_own)
    ff_grads = sds((4, ndp, padded, ff // 2), BF)

    def mlp_half(name, side, w, after=()):
        return call(
            name,
            functools.partial(mlp_half_kernel, sizes, side),
            [sds((total, ff), BF), sds((total, ff), BF), sds((8, ff), F32), ff_grads],
            mib=32,
            after=after,
        )(n2, cot_in, w, ub)

    hid_own, hgr_own, ub_own, g2_own = mlp_half("mlp_own", 0, w2_own)
    hid_oth, hgr_oth, ub_oth, g2_oth = mlp_half("mlp_oth", 1, w2_oth, [ub_own])
    bo, dmid, dctx, g_out, vgrad = call(
        "mlp_sums",
        one(mlp_sums_kernel),
        [
            sds((total, width), BF), sds((total, width), F32), sds((total, width), BF), sds((width, width), F32),
            sds((EXTRA, width), F32),
        ],
        mib=32,
    )(mid, ctx, wot, vec, cot_in, w2_own, w2_oth, hid_own, hid_oth, hgr_own, hgr_oth)

    def core_sums(name, own, oth, after=()):
        outs = [sds(own.shape[1:], BF)] * nctx
        return call(name, functools.partial(sum_core_kernel, nctx), outs, after=after)(own, other(oth))

    def by_image(v):
        return jnp.transpose(v.reshape(slots, images, width), (1, 0, 2))

    s2_send = core_sums("sum_core_ff", g2_own, g2_oth, after=[vgrad])
    s2 = over("ctx", nctx, s2_send)
    ig, g1_own, g1_oth = call(
        "attention_back",
        one(attention_back_kernel),
        [sds((total, width), BF)] + [sds((4, ndp, padded + padded // 2 + EXTRA, TILE), BF)] * 2,
        scratch=[pltpu.VMEM((total, 3 * width), BF)],
        mib=32,
        after=[s2_send[0]],
    )(qkv, dctx, lse, ctx_full, n1, x, dmid, wqkv, vec, g_out, vgrad, ub_own, ub_oth)
    half = sds((ndp // 2,) + s2[0].shape[1:], BF)
    keep, send = call(
        "sum_ctx_ff", functools.partial(sum_ctx_halves_kernel, nctx), [half, half], after=[g1_own]
    )(*s2)
    s1_send = core_sums("sum_core_attn", g1_own, g1_oth, after=[keep])
    s1 = over("ctx", nctx, s1_send)
    back = call(
        "returns",
        one(returns_kernel),
        sds((nctx, 2 * main + EXTRA, width), BF),
        after=[s1[1]],
    )(bo, ig)
    returned = lax.all_to_all(back, "ctx", 0, 0)
    u1_send = call(
        "sum_ctx_attn",
        functools.partial(sum_ctx_kernel, nctx, ndp),
        [sds(s1[0].shape[1:], BF)] * ndp,
        after=[back],
    )(*s1)
    u1 = over("dp", ndp, u1_send)
    stride = 2
    while stride < ndp:
        half = sds((keep.shape[0] // 2,) + keep.shape[1:], BF)
        keep, send = call(
            "add_dp_ff", functools.partial(add_halves_kernel, stride), [half, half], after=[u1_send[0]]
        )(keep, lax.ppermute(send, "dp", xor(ndp, stride // 2)))
        stride *= 2
    summed = call(
        "sum_dp", functools.partial(sum_dp_kernel, ndp), sds((padded + -(-s1[0].shape[1] // (3 * EXTRA)) * EXTRA, ff // 2), BF)
    )(keep, lax.ppermute(send, "dp", xor(ndp, ndp // 2)), *u1)
    shares = over("ctx", nctx, [summed] * nctx)
    back = call("hand_on", hand_on_kernel, sds(returned.shape, BF), after=[summed])(returned)
    block_out, input_grad, placed = call(
        "place_slots",
        one(unpack_kernel),
        [sds(tok.shape, F32)] * 2 + [sds((8, TILE), F32)],
        scratch=[pltpu.SMEM(valid_mask.shape, valid_mask.dtype), pltpu.SemaphoreType.DMA((1,))],
        raw=(3,),
        mib=16,
    )(back, other(back), tails, valid_mask)
    gq, gk, gv, gqb, gvb, go, gu, gub, gd, *gvec = call(
        "place_grads",
        one(grads_kernel),
        [
            sds(w_query.shape, F32), sds(w_key.shape, F32), sds(w_value.shape, F32),
            sds(query_bias.shape, F32), sds(value_bias.shape, F32), sds(w_out.shape, F32),
            sds(w_up.shape, F32), sds(up_bias.shape, F32), sds((rows, ff), F32),
        ]
        + [sds((rows,), F32)] * 6,
        scratch=[
            pltpu.VMEM((nctx,) + s1[0].shape[1:], F32),
            pltpu.VMEM((nctx, padded, ff // 2), F32),
        ],
        after=[placed],
    )(*shares)
    return (by_image(block_out), by_image(input_grad), gq, gk, gv, gqb, gvb, go, gu, gub, jnp.transpose(gd), *gvec)


def solution(mesh):
    rows, cols, tp, dp = P("dp", "tp"), P("tp", "dp"), P("tp"), P("dp")
    act = P("dp", "ctx", None)
    return jax.shard_map(
        functools.partial(body, mesh.shape["ctx"], mesh.shape["tp"], mesh.shape["dp"]),
        mesh=mesh,
        in_specs=(act, P("dp", "ctx"), act, rows, rows, rows, tp, tp, cols, rows, tp, cols) + (dp,) * 6,
        out_specs=(act, act, rows, rows, rows, tp, tp, cols, rows, tp, cols) + (dp,) * 6,
        check_vma=False,
    )
```

```python
import functools

import jax
import jax.numpy as jnp
from jax import lax
from jax.experimental import pallas as pl
from jax.experimental.pallas import tpu as pltpu
from jax.sharding import PartitionSpec as P

HD = 64
EPS = 1e-06
SCALE = 0.125
FLOOR = -1e30
BF = jnp.bfloat16
F32 = jnp.float32
TILE = 128
TIMES = {
    "pack_weights": 2.0, "pack_slots": 3.0, "pack_cotangent": 2.0, "attention": 0.0, "mlp_own": 4.0, "mlp_oth": 4.0, "mlp_sums": 2.0, "attention_back": 11.0,
    "place_grads": 1.0, "place_slots": 2.3, "join_quarter": 20.0, "sum_ctx_attn": 0.5, "sum_dp": 5.0, "sum_ctx_first": 50.0,
}
EXTRA = 16


def call(name, kernel, out_shape, scratch=(), mib=8, after=(), raw=()):
    after = list(after)

    def ordered(*refs):
        kernel(*refs[len(after) :])

    def run(*args):
        specs = [pl.BlockSpec(memory_space=pl.ANY)] * len(after) + [
            pl.BlockSpec(memory_space=pltpu.HBM if i in raw else pltpu.VMEM)
            for i in range(len(args))
        ]
        return pl.pallas_call(
            ordered,
            name=name,
            out_shape=out_shape,
            in_specs=specs,
            out_specs=jax.tree.map(lambda _: pl.BlockSpec(memory_space=pltpu.VMEM), out_shape),
            scratch_shapes=list(scratch),
            compiler_params=pltpu.CompilerParams(vmem_limit_bytes=mib << 20),
            cost_estimate=pl.CostEstimate(
                flops=int(TIMES.get(name, 0.2) * 1.15e9), bytes_accessed=1, transcendentals=0
            ),
        )(*after, *args)

    return run


def sds(shape, dtype):
    return jax.ShapeDtypeStruct(shape, dtype)


def nn(a, b):
    return lax.dot_general(a, b, (((1,), (0,)), ((), ())), preferred_element_type=F32)


def nt(a, b):
    return lax.dot_general(a, b, (((1,), (1,)), ((), ())), preferred_element_type=F32)


def tn(a, b):
    return lax.dot_general(a, b, (((0,), (0,)), ((), ())), preferred_element_type=F32)


def swap(v):
    return pltpu.roll(v, HD, axis=1)


def low_lanes(shape):
    return lax.broadcasted_iota(jnp.int32, shape, 1) < HD


def row_is(shape, row):
    return lax.broadcasted_iota(jnp.int32, shape, 0) == row


def tile(v, i):
    return v[:, i * TILE : (i + 1) * TILE]


def assemble(own, oth):
    low = low_lanes((own.shape[0], TILE))
    own_qk, own_vo, oth_qk, oth_vo = tile(own, 4), tile(own, 5), tile(oth, 4), tile(oth, 5)
    qkv = [
        tile(own, 0), tile(oth, 0), jnp.where(low, own_qk, swap(oth_qk)),
        tile(own, 1), tile(oth, 1), jnp.where(low, swap(own_qk), oth_qk),
        tile(own, 2), tile(oth, 2), jnp.where(low, own_vo, swap(oth_vo)),
    ]
    out = [tile(own, 3), tile(oth, 3), jnp.where(low, swap(own_vo), oth_vo)]
    return qkv, out


def disassemble(qkv, out):
    low = low_lanes(qkv[0].shape)
    own = [qkv[0], qkv[3], qkv[6], out[0], jnp.where(low, qkv[2], swap(qkv[5])), jnp.where(low, qkv[8], swap(out[2]))]
    oth = [qkv[1], qkv[4], qkv[7], out[1], jnp.where(low, swap(qkv[2]), qkv[5]), jnp.where(low, swap(qkv[8]), out[2])]
    return own, oth


def norm_stats(v):
    mean = jnp.mean(v, axis=-1, keepdims=True)
    centered = v - mean
    r = lax.rsqrt(jnp.mean(centered * centered, axis=-1, keepdims=True) + EPS)
    return centered * r, r


def norm_back(e, xhat, r):
    return r * (
        e
        - jnp.mean(e, axis=-1, keepdims=True)
        - xhat * jnp.mean(e * xhat, axis=-1, keepdims=True)
    )


def gelu_pair(v):
    phi = 0.5 + 0.5 * lax.erf(v * 0.7071067811865476)
    return v * phi, phi + (0.3989422804014327 * v) * jnp.exp(-0.5 * v * v)


BLOCK = 16


def one_hot(shape, hit):
    r, c = (lax.broadcasted_iota(jnp.int32, shape, i) for i in range(2))
    return hit(r, c).astype(F32).astype(BF)


def picker(wanted, images):
    def hit(r, c):
        img = wanted[-1]
        for k in range(len(wanted) - 1):
            img = jnp.where(r // BLOCK == k, wanted[k], img)
        return c == (r % BLOCK) * images + img

    return one_hot((len(wanted) * BLOCK, images * BLOCK), hit)


def take_images(ref, outs, at, pick, images, count):
    for b in range(count // BLOCK):
        got = nn(pick, ref[b * BLOCK * images : (b + 1) * BLOCK * images, :].astype(BF)).astype(BF)
        for k in range(len(outs)):
            outs[k][at + b * BLOCK : at + (b + 1) * BLOCK, :] = got[k * BLOCK : (k + 1) * BLOCK]


def fetch(sources, held, sem):
    copies = [pltpu.make_async_copy(sources[i], held[i], sem.at[i]) for i in range(len(sources))]
    for c in copies:
        c.start()
    return copies


def pack_weights_kernel(sizes, count, *refs):
    nctx, ntp, ndp, main, width, rows, padded = sizes
    sources, (p1, p2q, done), refs = refs[:count], refs[count : count + 3], refs[count + 3 :]
    held, sem = refs[:count], refs[count]
    copies = fetch(sources, held, sem)
    wq, wk, wv, wo, wu, wd, qb, vb, ub = held[:9]
    vecs = held[9:]
    me_c, me_d = lax.axis_index("ctx"), lax.axis_index("dp")
    for c in copies:
        c.wait()
    if padded > rows:
        p1[0:padded, :] = jnp.zeros((padded, p1.shape[1]), BF)
        p2q[...] = jnp.zeros(p2q.shape, BF)
    quarter = p2q.shape[1]
    for j in range(nctx):
        src = (wu, wd)[j // 2][:, (j % 2) * quarter : (j % 2 + 1) * quarter]

        @pl.when(me_c == j)
        def _(src=src):
            p2q[0:rows, :] = src

    def put(lo, value):
        p1[0:rows, lo : lo + value.shape[1]] = value.astype(BF)

    fq, fk, fv = wq[...].astype(F32), wk[...].astype(F32), wv[...].astype(F32)
    fo = jnp.transpose(wo[...].astype(F32))
    for i, w in enumerate((fq, fk, fv, fo)):
        put(i * TILE, tile(w, 0))
    put(4 * TILE, jnp.concatenate([fq[:, TILE:], fk[:, TILE:]], axis=1))
    put(5 * TILE, jnp.concatenate([fv[:, TILE:], fo[:, TILE:]], axis=1))
    cols = p1.shape[1]
    fqb, fvb = qb[...].astype(F32)[None, :], vb[...].astype(F32)[None, :]
    none = jnp.zeros((1, TILE), F32)
    short = jnp.zeros((1, HD), F32)
    bias = jnp.concatenate(
        [fqb[:, :TILE], none, fvb[:, :TILE], none, fqb[:, TILE:], short, fvb[:, TILE:], short], axis=1
    )
    spread = one_hot((rows, width), lambda r, c: c == r + rows * me_d)
    block = jnp.where(row_is((EXTRA, cols), 0), bias, 0.0)
    block = jnp.where(row_is((EXTRA, cols), 7), ub[...].astype(F32)[None, :], block)
    lanes = jnp.zeros((EXTRA, rows), F32)
    for i in range(6):
        lanes = jnp.where(row_is((EXTRA, rows), 1 + i), vecs[i][...].astype(F32)[None, :], lanes)
    lanes = nn(lanes.astype(BF), spread)
    p1[padded : padded + EXTRA, :] = block.astype(BF)
    mixed = jnp.where(
        (lax.broadcasted_iota(jnp.int32, (EXTRA, width), 0) - 1).astype(jnp.uint32) < 6,
        lanes,
        block[:, :width],
    )
    p1[padded : padded + EXTRA, 0:width] = mixed.astype(BF)
    done[...] = jnp.zeros_like(done)


def pack_slots_kernel(sizes, *refs):
    nctx, ntp, ndp, main, width, rows, padded = sizes
    sources, sent, tails, refs = refs[:3], refs[3 : 3 + nctx], refs[3 + nctx], refs[4 + nctx :]
    held, sem = refs[:3], refs[3]
    copies = fetch(sources, held, sem)
    tok, cot, mask = held
    images = nctx * ntp
    me_c, me_t = lax.axis_index("ctx"), lax.axis_index("tp")
    wanted = [(me_c ^ k) * ntp + me_t for k in range(nctx)]
    pick = picker(wanted, images)
    for i in range(2):
        copies[i].wait()
        take_images(held[i], sent, i * (main + EXTRA), pick, images, main)
        tails[i] = held[i][main * images :, :]
    copies[2].wait()
    for k in range(nctx):
        gate = mask[wanted[k], main].astype(F32)
        te = tok[pl.ds(main * images + wanted[k], 1), :] * gate
        ce = cot[pl.ds(main * images + wanted[k], 1), :] * gate
        shape = (EXTRA, width)
        sent[k][main : main + EXTRA, :] = jnp.where(
            row_is(shape, 0), te, jnp.where(row_is(shape, 1), ce, 0.0)
        ).astype(BF)


def join_kernel(axis, stride, own, got, out):
    bit = lax.rem(lax.div(lax.axis_index(axis), stride), 2)
    for i in range(own.shape[0]):
        out[2 * i + bit] = own[i]
        out[2 * i + 1 - bit] = got[i]


def place_rows(stage, own, got, rows):
    bit = lax.rem(lax.axis_index("dp"), 2)
    for i in range(own.shape[0]):
        for piece, last in ((own, bit), (got, 1 - bit)):
            at = pl.ds(pl.multiple_of((2 * i + last) * rows, 16 if rows % 16 == 0 else 8), rows)
            stage[at, :] = piece[i].astype(stage.dtype)[:rows]


def merge_quarter_kernel(sizes, attn, own, got, out, attn_out, stage):
    place_rows(stage, own, got, sizes[5])
    out[...] = stage[...].astype(BF)
    attn_out[...] = attn[...]


def split_kernel(got, *outs):
    for i, out in enumerate(outs):
        cols = out.shape[2]
        out[...] = got[:, :, i * cols : (i + 1) * cols]


def merge_ff_kernel(nctx, *refs):
    out = refs[nctx]
    me_c = lax.axis_index("ctx")
    for k in range(nctx):
        quarter = refs[k].shape[1]
        out[:, pl.ds(pl.multiple_of((me_c ^ k) * quarter, quarter), quarter)] = refs[k][...]


def attention_kernel(sizes, *refs):
    nctx, ntp, ndp, main, width, rows, padded = sizes
    t_in, (own, got, own_oth, got_oth_a, got_oth_b), refs = refs[:nctx], refs[nctx : nctx + 5], refs[nctx + 5 :]
    x_out, mid_out, n1_out, n2_out, qkv, ctx, ctx_full, lse, wqkv, wot, vec, ub, cot, stage, stage_oth = refs
    body = nctx * main
    total = body + EXTRA
    half = got_oth_a.shape[2]
    place_rows(stage, own, got, rows)
    place_rows(stage_oth.at[:, :half], own_oth.at[:, :, :half], got_oth_a, rows)
    place_rows(stage_oth.at[:, half:], own_oth.at[:, :, half:], got_oth_b, rows)
    tiles, outs = assemble(stage[...].astype(F32), stage_oth[...].astype(F32))
    for i, v in enumerate(tiles):
        wqkv[:, i * TILE : (i + 1) * TILE] = v.astype(BF)
    for i, v in enumerate(outs):
        wot[:, i * TILE : (i + 1) * TILE] = v.astype(BF)
    extra = own[0, padded:, :].astype(F32)
    extra_oth = own_oth[0, padded:, :].astype(F32)
    tiles, _ = assemble(extra, extra_oth)
    bias = jnp.concatenate([v[0:1] for v in tiles], axis=1)
    vec_sum = jnp.zeros((EXTRA, width), F32)
    for i in range(own.shape[0]):
        vec_sum += own[i, padded:, :width].astype(F32) + got[i, padded:, :width].astype(F32)
    vec[...] = vec_sum
    ub[...] = jnp.broadcast_to(jnp.concatenate([extra[7:8], extra_oth[7:8]], axis=1), ub.shape)
    extra = jnp.zeros((EXTRA, width), F32)
    for k in range(nctx):
        x_out[k * main : (k + 1) * main, :] = t_in[k][0:main, :].astype(F32)
        cot[k * main : (k + 1) * main, :] = t_in[k][main + EXTRA :, :]
        extra += t_in[k][main : main + EXTRA, :].astype(F32)
    x_out[body:, :] = jnp.where(row_is((EXTRA, width), 0), extra, 0.0)
    cot[body:, :] = jnp.where(row_is((EXTRA, width), 0), extra[1:2, :], 0.0).astype(BF)
    x = x_out[...]
    xhat, _ = norm_stats(x)
    n1 = (xhat * vec_sum[1:2, :] + vec_sum[2:3, :]).astype(BF)
    n1_out[...] = n1
    proj = nn(n1, wqkv[...]) + bias
    qkv[0:total, 0:width] = (proj[:, 0:width].astype(BF).astype(F32) * SCALE).astype(BF)
    qkv[0:total, width:] = proj[:, width:].astype(BF)
    keys = qkv.shape[0]
    qkv[total:, :] = jnp.zeros((keys - total, qkv.shape[1]), BF)
    off = jnp.where(lax.broadcasted_iota(jnp.int32, (1, keys), 1) > body, FLOOR, 0.0)
    low = low_lanes((total, TILE))
    lane = lax.broadcasted_iota(jnp.int32, (total, TILE), 1)
    all_lse = jnp.zeros((total, TILE), F32)
    for p in range(3):
        qp = qkv[0:total, p * TILE : (p + 1) * TILE]
        kp = qkv[:, width + p * TILE : width + (p + 1) * TILE]
        vp = qkv[:, 2 * width + p * TILE : 2 * width + (p + 1) * TILE]
        parts = []
        for a in range(2):
            qa = jnp.where(low if a == 0 else ~low, qp, jnp.zeros_like(qp))
            s = nt(qa, kp) + off
            m = jnp.max(s, axis=-1, keepdims=True)
            e = jnp.exp(s - m)
            l = jnp.sum(e, axis=-1, keepdims=True)
            parts.append(nn(e.astype(BF), vp) * (1.0 / l))
            all_lse = jnp.where(lane == 2 * p + a, m + jnp.log(l), all_lse)
        ctx_full[:, p * TILE : (p + 1) * TILE] = jnp.where(low, parts[0], parts[1])
    ctx[...] = ctx_full[...].astype(BF)
    lse[...] = all_lse
    attended = nt(ctx[...], wot[...]) + vec_sum[5:6, :]
    valid = lax.broadcasted_iota(jnp.int32, (total, 1), 0) <= body
    middle = x_out[...] + jnp.where(valid, attended, 0.0)
    mid_out[...] = middle
    xhat2, _ = norm_stats(middle)
    n2_out[...] = (xhat2 * vec_sum[3:4, :] + vec_sum[4:5, :]).astype(BF)


def ff_half(n2v, dcot, w, ub, hid, hgr, ubgrad, grads, ndp, rows):
    half = w.shape[1] // 2
    quarter = half // 2
    for lo in range(0, half, 256):
        sl = slice(lo, lo + 256)
        pre = nn(n2v, w[:, sl]) + ub[0:1, sl]
        hc = nn(dcot, w[:, half + lo : half + lo + 256])
        act, slope = gelu_pair(pre)
        h = act.astype(BF)
        hg = (hc * slope).astype(BF)
        hid[:, sl] = h
        hgr[:, sl] = hg
        ubgrad[:, sl] = jnp.broadcast_to(jnp.sum(hg.astype(F32), axis=0, keepdims=True), (8, 256))
        for part, g in ((0, tn(n2v, hg).astype(BF)), (1, tn(dcot, h).astype(BF))):
            for d in range(ndp):
                for c in range(2):
                    col = lo + c * TILE
                    at = slice(col % quarter, col % quarter + TILE)
                    grads[2 * part + col // quarter, d, 0:rows, at] = (
                        g[d * rows : (d + 1) * rows, c * TILE : (c + 1) * TILE]
                    )


def mlp_half_kernel(sizes, side, n2, cot, w, ub, hid, hgr, ubgrad, grads):
    half = w.shape[1] // 2
    ff_half(
        n2[...], cot[...], w[...], ub[:, side * half : (side + 1) * half], hid, hgr, ubgrad, grads, sizes[2], sizes[5]
    )


def mlp_sums_kernel(sizes, mid, ctx, wot, vec, cot, w_own, w_oth, hid_own, hid_oth, hgr_own, hgr_oth, bo, dmid, dctx, g_out, vgrad):
    nctx, ntp, ndp, main, width, rows, padded = sizes
    body = nctx * main
    total = body + EXTRA
    half = w_own.shape[1] // 2
    dcot = cot[...]
    middle = mid[...]
    valid = lax.broadcasted_iota(jnp.int32, (total, 1), 0) <= body
    n2g = nt(hgr_own[...], w_own[:, :half]) + nt(hgr_oth[...], w_oth[:, :half])
    xhat, r = norm_stats(middle)
    back = norm_back(n2g * vec[3:4, :], xhat, r)
    middle_grad = dcot.astype(F32) + back
    dmid[...] = middle_grad
    agrad = jnp.where(valid, middle_grad, 0.0).astype(BF)
    dctx[...] = nn(agrad, wot[...]).astype(BF)
    g_out[...] = tn(agrad, ctx[...])
    mlp_out = nt(hid_own[...], w_own[:, half:]) + nt(hid_oth[...], w_oth[:, half:]) + vec[6:7, :]
    bo[...] = (middle + jnp.where(valid, mlp_out, 0.0)).astype(BF)
    shape = vgrad.shape
    v = jnp.where(row_is(shape, 2), jnp.sum(n2g * xhat, axis=0, keepdims=True), 0.0)
    v = jnp.where(row_is(shape, 3), jnp.sum(n2g, axis=0, keepdims=True), v)
    v = jnp.where(row_is(shape, 4), jnp.sum(agrad.astype(F32), axis=0, keepdims=True), v)
    v = jnp.where(row_is(shape, 5), jnp.sum(dcot.astype(F32), axis=0, keepdims=True), v)
    vgrad[...] = v


def pair_back(p, width, total, body, qkv, dctx, lse, ctx):
    keys = qkv.shape[0]
    off = jnp.where(lax.broadcasted_iota(jnp.int32, (1, keys), 1) > body, FLOOR, 0.0)
    low = low_lanes((total, TILE))
    at = slice(p * TILE, (p + 1) * TILE)
    qp = qkv[0:total, at]
    kp = qkv[:, width + p * TILE : width + (p + 1) * TILE]
    vp = qkv[:, 2 * width + p * TILE : 2 * width + (p + 1) * TILE]
    dp = dctx[:, at]
    both = dp.astype(F32) * ctx[:, at]
    qt = jnp.transpose(qp.astype(F32)).astype(BF)
    dt = jnp.transpose(dp.astype(F32)).astype(BF)
    dq, dk, dv = [], [], []
    for a in range(2):
        sel = low if a == 0 else ~low
        qa = jnp.where(sel, qp, jnp.zeros_like(qp))
        da = jnp.where(sel, dp, jnp.zeros_like(dp))
        inner = jnp.sum(jnp.where(sel, both, 0.0), axis=-1, keepdims=True)
        prob = jnp.exp(nt(qa, kp) + off - lse[:, 2 * p + a : 2 * p + a + 1])
        ds = (prob * (nt(da, vp) - inner)).astype(BF)
        dq.append(nn(ds, kp))
        dk.append(nn(qt[a * HD : (a + 1) * HD], ds))
        dv.append(nn(dt[a * HD : (a + 1) * HD], prob.astype(BF)))
    dq = jnp.where(low, dq[0], dq[1]) * SCALE
    dk, dv = (jnp.transpose(jnp.concatenate(v, axis=0))[0:total] for v in (dk, dv))
    return dq.astype(BF), dk.astype(BF), dv.astype(BF)


def attention_back_kernel(sizes, *refs):
    nctx, ntp, ndp, main, width, rows, padded = sizes
    qkv, dctx, lse, ctx, n1, x_in, dmid, wqkv, vec, g_out, vgrad, ub_own, ub_oth = refs[:13]
    ig, g_own, g_oth, dqkv = refs[13:]
    body = nctx * main
    total = body + EXTRA
    for p in range(3):
        for i, v in enumerate(pair_back(p, width, total, body, qkv, dctx, lse, ctx)):
            dqkv[:, i * width + p * TILE : i * width + (p + 1) * TILE] = v
    d = dqkv[...]
    bias = jnp.sum(d.astype(F32), axis=0, keepdims=True)
    g = tn(n1[...], d)
    go = g_out[...]
    own, oth = disassemble([tile(g, i) for i in range(9)], [tile(go, i) for i in range(3)])
    half = padded // 2
    for to, tiles in ((g_own, own), (g_oth, oth)):
        for j in range(4):
            lo = j % 2 * half
            for e in range(ndp):
                to[j, e, 0:rows, :] = tiles[j][e * rows : (e + 1) * rows].astype(BF)
                shared = tiles[4 + j // 2][e * rows + lo : e * rows + min(rows, lo + half)]
                to[j, e, padded : padded + shared.shape[0], :] = shared.astype(BF)
    dn1 = nt(d, wqkv[...])
    xhat, r = norm_stats(x_in[...])
    grad = dmid[...] + norm_back(dn1 * vec[1:2, :], xhat, r)
    ig[...] = grad.astype(BF)
    gains = jnp.sum(dn1 * xhat, axis=0, keepdims=True)
    shifts = jnp.sum(dn1, axis=0, keepdims=True)
    vecs = [gains, shifts] + [vgrad[i : i + 1, :] for i in range(2, 6)]
    zero = [jnp.zeros((1, TILE), F32)] * 3
    bias_own, bias_oth = disassemble([tile(bias, i) for i in range(9)], zero)
    for to, tiles, ub in ((g_own, bias_own, ub_own), (g_oth, bias_oth, ub_oth)):
        rows_ = [tile(v, i) for v in vecs for i in range(3)] + tiles
        rows_ += [ub[0:1, i * TILE : (i + 1) * TILE] for i in range(6)]
        for j in range(4):
            block = jnp.zeros((EXTRA, TILE), F32)
            for i, v in enumerate(rows_[8 * j : 8 * (j + 1)]):
                block = jnp.where(row_is(block.shape, i), v, block)
            for e in range(ndp):
                to[j, e, padded + half :, :] = block.astype(BF)


def sum_core_kernel(n, own, oth, *outs):
    me = lax.axis_index("ctx")
    for k in range(n):
        outs[k][...] = (own[me ^ k].astype(F32) + oth[me ^ k].astype(F32)).astype(BF)


def sum_ctx_kernel(n, ndp, *refs):
    me = lax.axis_index("dp")
    for k in range(ndp):
        v = refs[0][me ^ k].astype(F32)
        for i in range(1, n):
            v = v + refs[i][me ^ k].astype(F32)
        refs[n + k][...] = v.astype(BF)


def halve(stride, item, keep, send):
    bit = lax.rem(lax.div(lax.axis_index("dp"), stride), 2)
    for j in range(keep.shape[0]):
        keep[j] = item(2 * j + bit).astype(BF)
        send[j] = item(2 * j + 1 - bit).astype(BF)


def ctx_bits():
    me = lax.axis_index("ctx")
    return lax.rem(me, 2), lax.div(me, 2)


def sum_core_ff_kernel(own, oth, keep_a, send_a, keep_b, send_b):
    low, high = ctx_bits()
    half = own.shape[1] // 2

    def put(to, i, quarter, blocks):
        to[i] = (own[quarter, blocks].astype(F32) + oth[quarter, blocks].astype(F32)).astype(BF)

    for i in range(2):
        first, second = slice(0, half), slice(half, 2 * half)
        put(keep_a, i, 2 * i + low, first)
        put(send_a, i, 2 * i + 1 - low, first)
        put(keep_b, i, 2 * high + i, second)
        put(send_b, i, 2 * (1 - high) + i, second)


def sum_ctx_first_kernel(own_a, got_a, own_b, got_b, keep_a, send_a, keep_b, send_b):
    low, high = ctx_bits()
    for own, got, keep, send, bit in (
        (own_a, got_a, keep_a, send_a, high),
        (own_b, got_b, keep_b, send_b, low),
    ):
        keep[...] = (own[bit].astype(F32) + got[bit].astype(F32)).astype(BF)
        send[...] = (own[1 - bit].astype(F32) + got[1 - bit].astype(F32)).astype(BF)


def sum_ctx_second_kernel(own_a, got_a, own_b, got_b, keep, send):
    bit = lax.rem(lax.axis_index("dp"), 2)
    half = own_a.shape[0]
    for j in range(keep.shape[0]):
        own, got, at = (own_a, got_a, 2 * j) if 2 * j < half else (own_b, got_b, 2 * j - half)
        for to, i in ((keep, at + bit), (send, at + 1 - bit)):
            to[j] = (own[i].astype(F32) + got[i].astype(F32)).astype(BF)


def add_halves_kernel(stride, own, got, keep, send):
    halve(stride, lambda i: own[i].astype(F32) + got[i].astype(F32), keep, send)


def sum_dp_kernel(n, own, got, *refs):
    out = refs[n]
    rows = own.shape[1]
    out[:rows, :] = (own[0].astype(F32) + got[0, 0:rows, :].astype(F32)).astype(BF)
    v = refs[0][...].astype(F32)
    for r in refs[1:n]:
        v = v + r[...].astype(F32)
    span = out.shape[0] - rows
    out[rows:, :] = jnp.zeros((span, out.shape[1]), BF)
    for i in range(out.shape[1] // TILE):
        part = v[i * span : (i + 1) * span].astype(BF)
        if part.shape[0]:
            out[rows : rows + part.shape[0], i * TILE : (i + 1) * TILE] = part


def returns_kernel(sizes, bo, ig, out):
    nctx, ntp, ndp, main, width, rows, padded = sizes
    me = lax.axis_index("ctx")
    body = nctx * main
    shape = (EXTRA, width)
    extra = jnp.where(
        row_is(shape, 0),
        bo[body:, :].astype(F32),
        jnp.where(row_is(shape, 1), ig[body:, :].astype(F32)[0:1, :], 0.0),
    ).astype(BF)
    for k in range(nctx):
        at = slice(k * main, (k + 1) * main)
        out[me ^ k, 0:main, :] = bo[at, :]
        out[me ^ k, main : main + EXTRA, :] = extra
        out[me ^ k, main + EXTRA :, :] = ig[at, :]


def hand_on_kernel(held, out):
    out[...] = held[...]


def grads_kernel(sizes, *refs):
    nctx, ntp, ndp, main, width, rows, padded = sizes
    parts, refs = refs[:nctx], refs[nctx:]
    gq, gk, gv, gqb, gvb, go, gu, gub, gd = refs[:9]
    gvec, f, f2 = refs[9:15], refs[15], refs[16]
    me, me_d = lax.axis_index("ctx"), lax.axis_index("dp")
    span = parts[0].shape[0] - padded
    for k in range(nctx):
        f2[me ^ k] = parts[k][0:padded, :].astype(F32)
        for i in range(f2.shape[2] // TILE):
            n = min(span, f.shape[1] - i * span)
            if n > 0:
                f[me ^ k, i * span : i * span + n, :] = parts[k][
                    padded : padded + n, i * TILE : (i + 1) * TILE
                ].astype(F32)
    half = f2.shape[2]
    for j in range(2):
        gu[:, j * half : (j + 1) * half] = f2[j, 0:rows, :]
        gd[:, j * half : (j + 1) * half] = f2[2 + j, 0:rows, :]
    q01, k01, v01, o01 = (f[j, 0:rows, :] for j in range(4))
    low, high = slice(padded, padded + padded // 2), slice(padded, padded + rows - padded // 2)
    qk2 = jnp.concatenate([f[0, low, :], f[1, high, :]], axis=0)
    vo2 = jnp.concatenate([f[2, low, :], f[3, high, :]], axis=0)
    gq[:, 0:TILE] = q01
    gq[:, TILE:] = qk2[:, 0:HD]
    gk[:, 0:TILE] = k01
    gk[:, TILE:] = swap(qk2)[:, 0:HD]
    gv[:, 0:TILE] = v01
    gv[:, TILE:] = vo2[:, 0:HD]
    go[0:TILE, :] = jnp.transpose(o01)
    go[TILE:, :] = jnp.transpose(vo2)[HD:, :]

    def line(i):
        at = padded + padded // 2 + i % 8
        return f[i // 8, at : at + 1, :]

    for i in range(6):
        v = jnp.concatenate([line(3 * i), line(3 * i + 1), line(3 * i + 2)], axis=1)
        v = jnp.broadcast_to(v, (8, width))
        v = pltpu.roll(v, lax.rem(width - me_d * rows, width), axis=1)
        gvec[i][...] = v[0, 0:rows]
    b = [line(18 + i) for i in range(6)]
    gqb[...] = jnp.concatenate([b[0], b[4][:, 0:HD]], axis=1)[0]
    gvb[...] = jnp.concatenate([b[2], b[5][:, 0:HD]], axis=1)[0]
    gub[...] = jnp.concatenate([line(24 + i) for i in range(6)], axis=1)[0]


def unpack_kernel(sizes, own, oth, tails, mask, *refs):
    nctx, ntp, ndp, main, width, rows, padded = sizes
    outs, done, valid, sem = refs[:2], refs[2], refs[3], refs[4]
    images = nctx * ntp
    me_t = lax.axis_index("tp")
    where = [j * ntp + t for t in (me_t, 1 - me_t) for j in range(nctx)]
    sources = [v.at[j] for v in (own, oth) for j in range(nctx)]
    get_valid = pltpu.make_async_copy(mask, valid, sem.at[0])
    get_valid.start()

    def hit(r, c):
        img = where[-1]
        for j in range(images - 1):
            img = jnp.where(c // BLOCK == j, where[j], img)
        return r == (c % BLOCK) * images + img

    put = one_hot((images * BLOCK, images * BLOCK), hit)
    for i in range(2):
        for b in range(main // BLOCK):
            lo = i * (main + EXTRA) + b * BLOCK
            got = jnp.concatenate([src[lo : lo + BLOCK, :] for src in sources], axis=0)
            outs[i][b * BLOCK * images : (b + 1) * BLOCK * images, :] = nn(put, got)
    get_valid.wait()
    for i in range(2):
        for src, img in zip(sources, where):
            got = src[main : main + EXTRA, :].astype(F32)[i : i + 1, :]
            outs[i][pl.ds(main * images + img, 1), :] = jnp.where(
                valid[img, main] > 0, got, tails[i, pl.ds(img, 1), :]
            )
    done[...] = jnp.zeros_like(done)


def xor(n, k):
    return [(i, i ^ k) for i in range(n)]


def over(axis, n, items):
    return [items[0]] + [lax.ppermute(items[k], axis, xor(n, k)) for k in range(1, n)]


def body(nctx, ntp, ndp, *args):
    (tokens, valid_mask, cotangent, w_query, w_key, w_value, query_bias, value_bias, w_out, w_up, up_bias, w_down) = args[:12]
    vecs = args[12:]
    images, slots, width = tokens.shape
    main = slots - 1
    rows = w_query.shape[0]
    padded = -(-rows // EXTRA) * EXTRA
    ff = w_up.shape[1]
    p1_cols = 4 * w_query.shape[1]
    sizes = (nctx, ntp, ndp, main, width, rows, padded)
    total = nctx * main + EXTRA
    keys = -(-total // TILE) * TILE
    stage = BF if rows % 16 == 0 else F32
    flip = xor(ntp, 1)
    tok = jnp.transpose(tokens, (1, 0, 2)).reshape(slots * images, width)
    cot = jnp.transpose(cotangent, (1, 0, 2)).reshape(slots * images, width)

    def one(f):
        return functools.partial(f, sizes)

    def other(v):
        return lax.ppermute(v, "tp", flip)

    def held(arrays):
        return [
            (pltpu.SMEM if v.dtype == jnp.int32 else pltpu.VMEM)(v.shape, v.dtype) for v in arrays
        ] + [pltpu.SemaphoreType.DMA((len(arrays),))]

    def gather_dp(name, piece, after):
        v = piece[None]
        stride = ndp // 2
        while stride > 1:
            v = call(
                name,
                functools.partial(join_kernel, "dp", stride),
                sds((2 * v.shape[0],) + v.shape[1:], v.dtype),
                after=after,
            )(v, lax.ppermute(v, "dp", xor(ndp, stride)))
            stride //= 2
        return v, lax.ppermute(v, "dp", xor(ndp, 1))

    sources = [w_query, w_key, w_value, w_out, w_up, jnp.transpose(w_down), query_bias, value_bias, up_bias, *vecs]
    p1, p2q, packed = call(
        "pack_weights",
        functools.partial(pack_weights_kernel, sizes, len(sources)),
        [sds((padded + EXTRA, p1_cols), BF), sds((padded, ff // 2), BF), sds((8, TILE), F32)],
        scratch=held(sources),
        mib=56,
        raw=range(len(sources)),
    )(*sources)
    sources = [tok, cot, valid_mask]
    *sent, tails = call(
        "pack_slots",
        one(pack_slots_kernel),
        [sds((2 * main + EXTRA, width), BF)] * nctx + [sds((2, images, width), F32)],
        scratch=held(sources),
        mib=48,
        raw=range(3),
    )(*sources)
    t_in = over("ctx", nctx, sent)
    w2q = gather_dp("join_quarter", p2q, [])
    w1, w1_got = gather_dp("join_attn", p1, [])
    w2q, w1_early = call(
        "merge_quarter",
        one(merge_quarter_kernel),
        [sds((width, ff // 2), BF), sds(w1.shape, BF)],
        scratch=[pltpu.VMEM((width, ff // 2), stage)],
        after=t_in[1:],
    )(w1, *w2q)
    w1_oth = other(w1_early)
    w2q = over("ctx", nctx, [w2q] * nctx)
    late = call(
        "split_attn",
        split_kernel,
        [sds(w1.shape[:2] + (p1_cols // 2,), BF)] * 2,
        after=[w1_oth, w2q[0]],
    )(w1_got)
    w1 = [w1, w1_got, w1_oth, *[other(v) for v in late]]
    x, mid, n1, n2, qkv, ctx, ctx_full, lse, wqkv, wot, vec, ub, cot_in = call(
        "attention",
        one(attention_kernel),
        [
            sds((total, width), F32), sds((total, width), F32), sds((total, width), BF), sds((total, width), BF),
            sds((keys, 3 * width), BF), sds((total, width), BF), sds((total, width), F32), sds((total, TILE), F32),
            sds((width, 3 * width), BF), sds((width, width), BF), sds((EXTRA, width), F32), sds((8, 2 * ff), F32),
            sds((total, width), BF),
        ],
        scratch=[pltpu.VMEM((width, p1_cols), stage)] * 2,
        mib=32,
    )(*t_in, *w1)
    w2_own = call(
        "merge_ff", functools.partial(merge_ff_kernel, nctx), sds((width, 2 * ff), BF), after=[vec]
    )(*w2q)
    w2_oth = other(w2_own)
    ff_grads = sds((4, ndp, padded, ff // 2), BF)

    def mlp_half(name, side, w, after=()):
        return call(
            name,
            functools.partial(mlp_half_kernel, sizes, side),
            [sds((total, ff), BF), sds((total, ff), BF), sds((8, ff), F32), ff_grads],
            mib=32,
            after=after,
        )(n2, cot_in, w, ub)

    hid_own, hgr_own, ub_own, g2_own = mlp_half("mlp_own", 0, w2_own)
    hid_oth, hgr_oth, ub_oth, g2_oth = mlp_half("mlp_oth", 1, w2_oth, [ub_own])
    bo, dmid, dctx, g_out, vgrad = call(
        "mlp_sums",
        one(mlp_sums_kernel),
        [
            sds((total, width), BF), sds((total, width), F32), sds((total, width), BF), sds((width, width), F32),
            sds((EXTRA, width), F32),
        ],
        mib=32,
    )(mid, ctx, wot, vec, cot_in, w2_own, w2_oth, hid_own, hid_oth, hgr_own, hgr_oth)

    def core_sums(name, own, oth, after=()):
        outs = [sds(own.shape[1:], BF)] * nctx
        return call(name, functools.partial(sum_core_kernel, nctx), outs, after=after)(own, other(oth))

    def by_image(v):
        return jnp.transpose(v.reshape(slots, images, width), (1, 0, 2))

    pairs = sds((2, ndp // 2, padded, ff // 2), BF)
    keep_a, send_a, keep_b, send_b = call("sum_core_ff", sum_core_ff_kernel, [pairs] * 4, after=[vgrad])(
        g2_own, other(g2_oth)
    )
    got_a, got_b = lax.ppermute(send_a, "ctx", xor(nctx, 1)), lax.ppermute(send_b, "ctx", xor(nctx, 2))
    ig, g1_own, g1_oth = call(
        "attention_back",
        one(attention_back_kernel),
        [sds((total, width), BF)] + [sds((4, ndp, padded + padded // 2 + EXTRA, TILE), BF)] * 2,
        scratch=[pltpu.VMEM((total, 3 * width), BF)],
        mib=32,
        after=[keep_a],
    )(qkv, dctx, lse, ctx_full, n1, x, dmid, wqkv, vec, g_out, vgrad, ub_own, ub_oth)
    one_quarter = sds(pairs.shape[1:], BF)
    keep_a, send_a, keep_b, send_b = call(
        "sum_ctx_first", sum_ctx_first_kernel, [one_quarter] * 4, after=[g1_own]
    )(keep_a, got_a, keep_b, got_b)
    got_a, got_b = lax.ppermute(send_a, "ctx", xor(nctx, 2)), lax.ppermute(send_b, "ctx", xor(nctx, 1))
    s1_send = core_sums("sum_core_attn", g1_own, g1_oth, after=[keep_a])
    s1 = over("ctx", nctx, s1_send)
    keep, send = call("sum_ctx_second", sum_ctx_second_kernel, [one_quarter] * 2, after=[s1_send[0]])(
        keep_a, got_a, keep_b, got_b
    )
    back = call(
        "returns",
        one(returns_kernel),
        sds((nctx, 2 * main + EXTRA, width), BF),
        after=[keep],
    )(bo, ig)
    returned = lax.all_to_all(back, "ctx", 0, 0)
    u1_send = call(
        "sum_ctx_attn",
        functools.partial(sum_ctx_kernel, nctx, ndp),
        [sds(s1[0].shape[1:], BF)] * ndp,
        after=[back],
    )(*s1)
    u1 = over("dp", ndp, u1_send)
    stride = 2
    while stride < ndp:
        half = sds((keep.shape[0] // 2,) + keep.shape[1:], BF)
        keep, send = call(
            "add_dp_ff", functools.partial(add_halves_kernel, stride), [half, half], after=[u1_send[0]]
        )(keep, lax.ppermute(send, "dp", xor(ndp, stride // 2)))
        stride *= 2
    summed = call(
        "sum_dp", functools.partial(sum_dp_kernel, ndp), sds((padded + -(-s1[0].shape[1] // (3 * EXTRA)) * EXTRA, ff // 2), BF)
    )(keep, lax.ppermute(send, "dp", xor(ndp, ndp // 2)), *u1)
    shares = over("ctx", nctx, [summed] * nctx)
    back = call("hand_on", hand_on_kernel, sds(returned.shape, BF), after=[summed])(returned)
    block_out, input_grad, placed = call(
        "place_slots",
        one(unpack_kernel),
        [sds(tok.shape, F32)] * 2 + [sds((8, TILE), F32)],
        scratch=[pltpu.SMEM(valid_mask.shape, valid_mask.dtype), pltpu.SemaphoreType.DMA((1,))],
        raw=(3,),
        mib=16,
    )(back, other(back), tails, valid_mask)
    gq, gk, gv, gqb, gvb, go, gu, gub, gd, *gvec = call(
        "place_grads",
        one(grads_kernel),
        [
            sds(w_query.shape, F32), sds(w_key.shape, F32), sds(w_value.shape, F32),
            sds(query_bias.shape, F32), sds(value_bias.shape, F32), sds(w_out.shape, F32),
            sds(w_up.shape, F32), sds(up_bias.shape, F32), sds((rows, ff), F32),
        ]
        + [sds((rows,), F32)] * 6,
        scratch=[
            pltpu.VMEM((nctx,) + s1[0].shape[1:], F32),
            pltpu.VMEM((nctx, padded, ff // 2), F32),
        ],
        after=[placed],
    )(*shares)
    return (by_image(block_out), by_image(input_grad), gq, gk, gv, gqb, gvb, go, gu, gub, jnp.transpose(gd), *gvec)


def solution(mesh):
    rows, cols, tp, dp = P("dp", "tp"), P("tp", "dp"), P("tp"), P("dp")
    act = P("dp", "ctx", None)
    return jax.shard_map(
        functools.partial(body, mesh.shape["ctx"], mesh.shape["tp"], mesh.shape["dp"]),
        mesh=mesh,
        in_specs=(act, P("dp", "ctx"), act, rows, rows, rows, tp, tp, cols, rows, tp, cols) + (dp,) * 6,
        out_specs=(act, act, rows, rows, rows, tp, tp, cols, rows, tp, cols) + (dp,) * 6,
        check_vma=False,
    )
```

```python
import functools

import jax
import jax.numpy as jnp
from jax import lax
from jax.experimental import pallas as pl
from jax.experimental.pallas import tpu as pltpu
from jax.sharding import PartitionSpec as P

HD = 64
EPS = 1e-06
SCALE = 0.125
FLOOR = -1e30
BF = jnp.bfloat16
F32 = jnp.float32
TILE = 128
TIMES = {
    "pack_weights": 2.0, "pack_slots": 3.0, "pack_cotangent": 2.0, "attention": 0.0, "mlp_own": 4.0, "mlp_oth": 4.0, "mlp_sums": 2.0, "attention_back": 11.0,
    "place_grads": 1.0, "place_slots": 2.3, "join_quarter": 20.0, "sum_ctx_attn": 0.5, "sum_dp": 5.0, "sum_ctx_first": 50.0,
}
EXTRA = 16


def call(name, kernel, out_shape, scratch=(), mib=8, after=(), raw=()):
    after = list(after)

    def ordered(*refs):
        kernel(*refs[len(after) :])

    def run(*args):
        specs = [pl.BlockSpec(memory_space=pl.ANY)] * len(after) + [
            pl.BlockSpec(memory_space=pltpu.HBM if i in raw else pltpu.VMEM)
            for i in range(len(args))
        ]
        return pl.pallas_call(
            ordered,
            name=name,
            out_shape=out_shape,
            in_specs=specs,
            out_specs=jax.tree.map(lambda _: pl.BlockSpec(memory_space=pltpu.VMEM), out_shape),
            scratch_shapes=list(scratch),
            compiler_params=pltpu.CompilerParams(vmem_limit_bytes=mib << 20),
            cost_estimate=pl.CostEstimate(
                flops=int(TIMES.get(name, 0.2) * 1.15e9), bytes_accessed=1, transcendentals=0
            ),
        )(*after, *args)

    return run


def sds(shape, dtype):
    return jax.ShapeDtypeStruct(shape, dtype)


def nn(a, b):
    return lax.dot_general(a, b, (((1,), (0,)), ((), ())), preferred_element_type=F32)


def nt(a, b):
    return lax.dot_general(a, b, (((1,), (1,)), ((), ())), preferred_element_type=F32)


def tn(a, b):
    return lax.dot_general(a, b, (((0,), (0,)), ((), ())), preferred_element_type=F32)


def swap(v):
    return pltpu.roll(v, HD, axis=1)


def low_lanes(shape):
    return lax.broadcasted_iota(jnp.int32, shape, 1) < HD


def row_is(shape, row):
    return lax.broadcasted_iota(jnp.int32, shape, 0) == row


def tile(v, i):
    return v[:, i * TILE : (i + 1) * TILE]


def assemble(own, oth):
    low = low_lanes((own.shape[0], TILE))
    own_qk, own_vo, oth_qk, oth_vo = tile(own, 4), tile(own, 5), tile(oth, 4), tile(oth, 5)
    qkv = [
        tile(own, 0), tile(oth, 0), jnp.where(low, own_qk, swap(oth_qk)),
        tile(own, 1), tile(oth, 1), jnp.where(low, swap(own_qk), oth_qk),
        tile(own, 2), tile(oth, 2), jnp.where(low, own_vo, swap(oth_vo)),
    ]
    out = [tile(own, 3), tile(oth, 3), jnp.where(low, swap(own_vo), oth_vo)]
    return qkv, out


def disassemble(qkv, out):
    low = low_lanes(qkv[0].shape)
    own = [qkv[0], qkv[3], qkv[6], out[0], jnp.where(low, qkv[2], swap(qkv[5])), jnp.where(low, qkv[8], swap(out[2]))]
    oth = [qkv[1], qkv[4], qkv[7], out[1], jnp.where(low, swap(qkv[2]), qkv[5]), jnp.where(low, swap(qkv[8]), out[2])]
    return own, oth


def norm_stats(v):
    mean = jnp.mean(v, axis=-1, keepdims=True)
    centered = v - mean
    r = lax.rsqrt(jnp.mean(centered * centered, axis=-1, keepdims=True) + EPS)
    return centered * r, r


def norm_back(e, xhat, r):
    return r * (
        e
        - jnp.mean(e, axis=-1, keepdims=True)
        - xhat * jnp.mean(e * xhat, axis=-1, keepdims=True)
    )


def gelu_pair(v):
    phi = 0.5 + 0.5 * lax.erf(v * 0.7071067811865476)
    return v * phi, phi + (0.3989422804014327 * v) * jnp.exp(-0.5 * v * v)


BLOCK = 16


def one_hot(shape, hit):
    r, c = (lax.broadcasted_iota(jnp.int32, shape, i) for i in range(2))
    return hit(r, c).astype(F32).astype(BF)


def picker(wanted, images):
    def hit(r, c):
        img = wanted[-1]
        for k in range(len(wanted) - 1):
            img = jnp.where(r // BLOCK == k, wanted[k], img)
        return c == (r % BLOCK) * images + img

    return one_hot((len(wanted) * BLOCK, images * BLOCK), hit)


def take_images(ref, outs, at, pick, images, count):
    for b in range(count // BLOCK):
        got = nn(pick, ref[b * BLOCK * images : (b + 1) * BLOCK * images, :].astype(BF)).astype(BF)
        for k in range(len(outs)):
            outs[k][at + b * BLOCK : at + (b + 1) * BLOCK, :] = got[k * BLOCK : (k + 1) * BLOCK]


def fetch(sources, held, sem):
    copies = [pltpu.make_async_copy(sources[i], held[i], sem.at[i]) for i in range(len(sources))]
    for c in copies:
        c.start()
    return copies


def pack_weights_kernel(sizes, count, *refs):
    nctx, ntp, ndp, main, width, rows, padded = sizes
    sources, (p1, p2q, done), refs = refs[:count], refs[count : count + 3], refs[count + 3 :]
    held, sem = refs[:count], refs[count]
    copies = fetch(sources, held, sem)
    wq, wk, wv, wo, wu, wd, qb, vb, ub = held[:9]
    vecs = held[9:]
    me_c, me_d = lax.axis_index("ctx"), lax.axis_index("dp")
    for c in copies:
        c.wait()
    if padded > rows:
        p1[0:padded, :] = jnp.zeros((padded, p1.shape[1]), BF)
        p2q[...] = jnp.zeros(p2q.shape, BF)
    quarter = p2q.shape[1]
    for j in range(nctx):
        src = (wu, wd)[j // 2][:, (j % 2) * quarter : (j % 2 + 1) * quarter]

        @pl.when(me_c == j)
        def _(src=src):
            p2q[0:rows, :] = src

    def put(lo, value):
        p1[0:rows, lo : lo + value.shape[1]] = value.astype(BF)

    fq, fk, fv = wq[...].astype(F32), wk[...].astype(F32), wv[...].astype(F32)
    fo = jnp.transpose(wo[...].astype(F32))
    for i, w in enumerate((fq, fk, fv, fo)):
        put(i * TILE, tile(w, 0))
    put(4 * TILE, jnp.concatenate([fq[:, TILE:], fk[:, TILE:]], axis=1))
    put(5 * TILE, jnp.concatenate([fv[:, TILE:], fo[:, TILE:]], axis=1))
    cols = p1.shape[1]
    fqb, fvb = qb[...].astype(F32)[None, :], vb[...].astype(F32)[None, :]
    none = jnp.zeros((1, TILE), F32)
    short = jnp.zeros((1, HD), F32)
    bias = jnp.concatenate(
        [fqb[:, :TILE], none, fvb[:, :TILE], none, fqb[:, TILE:], short, fvb[:, TILE:], short], axis=1
    )
    spread = one_hot((rows, width), lambda r, c: c == r + rows * me_d)
    block = jnp.where(row_is((EXTRA, cols), 0), bias, 0.0)
    block = jnp.where(row_is((EXTRA, cols), 7), ub[...].astype(F32)[None, :], block)
    lanes = jnp.zeros((EXTRA, rows), F32)
    for i in range(6):
        lanes = jnp.where(row_is((EXTRA, rows), 1 + i), vecs[i][...].astype(F32)[None, :], lanes)
    lanes = nn(lanes.astype(BF), spread)
    p1[padded : padded + EXTRA, :] = block.astype(BF)
    mixed = jnp.where(
        (lax.broadcasted_iota(jnp.int32, (EXTRA, width), 0) - 1).astype(jnp.uint32) < 6,
        lanes,
        block[:, :width],
    )
    p1[padded : padded + EXTRA, 0:width] = mixed.astype(BF)
    done[...] = jnp.zeros_like(done)


def pack_slots_kernel(sizes, *refs):
    nctx, ntp, ndp, main, width, rows, padded = sizes
    sources, sent, tails, refs = refs[:3], refs[3 : 3 + nctx], refs[3 + nctx], refs[4 + nctx :]
    held, sem = refs[:3], refs[3]
    copies = fetch(sources, held, sem)
    tok, cot, mask = held
    images = nctx * ntp
    me_c, me_t = lax.axis_index("ctx"), lax.axis_index("tp")
    wanted = [(me_c ^ k) * ntp + me_t for k in range(nctx)]
    pick = picker(wanted, images)
    for i in range(2):
        copies[i].wait()
        take_images(held[i], sent, i * (main + EXTRA), pick, images, main)
        tails[i] = held[i][main * images :, :]
    copies[2].wait()
    for k in range(nctx):
        gate = mask[wanted[k], main].astype(F32)
        te = tok[pl.ds(main * images + wanted[k], 1), :] * gate
        ce = cot[pl.ds(main * images + wanted[k], 1), :] * gate
        shape = (EXTRA, width)
        sent[k][main : main + EXTRA, :] = jnp.where(
            row_is(shape, 0), te, jnp.where(row_is(shape, 1), ce, 0.0)
        ).astype(BF)


def join_kernel(axis, stride, own, got, out):
    bit = lax.rem(lax.div(lax.axis_index(axis), stride), 2)
    for i in range(own.shape[0]):
        out[2 * i + bit] = own[i]
        out[2 * i + 1 - bit] = got[i]


def place_rows(stage, own, got, rows):
    bit = lax.rem(lax.axis_index("dp"), 2)
    for i in range(own.shape[0]):
        for piece, last in ((own, bit), (got, 1 - bit)):
            at = pl.ds(pl.multiple_of((2 * i + last) * rows, 16 if rows % 16 == 0 else 8), rows)
            stage[at, :] = piece[i].astype(stage.dtype)[:rows]


def merge_quarter_kernel(sizes, attn, own, got, out, attn_out, stage):
    place_rows(stage, own, got, sizes[5])
    out[...] = stage[...].astype(BF)
    attn_out[...] = attn[...]


def split_kernel(got, *outs):
    for i, out in enumerate(outs):
        cols = out.shape[2]
        out[...] = got[:, :, i * cols : (i + 1) * cols]


def merge_ff_kernel(nctx, *refs):
    out = refs[nctx]
    me_c = lax.axis_index("ctx")
    for k in range(nctx):
        quarter = refs[k].shape[1]
        out[:, pl.ds(pl.multiple_of((me_c ^ k) * quarter, quarter), quarter)] = refs[k][...]


def attention_kernel(sizes, *refs):
    nctx, ntp, ndp, main, width, rows, padded = sizes
    t_in, (own, got, own_oth, got_oth_a, got_oth_b), refs = refs[:nctx], refs[nctx : nctx + 5], refs[nctx + 5 :]
    x_out, mid_out, n1_out, n2_out, qkv, ctx, ctx_full, lse, wqkv, wot, vec, ub, cot, stage, stage_oth = refs
    body = nctx * main
    total = body + EXTRA
    half = got_oth_a.shape[2]
    place_rows(stage, own, got, rows)
    place_rows(stage_oth.at[:, :half], own_oth.at[:, :, :half], got_oth_a, rows)
    place_rows(stage_oth.at[:, half:], own_oth.at[:, :, half:], got_oth_b, rows)
    tiles, outs = assemble(stage[...].astype(F32), stage_oth[...].astype(F32))
    for i, v in enumerate(tiles):
        wqkv[:, i * TILE : (i + 1) * TILE] = v.astype(BF)
    for i, v in enumerate(outs):
        wot[:, i * TILE : (i + 1) * TILE] = v.astype(BF)
    extra = own[0, padded:, :].astype(F32)
    extra_oth = own_oth[0, padded:, :].astype(F32)
    tiles, _ = assemble(extra, extra_oth)
    bias = jnp.concatenate([v[0:1] for v in tiles], axis=1)
    vec_sum = jnp.zeros((EXTRA, width), F32)
    for i in range(own.shape[0]):
        vec_sum += own[i, padded:, :width].astype(F32) + got[i, padded:, :width].astype(F32)
    vec[...] = vec_sum
    ub[...] = jnp.broadcast_to(jnp.concatenate([extra[7:8], extra_oth[7:8]], axis=1), ub.shape)
    extra = jnp.zeros((EXTRA, width), F32)
    for k in range(nctx):
        x_out[k * main : (k + 1) * main, :] = t_in[k][0:main, :].astype(F32)
        cot[k * main : (k + 1) * main, :] = t_in[k][main + EXTRA :, :]
        extra += t_in[k][main : main + EXTRA, :].astype(F32)
    x_out[body:, :] = jnp.where(row_is((EXTRA, width), 0), extra, 0.0)
    cot[body:, :] = jnp.where(row_is((EXTRA, width), 0), extra[1:2, :], 0.0).astype(BF)
    x = x_out[...]
    xhat, _ = norm_stats(x)
    n1 = (xhat * vec_sum[1:2, :] + vec_sum[2:3, :]).astype(BF)
    n1_out[...] = n1
    proj = nn(n1, wqkv[...]) + bias
    qkv[0:total, 0:width] = (proj[:, 0:width].astype(BF).astype(F32) * SCALE).astype(BF)
    qkv[0:total, width:] = proj[:, width:].astype(BF)
    keys = qkv.shape[0]
    qkv[total:, :] = jnp.zeros((keys - total, qkv.shape[1]), BF)
    off = jnp.where(lax.broadcasted_iota(jnp.int32, (1, keys), 1) > body, FLOOR, 0.0)
    low = low_lanes((total, TILE))
    lane = lax.broadcasted_iota(jnp.int32, (total, TILE), 1)
    all_lse = jnp.zeros((total, TILE), F32)
    for p in range(3):
        qp = qkv[0:total, p * TILE : (p + 1) * TILE]
        kp = qkv[:, width + p * TILE : width + (p + 1) * TILE]
        vp = qkv[:, 2 * width + p * TILE : 2 * width + (p + 1) * TILE]
        parts = []
        for a in range(2):
            qa = jnp.where(low if a == 0 else ~low, qp, jnp.zeros_like(qp))
            s = nt(qa, kp) + off
            m = jnp.max(s, axis=-1, keepdims=True)
            e = jnp.exp(s - m)
            l = jnp.sum(e, axis=-1, keepdims=True)
            parts.append(nn(e.astype(BF), vp) * (1.0 / l))
            all_lse = jnp.where(lane == 2 * p + a, m + jnp.log(l), all_lse)
        ctx_full[:, p * TILE : (p + 1) * TILE] = jnp.where(low, parts[0], parts[1])
    ctx[...] = ctx_full[...].astype(BF)
    lse[...] = all_lse
    attended = nt(ctx[...], wot[...]) + vec_sum[5:6, :]
    valid = lax.broadcasted_iota(jnp.int32, (total, 1), 0) <= body
    middle = x_out[...] + jnp.where(valid, attended, 0.0)
    mid_out[...] = middle
    xhat2, _ = norm_stats(middle)
    n2_out[...] = (xhat2 * vec_sum[3:4, :] + vec_sum[4:5, :]).astype(BF)


def mlp_half_kernel(sizes, side, n2, cot, w, ub, hid, hgr, ubgrad, grads):
    nctx, ntp, ndp, main, width, rows, padded = sizes
    half = w.shape[1] // 2
    n2v, dcot = n2[...], cot[...]
    act, slope = gelu_pair(nn(n2v, w[:, :half]) + ub[0:1, side * half : (side + 1) * half])
    h = act.astype(BF)
    hg = (nn(dcot, w[:, half:]) * slope).astype(BF)
    hid[...] = h
    hgr[...] = hg
    ubgrad[...] = jnp.broadcast_to(jnp.sum(hg.astype(F32), axis=0, keepdims=True), ubgrad.shape)
    cols = grads.shape[3]
    for part, g in ((0, tn(n2v, hg).astype(BF)), (1, tn(dcot, h).astype(BF))):
        for d in range(ndp):
            for c in range(half // cols):
                grads[2 * part + c, d, 0:rows, :] = g[d * rows : (d + 1) * rows, c * cols : (c + 1) * cols]


def mlp_sums_kernel(sizes, mid, ctx, wot, vec, cot, w_own, w_oth, hid_own, hid_oth, hgr_own, hgr_oth, bo, dmid, dctx, g_out, vgrad):
    nctx, ntp, ndp, main, width, rows, padded = sizes
    body = nctx * main
    total = body + EXTRA
    half = w_own.shape[1] // 2
    dcot = cot[...]
    middle = mid[...]
    valid = lax.broadcasted_iota(jnp.int32, (total, 1), 0) <= body
    n2g = nt(hgr_own[...], w_own[:, :half]) + nt(hgr_oth[...], w_oth[:, :half])
    xhat, r = norm_stats(middle)
    back = norm_back(n2g * vec[3:4, :], xhat, r)
    middle_grad = dcot.astype(F32) + back
    dmid[...] = middle_grad
    agrad = jnp.where(valid, middle_grad, 0.0).astype(BF)
    dctx[...] = nn(agrad, wot[...]).astype(BF)
    g_out[...] = tn(agrad, ctx[...])
    mlp_out = nt(hid_own[...], w_own[:, half:]) + nt(hid_oth[...], w_oth[:, half:]) + vec[6:7, :]
    bo[...] = (middle + jnp.where(valid, mlp_out, 0.0)).astype(BF)
    shape = vgrad.shape
    v = jnp.where(row_is(shape, 2), jnp.sum(n2g * xhat, axis=0, keepdims=True), 0.0)
    v = jnp.where(row_is(shape, 3), jnp.sum(n2g, axis=0, keepdims=True), v)
    v = jnp.where(row_is(shape, 4), jnp.sum(agrad.astype(F32), axis=0, keepdims=True), v)
    v = jnp.where(row_is(shape, 5), jnp.sum(dcot.astype(F32), axis=0, keepdims=True), v)
    vgrad[...] = v


def pair_back(p, width, total, body, qkv, dctx, lse, ctx):
    keys = qkv.shape[0]
    off = jnp.where(lax.broadcasted_iota(jnp.int32, (1, keys), 1) > body, FLOOR, 0.0)
    low = low_lanes((total, TILE))
    at = slice(p * TILE, (p + 1) * TILE)
    qp = qkv[0:total, at]
    kp = qkv[:, width + p * TILE : width + (p + 1) * TILE]
    vp = qkv[:, 2 * width + p * TILE : 2 * width + (p + 1) * TILE]
    dp = dctx[:, at]
    both = dp.astype(F32) * ctx[:, at]
    qt = jnp.transpose(qp.astype(F32)).astype(BF)
    dt = jnp.transpose(dp.astype(F32)).astype(BF)
    dk, dv = [], []
    zero = jnp.zeros_like(qp)
    qs = jnp.concatenate([jnp.where(low, qp, zero), jnp.where(low, zero, qp)], axis=0)
    ds_ = jnp.concatenate([jnp.where(low, dp, zero), jnp.where(low, zero, dp)], axis=0)
    bs = jnp.concatenate([jnp.where(low, both, 0.0), jnp.where(low, 0.0, both)], axis=0)
    inner = jnp.sum(bs, axis=-1, keepdims=True)
    ls = jnp.concatenate([lse[:, 2 * p : 2 * p + 1], lse[:, 2 * p + 1 : 2 * p + 2]], axis=0)
    prob = jnp.exp(nt(qs, kp) + off - ls)
    ds = (prob * (nt(ds_, vp) - inner)).astype(BF)
    w = prob.astype(BF)
    dq = nn(ds, kp)
    dq = jnp.where(low, dq[0:total], dq[total:]) * SCALE
    for a in range(2):
        dk.append(nn(qt[a * HD : (a + 1) * HD], ds[a * total : (a + 1) * total]))
        dv.append(nn(dt[a * HD : (a + 1) * HD], w[a * total : (a + 1) * total]))
    dk, dv = (jnp.transpose(jnp.concatenate(v, axis=0))[0:total] for v in (dk, dv))
    return dq.astype(BF), dk.astype(BF), dv.astype(BF)


def attention_back_kernel(sizes, *refs):
    nctx, ntp, ndp, main, width, rows, padded = sizes
    qkv, dctx, lse, ctx, n1, x_in, dmid, wqkv, vec, g_out, vgrad, ub_own, ub_oth = refs[:13]
    ig, g_own, g_oth, dqkv = refs[13:]
    body = nctx * main
    total = body + EXTRA
    for p in range(3):
        for i, v in enumerate(pair_back(p, width, total, body, qkv, dctx, lse, ctx)):
            dqkv[:, i * width + p * TILE : i * width + (p + 1) * TILE] = v
    d = dqkv[...]
    bias = jnp.sum(d.astype(F32), axis=0, keepdims=True)
    g = tn(n1[...], d)
    go = g_out[...]
    own, oth = disassemble([tile(g, i) for i in range(9)], [tile(go, i) for i in range(3)])
    half = padded // 2
    for to, tiles in ((g_own, own), (g_oth, oth)):
        for j in range(4):
            lo = j % 2 * half
            for e in range(ndp):
                to[j, e, 0:rows, :] = tiles[j][e * rows : (e + 1) * rows].astype(BF)
                shared = tiles[4 + j // 2][e * rows + lo : e * rows + min(rows, lo + half)]
                to[j, e, padded : padded + shared.shape[0], :] = shared.astype(BF)
    dn1 = nt(d, wqkv[...])
    xhat, r = norm_stats(x_in[...])
    grad = dmid[...] + norm_back(dn1 * vec[1:2, :], xhat, r)
    ig[...] = grad.astype(BF)
    gains = jnp.sum(dn1 * xhat, axis=0, keepdims=True)
    shifts = jnp.sum(dn1, axis=0, keepdims=True)
    vecs = [gains, shifts] + [vgrad[i : i + 1, :] for i in range(2, 6)]
    zero = [jnp.zeros((1, TILE), F32)] * 3
    bias_own, bias_oth = disassemble([tile(bias, i) for i in range(9)], zero)
    for to, tiles, ub in ((g_own, bias_own, ub_own), (g_oth, bias_oth, ub_oth)):
        rows_ = [tile(v, i) for v in vecs for i in range(3)] + tiles
        rows_ += [ub[0:1, i * TILE : (i + 1) * TILE] for i in range(6)]
        for j in range(4):
            block = jnp.zeros((EXTRA, TILE), F32)
            for i, v in enumerate(rows_[8 * j : 8 * (j + 1)]):
                block = jnp.where(row_is(block.shape, i), v, block)
            for e in range(ndp):
                to[j, e, padded + half :, :] = block.astype(BF)


def sum_core_kernel(n, own, oth, *outs):
    me = lax.axis_index("ctx")
    for k in range(n):
        outs[k][...] = (own[me ^ k].astype(F32) + oth[me ^ k].astype(F32)).astype(BF)


def sum_ctx_kernel(n, ndp, *refs):
    me = lax.axis_index("dp")
    for k in range(ndp):
        v = refs[0][me ^ k].astype(F32)
        for i in range(1, n):
            v = v + refs[i][me ^ k].astype(F32)
        refs[n + k][...] = v.astype(BF)


def halve(stride, item, keep, send):
    bit = lax.rem(lax.div(lax.axis_index("dp"), stride), 2)
    for j in range(keep.shape[0]):
        keep[j] = item(2 * j + bit).astype(BF)
        send[j] = item(2 * j + 1 - bit).astype(BF)


def ctx_bits():
    me = lax.axis_index("ctx")
    return lax.rem(me, 2), lax.div(me, 2)


def sum_core_ff_kernel(own, oth, keep_a, send_a, keep_b, send_b):
    low, high = ctx_bits()
    half = own.shape[1] // 2

    def put(to, i, quarter, blocks):
        to[i] = (own[quarter, blocks].astype(F32) + oth[quarter, blocks].astype(F32)).astype(BF)

    for i in range(2):
        first, second = slice(0, half), slice(half, 2 * half)
        put(keep_a, i, 2 * i + low, first)
        put(send_a, i, 2 * i + 1 - low, first)
        put(keep_b, i, 2 * high + i, second)
        put(send_b, i, 2 * (1 - high) + i, second)


def sum_ctx_first_kernel(own_a, got_a, own_b, got_b, keep_a, send_a, keep_b, send_b):
    low, high = ctx_bits()
    for own, got, keep, send, bit in (
        (own_a, got_a, keep_a, send_a, high),
        (own_b, got_b, keep_b, send_b, low),
    ):
        keep[...] = (own[bit].astype(F32) + got[bit].astype(F32)).astype(BF)
        send[...] = (own[1 - bit].astype(F32) + got[1 - bit].astype(F32)).astype(BF)


def sum_ctx_second_kernel(own_a, got_a, own_b, got_b, keep, send):
    bit = lax.rem(lax.axis_index("dp"), 2)
    half = own_a.shape[0]
    for j in range(keep.shape[0]):
        own, got, at = (own_a, got_a, 2 * j) if 2 * j < half else (own_b, got_b, 2 * j - half)
        for to, i in ((keep, at + bit), (send, at + 1 - bit)):
            to[j] = (own[i].astype(F32) + got[i].astype(F32)).astype(BF)


def add_halves_kernel(stride, own, got, keep, send):
    halve(stride, lambda i: own[i].astype(F32) + got[i].astype(F32), keep, send)


def sum_dp_kernel(n, own, got, *refs):
    out = refs[n]
    rows = own.shape[1]
    out[:rows, :] = (own[0].astype(F32) + got[0, 0:rows, :].astype(F32)).astype(BF)
    v = refs[0][...].astype(F32)
    for r in refs[1:n]:
        v = v + r[...].astype(F32)
    span = out.shape[0] - rows
    out[rows:, :] = jnp.zeros((span, out.shape[1]), BF)
    for i in range(out.shape[1] // TILE):
        part = v[i * span : (i + 1) * span].astype(BF)
        if part.shape[0]:
            out[rows : rows + part.shape[0], i * TILE : (i + 1) * TILE] = part


def returns_kernel(sizes, bo, ig, out):
    nctx, ntp, ndp, main, width, rows, padded = sizes
    me = lax.axis_index("ctx")
    body = nctx * main
    shape = (EXTRA, width)
    extra = jnp.where(
        row_is(shape, 0),
        bo[body:, :].astype(F32),
        jnp.where(row_is(shape, 1), ig[body:, :].astype(F32)[0:1, :], 0.0),
    ).astype(BF)
    for k in range(nctx):
        at = slice(k * main, (k + 1) * main)
        out[me ^ k, 0:main, :] = bo[at, :]
        out[me ^ k, main : main + EXTRA, :] = extra
        out[me ^ k, main + EXTRA :, :] = ig[at, :]


def hand_on_kernel(held, out):
    out[...] = held[...]


def grads_kernel(sizes, *refs):
    nctx, ntp, ndp, main, width, rows, padded = sizes
    parts, refs = refs[:nctx], refs[nctx:]
    gq, gk, gv, gqb, gvb, go, gu, gub, gd = refs[:9]
    gvec, f, f2 = refs[9:15], refs[15], refs[16]
    me, me_d = lax.axis_index("ctx"), lax.axis_index("dp")
    span = parts[0].shape[0] - padded
    for k in range(nctx):
        f2[me ^ k] = parts[k][0:padded, :].astype(F32)
        for i in range(f2.shape[2] // TILE):
            n = min(span, f.shape[1] - i * span)
            if n > 0:
                f[me ^ k, i * span : i * span + n, :] = parts[k][
                    padded : padded + n, i * TILE : (i + 1) * TILE
                ].astype(F32)
    half = f2.shape[2]
    for j in range(2):
        gu[:, j * half : (j + 1) * half] = f2[j, 0:rows, :]
        gd[:, j * half : (j + 1) * half] = f2[2 + j, 0:rows, :]
    q01, k01, v01, o01 = (f[j, 0:rows, :] for j in range(4))
    low, high = slice(padded, padded + padded // 2), slice(padded, padded + rows - padded // 2)
    qk2 = jnp.concatenate([f[0, low, :], f[1, high, :]], axis=0)
    vo2 = jnp.concatenate([f[2, low, :], f[3, high, :]], axis=0)
    gq[:, 0:TILE] = q01
    gq[:, TILE:] = qk2[:, 0:HD]
    gk[:, 0:TILE] = k01
    gk[:, TILE:] = swap(qk2)[:, 0:HD]
    gv[:, 0:TILE] = v01
    gv[:, TILE:] = vo2[:, 0:HD]
    go[0:TILE, :] = jnp.transpose(o01)
    go[TILE:, :] = jnp.transpose(vo2)[HD:, :]

    def line(i):
        at = padded + padded // 2 + i % 8
        return f[i // 8, at : at + 1, :]

    for i in range(6):
        v = jnp.concatenate([line(3 * i), line(3 * i + 1), line(3 * i + 2)], axis=1)
        v = jnp.broadcast_to(v, (8, width))
        v = pltpu.roll(v, lax.rem(width - me_d * rows, width), axis=1)
        gvec[i][...] = v[0, 0:rows]
    b = [line(18 + i) for i in range(6)]
    gqb[...] = jnp.concatenate([b[0], b[4][:, 0:HD]], axis=1)[0]
    gvb[...] = jnp.concatenate([b[2], b[5][:, 0:HD]], axis=1)[0]
    gub[...] = jnp.concatenate([line(24 + i) for i in range(6)], axis=1)[0]


def unpack_kernel(sizes, own, oth, tails, mask, *refs):
    nctx, ntp, ndp, main, width, rows, padded = sizes
    outs, done, valid, sem = refs[:2], refs[2], refs[3], refs[4]
    images = nctx * ntp
    me_t = lax.axis_index("tp")
    where = [j * ntp + t for t in (me_t, 1 - me_t) for j in range(nctx)]
    sources = [v.at[j] for v in (own, oth) for j in range(nctx)]
    get_valid = pltpu.make_async_copy(mask, valid, sem.at[0])
    get_valid.start()

    def hit(r, c):
        img = where[-1]
        for j in range(images - 1):
            img = jnp.where(c // BLOCK == j, where[j], img)
        return r == (c % BLOCK) * images + img

    put = one_hot((images * BLOCK, images * BLOCK), hit)
    for i in range(2):
        for b in range(main // BLOCK):
            lo = i * (main + EXTRA) + b * BLOCK
            got = jnp.concatenate([src[lo : lo + BLOCK, :] for src in sources], axis=0)
            outs[i][b * BLOCK * images : (b + 1) * BLOCK * images, :] = nn(put, got)
    get_valid.wait()
    for i in range(2):
        for src, img in zip(sources, where):
            got = src[main : main + EXTRA, :].astype(F32)[i : i + 1, :]
            outs[i][pl.ds(main * images + img, 1), :] = jnp.where(
                valid[img, main] > 0, got, tails[i, pl.ds(img, 1), :]
            )
    done[...] = jnp.zeros_like(done)


def xor(n, k):
    return [(i, i ^ k) for i in range(n)]


def over(axis, n, items):
    return [items[0]] + [lax.ppermute(items[k], axis, xor(n, k)) for k in range(1, n)]


def body(nctx, ntp, ndp, *args):
    (tokens, valid_mask, cotangent, w_query, w_key, w_value, query_bias, value_bias, w_out, w_up, up_bias, w_down) = args[:12]
    vecs = args[12:]
    images, slots, width = tokens.shape
    main = slots - 1
    rows = w_query.shape[0]
    padded = -(-rows // EXTRA) * EXTRA
    ff = w_up.shape[1]
    p1_cols = 4 * w_query.shape[1]
    sizes = (nctx, ntp, ndp, main, width, rows, padded)
    total = nctx * main + EXTRA
    keys = -(-total // TILE) * TILE
    stage = BF if rows % 16 == 0 else F32
    flip = xor(ntp, 1)
    tok = jnp.transpose(tokens, (1, 0, 2)).reshape(slots * images, width)
    cot = jnp.transpose(cotangent, (1, 0, 2)).reshape(slots * images, width)

    def one(f):
        return functools.partial(f, sizes)

    def other(v):
        return lax.ppermute(v, "tp", flip)

    def held(arrays):
        return [
            (pltpu.SMEM if v.dtype == jnp.int32 else pltpu.VMEM)(v.shape, v.dtype) for v in arrays
        ] + [pltpu.SemaphoreType.DMA((len(arrays),))]

    def gather_dp(name, piece, after):
        v = piece[None]
        stride = ndp // 2
        while stride > 1:
            v = call(
                name,
                functools.partial(join_kernel, "dp", stride),
                sds((2 * v.shape[0],) + v.shape[1:], v.dtype),
                after=after,
            )(v, lax.ppermute(v, "dp", xor(ndp, stride)))
            stride //= 2
        return v, lax.ppermute(v, "dp", xor(ndp, 1))

    sources = [w_query, w_key, w_value, w_out, w_up, jnp.transpose(w_down), query_bias, value_bias, up_bias, *vecs]
    p1, p2q, packed = call(
        "pack_weights",
        functools.partial(pack_weights_kernel, sizes, len(sources)),
        [sds((padded + EXTRA, p1_cols), BF), sds((padded, ff // 2), BF), sds((8, TILE), F32)],
        scratch=held(sources),
        mib=56,
        raw=range(len(sources)),
    )(*sources)
    sources = [tok, cot, valid_mask]
    *sent, tails = call(
        "pack_slots",
        one(pack_slots_kernel),
        [sds((2 * main + EXTRA, width), BF)] * nctx + [sds((2, images, width), F32)],
        scratch=held(sources),
        mib=48,
        raw=range(3),
    )(*sources)
    t_in = over("ctx", nctx, sent)
    w2q = gather_dp("join_quarter", p2q, [])
    w1, w1_got = gather_dp("join_attn", p1, [])
    w2q, w1_early = call(
        "merge_quarter",
        one(merge_quarter_kernel),
        [sds((width, ff // 2), BF), sds(w1.shape, BF)],
        scratch=[pltpu.VMEM((width, ff // 2), stage)],
        after=t_in[1:],
    )(w1, *w2q)
    w1_oth = other(w1_early)
    w2q = over("ctx", nctx, [w2q] * nctx)
    late = call(
        "split_attn",
        split_kernel,
        [sds(w1.shape[:2] + (p1_cols // 2,), BF)] * 2,
        after=[w1_oth, w2q[0]],
    )(w1_got)
    w1 = [w1, w1_got, w1_oth, *[other(v) for v in late]]
    x, mid, n1, n2, qkv, ctx, ctx_full, lse, wqkv, wot, vec, ub, cot_in = call(
        "attention",
        one(attention_kernel),
        [
            sds((total, width), F32), sds((total, width), F32), sds((total, width), BF), sds((total, width), BF),
            sds((keys, 3 * width), BF), sds((total, width), BF), sds((total, width), F32), sds((total, TILE), F32),
            sds((width, 3 * width), BF), sds((width, width), BF), sds((EXTRA, width), F32), sds((8, 2 * ff), F32),
            sds((total, width), BF),
        ],
        scratch=[pltpu.VMEM((width, p1_cols), stage)] * 2,
        mib=32,
    )(*t_in, *w1)
    w2_own = call(
        "merge_ff", functools.partial(merge_ff_kernel, nctx), sds((width, 2 * ff), BF), after=[vec]
    )(*w2q)
    w2_oth = other(w2_own)
    ff_grads = sds((4, ndp, padded, ff // 2), BF)

    def mlp_half(name, side, w, after=()):
        return call(
            name,
            functools.partial(mlp_half_kernel, sizes, side),
            [sds((total, ff), BF), sds((total, ff), BF), sds((8, ff), F32), ff_grads],
            mib=32,
            after=after,
        )(n2, cot_in, w, ub)

    hid_own, hgr_own, ub_own, g2_own = mlp_half("mlp_own", 0, w2_own)
    hid_oth, hgr_oth, ub_oth, g2_oth = mlp_half("mlp_oth", 1, w2_oth, [ub_own])
    bo, dmid, dctx, g_out, vgrad = call(
        "mlp_sums",
        one(mlp_sums_kernel),
        [
            sds((total, width), BF), sds((total, width), F32), sds((total, width), BF), sds((width, width), F32),
            sds((EXTRA, width), F32),
        ],
        mib=32,
    )(mid, ctx, wot, vec, cot_in, w2_own, w2_oth, hid_own, hid_oth, hgr_own, hgr_oth)

    def core_sums(name, own, oth, after=()):
        outs = [sds(own.shape[1:], BF)] * nctx
        return call(name, functools.partial(sum_core_kernel, nctx), outs, after=after)(own, other(oth))

    def by_image(v):
        return jnp.transpose(v.reshape(slots, images, width), (1, 0, 2))

    pairs = sds((2, ndp // 2, padded, ff // 2), BF)
    keep_a, send_a, keep_b, send_b = call("sum_core_ff", sum_core_ff_kernel, [pairs] * 4, after=[vgrad])(
        g2_own, other(g2_oth)
    )
    got_a, got_b = lax.ppermute(send_a, "ctx", xor(nctx, 1)), lax.ppermute(send_b, "ctx", xor(nctx, 2))
    ig, g1_own, g1_oth = call(
        "attention_back",
        one(attention_back_kernel),
        [sds((total, width), BF)] + [sds((4, ndp, padded + padded // 2 + EXTRA, TILE), BF)] * 2,
        scratch=[pltpu.VMEM((total, 3 * width), BF)],
        mib=32,
        after=[keep_a],
    )(qkv, dctx, lse, ctx_full, n1, x, dmid, wqkv, vec, g_out, vgrad, ub_own, ub_oth)
    one_quarter = sds(pairs.shape[1:], BF)
    keep_a, send_a, keep_b, send_b = call(
        "sum_ctx_first", sum_ctx_first_kernel, [one_quarter] * 4, after=[g1_own]
    )(keep_a, got_a, keep_b, got_b)
    got_a, got_b = lax.ppermute(send_a, "ctx", xor(nctx, 2)), lax.ppermute(send_b, "ctx", xor(nctx, 1))
    s1_send = core_sums("sum_core_attn", g1_own, g1_oth, after=[keep_a])
    s1 = over("ctx", nctx, s1_send)
    keep, send = call("sum_ctx_second", sum_ctx_second_kernel, [one_quarter] * 2, after=[s1_send[0]])(
        keep_a, got_a, keep_b, got_b
    )
    back = call(
        "returns",
        one(returns_kernel),
        sds((nctx, 2 * main + EXTRA, width), BF),
        after=[keep],
    )(bo, ig)
    returned = lax.all_to_all(back, "ctx", 0, 0)
    u1_send = call(
        "sum_ctx_attn",
        functools.partial(sum_ctx_kernel, nctx, ndp),
        [sds(s1[0].shape[1:], BF)] * ndp,
        after=[back],
    )(*s1)
    u1 = over("dp", ndp, u1_send)
    stride = 2
    while stride < ndp:
        half = sds((keep.shape[0] // 2,) + keep.shape[1:], BF)
        keep, send = call(
            "add_dp_ff", functools.partial(add_halves_kernel, stride), [half, half], after=[u1_send[0]]
        )(keep, lax.ppermute(send, "dp", xor(ndp, stride // 2)))
        stride *= 2
    summed = call(
        "sum_dp", functools.partial(sum_dp_kernel, ndp), sds((padded + -(-s1[0].shape[1] // (3 * EXTRA)) * EXTRA, ff // 2), BF)
    )(keep, lax.ppermute(send, "dp", xor(ndp, ndp // 2)), *u1)
    shares = over("ctx", nctx, [summed] * nctx)
    back = call("hand_on", hand_on_kernel, sds(returned.shape, BF), after=[summed])(returned)
    block_out, input_grad, placed = call(
        "place_slots",
        one(unpack_kernel),
        [sds(tok.shape, F32)] * 2 + [sds((8, TILE), F32)],
        scratch=[pltpu.SMEM(valid_mask.shape, valid_mask.dtype), pltpu.SemaphoreType.DMA((1,))],
        raw=(3,),
        mib=16,
    )(back, other(back), tails, valid_mask)
    gq, gk, gv, gqb, gvb, go, gu, gub, gd, *gvec = call(
        "place_grads",
        one(grads_kernel),
        [
            sds(w_query.shape, F32), sds(w_key.shape, F32), sds(w_value.shape, F32),
            sds(query_bias.shape, F32), sds(value_bias.shape, F32), sds(w_out.shape, F32),
            sds(w_up.shape, F32), sds(up_bias.shape, F32), sds((rows, ff), F32),
        ]
        + [sds((rows,), F32)] * 6,
        scratch=[
            pltpu.VMEM((nctx,) + s1[0].shape[1:], F32),
            pltpu.VMEM((nctx, padded, ff // 2), F32),
        ],
        after=[placed],
    )(*shares)
    return (by_image(block_out), by_image(input_grad), gq, gk, gv, gqb, gvb, go, gu, gub, jnp.transpose(gd), *gvec)


def solution(mesh):
    rows, cols, tp, dp = P("dp", "tp"), P("tp", "dp"), P("tp"), P("dp")
    act = P("dp", "ctx", None)
    return jax.shard_map(
        functools.partial(body, mesh.shape["ctx"], mesh.shape["tp"], mesh.shape["dp"]),
        mesh=mesh,
        in_specs=(act, P("dp", "ctx"), act, rows, rows, rows, tp, tp, cols, rows, tp, cols) + (dp,) * 6,
        out_specs=(act, act, rows, rows, rows, tp, tp, cols, rows, tp, cols) + (dp,) * 6,
        check_vma=False,
    )
```

```python
import functools

import jax
import jax.numpy as jnp
from jax import lax
from jax.experimental import pallas as pl
from jax.experimental.pallas import tpu as pltpu
from jax.sharding import PartitionSpec as P

HD = 64
EPS = 1e-06
SCALE = 0.125
FLOOR = -1e30
BF = jnp.bfloat16
F32 = jnp.float32
TILE = 128
TIMES = {
    "pack_weights": 2.0, "pack_slots": 3.0, "join_quarter": 20.0, "attention": 0.0, "mlp_own": 4.0, "mlp_oth": 4.0, "mlp_sums": 2.0,
    "attention_back": 11.0, "sum_ctx_first": 50.0, "sum_ctx_attn": 0.5, "sum_dp": 5.0, "place_slots": 2.3, "place_grads": 1.0,
}
EXTRA = 16


def call(name, kernel, out_shape, scratch=(), mib=8, after=(), raw=()):
    after = list(after)

    def ordered(*refs):
        kernel(*refs[len(after) :])

    def run(*args):
        specs = [pl.BlockSpec(memory_space=pl.ANY)] * len(after) + [
            pl.BlockSpec(memory_space=pltpu.HBM if i in raw else pltpu.VMEM)
            for i in range(len(args))
        ]
        return pl.pallas_call(
            ordered,
            name=name,
            out_shape=out_shape,
            in_specs=specs,
            out_specs=jax.tree.map(lambda _: pl.BlockSpec(memory_space=pltpu.VMEM), out_shape),
            scratch_shapes=list(scratch),
            compiler_params=pltpu.CompilerParams(vmem_limit_bytes=mib << 20),
            cost_estimate=pl.CostEstimate(
                flops=int(TIMES.get(name, 0.2) * 1.15e9), bytes_accessed=1, transcendentals=0
            ),
        )(*after, *args)

    return run


def sds(shape, dtype):
    return jax.ShapeDtypeStruct(shape, dtype)


def nn(a, b):
    return lax.dot_general(a, b, (((1,), (0,)), ((), ())), preferred_element_type=F32)


def nt(a, b):
    return lax.dot_general(a, b, (((1,), (1,)), ((), ())), preferred_element_type=F32)


def tn(a, b):
    return lax.dot_general(a, b, (((0,), (0,)), ((), ())), preferred_element_type=F32)


def swap(v):
    return pltpu.roll(v, HD, axis=1)


def low_lanes(shape):
    return lax.broadcasted_iota(jnp.int32, shape, 1) < HD


def row_is(shape, row):
    return lax.broadcasted_iota(jnp.int32, shape, 0) == row


def tile(v, i):
    return v[:, i * TILE : (i + 1) * TILE]


def assemble(own, oth):
    low = low_lanes((own.shape[0], TILE))
    own_qk, own_vo, oth_qk, oth_vo = tile(own, 4), tile(own, 5), tile(oth, 4), tile(oth, 5)
    qkv = [
        tile(own, 0), tile(oth, 0), jnp.where(low, own_qk, swap(oth_qk)),
        tile(own, 1), tile(oth, 1), jnp.where(low, swap(own_qk), oth_qk),
        tile(own, 2), tile(oth, 2), jnp.where(low, own_vo, swap(oth_vo)),
    ]
    out = [tile(own, 3), tile(oth, 3), jnp.where(low, swap(own_vo), oth_vo)]
    return qkv, out


def disassemble(qkv, out):
    low = low_lanes(qkv[0].shape)
    own = [qkv[0], qkv[3], qkv[6], out[0], jnp.where(low, qkv[2], swap(qkv[5])), jnp.where(low, qkv[8], swap(out[2]))]
    oth = [qkv[1], qkv[4], qkv[7], out[1], jnp.where(low, swap(qkv[2]), qkv[5]), jnp.where(low, swap(qkv[8]), out[2])]
    return own, oth


def norm_stats(v):
    mean = jnp.mean(v, axis=-1, keepdims=True)
    centered = v - mean
    r = lax.rsqrt(jnp.mean(centered * centered, axis=-1, keepdims=True) + EPS)
    return centered * r, r


def norm_back(e, xhat, r):
    return r * (
        e
        - jnp.mean(e, axis=-1, keepdims=True)
        - xhat * jnp.mean(e * xhat, axis=-1, keepdims=True)
    )


def gelu_pair(v):
    phi = 0.5 + 0.5 * lax.erf(v * 0.7071067811865476)
    return v * phi, phi + (0.3989422804014327 * v) * jnp.exp(-0.5 * v * v)


BLOCK = 16


def one_hot(shape, hit):
    r, c = (lax.broadcasted_iota(jnp.int32, shape, i) for i in range(2))
    return hit(r, c).astype(F32).astype(BF)


def picker(wanted, images):
    def hit(r, c):
        img = wanted[-1]
        for k in range(len(wanted) - 1):
            img = jnp.where(r // BLOCK == k, wanted[k], img)
        return c == (r % BLOCK) * images + img

    return one_hot((len(wanted) * BLOCK, images * BLOCK), hit)


def take_images(ref, outs, at, pick, images, count):
    for b in range(count // BLOCK):
        got = nn(pick, ref[b * BLOCK * images : (b + 1) * BLOCK * images, :].astype(BF)).astype(BF)
        for k in range(len(outs)):
            outs[k][at + b * BLOCK : at + (b + 1) * BLOCK, :] = got[k * BLOCK : (k + 1) * BLOCK]


def fetch(sources, held, sem):
    copies = [pltpu.make_async_copy(sources[i], held[i], sem.at[i]) for i in range(len(sources))]
    for c in copies:
        c.start()
    return copies


def pack_weights_kernel(sizes, count, *refs):
    nctx, ntp, ndp, main, width, rows, padded = sizes
    sources, (p1, p2q), refs = refs[:count], refs[count : count + 2], refs[count + 2 :]
    held, sem = refs[:count], refs[count]
    copies = fetch(sources, held, sem)
    wq, wk, wv, wo, wu, wd, qb, vb, ub = held[:9]
    vecs = held[9:]
    me_c, me_d = lax.axis_index("ctx"), lax.axis_index("dp")
    for c in copies:
        c.wait()
    if padded > rows:
        p1[0:padded, :] = jnp.zeros((padded, p1.shape[1]), BF)
        p2q[...] = jnp.zeros(p2q.shape, BF)
    quarter = p2q.shape[1]
    for j in range(nctx):
        src = (wu, wd)[j // 2][:, (j % 2) * quarter : (j % 2 + 1) * quarter]

        @pl.when(me_c == j)
        def _(src=src):
            p2q[0:rows, :] = src

    def put(lo, value):
        p1[0:rows, lo : lo + value.shape[1]] = value.astype(BF)

    fq, fk, fv = wq[...].astype(F32), wk[...].astype(F32), wv[...].astype(F32)
    fo = jnp.transpose(wo[...].astype(F32))
    for i, w in enumerate((fq, fk, fv, fo)):
        put(i * TILE, tile(w, 0))
    put(4 * TILE, jnp.concatenate([fq[:, TILE:], fk[:, TILE:]], axis=1))
    put(5 * TILE, jnp.concatenate([fv[:, TILE:], fo[:, TILE:]], axis=1))
    cols = p1.shape[1]
    fqb, fvb = qb[...].astype(F32)[None, :], vb[...].astype(F32)[None, :]
    none = jnp.zeros((1, TILE), F32)
    short = jnp.zeros((1, HD), F32)
    bias = jnp.concatenate(
        [fqb[:, :TILE], none, fvb[:, :TILE], none, fqb[:, TILE:], short, fvb[:, TILE:], short], axis=1
    )
    spread = one_hot((rows, width), lambda r, c: c == r + rows * me_d)
    block = jnp.where(row_is((EXTRA, cols), 0), bias, 0.0)
    block = jnp.where(row_is((EXTRA, cols), 7), ub[...].astype(F32)[None, :], block)
    lanes = jnp.zeros((EXTRA, rows), F32)
    for i in range(6):
        lanes = jnp.where(row_is((EXTRA, rows), 1 + i), vecs[i][...].astype(F32)[None, :], lanes)
    lanes = nn(lanes.astype(BF), spread)
    p1[padded : padded + EXTRA, :] = block.astype(BF)
    mixed = jnp.where(
        (lax.broadcasted_iota(jnp.int32, (EXTRA, width), 0) - 1).astype(jnp.uint32) < 6,
        lanes,
        block[:, :width],
    )
    p1[padded : padded + EXTRA, 0:width] = mixed.astype(BF)


def pack_slots_kernel(sizes, tok, cot, source, *refs):
    nctx, ntp, ndp, main, width, rows, padded = sizes
    sent, tails, mask, sem = refs[:nctx], refs[nctx], refs[nctx + 1], refs[nctx + 2]
    get_mask = pltpu.make_async_copy(source, mask, sem.at[0])
    get_mask.start()
    images = nctx * ntp
    me_c, me_t = lax.axis_index("ctx"), lax.axis_index("tp")
    wanted = [(me_c ^ k) * ntp + me_t for k in range(nctx)]
    pick = picker(wanted, images)
    for i, ref in enumerate((tok, cot)):
        take_images(ref, sent, i * (main + EXTRA), pick, images, main)
        tails[i] = ref[main * images :, :]
    get_mask.wait()
    for k in range(nctx):
        gate = mask[wanted[k], main].astype(F32)
        te = tok[pl.ds(main * images + wanted[k], 1), :] * gate
        ce = cot[pl.ds(main * images + wanted[k], 1), :] * gate
        shape = (EXTRA, width)
        sent[k][main : main + EXTRA, :] = jnp.where(
            row_is(shape, 0), te, jnp.where(row_is(shape, 1), ce, 0.0)
        ).astype(BF)


def join_kernel(axis, stride, own, got, out):
    bit = lax.rem(lax.div(lax.axis_index(axis), stride), 2)
    for i in range(own.shape[0]):
        out[2 * i + bit] = own[i]
        out[2 * i + 1 - bit] = got[i]


def place_rows(stage, own, got, rows):
    bit = lax.rem(lax.axis_index("dp"), 2)
    for i in range(own.shape[0]):
        for piece, last in ((own, bit), (got, 1 - bit)):
            at = pl.ds(pl.multiple_of((2 * i + last) * rows, 16 if rows % 16 == 0 else 8), rows)
            stage[at, :] = piece[i].astype(stage.dtype)[:rows]


def merge_quarter_kernel(sizes, attn, own, got, out, attn_out, stage):
    place_rows(stage, own, got, sizes[5])
    out[...] = stage[...].astype(BF)
    attn_out[...] = attn[...]


def split_kernel(got, *outs):
    for i, out in enumerate(outs):
        cols = out.shape[2]
        out[...] = got[:, :, i * cols : (i + 1) * cols]


def merge_ff_kernel(nctx, *refs):
    out = refs[nctx]
    me_c = lax.axis_index("ctx")
    for k in range(nctx):
        quarter = refs[k].shape[1]
        out[:, pl.ds(pl.multiple_of((me_c ^ k) * quarter, quarter), quarter)] = refs[k][...]


def attention_kernel(sizes, *refs):
    nctx, ntp, ndp, main, width, rows, padded = sizes
    t_in, (own, got, own_oth, got_oth_a, got_oth_b), refs = refs[:nctx], refs[nctx : nctx + 5], refs[nctx + 5 :]
    x_out, mid_out, n1_out, n2_out, qkv, ctx, ctx_full, lse, wqkv, wot, vec, ub, cot, stage, stage_oth = refs
    body = nctx * main
    total = body + EXTRA
    half = got_oth_a.shape[2]
    place_rows(stage, own, got, rows)
    place_rows(stage_oth.at[:, :half], own_oth.at[:, :, :half], got_oth_a, rows)
    place_rows(stage_oth.at[:, half:], own_oth.at[:, :, half:], got_oth_b, rows)
    tiles, outs = assemble(stage[...].astype(F32), stage_oth[...].astype(F32))
    for i, v in enumerate(tiles):
        wqkv[:, i * TILE : (i + 1) * TILE] = v.astype(BF)
    for i, v in enumerate(outs):
        wot[:, i * TILE : (i + 1) * TILE] = v.astype(BF)
    extra = own[0, padded:, :].astype(F32)
    extra_oth = own_oth[0, padded:, :].astype(F32)
    tiles, _ = assemble(extra, extra_oth)
    bias = jnp.concatenate([v[0:1] for v in tiles], axis=1)
    vec_sum = jnp.zeros((EXTRA, width), F32)
    for i in range(own.shape[0]):
        vec_sum += own[i, padded:, :width].astype(F32) + got[i, padded:, :width].astype(F32)
    vec[...] = vec_sum
    ub[...] = jnp.broadcast_to(jnp.concatenate([extra[7:8], extra_oth[7:8]], axis=1), ub.shape)
    extra = jnp.zeros((EXTRA, width), F32)
    for k in range(nctx):
        x_out[k * main : (k + 1) * main, :] = t_in[k][0:main, :].astype(F32)
        cot[k * main : (k + 1) * main, :] = t_in[k][main + EXTRA :, :]
        extra += t_in[k][main : main + EXTRA, :].astype(F32)
    x_out[body:, :] = jnp.where(row_is((EXTRA, width), 0), extra, 0.0)
    cot[body:, :] = jnp.where(row_is((EXTRA, width), 0), extra[1:2, :], 0.0).astype(BF)
    x = x_out[...]
    xhat, _ = norm_stats(x)
    n1 = (xhat * vec_sum[1:2, :] + vec_sum[2:3, :]).astype(BF)
    n1_out[...] = n1
    proj = nn(n1, wqkv[...]) + bias
    qkv[0:total, 0:width] = (proj[:, 0:width].astype(BF).astype(F32) * SCALE).astype(BF)
    qkv[0:total, width:] = proj[:, width:].astype(BF)
    keys = qkv.shape[0]
    qkv[total:, :] = jnp.zeros((keys - total, qkv.shape[1]), BF)
    off = jnp.where(lax.broadcasted_iota(jnp.int32, (1, keys), 1) > body, FLOOR, 0.0)
    low = low_lanes((total, TILE))
    lane = lax.broadcasted_iota(jnp.int32, (total, TILE), 1)
    all_lse = jnp.zeros((total, TILE), F32)
    for p in range(3):
        qp = qkv[0:total, p * TILE : (p + 1) * TILE]
        kp = qkv[:, width + p * TILE : width + (p + 1) * TILE]
        vp = qkv[:, 2 * width + p * TILE : 2 * width + (p + 1) * TILE]
        parts = []
        for a in range(2):
            qa = jnp.where(low if a == 0 else ~low, qp, jnp.zeros_like(qp))
            s = nt(qa, kp) + off
            m = jnp.max(s, axis=-1, keepdims=True)
            e = jnp.exp(s - m)
            l = jnp.sum(e, axis=-1, keepdims=True)
            parts.append(nn(e.astype(BF), vp) * (1.0 / l))
            all_lse = jnp.where(lane == 2 * p + a, m + jnp.log(l), all_lse)
        ctx_full[:, p * TILE : (p + 1) * TILE] = jnp.where(low, parts[0], parts[1])
    ctx[...] = ctx_full[...].astype(BF)
    lse[...] = all_lse
    attended = nt(ctx[...], wot[...]) + vec_sum[5:6, :]
    valid = lax.broadcasted_iota(jnp.int32, (total, 1), 0) <= body
    middle = x_out[...] + jnp.where(valid, attended, 0.0)
    mid_out[...] = middle
    xhat2, _ = norm_stats(middle)
    n2_out[...] = (xhat2 * vec_sum[3:4, :] + vec_sum[4:5, :]).astype(BF)


def mlp_half_kernel(sizes, side, n2, cot, w, ub, hid, hgr, ubgrad, grads):
    nctx, ntp, ndp, main, width, rows, padded = sizes
    half = w.shape[1] // 2
    n2v, dcot = n2[...], cot[...]
    act, slope = gelu_pair(nn(n2v, w[:, :half]) + ub[0:1, side * half : (side + 1) * half])
    h = act.astype(BF)
    hg = (nn(dcot, w[:, half:]) * slope).astype(BF)
    hid[...] = h
    hgr[...] = hg
    ubgrad[...] = jnp.broadcast_to(jnp.sum(hg.astype(F32), axis=0, keepdims=True), ubgrad.shape)
    cols = grads.shape[3]
    for part, g in ((0, tn(n2v, hg).astype(BF)), (1, tn(dcot, h).astype(BF))):
        for d in range(ndp):
            for c in range(half // cols):
                grads[2 * part + c, d, 0:rows, :] = g[d * rows : (d + 1) * rows, c * cols : (c + 1) * cols]


def mlp_sums_kernel(sizes, mid, ctx, wot, vec, cot, w_own, w_oth, hid_own, hid_oth, hgr_own, hgr_oth, bo, dmid, dctx, g_out, vgrad):
    nctx, ntp, ndp, main, width, rows, padded = sizes
    body = nctx * main
    total = body + EXTRA
    half = w_own.shape[1] // 2
    dcot = cot[...]
    middle = mid[...]
    valid = lax.broadcasted_iota(jnp.int32, (total, 1), 0) <= body
    n2g = nt(hgr_own[...], w_own[:, :half]) + nt(hgr_oth[...], w_oth[:, :half])
    xhat, r = norm_stats(middle)
    back = norm_back(n2g * vec[3:4, :], xhat, r)
    middle_grad = dcot.astype(F32) + back
    dmid[...] = middle_grad
    agrad = jnp.where(valid, middle_grad, 0.0).astype(BF)
    dctx[...] = nn(agrad, wot[...]).astype(BF)
    g_out[...] = tn(agrad, ctx[...])
    mlp_out = nt(hid_own[...], w_own[:, half:]) + nt(hid_oth[...], w_oth[:, half:]) + vec[6:7, :]
    bo[...] = (middle + jnp.where(valid, mlp_out, 0.0)).astype(BF)
    shape = vgrad.shape
    v = jnp.where(row_is(shape, 2), jnp.sum(n2g * xhat, axis=0, keepdims=True), 0.0)
    v = jnp.where(row_is(shape, 3), jnp.sum(n2g, axis=0, keepdims=True), v)
    v = jnp.where(row_is(shape, 4), jnp.sum(agrad.astype(F32), axis=0, keepdims=True), v)
    v = jnp.where(row_is(shape, 5), jnp.sum(dcot.astype(F32), axis=0, keepdims=True), v)
    vgrad[...] = v


def pair_back(p, width, total, body, qkv, dctx, lse, ctx):
    keys = qkv.shape[0]
    off = jnp.where(lax.broadcasted_iota(jnp.int32, (1, keys), 1) > body, FLOOR, 0.0)
    low = low_lanes((total, TILE))
    at = slice(p * TILE, (p + 1) * TILE)
    qp = qkv[0:total, at]
    kp = qkv[:, width + p * TILE : width + (p + 1) * TILE]
    vp = qkv[:, 2 * width + p * TILE : 2 * width + (p + 1) * TILE]
    dp = dctx[:, at]
    both = dp.astype(F32) * ctx[:, at]
    qt = jnp.transpose(qp.astype(F32)).astype(BF)
    dt = jnp.transpose(dp.astype(F32)).astype(BF)
    dk, dv = [], []
    zero = jnp.zeros_like(qp)
    qs = jnp.concatenate([jnp.where(low, qp, zero), jnp.where(low, zero, qp)], axis=0)
    ds_ = jnp.concatenate([jnp.where(low, dp, zero), jnp.where(low, zero, dp)], axis=0)
    bs = jnp.concatenate([jnp.where(low, both, 0.0), jnp.where(low, 0.0, both)], axis=0)
    inner = jnp.sum(bs, axis=-1, keepdims=True)
    ls = jnp.concatenate([lse[:, 2 * p : 2 * p + 1], lse[:, 2 * p + 1 : 2 * p + 2]], axis=0)
    prob = jnp.exp(nt(qs, kp) + off - ls)
    ds = (prob * (nt(ds_, vp) - inner)).astype(BF)
    w = prob.astype(BF)
    dq = nn(ds, kp)
    dq = jnp.where(low, dq[0:total], dq[total:]) * SCALE
    for a in range(2):
        dk.append(nn(qt[a * HD : (a + 1) * HD], ds[a * total : (a + 1) * total]))
        dv.append(nn(dt[a * HD : (a + 1) * HD], w[a * total : (a + 1) * total]))
    dk, dv = (jnp.transpose(jnp.concatenate(v, axis=0))[0:total] for v in (dk, dv))
    return dq.astype(BF), dk.astype(BF), dv.astype(BF)


def attention_back_kernel(sizes, *refs):
    nctx, ntp, ndp, main, width, rows, padded = sizes
    qkv, dctx, lse, ctx, n1, x_in, dmid, wqkv, vec, g_out, vgrad, ub_own, ub_oth = refs[:13]
    ig, g_own, g_oth, dqkv = refs[13:]
    body = nctx * main
    total = body + EXTRA
    for p in range(3):
        for i, v in enumerate(pair_back(p, width, total, body, qkv, dctx, lse, ctx)):
            dqkv[:, i * width + p * TILE : i * width + (p + 1) * TILE] = v
    d = dqkv[...]
    bias = jnp.sum(d.astype(F32), axis=0, keepdims=True)
    g = tn(n1[...], d)
    go = g_out[...]
    own, oth = disassemble([tile(g, i) for i in range(9)], [tile(go, i) for i in range(3)])
    half = padded // 2
    for to, tiles in ((g_own, own), (g_oth, oth)):
        for j in range(4):
            lo = j % 2 * half
            for e in range(ndp):
                to[j, e, 0:rows, :] = tiles[j][e * rows : (e + 1) * rows].astype(BF)
                shared = tiles[4 + j // 2][e * rows + lo : e * rows + min(rows, lo + half)]
                to[j, e, padded : padded + shared.shape[0], :] = shared.astype(BF)
    dn1 = nt(d, wqkv[...])
    xhat, r = norm_stats(x_in[...])
    grad = dmid[...] + norm_back(dn1 * vec[1:2, :], xhat, r)
    ig[...] = grad.astype(BF)
    gains = jnp.sum(dn1 * xhat, axis=0, keepdims=True)
    shifts = jnp.sum(dn1, axis=0, keepdims=True)
    vecs = [gains, shifts] + [vgrad[i : i + 1, :] for i in range(2, 6)]
    zero = [jnp.zeros((1, TILE), F32)] * 3
    bias_own, bias_oth = disassemble([tile(bias, i) for i in range(9)], zero)
    for to, tiles, ub in ((g_own, bias_own, ub_own), (g_oth, bias_oth, ub_oth)):
        rows_ = [tile(v, i) for v in vecs for i in range(3)] + tiles
        rows_ += [ub[0:1, i * TILE : (i + 1) * TILE] for i in range(6)]
        for j in range(4):
            block = jnp.zeros((EXTRA, TILE), F32)
            for i, v in enumerate(rows_[8 * j : 8 * (j + 1)]):
                block = jnp.where(row_is(block.shape, i), v, block)
            for e in range(ndp):
                to[j, e, padded + half :, :] = block.astype(BF)


def sum_core_kernel(n, own, oth, *outs):
    me = lax.axis_index("ctx")
    for k in range(n):
        outs[k][...] = (own[me ^ k].astype(F32) + oth[me ^ k].astype(F32)).astype(BF)


def sum_ctx_kernel(n, ndp, *refs):
    me = lax.axis_index("dp")
    for k in range(ndp):
        v = refs[0][me ^ k].astype(F32)
        for i in range(1, n):
            v = v + refs[i][me ^ k].astype(F32)
        refs[n + k][...] = v.astype(BF)


def halve(stride, item, keep, send):
    bit = lax.rem(lax.div(lax.axis_index("dp"), stride), 2)
    for j in range(keep.shape[0]):
        keep[j] = item(2 * j + bit).astype(BF)
        send[j] = item(2 * j + 1 - bit).astype(BF)


def ctx_bits():
    me = lax.axis_index("ctx")
    return lax.rem(me, 2), lax.div(me, 2)


def sum_core_ff_kernel(own, oth, keep_a, send_a, keep_b, send_b):
    low, high = ctx_bits()
    half = own.shape[1] // 2

    def put(to, i, quarter, blocks):
        to[i] = (own[quarter, blocks].astype(F32) + oth[quarter, blocks].astype(F32)).astype(BF)

    for i in range(2):
        first, second = slice(0, half), slice(half, 2 * half)
        put(keep_a, i, 2 * i + low, first)
        put(send_a, i, 2 * i + 1 - low, first)
        put(keep_b, i, 2 * high + i, second)
        put(send_b, i, 2 * (1 - high) + i, second)


def sum_ctx_first_kernel(own_a, got_a, own_b, got_b, keep_a, send_a, keep_b, send_b):
    low, high = ctx_bits()
    for own, got, keep, send, bit in (
        (own_a, got_a, keep_a, send_a, high),
        (own_b, got_b, keep_b, send_b, low),
    ):
        keep[...] = (own[bit].astype(F32) + got[bit].astype(F32)).astype(BF)
        send[...] = (own[1 - bit].astype(F32) + got[1 - bit].astype(F32)).astype(BF)


def sum_ctx_second_kernel(own_a, got_a, own_b, got_b, keep, send):
    bit = lax.rem(lax.axis_index("dp"), 2)
    half = own_a.shape[0]
    for j in range(keep.shape[0]):
        own, got, at = (own_a, got_a, 2 * j) if 2 * j < half else (own_b, got_b, 2 * j - half)
        for to, i in ((keep, at + bit), (send, at + 1 - bit)):
            to[j] = (own[i].astype(F32) + got[i].astype(F32)).astype(BF)


def add_halves_kernel(stride, own, got, keep, send):
    halve(stride, lambda i: own[i].astype(F32) + got[i].astype(F32), keep, send)


def sum_dp_kernel(n, own, got, *refs):
    out = refs[n]
    rows = own.shape[1]
    out[:rows, :] = (own[0].astype(F32) + got[0, 0:rows, :].astype(F32)).astype(BF)
    v = refs[0][...].astype(F32)
    for r in refs[1:n]:
        v = v + r[...].astype(F32)
    span = out.shape[0] - rows
    out[rows:, :] = jnp.zeros((span, out.shape[1]), BF)
    for i in range(out.shape[1] // TILE):
        part = v[i * span : (i + 1) * span].astype(BF)
        if part.shape[0]:
            out[rows : rows + part.shape[0], i * TILE : (i + 1) * TILE] = part


def returns_kernel(sizes, bo, ig, out):
    nctx, ntp, ndp, main, width, rows, padded = sizes
    me = lax.axis_index("ctx")
    body = nctx * main
    shape = (EXTRA, width)
    extra = jnp.where(
        row_is(shape, 0),
        bo[body:, :].astype(F32),
        jnp.where(row_is(shape, 1), ig[body:, :].astype(F32)[0:1, :], 0.0),
    ).astype(BF)
    for k in range(nctx):
        at = slice(k * main, (k + 1) * main)
        out[me ^ k, 0:main, :] = bo[at, :]
        out[me ^ k, main : main + EXTRA, :] = extra
        out[me ^ k, main + EXTRA :, :] = ig[at, :]


def hand_on_kernel(held, out):
    out[...] = held[...]


def grads_kernel(sizes, *refs):
    nctx, ntp, ndp, main, width, rows, padded = sizes
    parts, refs = refs[:nctx], refs[nctx:]
    gq, gk, gv, gqb, gvb, go, gu, gub, gd = refs[:9]
    gvec, f, f2 = refs[9:15], refs[15], refs[16]
    me, me_d = lax.axis_index("ctx"), lax.axis_index("dp")
    span = parts[0].shape[0] - padded
    for k in range(nctx):
        f2[me ^ k] = parts[k][0:padded, :].astype(F32)
        for i in range(f2.shape[2] // TILE):
            n = min(span, f.shape[1] - i * span)
            if n > 0:
                f[me ^ k, i * span : i * span + n, :] = parts[k][
                    padded : padded + n, i * TILE : (i + 1) * TILE
                ].astype(F32)
    half = f2.shape[2]
    for j in range(2):
        gu[:, j * half : (j + 1) * half] = f2[j, 0:rows, :]
        gd[:, j * half : (j + 1) * half] = f2[2 + j, 0:rows, :]
    q01, k01, v01, o01 = (f[j, 0:rows, :] for j in range(4))
    low, high = slice(padded, padded + padded // 2), slice(padded, padded + rows - padded // 2)
    qk2 = jnp.concatenate([f[0, low, :], f[1, high, :]], axis=0)
    vo2 = jnp.concatenate([f[2, low, :], f[3, high, :]], axis=0)
    gq[:, 0:TILE] = q01
    gq[:, TILE:] = qk2[:, 0:HD]
    gk[:, 0:TILE] = k01
    gk[:, TILE:] = swap(qk2)[:, 0:HD]
    gv[:, 0:TILE] = v01
    gv[:, TILE:] = vo2[:, 0:HD]
    go[0:TILE, :] = jnp.transpose(o01)
    go[TILE:, :] = jnp.transpose(vo2)[HD:, :]

    def line(i):
        at = padded + padded // 2 + i % 8
        return f[i // 8, at : at + 1, :]

    for i in range(6):
        v = jnp.concatenate([line(3 * i), line(3 * i + 1), line(3 * i + 2)], axis=1)
        v = jnp.broadcast_to(v, (8, width))
        v = pltpu.roll(v, lax.rem(width - me_d * rows, width), axis=1)
        gvec[i][...] = v[0, 0:rows]
    b = [line(18 + i) for i in range(6)]
    gqb[...] = jnp.concatenate([b[0], b[4][:, 0:HD]], axis=1)[0]
    gvb[...] = jnp.concatenate([b[2], b[5][:, 0:HD]], axis=1)[0]
    gub[...] = jnp.concatenate([line(24 + i) for i in range(6)], axis=1)[0]


def unpack_kernel(sizes, own, oth, tails, mask, *refs):
    nctx, ntp, ndp, main, width, rows, padded = sizes
    outs, done, valid, sem = refs[:2], refs[2], refs[3], refs[4]
    images = nctx * ntp
    me_t = lax.axis_index("tp")
    where = [j * ntp + t for t in (me_t, 1 - me_t) for j in range(nctx)]
    sources = [v.at[j] for v in (own, oth) for j in range(nctx)]
    get_valid = pltpu.make_async_copy(mask, valid, sem.at[0])
    get_valid.start()

    def hit(r, c):
        img = where[-1]
        for j in range(images - 1):
            img = jnp.where(c // BLOCK == j, where[j], img)
        return r == (c % BLOCK) * images + img

    put = one_hot((images * BLOCK, images * BLOCK), hit)
    for i in range(2):
        for b in range(main // BLOCK):
            lo = i * (main + EXTRA) + b * BLOCK
            got = jnp.concatenate([src[lo : lo + BLOCK, :] for src in sources], axis=0)
            outs[i][b * BLOCK * images : (b + 1) * BLOCK * images, :] = nn(put, got)
    get_valid.wait()
    for i in range(2):
        for src, img in zip(sources, where):
            got = src[main : main + EXTRA, :].astype(F32)[i : i + 1, :]
            outs[i][pl.ds(main * images + img, 1), :] = jnp.where(
                valid[img, main] > 0, got, tails[i, pl.ds(img, 1), :]
            )
    done[...] = jnp.zeros_like(done)


def xor(n, k):
    return [(i, i ^ k) for i in range(n)]


def over(axis, n, items):
    return [items[0]] + [lax.ppermute(items[k], axis, xor(n, k)) for k in range(1, n)]


def body(nctx, ntp, ndp, *args):
    (tokens, valid_mask, cotangent, w_query, w_key, w_value, query_bias, value_bias, w_out, w_up, up_bias, w_down) = args[:12]
    vecs = args[12:]
    images, slots, width = tokens.shape
    main = slots - 1
    rows = w_query.shape[0]
    padded = -(-rows // EXTRA) * EXTRA
    ff = w_up.shape[1]
    p1_cols = 4 * w_query.shape[1]
    sizes = (nctx, ntp, ndp, main, width, rows, padded)
    total = nctx * main + EXTRA
    keys = -(-total // TILE) * TILE
    stage = BF if rows % 16 == 0 else F32
    flip = xor(ntp, 1)
    tok = jnp.transpose(tokens, (1, 0, 2)).reshape(slots * images, width)
    cot = jnp.transpose(cotangent, (1, 0, 2)).reshape(slots * images, width)

    def one(f):
        return functools.partial(f, sizes)

    def other(v):
        return lax.ppermute(v, "tp", flip)

    def held(arrays):
        return [
            (pltpu.SMEM if v.dtype == jnp.int32 else pltpu.VMEM)(v.shape, v.dtype) for v in arrays
        ] + [pltpu.SemaphoreType.DMA((len(arrays),))]

    def gather_dp(name, piece, after):
        v = piece[None]
        stride = ndp // 2
        while stride > 1:
            v = call(
                name,
                functools.partial(join_kernel, "dp", stride),
                sds((2 * v.shape[0],) + v.shape[1:], v.dtype),
                after=after,
            )(v, lax.ppermute(v, "dp", xor(ndp, stride)))
            stride //= 2
        return v, lax.ppermute(v, "dp", xor(ndp, 1))

    sources = [w_query, w_key, w_value, w_out, w_up, jnp.transpose(w_down), query_bias, value_bias, up_bias, *vecs]
    p1, p2q = call(
        "pack_weights",
        functools.partial(pack_weights_kernel, sizes, len(sources)),
        [sds((padded + EXTRA, p1_cols), BF), sds((padded, ff // 2), BF)],
        scratch=held(sources),
        mib=56,
        raw=range(len(sources)),
    )(*sources)
    *sent, tails = call(
        "pack_slots",
        one(pack_slots_kernel),
        [sds((2 * main + EXTRA, width), BF)] * nctx + [sds((2, images, width), F32)],
        scratch=[pltpu.SMEM(valid_mask.shape, valid_mask.dtype), pltpu.SemaphoreType.DMA((1,))],
        mib=48,
        raw=(2,),
    )(tok, cot, valid_mask)
    t_in = over("ctx", nctx, sent)
    w2q = gather_dp("join_quarter", p2q, [])
    w1, w1_got = gather_dp("join_attn", p1, [])
    w2q, w1_early = call(
        "merge_quarter",
        one(merge_quarter_kernel),
        [sds((width, ff // 2), BF), sds(w1.shape, BF)],
        scratch=[pltpu.VMEM((width, ff // 2), stage)],
        after=t_in[1:],
    )(w1, *w2q)
    w1_oth = other(w1_early)
    w2q = over("ctx", nctx, [w2q] * nctx)
    late = call(
        "split_attn",
        split_kernel,
        [sds(w1.shape[:2] + (p1_cols // 2,), BF)] * 2,
        after=[w1_oth, w2q[0]],
    )(w1_got)
    w1 = [w1, w1_got, w1_oth, *[other(v) for v in late]]
    x, mid, n1, n2, qkv, ctx, ctx_full, lse, wqkv, wot, vec, ub, cot_in = call(
        "attention",
        one(attention_kernel),
        [
            sds((total, width), F32), sds((total, width), F32), sds((total, width), BF), sds((total, width), BF),
            sds((keys, 3 * width), BF), sds((total, width), BF), sds((total, width), F32), sds((total, TILE), F32),
            sds((width, 3 * width), BF), sds((width, width), BF), sds((EXTRA, width), F32), sds((8, 2 * ff), F32),
            sds((total, width), BF),
        ],
        scratch=[pltpu.VMEM((width, p1_cols), stage)] * 2,
        mib=32,
    )(*t_in, *w1)
    w2_own = call(
        "merge_ff", functools.partial(merge_ff_kernel, nctx), sds((width, 2 * ff), BF), after=[vec]
    )(*w2q)
    w2_oth = other(w2_own)
    ff_grads = sds((4, ndp, padded, ff // 2), BF)

    def mlp_half(name, side, w, after=()):
        return call(
            name,
            functools.partial(mlp_half_kernel, sizes, side),
            [sds((total, ff), BF), sds((total, ff), BF), sds((8, ff), F32), ff_grads],
            mib=32,
            after=after,
        )(n2, cot_in, w, ub)

    hid_own, hgr_own, ub_own, g2_own = mlp_half("mlp_own", 0, w2_own)
    hid_oth, hgr_oth, ub_oth, g2_oth = mlp_half("mlp_oth", 1, w2_oth, [ub_own])
    bo, dmid, dctx, g_out, vgrad = call(
        "mlp_sums",
        one(mlp_sums_kernel),
        [
            sds((total, width), BF), sds((total, width), F32), sds((total, width), BF), sds((width, width), F32),
            sds((EXTRA, width), F32),
        ],
        mib=32,
    )(mid, ctx, wot, vec, cot_in, w2_own, w2_oth, hid_own, hid_oth, hgr_own, hgr_oth)

    def core_sums(name, own, oth, after=()):
        outs = [sds(own.shape[1:], BF)] * nctx
        return call(name, functools.partial(sum_core_kernel, nctx), outs, after=after)(own, other(oth))

    def by_image(v):
        return jnp.transpose(v.reshape(slots, images, width), (1, 0, 2))

    pairs = sds((2, ndp // 2, padded, ff // 2), BF)
    keep_a, send_a, keep_b, send_b = call("sum_core_ff", sum_core_ff_kernel, [pairs] * 4, after=[vgrad])(
        g2_own, other(g2_oth)
    )
    got_a, got_b = lax.ppermute(send_a, "ctx", xor(nctx, 1)), lax.ppermute(send_b, "ctx", xor(nctx, 2))
    ig, g1_own, g1_oth = call(
        "attention_back",
        one(attention_back_kernel),
        [sds((total, width), BF)] + [sds((4, ndp, padded + padded // 2 + EXTRA, TILE), BF)] * 2,
        scratch=[pltpu.VMEM((total, 3 * width), BF)],
        mib=32,
        after=[keep_a],
    )(qkv, dctx, lse, ctx_full, n1, x, dmid, wqkv, vec, g_out, vgrad, ub_own, ub_oth)
    one_quarter = sds(pairs.shape[1:], BF)
    keep_a, send_a, keep_b, send_b = call(
        "sum_ctx_first", sum_ctx_first_kernel, [one_quarter] * 4, after=[g1_own]
    )(keep_a, got_a, keep_b, got_b)
    got_a, got_b = lax.ppermute(send_a, "ctx", xor(nctx, 2)), lax.ppermute(send_b, "ctx", xor(nctx, 1))
    s1_send = core_sums("sum_core_attn", g1_own, g1_oth, after=[keep_a])
    s1 = over("ctx", nctx, s1_send)
    keep, send = call("sum_ctx_second", sum_ctx_second_kernel, [one_quarter] * 2, after=[s1_send[0]])(
        keep_a, got_a, keep_b, got_b
    )
    back = call(
        "returns",
        one(returns_kernel),
        sds((nctx, 2 * main + EXTRA, width), BF),
        after=[keep],
    )(bo, ig)
    returned = lax.all_to_all(back, "ctx", 0, 0)
    u1_send = call(
        "sum_ctx_attn",
        functools.partial(sum_ctx_kernel, nctx, ndp),
        [sds(s1[0].shape[1:], BF)] * ndp,
        after=[back],
    )(*s1)
    u1 = over("dp", ndp, u1_send)
    stride = 2
    while stride < ndp:
        half = sds((keep.shape[0] // 2,) + keep.shape[1:], BF)
        keep, send = call(
            "add_dp_ff", functools.partial(add_halves_kernel, stride), [half, half], after=[u1_send[0]]
        )(keep, lax.ppermute(send, "dp", xor(ndp, stride // 2)))
        stride *= 2
    summed = call(
        "sum_dp", functools.partial(sum_dp_kernel, ndp), sds((padded + -(-s1[0].shape[1] // (3 * EXTRA)) * EXTRA, ff // 2), BF)
    )(keep, lax.ppermute(send, "dp", xor(ndp, ndp // 2)), *u1)
    shares = over("ctx", nctx, [summed] * nctx)
    back = call("hand_on", hand_on_kernel, sds(returned.shape, BF), after=[summed])(returned)
    block_out, input_grad, placed = call(
        "place_slots",
        one(unpack_kernel),
        [sds(tok.shape, F32)] * 2 + [sds((8, TILE), F32)],
        scratch=[pltpu.SMEM(valid_mask.shape, valid_mask.dtype), pltpu.SemaphoreType.DMA((1,))],
        raw=(3,),
        mib=16,
    )(back, other(back), tails, valid_mask)
    gq, gk, gv, gqb, gvb, go, gu, gub, gd, *gvec = call(
        "place_grads",
        one(grads_kernel),
        [
            sds(w_query.shape, F32), sds(w_key.shape, F32), sds(w_value.shape, F32),
            sds(query_bias.shape, F32), sds(value_bias.shape, F32), sds(w_out.shape, F32),
            sds(w_up.shape, F32), sds(up_bias.shape, F32), sds((rows, ff), F32),
        ]
        + [sds((rows,), F32)] * 6,
        scratch=[
            pltpu.VMEM((nctx,) + s1[0].shape[1:], F32),
            pltpu.VMEM((nctx, padded, ff // 2), F32),
        ],
        after=[placed],
    )(*shares)
    return (by_image(block_out), by_image(input_grad), gq, gk, gv, gqb, gvb, go, gu, gub, jnp.transpose(gd), *gvec)


def solution(mesh):
    rows, cols, tp, dp = P("dp", "tp"), P("tp", "dp"), P("tp"), P("dp")
    act = P("dp", "ctx", None)
    return jax.shard_map(
        functools.partial(body, mesh.shape["ctx"], mesh.shape["tp"], mesh.shape["dp"]),
        mesh=mesh,
        in_specs=(act, P("dp", "ctx"), act, rows, rows, rows, tp, tp, cols, rows, tp, cols) + (dp,) * 6,
        out_specs=(act, act, rows, rows, rows, tp, tp, cols, rows, tp, cols) + (dp,) * 6,
        check_vma=False,
    )
```

```python
import functools

import jax
import jax.numpy as jnp
from jax import lax
from jax.experimental import pallas as pl
from jax.experimental.pallas import tpu as pltpu
from jax.sharding import PartitionSpec as P

HD = 64
EPS = 1e-06
SCALE = 0.125
FLOOR = -1e30
BF = jnp.bfloat16
F32 = jnp.float32
TILE = 128
TIMES = {
    "pack_weights": 2.0, "pack_slots": 3.0, "join_quarter": 20.0, "attention": 0.0, "mlp_own": 4.0, "mlp_oth": 4.0, "mlp_sums": 2.0,
    "attention_back": 11.0, "sum_ctx_first": 50.0, "sum_ctx_attn": 0.5, "sum_dp": 5.0, "place_slots": 2.3, "place_grads": 1.0,
}
EXTRA = 16


def call(name, kernel, out_shape, scratch=(), mib=8, after=(), raw=()):
    after = list(after)

    def ordered(*refs):
        kernel(*refs[len(after) :])

    def run(*args):
        specs = [pl.BlockSpec(memory_space=pl.ANY)] * len(after) + [
            pl.BlockSpec(memory_space=pltpu.HBM if i in raw else pltpu.VMEM)
            for i in range(len(args))
        ]
        return pl.pallas_call(
            ordered,
            name=name,
            out_shape=out_shape,
            in_specs=specs,
            out_specs=jax.tree.map(lambda _: pl.BlockSpec(memory_space=pltpu.VMEM), out_shape),
            scratch_shapes=list(scratch),
            compiler_params=pltpu.CompilerParams(vmem_limit_bytes=mib << 20),
            cost_estimate=pl.CostEstimate(
                flops=int(TIMES.get(name, 0.2) * 1.15e9), bytes_accessed=1, transcendentals=0
            ),
        )(*after, *args)

    return run


def sds(shape, dtype):
    return jax.ShapeDtypeStruct(shape, dtype)


def nn(a, b):
    return lax.dot_general(a, b, (((1,), (0,)), ((), ())), preferred_element_type=F32)


def nt(a, b):
    return lax.dot_general(a, b, (((1,), (1,)), ((), ())), preferred_element_type=F32)


def tn(a, b):
    return lax.dot_general(a, b, (((0,), (0,)), ((), ())), preferred_element_type=F32)


def swap(v):
    return pltpu.roll(v, HD, axis=1)


def low_lanes(shape):
    return lax.broadcasted_iota(jnp.int32, shape, 1) < HD


def row_is(shape, row):
    return lax.broadcasted_iota(jnp.int32, shape, 0) == row


def tile(v, i):
    return v[:, i * TILE : (i + 1) * TILE]


def assemble(own, oth):
    low = low_lanes((own.shape[0], TILE))
    own_qk, own_vo, oth_qk, oth_vo = tile(own, 4), tile(own, 5), tile(oth, 4), tile(oth, 5)
    qkv = [
        tile(own, 0), tile(oth, 0), jnp.where(low, own_qk, swap(oth_qk)),
        tile(own, 1), tile(oth, 1), jnp.where(low, swap(own_qk), oth_qk),
        tile(own, 2), tile(oth, 2), jnp.where(low, own_vo, swap(oth_vo)),
    ]
    out = [tile(own, 3), tile(oth, 3), jnp.where(low, swap(own_vo), oth_vo)]
    return qkv, out


def disassemble(qkv, out):
    low = low_lanes(qkv[0].shape)
    own = [qkv[0], qkv[3], qkv[6], out[0], jnp.where(low, qkv[2], swap(qkv[5])), jnp.where(low, qkv[8], swap(out[2]))]
    oth = [qkv[1], qkv[4], qkv[7], out[1], jnp.where(low, swap(qkv[2]), qkv[5]), jnp.where(low, swap(qkv[8]), out[2])]
    return own, oth


def norm_stats(v):
    mean = jnp.mean(v, axis=-1, keepdims=True)
    centered = v - mean
    r = lax.rsqrt(jnp.mean(centered * centered, axis=-1, keepdims=True) + EPS)
    return centered * r, r


def norm_back(e, xhat, r):
    return r * (
        e
        - jnp.mean(e, axis=-1, keepdims=True)
        - xhat * jnp.mean(e * xhat, axis=-1, keepdims=True)
    )


def gelu_pair(v):
    phi = 0.5 + 0.5 * lax.erf(v * 0.7071067811865476)
    return v * phi, phi + (0.3989422804014327 * v) * jnp.exp(-0.5 * v * v)


BLOCK = 16


def one_hot(shape, hit):
    r, c = (lax.broadcasted_iota(jnp.int32, shape, i) for i in range(2))
    return hit(r, c).astype(F32).astype(BF)


def picker(wanted, images):
    def hit(r, c):
        img = wanted[-1]
        for k in range(len(wanted) - 1):
            img = jnp.where(r // BLOCK == k, wanted[k], img)
        return c == (r % BLOCK) * images + img

    return one_hot((len(wanted) * BLOCK, images * BLOCK), hit)


def take_images(ref, outs, at, pick, images, count):
    for b in range(count // BLOCK):
        got = nn(pick, ref[b * BLOCK * images : (b + 1) * BLOCK * images, :].astype(BF)).astype(BF)
        for k in range(len(outs)):
            outs[k][at + b * BLOCK : at + (b + 1) * BLOCK, :] = got[k * BLOCK : (k + 1) * BLOCK]


def fetch(sources, held, sem):
    copies = [pltpu.make_async_copy(sources[i], held[i], sem.at[i]) for i in range(len(sources))]
    for c in copies:
        c.start()
    return copies


def pack_weights_kernel(sizes, count, *refs):
    nctx, ntp, ndp, main, width, rows, padded = sizes
    sources, (p1, p2q), refs = refs[:count], refs[count : count + 2], refs[count + 2 :]
    held, sem = refs[:count], refs[count]
    copies = fetch(sources, held, sem)
    wq, wk, wv, wo, wu, wd, qb, vb, ub = held[:9]
    vecs = held[9:]
    me_c, me_d = lax.axis_index("ctx"), lax.axis_index("dp")
    for c in copies:
        c.wait()
    if padded > rows:
        p1[0:padded, :] = jnp.zeros((padded, p1.shape[1]), BF)
        p2q[...] = jnp.zeros(p2q.shape, BF)
    quarter = p2q.shape[1]
    for j in range(nctx):
        src = (wu, wd)[j // 2][:, (j % 2) * quarter : (j % 2 + 1) * quarter]

        @pl.when(me_c == j)
        def _(src=src):
            p2q[0:rows, :] = src

    def put(lo, value):
        p1[0:rows, lo : lo + value.shape[1]] = value.astype(BF)

    fq, fk, fv = wq[...].astype(F32), wk[...].astype(F32), wv[...].astype(F32)
    fo = jnp.transpose(wo[...].astype(F32))
    for i, w in enumerate((fq, fk, fv, fo)):
        put(i * TILE, tile(w, 0))
    put(4 * TILE, jnp.concatenate([fq[:, TILE:], fk[:, TILE:]], axis=1))
    put(5 * TILE, jnp.concatenate([fv[:, TILE:], fo[:, TILE:]], axis=1))
    cols = p1.shape[1]
    fqb, fvb = qb[...].astype(F32)[None, :], vb[...].astype(F32)[None, :]
    none = jnp.zeros((1, TILE), F32)
    short = jnp.zeros((1, HD), F32)
    bias = jnp.concatenate(
        [fqb[:, :TILE], none, fvb[:, :TILE], none, fqb[:, TILE:], short, fvb[:, TILE:], short], axis=1
    )
    spread = one_hot((rows, width), lambda r, c: c == r + rows * me_d)
    block = jnp.where(row_is((EXTRA, cols), 0), bias, 0.0)
    block = jnp.where(row_is((EXTRA, cols), 7), ub[...].astype(F32)[None, :], block)
    lanes = jnp.zeros((EXTRA, rows), F32)
    for i in range(6):
        lanes = jnp.where(row_is((EXTRA, rows), 1 + i), vecs[i][...].astype(F32)[None, :], lanes)
    lanes = nn(lanes.astype(BF), spread)
    p1[padded : padded + EXTRA, :] = block.astype(BF)
    mixed = jnp.where(
        (lax.broadcasted_iota(jnp.int32, (EXTRA, width), 0) - 1).astype(jnp.uint32) < 6,
        lanes,
        block[:, :width],
    )
    p1[padded : padded + EXTRA, 0:width] = mixed.astype(BF)


def pack_slots_kernel(sizes, tok, cot, source, *refs):
    nctx, ntp, ndp, main, width, rows, padded = sizes
    sent, tails, mask, sem = refs[:nctx], refs[nctx], refs[nctx + 1], refs[nctx + 2]
    get_mask = pltpu.make_async_copy(source, mask, sem.at[0])
    get_mask.start()
    images = nctx * ntp
    me_c, me_t = lax.axis_index("ctx"), lax.axis_index("tp")
    wanted = [(me_c ^ k) * ntp + me_t for k in range(nctx)]
    pick = picker(wanted, images)
    for i, ref in enumerate((tok, cot)):
        take_images(ref, sent, i * (main + EXTRA), pick, images, main)
        tails[i] = ref[main * images :, :]
    get_mask.wait()
    for k in range(nctx):
        gate = mask[wanted[k], main].astype(F32)
        te = tok[pl.ds(main * images + wanted[k], 1), :] * gate
        ce = cot[pl.ds(main * images + wanted[k], 1), :] * gate
        shape = (EXTRA, width)
        sent[k][main : main + EXTRA, :] = jnp.where(
            row_is(shape, 0), te, jnp.where(row_is(shape, 1), ce, 0.0)
        ).astype(BF)


def join_kernel(axis, stride, own, got, out):
    bit = lax.rem(lax.div(lax.axis_index(axis), stride), 2)
    for i in range(own.shape[0]):
        out[2 * i + bit] = own[i]
        out[2 * i + 1 - bit] = got[i]


def place_rows(stage, own, got, rows):
    bit = lax.rem(lax.axis_index("dp"), 2)
    for i in range(own.shape[0]):
        for piece, last in ((own, bit), (got, 1 - bit)):
            at = pl.ds(pl.multiple_of((2 * i + last) * rows, 16 if rows % 16 == 0 else 8), rows)
            stage[at, :] = piece[i].astype(stage.dtype)[:rows]


def merge_quarter_kernel(sizes, attn, own, got, out, attn_out, stage):
    place_rows(stage, own, got, sizes[5])
    out[...] = stage[...].astype(BF)
    attn_out[...] = attn[...]


def split_kernel(got, *outs):
    for i, out in enumerate(outs):
        cols = out.shape[2]
        out[...] = got[:, :, i * cols : (i + 1) * cols]


def merge_ff_kernel(nctx, *refs):
    out = refs[nctx]
    me_c = lax.axis_index("ctx")
    for k in range(nctx):
        quarter = refs[k].shape[1]
        out[:, pl.ds(pl.multiple_of((me_c ^ k) * quarter, quarter), quarter)] = refs[k][...]


def attention_kernel(sizes, *refs):
    nctx, ntp, ndp, main, width, rows, padded = sizes
    t_in, (own, got, own_oth, got_oth_a, got_oth_b), refs = refs[:nctx], refs[nctx : nctx + 5], refs[nctx + 5 :]
    x_out, mid_out, n1_out, n2_out, qkv, ctx, ctx_full, lse, wqkv, wot, vec, ub, cot, stage, stage_oth = refs
    body = nctx * main
    total = body + EXTRA
    half = got_oth_a.shape[2]
    place_rows(stage, own, got, rows)
    place_rows(stage_oth.at[:, :half], own_oth.at[:, :, :half], got_oth_a, rows)
    place_rows(stage_oth.at[:, half:], own_oth.at[:, :, half:], got_oth_b, rows)
    tiles, outs = assemble(stage[...].astype(F32), stage_oth[...].astype(F32))
    for i, v in enumerate(tiles):
        wqkv[:, i * TILE : (i + 1) * TILE] = v.astype(BF)
    for i, v in enumerate(outs):
        wot[:, i * TILE : (i + 1) * TILE] = v.astype(BF)
    extra = own[0, padded:, :].astype(F32)
    extra_oth = own_oth[0, padded:, :].astype(F32)
    tiles, _ = assemble(extra, extra_oth)
    bias = jnp.concatenate([v[0:1] for v in tiles], axis=1)
    vec_sum = jnp.zeros((EXTRA, width), F32)
    for i in range(own.shape[0]):
        vec_sum += own[i, padded:, :width].astype(F32) + got[i, padded:, :width].astype(F32)
    vec[...] = vec_sum
    ub[...] = jnp.broadcast_to(jnp.concatenate([extra[7:8], extra_oth[7:8]], axis=1), ub.shape)
    extra = jnp.zeros((EXTRA, width), F32)
    for k in range(nctx):
        x_out[k * main : (k + 1) * main, :] = t_in[k][0:main, :].astype(F32)
        cot[k * main : (k + 1) * main, :] = t_in[k][main + EXTRA :, :]
        extra += t_in[k][main : main + EXTRA, :].astype(F32)
    x_out[body:, :] = jnp.where(row_is((EXTRA, width), 0), extra, 0.0)
    cot[body:, :] = jnp.where(row_is((EXTRA, width), 0), extra[1:2, :], 0.0).astype(BF)
    x = x_out[...]
    xhat, _ = norm_stats(x)
    n1 = (xhat * vec_sum[1:2, :] + vec_sum[2:3, :]).astype(BF)
    n1_out[...] = n1
    proj = nn(n1, wqkv[...]) + bias
    qkv[0:total, 0:width] = (proj[:, 0:width].astype(BF).astype(F32) * SCALE).astype(BF)
    qkv[0:total, width:] = proj[:, width:].astype(BF)
    keys = qkv.shape[0]
    qkv[total:, :] = jnp.zeros((keys - total, qkv.shape[1]), BF)
    off = jnp.where(lax.broadcasted_iota(jnp.int32, (1, keys), 1) > body, FLOOR, 0.0)
    low = low_lanes((total, TILE))
    lane = lax.broadcasted_iota(jnp.int32, (total, TILE), 1)
    all_lse = jnp.zeros((total, TILE), F32)
    for p in range(3):
        qp = qkv[0:total, p * TILE : (p + 1) * TILE]
        kp = qkv[:, width + p * TILE : width + (p + 1) * TILE]
        vp = qkv[:, 2 * width + p * TILE : 2 * width + (p + 1) * TILE]
        parts = []
        for a in range(2):
            qa = jnp.where(low if a == 0 else ~low, qp, jnp.zeros_like(qp))
            s = nt(qa, kp) + off
            m = jnp.max(s, axis=-1, keepdims=True)
            e = jnp.exp(s - m)
            l = jnp.sum(e, axis=-1, keepdims=True)
            parts.append(nn(e.astype(BF), vp) * (1.0 / l))
            all_lse = jnp.where(lane == 2 * p + a, m + jnp.log(l), all_lse)
        ctx_full[:, p * TILE : (p + 1) * TILE] = jnp.where(low, parts[0], parts[1])
    ctx[...] = ctx_full[...].astype(BF)
    lse[...] = all_lse
    attended = nt(ctx[...], wot[...]) + vec_sum[5:6, :]
    valid = lax.broadcasted_iota(jnp.int32, (total, 1), 0) <= body
    middle = x_out[...] + jnp.where(valid, attended, 0.0)
    mid_out[...] = middle
    xhat2, _ = norm_stats(middle)
    n2_out[...] = (xhat2 * vec_sum[3:4, :] + vec_sum[4:5, :]).astype(BF)


def mlp_half_kernel(sizes, side, n2, cot, w, ub, hid, hgr, ubgrad, grads):
    nctx, ntp, ndp, main, width, rows, padded = sizes
    half = w.shape[1] // 2
    n2v, dcot = n2[...], cot[...]
    act, slope = gelu_pair(nn(n2v, w[:, :half]) + ub[0:1, side * half : (side + 1) * half])
    h = act.astype(BF)
    hg = (nn(dcot, w[:, half:]) * slope).astype(BF)
    hid[...] = h
    hgr[...] = hg
    ubgrad[...] = jnp.broadcast_to(jnp.sum(hg.astype(F32), axis=0, keepdims=True), ubgrad.shape)
    cols = grads.shape[3]
    for part, g in ((0, tn(n2v, hg).astype(BF)), (1, tn(dcot, h).astype(BF))):
        for d in range(ndp):
            for c in range(half // cols):
                grads[2 * part + c, d, 0:rows, :] = g[d * rows : (d + 1) * rows, c * cols : (c + 1) * cols]


def mlp_sums_kernel(sizes, mid, ctx, wot, vec, cot, w_own, w_oth, hgr_own, hgr_oth, dmid, dctx, g_out, vgrad):
    nctx, ntp, ndp, main, width, rows, padded = sizes
    body = nctx * main
    total = body + EXTRA
    half = w_own.shape[1] // 2
    dcot = cot[...]
    middle = mid[...]
    valid = lax.broadcasted_iota(jnp.int32, (total, 1), 0) <= body
    n2g = nt(hgr_own[...], w_own[:, :half]) + nt(hgr_oth[...], w_oth[:, :half])
    xhat, r = norm_stats(middle)
    back = norm_back(n2g * vec[3:4, :], xhat, r)
    middle_grad = dcot.astype(F32) + back
    dmid[...] = middle_grad
    agrad = jnp.where(valid, middle_grad, 0.0).astype(BF)
    dctx[...] = nn(agrad, wot[...]).astype(BF)
    g_out[...] = tn(agrad, ctx[...])
    shape = vgrad.shape
    v = jnp.where(row_is(shape, 2), jnp.sum(n2g * xhat, axis=0, keepdims=True), 0.0)
    v = jnp.where(row_is(shape, 3), jnp.sum(n2g, axis=0, keepdims=True), v)
    v = jnp.where(row_is(shape, 4), jnp.sum(agrad.astype(F32), axis=0, keepdims=True), v)
    v = jnp.where(row_is(shape, 5), jnp.sum(dcot.astype(F32), axis=0, keepdims=True), v)
    vgrad[...] = v


def block_out_kernel(sizes, mid, vec, w_own, w_oth, hid_own, hid_oth, bo):
    nctx, ntp, ndp, main, width, rows, padded = sizes
    body = nctx * main
    half = w_own.shape[1] // 2
    valid = lax.broadcasted_iota(jnp.int32, (body + EXTRA, 1), 0) <= body
    mlp_out = nt(hid_own[...], w_own[:, half:]) + nt(hid_oth[...], w_oth[:, half:]) + vec[6:7, :]
    bo[...] = (mid[...] + jnp.where(valid, mlp_out, 0.0)).astype(BF)


def pair_back(p, width, total, body, qkv, dctx, lse, ctx):
    keys = qkv.shape[0]
    off = jnp.where(lax.broadcasted_iota(jnp.int32, (1, keys), 1) > body, FLOOR, 0.0)
    low = low_lanes((total, TILE))
    at = slice(p * TILE, (p + 1) * TILE)
    qp = qkv[0:total, at]
    kp = qkv[:, width + p * TILE : width + (p + 1) * TILE]
    vp = qkv[:, 2 * width + p * TILE : 2 * width + (p + 1) * TILE]
    dp = dctx[:, at]
    both = dp.astype(F32) * ctx[:, at]
    qt = jnp.transpose(qp.astype(F32)).astype(BF)
    dt = jnp.transpose(dp.astype(F32)).astype(BF)
    dk, dv = [], []
    zero = jnp.zeros_like(qp)
    qs = jnp.concatenate([jnp.where(low, qp, zero), jnp.where(low, zero, qp)], axis=0)
    ds_ = jnp.concatenate([jnp.where(low, dp, zero), jnp.where(low, zero, dp)], axis=0)
    bs = jnp.concatenate([jnp.where(low, both, 0.0), jnp.where(low, 0.0, both)], axis=0)
    inner = jnp.sum(bs, axis=-1, keepdims=True)
    ls = jnp.concatenate([lse[:, 2 * p : 2 * p + 1], lse[:, 2 * p + 1 : 2 * p + 2]], axis=0)
    prob = jnp.exp(nt(qs, kp) + off - ls)
    ds = (prob * (nt(ds_, vp) - inner)).astype(BF)
    w = prob.astype(BF)
    dq = nn(ds, kp)
    dq = jnp.where(low, dq[0:total], dq[total:]) * SCALE
    for a in range(2):
        dk.append(nn(qt[a * HD : (a + 1) * HD], ds[a * total : (a + 1) * total]))
        dv.append(nn(dt[a * HD : (a + 1) * HD], w[a * total : (a + 1) * total]))
    dk, dv = (jnp.transpose(jnp.concatenate(v, axis=0))[0:total] for v in (dk, dv))
    return dq.astype(BF), dk.astype(BF), dv.astype(BF)


def attention_back_kernel(sizes, *refs):
    nctx, ntp, ndp, main, width, rows, padded = sizes
    qkv, dctx, lse, ctx, n1, x_in, dmid, wqkv, vec, g_out, vgrad, ub_own, ub_oth = refs[:13]
    ig, g_own, g_oth, dqkv = refs[13:]
    body = nctx * main
    total = body + EXTRA
    for p in range(3):
        for i, v in enumerate(pair_back(p, width, total, body, qkv, dctx, lse, ctx)):
            dqkv[:, i * width + p * TILE : i * width + (p + 1) * TILE] = v
    d = dqkv[...]
    bias = jnp.sum(d.astype(F32), axis=0, keepdims=True)
    g = tn(n1[...], d)
    go = g_out[...]
    own, oth = disassemble([tile(g, i) for i in range(9)], [tile(go, i) for i in range(3)])
    half = padded // 2
    for to, tiles in ((g_own, own), (g_oth, oth)):
        for j in range(4):
            lo = j % 2 * half
            for e in range(ndp):
                to[j, e, 0:rows, :] = tiles[j][e * rows : (e + 1) * rows].astype(BF)
                shared = tiles[4 + j // 2][e * rows + lo : e * rows + min(rows, lo + half)]
                to[j, e, padded : padded + shared.shape[0], :] = shared.astype(BF)
    dn1 = nt(d, wqkv[...])
    xhat, r = norm_stats(x_in[...])
    grad = dmid[...] + norm_back(dn1 * vec[1:2, :], xhat, r)
    ig[...] = grad.astype(BF)
    gains = jnp.sum(dn1 * xhat, axis=0, keepdims=True)
    shifts = jnp.sum(dn1, axis=0, keepdims=True)
    vecs = [gains, shifts] + [vgrad[i : i + 1, :] for i in range(2, 6)]
    zero = [jnp.zeros((1, TILE), F32)] * 3
    bias_own, bias_oth = disassemble([tile(bias, i) for i in range(9)], zero)
    for to, tiles, ub in ((g_own, bias_own, ub_own), (g_oth, bias_oth, ub_oth)):
        rows_ = [tile(v, i) for v in vecs for i in range(3)] + tiles
        rows_ += [ub[0:1, i * TILE : (i + 1) * TILE] for i in range(6)]
        for j in range(4):
            block = jnp.zeros((EXTRA, TILE), F32)
            for i, v in enumerate(rows_[8 * j : 8 * (j + 1)]):
                block = jnp.where(row_is(block.shape, i), v, block)
            for e in range(ndp):
                to[j, e, padded + half :, :] = block.astype(BF)


def sum_core_kernel(n, own, oth, *outs):
    me = lax.axis_index("ctx")
    for k in range(n):
        outs[k][...] = (own[me ^ k].astype(F32) + oth[me ^ k].astype(F32)).astype(BF)


def sum_ctx_kernel(n, ndp, *refs):
    me = lax.axis_index("dp")
    for k in range(ndp):
        v = refs[0][me ^ k].astype(F32)
        for i in range(1, n):
            v = v + refs[i][me ^ k].astype(F32)
        refs[n + k][...] = v.astype(BF)


def halve(stride, item, keep, send):
    bit = lax.rem(lax.div(lax.axis_index("dp"), stride), 2)
    for j in range(keep.shape[0]):
        keep[j] = item(2 * j + bit).astype(BF)
        send[j] = item(2 * j + 1 - bit).astype(BF)


def ctx_bits():
    me = lax.axis_index("ctx")
    return lax.rem(me, 2), lax.div(me, 2)


def sum_core_ff_kernel(own, oth, keep_a, send_a, keep_b, send_b):
    low, high = ctx_bits()
    half = own.shape[1] // 2

    def put(to, i, quarter, blocks):
        to[i] = (own[quarter, blocks].astype(F32) + oth[quarter, blocks].astype(F32)).astype(BF)

    for i in range(2):
        first, second = slice(0, half), slice(half, 2 * half)
        put(keep_a, i, 2 * i + low, first)
        put(send_a, i, 2 * i + 1 - low, first)
        put(keep_b, i, 2 * high + i, second)
        put(send_b, i, 2 * (1 - high) + i, second)


def sum_ctx_first_kernel(own_a, got_a, own_b, got_b, keep_a, send_a, keep_b, send_b):
    low, high = ctx_bits()
    for own, got, keep, send, bit in (
        (own_a, got_a, keep_a, send_a, high),
        (own_b, got_b, keep_b, send_b, low),
    ):
        keep[...] = (own[bit].astype(F32) + got[bit].astype(F32)).astype(BF)
        send[...] = (own[1 - bit].astype(F32) + got[1 - bit].astype(F32)).astype(BF)


def sum_ctx_second_kernel(own_a, got_a, own_b, got_b, keep, send):
    bit = lax.rem(lax.axis_index("dp"), 2)
    half = own_a.shape[0]
    for j in range(keep.shape[0]):
        own, got, at = (own_a, got_a, 2 * j) if 2 * j < half else (own_b, got_b, 2 * j - half)
        for to, i in ((keep, at + bit), (send, at + 1 - bit)):
            to[j] = (own[i].astype(F32) + got[i].astype(F32)).astype(BF)


def add_halves_kernel(stride, own, got, keep, send):
    halve(stride, lambda i: own[i].astype(F32) + got[i].astype(F32), keep, send)


def sum_dp_kernel(n, own, got, *refs):
    out = refs[n]
    rows = own.shape[1]
    out[:rows, :] = (own[0].astype(F32) + got[0, 0:rows, :].astype(F32)).astype(BF)
    v = refs[0][...].astype(F32)
    for r in refs[1:n]:
        v = v + r[...].astype(F32)
    span = out.shape[0] - rows
    out[rows:, :] = jnp.zeros((span, out.shape[1]), BF)
    for i in range(out.shape[1] // TILE):
        part = v[i * span : (i + 1) * span].astype(BF)
        if part.shape[0]:
            out[rows : rows + part.shape[0], i * TILE : (i + 1) * TILE] = part


def returns_kernel(sizes, bo, ig, out):
    nctx, ntp, ndp, main, width, rows, padded = sizes
    me = lax.axis_index("ctx")
    body = nctx * main
    shape = (EXTRA, width)
    extra = jnp.where(
        row_is(shape, 0),
        bo[body:, :].astype(F32),
        jnp.where(row_is(shape, 1), ig[body:, :].astype(F32)[0:1, :], 0.0),
    ).astype(BF)
    for k in range(nctx):
        at = slice(k * main, (k + 1) * main)
        out[me ^ k, 0:main, :] = bo[at, :]
        out[me ^ k, main : main + EXTRA, :] = extra
        out[me ^ k, main + EXTRA :, :] = ig[at, :]


def hand_on_kernel(held, out):
    out[...] = held[...]


def grads_kernel(sizes, *refs):
    nctx, ntp, ndp, main, width, rows, padded = sizes
    parts, refs = refs[:nctx], refs[nctx:]
    gq, gk, gv, gqb, gvb, go, gu, gub, gd = refs[:9]
    gvec, f, f2 = refs[9:15], refs[15], refs[16]
    me, me_d = lax.axis_index("ctx"), lax.axis_index("dp")
    span = parts[0].shape[0] - padded
    for k in range(nctx):
        f2[me ^ k] = parts[k][0:padded, :].astype(F32)
        for i in range(f2.shape[2] // TILE):
            n = min(span, f.shape[1] - i * span)
            if n > 0:
                f[me ^ k, i * span : i * span + n, :] = parts[k][
                    padded : padded + n, i * TILE : (i + 1) * TILE
                ].astype(F32)
    half = f2.shape[2]
    for j in range(2):
        gu[:, j * half : (j + 1) * half] = f2[j, 0:rows, :]
        gd[:, j * half : (j + 1) * half] = f2[2 + j, 0:rows, :]
    q01, k01, v01, o01 = (f[j, 0:rows, :] for j in range(4))
    low, high = slice(padded, padded + padded // 2), slice(padded, padded + rows - padded // 2)
    qk2 = jnp.concatenate([f[0, low, :], f[1, high, :]], axis=0)
    vo2 = jnp.concatenate([f[2, low, :], f[3, high, :]], axis=0)
    gq[:, 0:TILE] = q01
    gq[:, TILE:] = qk2[:, 0:HD]
    gk[:, 0:TILE] = k01
    gk[:, TILE:] = swap(qk2)[:, 0:HD]
    gv[:, 0:TILE] = v01
    gv[:, TILE:] = vo2[:, 0:HD]
    go[0:TILE, :] = jnp.transpose(o01)
    go[TILE:, :] = jnp.transpose(vo2)[HD:, :]

    def line(i):
        at = padded + padded // 2 + i % 8
        return f[i // 8, at : at + 1, :]

    for i in range(6):
        v = jnp.concatenate([line(3 * i), line(3 * i + 1), line(3 * i + 2)], axis=1)
        v = jnp.broadcast_to(v, (8, width))
        v = pltpu.roll(v, lax.rem(width - me_d * rows, width), axis=1)
        gvec[i][...] = v[0, 0:rows]
    b = [line(18 + i) for i in range(6)]
    gqb[...] = jnp.concatenate([b[0], b[4][:, 0:HD]], axis=1)[0]
    gvb[...] = jnp.concatenate([b[2], b[5][:, 0:HD]], axis=1)[0]
    gub[...] = jnp.concatenate([line(24 + i) for i in range(6)], axis=1)[0]


def unpack_kernel(sizes, own, oth, tails, mask, *refs):
    nctx, ntp, ndp, main, width, rows, padded = sizes
    outs, done, valid, sem = refs[:2], refs[2], refs[3], refs[4]
    images = nctx * ntp
    me_t = lax.axis_index("tp")
    where = [j * ntp + t for t in (me_t, 1 - me_t) for j in range(nctx)]
    sources = [v.at[j] for v in (own, oth) for j in range(nctx)]
    get_valid = pltpu.make_async_copy(mask, valid, sem.at[0])
    get_valid.start()

    def hit(r, c):
        img = where[-1]
        for j in range(images - 1):
            img = jnp.where(c // BLOCK == j, where[j], img)
        return r == (c % BLOCK) * images + img

    put = one_hot((images * BLOCK, images * BLOCK), hit)
    for i in range(2):
        for b in range(main // BLOCK):
            lo = i * (main + EXTRA) + b * BLOCK
            got = jnp.concatenate([src[lo : lo + BLOCK, :] for src in sources], axis=0)
            outs[i][b * BLOCK * images : (b + 1) * BLOCK * images, :] = nn(put, got)
    get_valid.wait()
    for i in range(2):
        for src, img in zip(sources, where):
            got = src[main : main + EXTRA, :].astype(F32)[i : i + 1, :]
            outs[i][pl.ds(main * images + img, 1), :] = jnp.where(
                valid[img, main] > 0, got, tails[i, pl.ds(img, 1), :]
            )
    done[...] = jnp.zeros_like(done)


def xor(n, k):
    return [(i, i ^ k) for i in range(n)]


def over(axis, n, items):
    return [items[0]] + [lax.ppermute(items[k], axis, xor(n, k)) for k in range(1, n)]


def body(nctx, ntp, ndp, *args):
    (tokens, valid_mask, cotangent, w_query, w_key, w_value, query_bias, value_bias, w_out, w_up, up_bias, w_down) = args[:12]
    vecs = args[12:]
    images, slots, width = tokens.shape
    main = slots - 1
    rows = w_query.shape[0]
    padded = -(-rows // EXTRA) * EXTRA
    ff = w_up.shape[1]
    p1_cols = 4 * w_query.shape[1]
    sizes = (nctx, ntp, ndp, main, width, rows, padded)
    total = nctx * main + EXTRA
    keys = -(-total // TILE) * TILE
    stage = BF if rows % 16 == 0 else F32
    flip = xor(ntp, 1)
    tok = jnp.transpose(tokens, (1, 0, 2)).reshape(slots * images, width)
    cot = jnp.transpose(cotangent, (1, 0, 2)).reshape(slots * images, width)

    def one(f):
        return functools.partial(f, sizes)

    def other(v):
        return lax.ppermute(v, "tp", flip)

    def held(arrays):
        return [
            (pltpu.SMEM if v.dtype == jnp.int32 else pltpu.VMEM)(v.shape, v.dtype) for v in arrays
        ] + [pltpu.SemaphoreType.DMA((len(arrays),))]

    def gather_dp(name, piece, after):
        v = piece[None]
        stride = ndp // 2
        while stride > 1:
            v = call(
                name,
                functools.partial(join_kernel, "dp", stride),
                sds((2 * v.shape[0],) + v.shape[1:], v.dtype),
                after=after,
            )(v, lax.ppermute(v, "dp", xor(ndp, stride)))
            stride //= 2
        return v, lax.ppermute(v, "dp", xor(ndp, 1))

    sources = [w_query, w_key, w_value, w_out, w_up, jnp.transpose(w_down), query_bias, value_bias, up_bias, *vecs]
    p1, p2q = call(
        "pack_weights",
        functools.partial(pack_weights_kernel, sizes, len(sources)),
        [sds((padded + EXTRA, p1_cols), BF), sds((padded, ff // 2), BF)],
        scratch=held(sources),
        mib=56,
        raw=range(len(sources)),
    )(*sources)
    *sent, tails = call(
        "pack_slots",
        one(pack_slots_kernel),
        [sds((2 * main + EXTRA, width), BF)] * nctx + [sds((2, images, width), F32)],
        scratch=[pltpu.SMEM(valid_mask.shape, valid_mask.dtype), pltpu.SemaphoreType.DMA((1,))],
        mib=48,
        raw=(2,),
    )(tok, cot, valid_mask)
    t_in = over("ctx", nctx, sent)
    w2q = gather_dp("join_quarter", p2q, [])
    w1, w1_got = gather_dp("join_attn", p1, [])
    w2q, w1_early = call(
        "merge_quarter",
        one(merge_quarter_kernel),
        [sds((width, ff // 2), BF), sds(w1.shape, BF)],
        scratch=[pltpu.VMEM((width, ff // 2), stage)],
        after=t_in[1:],
    )(w1, *w2q)
    w1_oth = other(w1_early)
    w2q = over("ctx", nctx, [w2q] * nctx)
    late = call(
        "split_attn",
        split_kernel,
        [sds(w1.shape[:2] + (p1_cols // 2,), BF)] * 2,
        after=[w1_oth, w2q[0]],
    )(w1_got)
    w1 = [w1, w1_got, w1_oth, *[other(v) for v in late]]
    x, mid, n1, n2, qkv, ctx, ctx_full, lse, wqkv, wot, vec, ub, cot_in = call(
        "attention",
        one(attention_kernel),
        [
            sds((total, width), F32), sds((total, width), F32), sds((total, width), BF), sds((total, width), BF),
            sds((keys, 3 * width), BF), sds((total, width), BF), sds((total, width), F32), sds((total, TILE), F32),
            sds((width, 3 * width), BF), sds((width, width), BF), sds((EXTRA, width), F32), sds((8, 2 * ff), F32),
            sds((total, width), BF),
        ],
        scratch=[pltpu.VMEM((width, p1_cols), stage)] * 2,
        mib=32,
    )(*t_in, *w1)
    w2_own = call(
        "merge_ff", functools.partial(merge_ff_kernel, nctx), sds((width, 2 * ff), BF), after=[vec]
    )(*w2q)
    w2_oth = other(w2_own)
    ff_grads = sds((4, ndp, padded, ff // 2), BF)

    def mlp_half(name, side, w, after=()):
        return call(
            name,
            functools.partial(mlp_half_kernel, sizes, side),
            [sds((total, ff), BF), sds((total, ff), BF), sds((8, ff), F32), ff_grads],
            mib=32,
            after=after,
        )(n2, cot_in, w, ub)

    hid_own, hgr_own, ub_own, g2_own = mlp_half("mlp_own", 0, w2_own)
    hid_oth, hgr_oth, ub_oth, g2_oth = mlp_half("mlp_oth", 1, w2_oth, [ub_own])
    dmid, dctx, g_out, vgrad = call(
        "mlp_sums",
        one(mlp_sums_kernel),
        [
            sds((total, width), F32), sds((total, width), BF), sds((width, width), F32), sds((EXTRA, width), F32),
        ],
        mib=32,
    )(mid, ctx, wot, vec, cot_in, w2_own, w2_oth, hgr_own, hgr_oth)

    def core_sums(name, own, oth, after=()):
        outs = [sds(own.shape[1:], BF)] * nctx
        return call(name, functools.partial(sum_core_kernel, nctx), outs, after=after)(own, other(oth))

    def by_image(v):
        return jnp.transpose(v.reshape(slots, images, width), (1, 0, 2))

    pairs = sds((2, ndp // 2, padded, ff // 2), BF)
    keep_a, send_a, keep_b, send_b = call("sum_core_ff", sum_core_ff_kernel, [pairs] * 4, after=[vgrad])(
        g2_own, other(g2_oth)
    )
    got_a, got_b = lax.ppermute(send_a, "ctx", xor(nctx, 1)), lax.ppermute(send_b, "ctx", xor(nctx, 2))
    ig, g1_own, g1_oth = call(
        "attention_back",
        one(attention_back_kernel),
        [sds((total, width), BF)] + [sds((4, ndp, padded + padded // 2 + EXTRA, TILE), BF)] * 2,
        scratch=[pltpu.VMEM((total, 3 * width), BF)],
        mib=32,
        after=[keep_a],
    )(qkv, dctx, lse, ctx_full, n1, x, dmid, wqkv, vec, g_out, vgrad, ub_own, ub_oth)
    one_quarter = sds(pairs.shape[1:], BF)
    keep_a, send_a, keep_b, send_b = call(
        "sum_ctx_first", sum_ctx_first_kernel, [one_quarter] * 4, after=[g1_own]
    )(keep_a, got_a, keep_b, got_b)
    got_a, got_b = lax.ppermute(send_a, "ctx", xor(nctx, 2)), lax.ppermute(send_b, "ctx", xor(nctx, 1))
    s1_send = core_sums("sum_core_attn", g1_own, g1_oth, after=[keep_a])
    s1 = over("ctx", nctx, s1_send)
    bo = call("block_out", one(block_out_kernel), sds((total, width), BF), mib=16, after=[s1_send[0]])(
        mid, vec, w2_own, w2_oth, hid_own, hid_oth
    )
    keep, send = call("sum_ctx_second", sum_ctx_second_kernel, [one_quarter] * 2, after=[bo])(
        keep_a, got_a, keep_b, got_b
    )
    back = call(
        "returns",
        one(returns_kernel),
        sds((nctx, 2 * main + EXTRA, width), BF),
        after=[keep],
    )(bo, ig)
    returned = lax.all_to_all(back, "ctx", 0, 0)
    u1_send = call(
        "sum_ctx_attn",
        functools.partial(sum_ctx_kernel, nctx, ndp),
        [sds(s1[0].shape[1:], BF)] * ndp,
        after=[back],
    )(*s1)
    u1 = over("dp", ndp, u1_send)
    stride = 2
    while stride < ndp:
        half = sds((keep.shape[0] // 2,) + keep.shape[1:], BF)
        keep, send = call(
            "add_dp_ff", functools.partial(add_halves_kernel, stride), [half, half], after=[u1_send[0]]
        )(keep, lax.ppermute(send, "dp", xor(ndp, stride // 2)))
        stride *= 2
    summed = call(
        "sum_dp", functools.partial(sum_dp_kernel, ndp), sds((padded + -(-s1[0].shape[1] // (3 * EXTRA)) * EXTRA, ff // 2), BF)
    )(keep, lax.ppermute(send, "dp", xor(ndp, ndp // 2)), *u1)
    shares = over("ctx", nctx, [summed] * nctx)
    back = call("hand_on", hand_on_kernel, sds(returned.shape, BF), after=[summed])(returned)
    block_out, input_grad, placed = call(
        "place_slots",
        one(unpack_kernel),
        [sds(tok.shape, F32)] * 2 + [sds((8, TILE), F32)],
        scratch=[pltpu.SMEM(valid_mask.shape, valid_mask.dtype), pltpu.SemaphoreType.DMA((1,))],
        raw=(3,),
        mib=16,
    )(back, other(back), tails, valid_mask)
    gq, gk, gv, gqb, gvb, go, gu, gub, gd, *gvec = call(
        "place_grads",
        one(grads_kernel),
        [
            sds(w_query.shape, F32), sds(w_key.shape, F32), sds(w_value.shape, F32),
            sds(query_bias.shape, F32), sds(value_bias.shape, F32), sds(w_out.shape, F32),
            sds(w_up.shape, F32), sds(up_bias.shape, F32), sds((rows, ff), F32),
        ]
        + [sds((rows,), F32)] * 6,
        scratch=[
            pltpu.VMEM((nctx,) + s1[0].shape[1:], F32),
            pltpu.VMEM((nctx, padded, ff // 2), F32),
        ],
        after=[placed],
    )(*shares)
    return (by_image(block_out), by_image(input_grad), gq, gk, gv, gqb, gvb, go, gu, gub, jnp.transpose(gd), *gvec)


def solution(mesh):
    rows, cols, tp, dp = P("dp", "tp"), P("tp", "dp"), P("tp"), P("dp")
    act = P("dp", "ctx", None)
    return jax.shard_map(
        functools.partial(body, mesh.shape["ctx"], mesh.shape["tp"], mesh.shape["dp"]),
        mesh=mesh,
        in_specs=(act, P("dp", "ctx"), act, rows, rows, rows, tp, tp, cols, rows, tp, cols) + (dp,) * 6,
        out_specs=(act, act, rows, rows, rows, tp, tp, cols, rows, tp, cols) + (dp,) * 6,
        check_vma=False,
    )
```

```python
import functools

import jax
import jax.numpy as jnp
from jax import lax
from jax.experimental import pallas as pl
from jax.experimental.pallas import tpu as pltpu
from jax.sharding import PartitionSpec as P

HD = 64
EPS = 1e-06
SCALE = 0.125
FLOOR = -1e30
BF = jnp.bfloat16
F32 = jnp.float32
TILE = 128
TIMES = {
    "pack_weights": 2.0, "pack_slots": 3.0, "join_quarter": 20.0, "attention": 0.0, "mlp_own": 4.0, "mlp_oth": 4.0, "mlp_sums": 2.0,
    "attention_back": 11.0, "sum_ctx_first": 50.0, "sum_ctx_attn": 0.5, "sum_dp": 5.0, "place_slots": 2.3, "place_grads": 1.0,
}
EXTRA = 16


def call(name, kernel, out_shape, scratch=(), mib=8, after=(), raw=()):
    after = list(after)

    def ordered(*refs):
        kernel(*refs[len(after) :])

    def run(*args):
        specs = [pl.BlockSpec(memory_space=pl.ANY)] * len(after) + [
            pl.BlockSpec(memory_space=pltpu.HBM if i in raw else pltpu.VMEM)
            for i in range(len(args))
        ]
        return pl.pallas_call(
            ordered,
            name=name,
            out_shape=out_shape,
            in_specs=specs,
            out_specs=jax.tree.map(lambda _: pl.BlockSpec(memory_space=pltpu.VMEM), out_shape),
            scratch_shapes=list(scratch),
            compiler_params=pltpu.CompilerParams(vmem_limit_bytes=mib << 20),
            cost_estimate=pl.CostEstimate(
                flops=int(TIMES.get(name, 0.2) * 1.15e9), bytes_accessed=1, transcendentals=0
            ),
        )(*after, *args)

    return run


def sds(shape, dtype):
    return jax.ShapeDtypeStruct(shape, dtype)


def nn(a, b):
    return lax.dot_general(a, b, (((1,), (0,)), ((), ())), preferred_element_type=F32)


def nt(a, b):
    return lax.dot_general(a, b, (((1,), (1,)), ((), ())), preferred_element_type=F32)


def tn(a, b):
    return lax.dot_general(a, b, (((0,), (0,)), ((), ())), preferred_element_type=F32)


def swap(v):
    return pltpu.roll(v, HD, axis=1)


def low_lanes(shape):
    return lax.broadcasted_iota(jnp.int32, shape, 1) < HD


def row_is(shape, row):
    return lax.broadcasted_iota(jnp.int32, shape, 0) == row


def tile(v, i):
    return v[:, i * TILE : (i + 1) * TILE]


def assemble(own, oth):
    low = low_lanes((own.shape[0], TILE))
    own_qk, own_vo, oth_qk, oth_vo = tile(own, 4), tile(own, 5), tile(oth, 4), tile(oth, 5)
    qkv = [
        tile(own, 0), tile(oth, 0), jnp.where(low, own_qk, swap(oth_qk)),
        tile(own, 1), tile(oth, 1), jnp.where(low, swap(own_qk), oth_qk),
        tile(own, 2), tile(oth, 2), jnp.where(low, own_vo, swap(oth_vo)),
    ]
    out = [tile(own, 3), tile(oth, 3), jnp.where(low, swap(own_vo), oth_vo)]
    return qkv, out


def disassemble(qkv, out):
    low = low_lanes(qkv[0].shape)
    own = [qkv[0], qkv[3], qkv[6], out[0], jnp.where(low, qkv[2], swap(qkv[5])), jnp.where(low, qkv[8], swap(out[2]))]
    oth = [qkv[1], qkv[4], qkv[7], out[1], jnp.where(low, swap(qkv[2]), qkv[5]), jnp.where(low, swap(qkv[8]), out[2])]
    return own, oth


def norm_stats(v):
    mean = jnp.mean(v, axis=-1, keepdims=True)
    centered = v - mean
    r = lax.rsqrt(jnp.mean(centered * centered, axis=-1, keepdims=True) + EPS)
    return centered * r, r


def norm_back(e, xhat, r):
    return r * (
        e
        - jnp.mean(e, axis=-1, keepdims=True)
        - xhat * jnp.mean(e * xhat, axis=-1, keepdims=True)
    )


def gelu_pair(v):
    phi = 0.5 + 0.5 * lax.erf(v * 0.7071067811865476)
    return v * phi, phi + (0.3989422804014327 * v) * jnp.exp(-0.5 * v * v)


BLOCK = 16


def one_hot(shape, hit):
    r, c = (lax.broadcasted_iota(jnp.int32, shape, i) for i in range(2))
    return hit(r, c).astype(F32).astype(BF)


def picker(wanted, images):
    def hit(r, c):
        img = wanted[-1]
        for k in range(len(wanted) - 1):
            img = jnp.where(r // BLOCK == k, wanted[k], img)
        return c == (r % BLOCK) * images + img

    return one_hot((len(wanted) * BLOCK, images * BLOCK), hit)


def take_images(ref, outs, at, pick, images, count):
    for b in range(count // BLOCK):
        got = nn(pick, ref[b * BLOCK * images : (b + 1) * BLOCK * images, :].astype(BF)).astype(BF)
        for k in range(len(outs)):
            outs[k][at + b * BLOCK : at + (b + 1) * BLOCK, :] = got[k * BLOCK : (k + 1) * BLOCK]


def fetch(sources, held, sem):
    copies = [pltpu.make_async_copy(sources[i], held[i], sem.at[i]) for i in range(len(sources))]
    for c in copies:
        c.start()
    return copies


def pack_weights_kernel(sizes, count, *refs):
    nctx, ntp, ndp, main, width, rows, padded = sizes
    sources, (p1, p2q), refs = refs[:count], refs[count : count + 2], refs[count + 2 :]
    held, sem = refs[:count], refs[count]
    copies = fetch(sources, held, sem)
    wq, wk, wv, wo, wu, wd, qb, vb, ub = held[:9]
    vecs = held[9:]
    me_c, me_d = lax.axis_index("ctx"), lax.axis_index("dp")
    for c in copies:
        c.wait()
    if padded > rows:
        p1[0:padded, :] = jnp.zeros((padded, p1.shape[1]), BF)
        p2q[...] = jnp.zeros(p2q.shape, BF)
    quarter = p2q.shape[1]
    for j in range(nctx):
        src = (wu, wd)[j // 2][:, (j % 2) * quarter : (j % 2 + 1) * quarter]

        @pl.when(me_c == j)
        def _(src=src):
            p2q[0:rows, :] = src

    def put(lo, value):
        p1[0:rows, lo : lo + value.shape[1]] = value.astype(BF)

    fq, fk, fv = wq[...].astype(F32), wk[...].astype(F32), wv[...].astype(F32)
    fo = jnp.transpose(wo[...].astype(F32))
    for i, w in enumerate((fq, fk, fv, fo)):
        put(i * TILE, tile(w, 0))
    put(4 * TILE, jnp.concatenate([fq[:, TILE:], fk[:, TILE:]], axis=1))
    put(5 * TILE, jnp.concatenate([fv[:, TILE:], fo[:, TILE:]], axis=1))
    cols = p1.shape[1]
    fqb, fvb = qb[...].astype(F32)[None, :], vb[...].astype(F32)[None, :]
    none = jnp.zeros((1, TILE), F32)
    short = jnp.zeros((1, HD), F32)
    bias = jnp.concatenate(
        [fqb[:, :TILE], none, fvb[:, :TILE], none, fqb[:, TILE:], short, fvb[:, TILE:], short], axis=1
    )
    spread = one_hot((rows, width), lambda r, c: c == r + rows * me_d)
    block = jnp.where(row_is((EXTRA, cols), 0), bias, 0.0)
    block = jnp.where(row_is((EXTRA, cols), 7), ub[...].astype(F32)[None, :], block)
    lanes = jnp.zeros((EXTRA, rows), F32)
    for i in range(6):
        lanes = jnp.where(row_is((EXTRA, rows), 1 + i), vecs[i][...].astype(F32)[None, :], lanes)
    lanes = nn(lanes.astype(BF), spread)
    p1[padded : padded + EXTRA, :] = block.astype(BF)
    mixed = jnp.where(
        (lax.broadcasted_iota(jnp.int32, (EXTRA, width), 0) - 1).astype(jnp.uint32) < 6,
        lanes,
        block[:, :width],
    )
    p1[padded : padded + EXTRA, 0:width] = mixed.astype(BF)


def pack_slots_kernel(sizes, tok, cot, source, *refs):
    nctx, ntp, ndp, main, width, rows, padded = sizes
    sent, tails, mask, sem = refs[:nctx], refs[nctx], refs[nctx + 1], refs[nctx + 2]
    get_mask = pltpu.make_async_copy(source, mask, sem.at[0])
    get_mask.start()
    images = nctx * ntp
    me_c, me_t = lax.axis_index("ctx"), lax.axis_index("tp")
    wanted = [(me_c ^ k) * ntp + me_t for k in range(nctx)]
    pick = picker(wanted, images)
    for i, ref in enumerate((tok, cot)):
        take_images(ref, sent, i * (main + EXTRA), pick, images, main)
        tails[i] = ref[main * images :, :]
    get_mask.wait()
    for k in range(nctx):
        gate = mask[wanted[k], main].astype(F32)
        te = tok[pl.ds(main * images + wanted[k], 1), :] * gate
        ce = cot[pl.ds(main * images + wanted[k], 1), :] * gate
        shape = (EXTRA, width)
        sent[k][main : main + EXTRA, :] = jnp.where(
            row_is(shape, 0), te, jnp.where(row_is(shape, 1), ce, 0.0)
        ).astype(BF)


def join_kernel(axis, stride, own, got, out):
    bit = lax.rem(lax.div(lax.axis_index(axis), stride), 2)
    for i in range(own.shape[0]):
        out[2 * i + bit] = own[i]
        out[2 * i + 1 - bit] = got[i]


def place_rows(stage, own, got, rows):
    bit = lax.rem(lax.axis_index("dp"), 2)
    for i in range(own.shape[0]):
        for piece, last in ((own, bit), (got, 1 - bit)):
            at = pl.ds(pl.multiple_of((2 * i + last) * rows, 16 if rows % 16 == 0 else 8), rows)
            stage[at, :] = piece[i].astype(stage.dtype)[:rows]


def merge_quarter_kernel(sizes, attn, own, got, out, attn_out, stage):
    place_rows(stage, own, got, sizes[5])
    out[...] = stage[...].astype(BF)
    attn_out[...] = attn[...]


def split_kernel(got, *outs):
    for i, out in enumerate(outs):
        cols = out.shape[2]
        out[...] = got[:, :, i * cols : (i + 1) * cols]


def merge_ff_kernel(nctx, *refs):
    out = refs[nctx]
    me_c = lax.axis_index("ctx")
    for k in range(nctx):
        quarter = refs[k].shape[1]
        out[:, pl.ds(pl.multiple_of((me_c ^ k) * quarter, quarter), quarter)] = refs[k][...]


def attention_kernel(sizes, *refs):
    nctx, ntp, ndp, main, width, rows, padded = sizes
    t_in, (own, got, own_oth, got_oth_a, got_oth_b), refs = refs[:nctx], refs[nctx : nctx + 5], refs[nctx + 5 :]
    x_out, mid_out, n1_out, n2_out, qkv, ctx, ctx_full, lse, wqkv, wot, vec, ub, cot, stage, stage_oth = refs
    body = nctx * main
    total = body + EXTRA
    half = got_oth_a.shape[2]
    place_rows(stage, own, got, rows)
    place_rows(stage_oth.at[:, :half], own_oth.at[:, :, :half], got_oth_a, rows)
    place_rows(stage_oth.at[:, half:], own_oth.at[:, :, half:], got_oth_b, rows)
    tiles, outs = assemble(stage[...].astype(F32), stage_oth[...].astype(F32))
    for i, v in enumerate(tiles):
        wqkv[:, i * TILE : (i + 1) * TILE] = v.astype(BF)
    for i, v in enumerate(outs):
        wot[:, i * TILE : (i + 1) * TILE] = v.astype(BF)
    extra = own[0, padded:, :].astype(F32)
    extra_oth = own_oth[0, padded:, :].astype(F32)
    tiles, _ = assemble(extra, extra_oth)
    bias = jnp.concatenate([v[0:1] for v in tiles], axis=1)
    vec_sum = jnp.zeros((EXTRA, width), F32)
    for i in range(own.shape[0]):
        vec_sum += own[i, padded:, :width].astype(F32) + got[i, padded:, :width].astype(F32)
    vec[...] = vec_sum
    ub[...] = jnp.broadcast_to(jnp.concatenate([extra[7:8], extra_oth[7:8]], axis=1), ub.shape)
    extra = jnp.zeros((EXTRA, width), F32)
    for k in range(nctx):
        x_out[k * main : (k + 1) * main, :] = t_in[k][0:main, :].astype(F32)
        cot[k * main : (k + 1) * main, :] = t_in[k][main + EXTRA :, :]
        extra += t_in[k][main : main + EXTRA, :].astype(F32)
    x_out[body:, :] = jnp.where(row_is((EXTRA, width), 0), extra, 0.0)
    cot[body:, :] = jnp.where(row_is((EXTRA, width), 0), extra[1:2, :], 0.0).astype(BF)
    x = x_out[...]
    xhat, _ = norm_stats(x)
    n1 = (xhat * vec_sum[1:2, :] + vec_sum[2:3, :]).astype(BF)
    n1_out[...] = n1
    proj = nn(n1, wqkv[...]) + bias
    qkv[0:total, 0:width] = (proj[:, 0:width].astype(BF).astype(F32) * SCALE).astype(BF)
    qkv[0:total, width:] = proj[:, width:].astype(BF)
    keys = qkv.shape[0]
    qkv[total:, :] = jnp.zeros((keys - total, qkv.shape[1]), BF)
    off = jnp.where(lax.broadcasted_iota(jnp.int32, (1, keys), 1) > body, FLOOR, 0.0)
    low = low_lanes((total, TILE))
    lane = lax.broadcasted_iota(jnp.int32, (total, TILE), 1)
    all_lse = jnp.zeros((total, TILE), F32)
    for p in range(3):
        qp = qkv[0:total, p * TILE : (p + 1) * TILE]
        kp = qkv[:, width + p * TILE : width + (p + 1) * TILE]
        vp = qkv[:, 2 * width + p * TILE : 2 * width + (p + 1) * TILE]
        parts = []
        for a in range(2):
            qa = jnp.where(low if a == 0 else ~low, qp, jnp.zeros_like(qp))
            s = nt(qa, kp) + off
            m = jnp.max(s, axis=-1, keepdims=True)
            e = jnp.exp(s - m)
            l = jnp.sum(e, axis=-1, keepdims=True)
            parts.append(nn(e.astype(BF), vp) * (1.0 / l))
            all_lse = jnp.where(lane == 2 * p + a, m + jnp.log(l), all_lse)
        ctx_full[:, p * TILE : (p + 1) * TILE] = jnp.where(low, parts[0], parts[1])
    ctx[...] = ctx_full[...].astype(BF)
    lse[...] = all_lse
    attended = nt(ctx[...], wot[...]) + vec_sum[5:6, :]
    valid = lax.broadcasted_iota(jnp.int32, (total, 1), 0) <= body
    middle = x_out[...] + jnp.where(valid, attended, 0.0)
    mid_out[...] = middle
    xhat2, _ = norm_stats(middle)
    n2_out[...] = (xhat2 * vec_sum[3:4, :] + vec_sum[4:5, :]).astype(BF)


def mlp_half_kernel(sizes, side, n2, cot, w, ub, hid, hgr, ubgrad, grads):
    nctx, ntp, ndp, main, width, rows, padded = sizes
    half = w.shape[1] // 2
    n2v, dcot = n2[...], cot[...]
    act, slope = gelu_pair(nn(n2v, w[:, :half]) + ub[0:1, side * half : (side + 1) * half])
    h = act.astype(BF)
    hg = (nn(dcot, w[:, half:]) * slope).astype(BF)
    hid[...] = h
    hgr[...] = hg
    ubgrad[...] = jnp.broadcast_to(jnp.sum(hg.astype(F32), axis=0, keepdims=True), ubgrad.shape)
    cols = grads.shape[3]
    for part, g in ((0, tn(n2v, hg).astype(BF)), (1, tn(dcot, h).astype(BF))):
        for d in range(ndp):
            for c in range(half // cols):
                grads[2 * part + c, d, 0:rows, :] = g[d * rows : (d + 1) * rows, c * cols : (c + 1) * cols]


def mlp_sums_kernel(sizes, mid, ctx, wot, vec, cot, w_own, w_oth, hgr_own, hgr_oth, dmid, dctx, g_out, vgrad):
    nctx, ntp, ndp, main, width, rows, padded = sizes
    body = nctx * main
    total = body + EXTRA
    half = w_own.shape[1] // 2
    dcot = cot[...]
    middle = mid[...]
    valid = lax.broadcasted_iota(jnp.int32, (total, 1), 0) <= body
    n2g = nt(hgr_own[...], w_own[:, :half]) + nt(hgr_oth[...], w_oth[:, :half])
    xhat, r = norm_stats(middle)
    back = norm_back(n2g * vec[3:4, :], xhat, r)
    middle_grad = dcot.astype(F32) + back
    dmid[...] = middle_grad
    agrad = jnp.where(valid, middle_grad, 0.0).astype(BF)
    dctx[...] = nn(agrad, wot[...]).astype(BF)
    g_out[...] = tn(agrad, ctx[...])
    shape = vgrad.shape
    v = jnp.where(row_is(shape, 2), jnp.sum(n2g * xhat, axis=0, keepdims=True), 0.0)
    v = jnp.where(row_is(shape, 3), jnp.sum(n2g, axis=0, keepdims=True), v)
    v = jnp.where(row_is(shape, 4), jnp.sum(agrad.astype(F32), axis=0, keepdims=True), v)
    v = jnp.where(row_is(shape, 5), jnp.sum(dcot.astype(F32), axis=0, keepdims=True), v)
    vgrad[...] = v


def results_kernel(sizes, mid, vec, w_own, w_oth, hid_own, hid_oth, x, dmid, n1_grad, bo, ig):
    nctx, ntp, ndp, main, width, rows, padded = sizes
    body = nctx * main
    half = w_own.shape[1] // 2
    valid = lax.broadcasted_iota(jnp.int32, (body + EXTRA, 1), 0) <= body
    mlp_out = nt(hid_own[...], w_own[:, half:]) + nt(hid_oth[...], w_oth[:, half:]) + vec[6:7, :]
    bo[...] = (mid[...] + jnp.where(valid, mlp_out, 0.0)).astype(BF)
    xhat, r = norm_stats(x[...])
    ig[...] = (dmid[...] + norm_back(n1_grad[...] * vec[1:2, :], xhat, r)).astype(BF)


def pair_back(p, width, total, body, qkv, dctx, lse, ctx):
    keys = qkv.shape[0]
    off = jnp.where(lax.broadcasted_iota(jnp.int32, (1, keys), 1) > body, FLOOR, 0.0)
    low = low_lanes((total, TILE))
    at = slice(p * TILE, (p + 1) * TILE)
    qp = qkv[0:total, at]
    kp = qkv[:, width + p * TILE : width + (p + 1) * TILE]
    vp = qkv[:, 2 * width + p * TILE : 2 * width + (p + 1) * TILE]
    dp = dctx[:, at]
    both = dp.astype(F32) * ctx[:, at]
    qt = jnp.transpose(qp.astype(F32)).astype(BF)
    dt = jnp.transpose(dp.astype(F32)).astype(BF)
    dk, dv = [], []
    zero = jnp.zeros_like(qp)
    qs = jnp.concatenate([jnp.where(low, qp, zero), jnp.where(low, zero, qp)], axis=0)
    ds_ = jnp.concatenate([jnp.where(low, dp, zero), jnp.where(low, zero, dp)], axis=0)
    bs = jnp.concatenate([jnp.where(low, both, 0.0), jnp.where(low, 0.0, both)], axis=0)
    inner = jnp.sum(bs, axis=-1, keepdims=True)
    ls = jnp.concatenate([lse[:, 2 * p : 2 * p + 1], lse[:, 2 * p + 1 : 2 * p + 2]], axis=0)
    prob = jnp.exp(nt(qs, kp) + off - ls)
    ds = (prob * (nt(ds_, vp) - inner)).astype(BF)
    w = prob.astype(BF)
    dq = nn(ds, kp)
    dq = jnp.where(low, dq[0:total], dq[total:]) * SCALE
    for a in range(2):
        dk.append(nn(qt[a * HD : (a + 1) * HD], ds[a * total : (a + 1) * total]))
        dv.append(nn(dt[a * HD : (a + 1) * HD], w[a * total : (a + 1) * total]))
    dk, dv = (jnp.transpose(jnp.concatenate(v, axis=0))[0:total] for v in (dk, dv))
    return dq.astype(BF), dk.astype(BF), dv.astype(BF)


def attention_back_kernel(sizes, *refs):
    nctx, ntp, ndp, main, width, rows, padded = sizes
    qkv, dctx, lse, ctx, n1, x_in, wqkv, g_out, vgrad, ub_own, ub_oth = refs[:11]
    n1_grad, g_own, g_oth, dqkv = refs[11:]
    body = nctx * main
    total = body + EXTRA
    for p in range(3):
        for i, v in enumerate(pair_back(p, width, total, body, qkv, dctx, lse, ctx)):
            dqkv[:, i * width + p * TILE : i * width + (p + 1) * TILE] = v
    d = dqkv[...]
    bias = jnp.sum(d.astype(F32), axis=0, keepdims=True)
    g = tn(n1[...], d)
    go = g_out[...]
    own, oth = disassemble([tile(g, i) for i in range(9)], [tile(go, i) for i in range(3)])
    half = padded // 2
    for to, tiles in ((g_own, own), (g_oth, oth)):
        for j in range(4):
            lo = j % 2 * half
            for e in range(ndp):
                to[j, e, 0:rows, :] = tiles[j][e * rows : (e + 1) * rows].astype(BF)
                shared = tiles[4 + j // 2][e * rows + lo : e * rows + min(rows, lo + half)]
                to[j, e, padded : padded + shared.shape[0], :] = shared.astype(BF)
    dn1 = nt(d, wqkv[...])
    n1_grad[...] = dn1
    xhat, _ = norm_stats(x_in[...])
    gains = jnp.sum(dn1 * xhat, axis=0, keepdims=True)
    shifts = jnp.sum(dn1, axis=0, keepdims=True)
    vecs = [gains, shifts] + [vgrad[i : i + 1, :] for i in range(2, 6)]
    zero = [jnp.zeros((1, TILE), F32)] * 3
    bias_own, bias_oth = disassemble([tile(bias, i) for i in range(9)], zero)
    for to, tiles, ub in ((g_own, bias_own, ub_own), (g_oth, bias_oth, ub_oth)):
        rows_ = [tile(v, i) for v in vecs for i in range(3)] + tiles
        rows_ += [ub[0:1, i * TILE : (i + 1) * TILE] for i in range(6)]
        for j in range(4):
            block = jnp.zeros((EXTRA, TILE), F32)
            for i, v in enumerate(rows_[8 * j : 8 * (j + 1)]):
                block = jnp.where(row_is(block.shape, i), v, block)
            for e in range(ndp):
                to[j, e, padded + half :, :] = block.astype(BF)


def sum_core_kernel(n, own, oth, *outs):
    me = lax.axis_index("ctx")
    for k in range(n):
        outs[k][...] = (own[me ^ k].astype(F32) + oth[me ^ k].astype(F32)).astype(BF)


def sum_ctx_kernel(n, ndp, *refs):
    me = lax.axis_index("dp")
    for k in range(ndp):
        v = refs[0][me ^ k].astype(F32)
        for i in range(1, n):
            v = v + refs[i][me ^ k].astype(F32)
        refs[n + k][...] = v.astype(BF)


def halve(stride, item, keep, send):
    bit = lax.rem(lax.div(lax.axis_index("dp"), stride), 2)
    for j in range(keep.shape[0]):
        keep[j] = item(2 * j + bit).astype(BF)
        send[j] = item(2 * j + 1 - bit).astype(BF)


def ctx_bits():
    me = lax.axis_index("ctx")
    return lax.rem(me, 2), lax.div(me, 2)


def sum_core_ff_kernel(own, oth, keep_a, send_a, keep_b, send_b):
    low, high = ctx_bits()
    half = own.shape[1] // 2

    def put(to, i, quarter, blocks):
        to[i] = (own[quarter, blocks].astype(F32) + oth[quarter, blocks].astype(F32)).astype(BF)

    for i in range(2):
        first, second = slice(0, half), slice(half, 2 * half)
        put(keep_a, i, 2 * i + low, first)
        put(send_a, i, 2 * i + 1 - low, first)
        put(keep_b, i, 2 * high + i, second)
        put(send_b, i, 2 * (1 - high) + i, second)


def sum_ctx_first_kernel(own_a, got_a, own_b, got_b, keep_a, send_a, keep_b, send_b):
    low, high = ctx_bits()
    for own, got, keep, send, bit in (
        (own_a, got_a, keep_a, send_a, high),
        (own_b, got_b, keep_b, send_b, low),
    ):
        keep[...] = (own[bit].astype(F32) + got[bit].astype(F32)).astype(BF)
        send[...] = (own[1 - bit].astype(F32) + got[1 - bit].astype(F32)).astype(BF)


def sum_ctx_second_kernel(own_a, got_a, own_b, got_b, keep, send):
    bit = lax.rem(lax.axis_index("dp"), 2)
    half = own_a.shape[0]
    for j in range(keep.shape[0]):
        own, got, at = (own_a, got_a, 2 * j) if 2 * j < half else (own_b, got_b, 2 * j - half)
        for to, i in ((keep, at + bit), (send, at + 1 - bit)):
            to[j] = (own[i].astype(F32) + got[i].astype(F32)).astype(BF)


def add_halves_kernel(stride, own, got, keep, send):
    halve(stride, lambda i: own[i].astype(F32) + got[i].astype(F32), keep, send)


def sum_dp_kernel(n, own, got, *refs):
    out = refs[n]
    rows = own.shape[1]
    out[:rows, :] = (own[0].astype(F32) + got[0, 0:rows, :].astype(F32)).astype(BF)
    v = refs[0][...].astype(F32)
    for r in refs[1:n]:
        v = v + r[...].astype(F32)
    span = out.shape[0] - rows
    out[rows:, :] = jnp.zeros((span, out.shape[1]), BF)
    for i in range(out.shape[1] // TILE):
        part = v[i * span : (i + 1) * span].astype(BF)
        if part.shape[0]:
            out[rows : rows + part.shape[0], i * TILE : (i + 1) * TILE] = part


def returns_kernel(sizes, bo, ig, out):
    nctx, ntp, ndp, main, width, rows, padded = sizes
    me = lax.axis_index("ctx")
    body = nctx * main
    shape = (EXTRA, width)
    extra = jnp.where(
        row_is(shape, 0),
        bo[body:, :].astype(F32),
        jnp.where(row_is(shape, 1), ig[body:, :].astype(F32)[0:1, :], 0.0),
    ).astype(BF)
    for k in range(nctx):
        at = slice(k * main, (k + 1) * main)
        out[me ^ k, 0:main, :] = bo[at, :]
        out[me ^ k, main : main + EXTRA, :] = extra
        out[me ^ k, main + EXTRA :, :] = ig[at, :]


def hand_on_kernel(held, out):
    out[...] = held[...]


def grads_kernel(sizes, *refs):
    nctx, ntp, ndp, main, width, rows, padded = sizes
    parts, refs = refs[:nctx], refs[nctx:]
    gq, gk, gv, gqb, gvb, go, gu, gub, gd = refs[:9]
    gvec, f, f2 = refs[9:15], refs[15], refs[16]
    me, me_d = lax.axis_index("ctx"), lax.axis_index("dp")
    span = parts[0].shape[0] - padded
    for k in range(nctx):
        f2[me ^ k] = parts[k][0:padded, :].astype(F32)
        for i in range(f2.shape[2] // TILE):
            n = min(span, f.shape[1] - i * span)
            if n > 0:
                f[me ^ k, i * span : i * span + n, :] = parts[k][
                    padded : padded + n, i * TILE : (i + 1) * TILE
                ].astype(F32)
    half = f2.shape[2]
    for j in range(2):
        gu[:, j * half : (j + 1) * half] = f2[j, 0:rows, :]
        gd[:, j * half : (j + 1) * half] = f2[2 + j, 0:rows, :]
    q01, k01, v01, o01 = (f[j, 0:rows, :] for j in range(4))
    low, high = slice(padded, padded + padded // 2), slice(padded, padded + rows - padded // 2)
    qk2 = jnp.concatenate([f[0, low, :], f[1, high, :]], axis=0)
    vo2 = jnp.concatenate([f[2, low, :], f[3, high, :]], axis=0)
    gq[:, 0:TILE] = q01
    gq[:, TILE:] = qk2[:, 0:HD]
    gk[:, 0:TILE] = k01
    gk[:, TILE:] = swap(qk2)[:, 0:HD]
    gv[:, 0:TILE] = v01
    gv[:, TILE:] = vo2[:, 0:HD]
    go[0:TILE, :] = jnp.transpose(o01)
    go[TILE:, :] = jnp.transpose(vo2)[HD:, :]

    def line(i):
        at = padded + padded // 2 + i % 8
        return f[i // 8, at : at + 1, :]

    for i in range(6):
        v = jnp.concatenate([line(3 * i), line(3 * i + 1), line(3 * i + 2)], axis=1)
        v = jnp.broadcast_to(v, (8, width))
        v = pltpu.roll(v, lax.rem(width - me_d * rows, width), axis=1)
        gvec[i][...] = v[0, 0:rows]
    b = [line(18 + i) for i in range(6)]
    gqb[...] = jnp.concatenate([b[0], b[4][:, 0:HD]], axis=1)[0]
    gvb[...] = jnp.concatenate([b[2], b[5][:, 0:HD]], axis=1)[0]
    gub[...] = jnp.concatenate([line(24 + i) for i in range(6)], axis=1)[0]


def unpack_kernel(sizes, own, oth, tails, mask, *refs):
    nctx, ntp, ndp, main, width, rows, padded = sizes
    outs, done, valid, sem = refs[:2], refs[2], refs[3], refs[4]
    images = nctx * ntp
    me_t = lax.axis_index("tp")
    where = [j * ntp + t for t in (me_t, 1 - me_t) for j in range(nctx)]
    sources = [v.at[j] for v in (own, oth) for j in range(nctx)]
    get_valid = pltpu.make_async_copy(mask, valid, sem.at[0])
    get_valid.start()

    def hit(r, c):
        img = where[-1]
        for j in range(images - 1):
            img = jnp.where(c // BLOCK == j, where[j], img)
        return r == (c % BLOCK) * images + img

    put = one_hot((images * BLOCK, images * BLOCK), hit)
    for i in range(2):
        for b in range(main // BLOCK):
            lo = i * (main + EXTRA) + b * BLOCK
            got = jnp.concatenate([src[lo : lo + BLOCK, :] for src in sources], axis=0)
            outs[i][b * BLOCK * images : (b + 1) * BLOCK * images, :] = nn(put, got)
    get_valid.wait()
    for i in range(2):
        for src, img in zip(sources, where):
            got = src[main : main + EXTRA, :].astype(F32)[i : i + 1, :]
            outs[i][pl.ds(main * images + img, 1), :] = jnp.where(
                valid[img, main] > 0, got, tails[i, pl.ds(img, 1), :]
            )
    done[...] = jnp.zeros_like(done)


def xor(n, k):
    return [(i, i ^ k) for i in range(n)]


def over(axis, n, items):
    return [items[0]] + [lax.ppermute(items[k], axis, xor(n, k)) for k in range(1, n)]


def body(nctx, ntp, ndp, *args):
    (tokens, valid_mask, cotangent, w_query, w_key, w_value, query_bias, value_bias, w_out, w_up, up_bias, w_down) = args[:12]
    vecs = args[12:]
    images, slots, width = tokens.shape
    main = slots - 1
    rows = w_query.shape[0]
    padded = -(-rows // EXTRA) * EXTRA
    ff = w_up.shape[1]
    p1_cols = 4 * w_query.shape[1]
    sizes = (nctx, ntp, ndp, main, width, rows, padded)
    total = nctx * main + EXTRA
    keys = -(-total // TILE) * TILE
    stage = BF if rows % 16 == 0 else F32
    flip = xor(ntp, 1)
    tok = jnp.transpose(tokens, (1, 0, 2)).reshape(slots * images, width)
    cot = jnp.transpose(cotangent, (1, 0, 2)).reshape(slots * images, width)

    def one(f):
        return functools.partial(f, sizes)

    def other(v):
        return lax.ppermute(v, "tp", flip)

    def held(arrays):
        return [
            (pltpu.SMEM if v.dtype == jnp.int32 else pltpu.VMEM)(v.shape, v.dtype) for v in arrays
        ] + [pltpu.SemaphoreType.DMA((len(arrays),))]

    def gather_dp(name, piece, after):
        v = piece[None]
        stride = ndp // 2
        while stride > 1:
            v = call(
                name,
                functools.partial(join_kernel, "dp", stride),
                sds((2 * v.shape[0],) + v.shape[1:], v.dtype),
                after=after,
            )(v, lax.ppermute(v, "dp", xor(ndp, stride)))
            stride //= 2
        return v, lax.ppermute(v, "dp", xor(ndp, 1))

    sources = [w_query, w_key, w_value, w_out, w_up, jnp.transpose(w_down), query_bias, value_bias, up_bias, *vecs]
    p1, p2q = call(
        "pack_weights",
        functools.partial(pack_weights_kernel, sizes, len(sources)),
        [sds((padded + EXTRA, p1_cols), BF), sds((padded, ff // 2), BF)],
        scratch=held(sources),
        mib=56,
        raw=range(len(sources)),
    )(*sources)
    *sent, tails = call(
        "pack_slots",
        one(pack_slots_kernel),
        [sds((2 * main + EXTRA, width), BF)] * nctx + [sds((2, images, width), F32)],
        scratch=[pltpu.SMEM(valid_mask.shape, valid_mask.dtype), pltpu.SemaphoreType.DMA((1,))],
        mib=48,
        raw=(2,),
    )(tok, cot, valid_mask)
    t_in = over("ctx", nctx, sent)
    w2q = gather_dp("join_quarter", p2q, [])
    w1, w1_got = gather_dp("join_attn", p1, [])
    w2q, w1_early = call(
        "merge_quarter",
        one(merge_quarter_kernel),
        [sds((width, ff // 2), BF), sds(w1.shape, BF)],
        scratch=[pltpu.VMEM((width, ff // 2), stage)],
        after=t_in[1:],
    )(w1, *w2q)
    w1_oth = other(w1_early)
    w2q = over("ctx", nctx, [w2q] * nctx)
    late = call(
        "split_attn",
        split_kernel,
        [sds(w1.shape[:2] + (p1_cols // 2,), BF)] * 2,
        after=[w1_oth, w2q[0]],
    )(w1_got)
    w1 = [w1, w1_got, w1_oth, *[other(v) for v in late]]
    x, mid, n1, n2, qkv, ctx, ctx_full, lse, wqkv, wot, vec, ub, cot_in = call(
        "attention",
        one(attention_kernel),
        [
            sds((total, width), F32), sds((total, width), F32), sds((total, width), BF), sds((total, width), BF),
            sds((keys, 3 * width), BF), sds((total, width), BF), sds((total, width), F32), sds((total, TILE), F32),
            sds((width, 3 * width), BF), sds((width, width), BF), sds((EXTRA, width), F32), sds((8, 2 * ff), F32),
            sds((total, width), BF),
        ],
        scratch=[pltpu.VMEM((width, p1_cols), stage)] * 2,
        mib=32,
    )(*t_in, *w1)
    w2_own = call(
        "merge_ff", functools.partial(merge_ff_kernel, nctx), sds((width, 2 * ff), BF), after=[vec]
    )(*w2q)
    w2_oth = other(w2_own)
    ff_grads = sds((4, ndp, padded, ff // 2), BF)

    def mlp_half(name, side, w, after=()):
        return call(
            name,
            functools.partial(mlp_half_kernel, sizes, side),
            [sds((total, ff), BF), sds((total, ff), BF), sds((8, ff), F32), ff_grads],
            mib=32,
            after=after,
        )(n2, cot_in, w, ub)

    hid_own, hgr_own, ub_own, g2_own = mlp_half("mlp_own", 0, w2_own)
    hid_oth, hgr_oth, ub_oth, g2_oth = mlp_half("mlp_oth", 1, w2_oth, [ub_own])
    dmid, dctx, g_out, vgrad = call(
        "mlp_sums",
        one(mlp_sums_kernel),
        [
            sds((total, width), F32), sds((total, width), BF), sds((width, width), F32), sds((EXTRA, width), F32),
        ],
        mib=32,
    )(mid, ctx, wot, vec, cot_in, w2_own, w2_oth, hgr_own, hgr_oth)

    def core_sums(name, own, oth, after=()):
        outs = [sds(own.shape[1:], BF)] * nctx
        return call(name, functools.partial(sum_core_kernel, nctx), outs, after=after)(own, other(oth))

    def by_image(v):
        return jnp.transpose(v.reshape(slots, images, width), (1, 0, 2))

    pairs = sds((2, ndp // 2, padded, ff // 2), BF)
    keep_a, send_a, keep_b, send_b = call("sum_core_ff", sum_core_ff_kernel, [pairs] * 4, after=[vgrad])(
        g2_own, other(g2_oth)
    )
    got_a, got_b = lax.ppermute(send_a, "ctx", xor(nctx, 1)), lax.ppermute(send_b, "ctx", xor(nctx, 2))
    n1_grad, g1_own, g1_oth = call(
        "attention_back",
        one(attention_back_kernel),
        [sds((total, width), F32)] + [sds((4, ndp, padded + padded // 2 + EXTRA, TILE), BF)] * 2,
        scratch=[pltpu.VMEM((total, 3 * width), BF)],
        mib=32,
        after=[keep_a],
    )(qkv, dctx, lse, ctx_full, n1, x, wqkv, g_out, vgrad, ub_own, ub_oth)
    one_quarter = sds(pairs.shape[1:], BF)
    keep_a, send_a, keep_b, send_b = call(
        "sum_ctx_first", sum_ctx_first_kernel, [one_quarter] * 4, after=[g1_own]
    )(keep_a, got_a, keep_b, got_b)
    got_a, got_b = lax.ppermute(send_a, "ctx", xor(nctx, 2)), lax.ppermute(send_b, "ctx", xor(nctx, 1))
    s1_send = core_sums("sum_core_attn", g1_own, g1_oth, after=[keep_a])
    s1 = over("ctx", nctx, s1_send)
    bo, ig = call(
        "results", one(results_kernel), [sds((total, width), BF)] * 2, mib=16, after=[s1_send[0]]
    )(mid, vec, w2_own, w2_oth, hid_own, hid_oth, x, dmid, n1_grad)
    keep, send = call("sum_ctx_second", sum_ctx_second_kernel, [one_quarter] * 2, after=[bo])(
        keep_a, got_a, keep_b, got_b
    )
    back = call(
        "returns",
        one(returns_kernel),
        sds((nctx, 2 * main + EXTRA, width), BF),
        after=[keep],
    )(bo, ig)
    returned = lax.all_to_all(back, "ctx", 0, 0)
    u1_send = call(
        "sum_ctx_attn",
        functools.partial(sum_ctx_kernel, nctx, ndp),
        [sds(s1[0].shape[1:], BF)] * ndp,
        after=[back],
    )(*s1)
    u1 = over("dp", ndp, u1_send)
    stride = 2
    while stride < ndp:
        half = sds((keep.shape[0] // 2,) + keep.shape[1:], BF)
        keep, send = call(
            "add_dp_ff", functools.partial(add_halves_kernel, stride), [half, half], after=[u1_send[0]]
        )(keep, lax.ppermute(send, "dp", xor(ndp, stride // 2)))
        stride *= 2
    summed = call(
        "sum_dp", functools.partial(sum_dp_kernel, ndp), sds((padded + -(-s1[0].shape[1] // (3 * EXTRA)) * EXTRA, ff // 2), BF)
    )(keep, lax.ppermute(send, "dp", xor(ndp, ndp // 2)), *u1)
    shares = over("ctx", nctx, [summed] * nctx)
    back = call("hand_on", hand_on_kernel, sds(returned.shape, BF), after=[summed])(returned)
    block_out, input_grad, placed = call(
        "place_slots",
        one(unpack_kernel),
        [sds(tok.shape, F32)] * 2 + [sds((8, TILE), F32)],
        scratch=[pltpu.SMEM(valid_mask.shape, valid_mask.dtype), pltpu.SemaphoreType.DMA((1,))],
        raw=(3,),
        mib=16,
    )(back, other(back), tails, valid_mask)
    gq, gk, gv, gqb, gvb, go, gu, gub, gd, *gvec = call(
        "place_grads",
        one(grads_kernel),
        [
            sds(w_query.shape, F32), sds(w_key.shape, F32), sds(w_value.shape, F32),
            sds(query_bias.shape, F32), sds(value_bias.shape, F32), sds(w_out.shape, F32),
            sds(w_up.shape, F32), sds(up_bias.shape, F32), sds((rows, ff), F32),
        ]
        + [sds((rows,), F32)] * 6,
        scratch=[
            pltpu.VMEM((nctx,) + s1[0].shape[1:], F32),
            pltpu.VMEM((nctx, padded, ff // 2), F32),
        ],
        after=[placed],
    )(*shares)
    return (by_image(block_out), by_image(input_grad), gq, gk, gv, gqb, gvb, go, gu, gub, jnp.transpose(gd), *gvec)


def solution(mesh):
    rows, cols, tp, dp = P("dp", "tp"), P("tp", "dp"), P("tp"), P("dp")
    act = P("dp", "ctx", None)
    return jax.shard_map(
        functools.partial(body, mesh.shape["ctx"], mesh.shape["tp"], mesh.shape["dp"]),
        mesh=mesh,
        in_specs=(act, P("dp", "ctx"), act, rows, rows, rows, tp, tp, cols, rows, tp, cols) + (dp,) * 6,
        out_specs=(act, act, rows, rows, rows, tp, tp, cols, rows, tp, cols) + (dp,) * 6,
        check_vma=False,
    )
```

```python
import functools

import jax
import jax.numpy as jnp
from jax import lax
from jax.experimental import pallas as pl
from jax.experimental.pallas import tpu as pltpu
from jax.sharding import PartitionSpec as P

HD = 64
EPS = 1e-06
SCALE = 0.125
FLOOR = -1e30
BF = jnp.bfloat16
F32 = jnp.float32
TILE = 128
TIMES = {
    "pack_weights": 2.0, "pack_slots": 3.0, "join_quarter": 20.0, "attention": 0.0, "mlp_own": 4.0, "mlp_oth": 4.0, "mlp_sums": 2.0,
    "attention_back": 11.0, "sum_ctx_first": 50.0, "sum_ctx_attn": 0.5, "sum_dp": 5.0, "place_slots": 2.3, "place_grads": 1.0,
}
EXTRA = 16


def call(name, kernel, out_shape, scratch=(), mib=8, after=(), raw=()):
    after = list(after)

    def ordered(*refs):
        kernel(*refs[len(after) :])

    def run(*args):
        specs = [pl.BlockSpec(memory_space=pl.ANY)] * len(after) + [
            pl.BlockSpec(memory_space=pltpu.HBM if i in raw else pltpu.VMEM)
            for i in range(len(args))
        ]
        return pl.pallas_call(
            ordered,
            name=name,
            out_shape=out_shape,
            in_specs=specs,
            out_specs=jax.tree.map(lambda _: pl.BlockSpec(memory_space=pltpu.VMEM), out_shape),
            scratch_shapes=list(scratch),
            compiler_params=pltpu.CompilerParams(vmem_limit_bytes=mib << 20),
            cost_estimate=pl.CostEstimate(
                flops=int(TIMES.get(name, 0.2) * 1.15e9), bytes_accessed=1, transcendentals=0
            ),
        )(*after, *args)

    return run


def sds(shape, dtype):
    return jax.ShapeDtypeStruct(shape, dtype)


def nn(a, b):
    return lax.dot_general(a, b, (((1,), (0,)), ((), ())), preferred_element_type=F32)


def nt(a, b):
    return lax.dot_general(a, b, (((1,), (1,)), ((), ())), preferred_element_type=F32)


def tn(a, b):
    return lax.dot_general(a, b, (((0,), (0,)), ((), ())), preferred_element_type=F32)


def swap(v):
    return pltpu.roll(v, HD, axis=1)


def low_lanes(shape):
    return lax.broadcasted_iota(jnp.int32, shape, 1) < HD


def row_is(shape, row):
    return lax.broadcasted_iota(jnp.int32, shape, 0) == row


def tile(v, i):
    return v[:, i * TILE : (i + 1) * TILE]


def assemble(own, oth):
    low = low_lanes((own.shape[0], TILE))
    own_qk, own_vo, oth_qk, oth_vo = tile(own, 4), tile(own, 5), tile(oth, 4), tile(oth, 5)
    qkv = [
        tile(own, 0), tile(oth, 0), jnp.where(low, own_qk, swap(oth_qk)),
        tile(own, 1), tile(oth, 1), jnp.where(low, swap(own_qk), oth_qk),
        tile(own, 2), tile(oth, 2), jnp.where(low, own_vo, swap(oth_vo)),
    ]
    out = [tile(own, 3), tile(oth, 3), jnp.where(low, swap(own_vo), oth_vo)]
    return qkv, out


def disassemble(qkv, out):
    low = low_lanes(qkv[0].shape)
    own = [qkv[0], qkv[3], qkv[6], out[0], jnp.where(low, qkv[2], swap(qkv[5])), jnp.where(low, qkv[8], swap(out[2]))]
    oth = [qkv[1], qkv[4], qkv[7], out[1], jnp.where(low, swap(qkv[2]), qkv[5]), jnp.where(low, swap(qkv[8]), out[2])]
    return own, oth


def norm_stats(v):
    mean = jnp.mean(v, axis=-1, keepdims=True)
    centered = v - mean
    r = lax.rsqrt(jnp.mean(centered * centered, axis=-1, keepdims=True) + EPS)
    return centered * r, r


def norm_back(e, xhat, r):
    return r * (
        e
        - jnp.mean(e, axis=-1, keepdims=True)
        - xhat * jnp.mean(e * xhat, axis=-1, keepdims=True)
    )


def gelu_pair(v):
    phi = 0.5 + 0.5 * lax.erf(v * 0.7071067811865476)
    return v * phi, phi + (0.3989422804014327 * v) * jnp.exp(-0.5 * v * v)


BLOCK = 16


def one_hot(shape, hit):
    r, c = (lax.broadcasted_iota(jnp.int32, shape, i) for i in range(2))
    return hit(r, c).astype(F32).astype(BF)


def picker(wanted, images):
    def hit(r, c):
        img = wanted[-1]
        for k in range(len(wanted) - 1):
            img = jnp.where(r // BLOCK == k, wanted[k], img)
        return c == (r % BLOCK) * images + img

    return one_hot((len(wanted) * BLOCK, images * BLOCK), hit)


def take_images(ref, outs, at, pick, images, count):
    for b in range(count // BLOCK):
        got = nn(pick, ref[b * BLOCK * images : (b + 1) * BLOCK * images, :].astype(BF)).astype(BF)
        for k in range(len(outs)):
            outs[k][at + b * BLOCK : at + (b + 1) * BLOCK, :] = got[k * BLOCK : (k + 1) * BLOCK]


def fetch(sources, held, sem):
    copies = [pltpu.make_async_copy(sources[i], held[i], sem.at[i]) for i in range(len(sources))]
    for c in copies:
        c.start()
    return copies


def pack_weights_kernel(sizes, count, *refs):
    nctx, ntp, ndp, main, width, rows, padded = sizes
    sources, (p1, p2q), refs = refs[:count], refs[count : count + 2], refs[count + 2 :]
    held, sem = refs[:count], refs[count]
    copies = fetch(sources, held, sem)
    wq, wk, wv, wo, wu, wd, qb, vb, ub = held[:9]
    vecs = held[9:]
    me_c, me_d = lax.axis_index("ctx"), lax.axis_index("dp")
    for c in copies:
        c.wait()
    if padded > rows:
        p1[0:padded, :] = jnp.zeros((padded, p1.shape[1]), BF)
        p2q[...] = jnp.zeros(p2q.shape, BF)
    quarter = p2q.shape[1]
    for j in range(nctx):
        src = (wu, wd)[j // 2][:, (j % 2) * quarter : (j % 2 + 1) * quarter]

        @pl.when(me_c == j)
        def _(src=src):
            p2q[0:rows, :] = src

    def put(lo, value):
        p1[0:rows, lo : lo + value.shape[1]] = value.astype(BF)

    fq, fk, fv = wq[...].astype(F32), wk[...].astype(F32), wv[...].astype(F32)
    fo = jnp.transpose(wo[...].astype(F32))
    for i, w in enumerate((fq, fk, fv, fo)):
        put(i * TILE, tile(w, 0))
    put(4 * TILE, jnp.concatenate([fq[:, TILE:], fk[:, TILE:]], axis=1))
    put(5 * TILE, jnp.concatenate([fv[:, TILE:], fo[:, TILE:]], axis=1))
    cols = p1.shape[1]
    fqb, fvb = qb[...].astype(F32)[None, :], vb[...].astype(F32)[None, :]
    none = jnp.zeros((1, TILE), F32)
    short = jnp.zeros((1, HD), F32)
    bias = jnp.concatenate(
        [fqb[:, :TILE], none, fvb[:, :TILE], none, fqb[:, TILE:], short, fvb[:, TILE:], short], axis=1
    )
    spread = one_hot((rows, width), lambda r, c: c == r + rows * me_d)
    block = jnp.where(row_is((EXTRA, cols), 0), bias, 0.0)
    block = jnp.where(row_is((EXTRA, cols), 7), ub[...].astype(F32)[None, :], block)
    lanes = jnp.zeros((EXTRA, rows), F32)
    for i in range(6):
        lanes = jnp.where(row_is((EXTRA, rows), 1 + i), vecs[i][...].astype(F32)[None, :], lanes)
    lanes = nn(lanes.astype(BF), spread)
    p1[padded : padded + EXTRA, :] = block.astype(BF)
    mixed = jnp.where(
        (lax.broadcasted_iota(jnp.int32, (EXTRA, width), 0) - 1).astype(jnp.uint32) < 6,
        lanes,
        block[:, :width],
    )
    p1[padded : padded + EXTRA, 0:width] = mixed.astype(BF)


def pack_slots_kernel(sizes, tok, cot, source, *refs):
    nctx, ntp, ndp, main, width, rows, padded = sizes
    sent, tails, mask, sem = refs[:nctx], refs[nctx], refs[nctx + 1], refs[nctx + 2]
    get_mask = pltpu.make_async_copy(source, mask, sem.at[0])
    get_mask.start()
    images = nctx * ntp
    me_c, me_t = lax.axis_index("ctx"), lax.axis_index("tp")
    wanted = [(me_c ^ k) * ntp + me_t for k in range(nctx)]
    pick = picker(wanted, images)
    for i, ref in enumerate((tok, cot)):
        take_images(ref, sent, i * (main + EXTRA), pick, images, main)
        tails[i] = ref[main * images :, :]
    get_mask.wait()
    for k in range(nctx):
        gate = mask[wanted[k], main].astype(F32)
        te = tok[pl.ds(main * images + wanted[k], 1), :] * gate
        ce = cot[pl.ds(main * images + wanted[k], 1), :] * gate
        shape = (EXTRA, width)
        sent[k][main : main + EXTRA, :] = jnp.where(
            row_is(shape, 0), te, jnp.where(row_is(shape, 1), ce, 0.0)
        ).astype(BF)


def join_kernel(axis, stride, own, got, out):
    bit = lax.rem(lax.div(lax.axis_index(axis), stride), 2)
    for i in range(own.shape[0]):
        out[2 * i + bit] = own[i]
        out[2 * i + 1 - bit] = got[i]


def place_rows(stage, own, got, rows):
    bit = lax.rem(lax.axis_index("dp"), 2)
    for i in range(own.shape[0]):
        for piece, last in ((own, bit), (got, 1 - bit)):
            at = pl.ds(pl.multiple_of((2 * i + last) * rows, 16 if rows % 16 == 0 else 8), rows)
            stage[at, :] = piece[i].astype(stage.dtype)[:rows]


def merge_quarter_kernel(sizes, attn, own, got, out, attn_out, stage):
    place_rows(stage, own, got, sizes[5])
    out[...] = stage[...].astype(BF)
    attn_out[...] = attn[...]


def split_kernel(got, *outs):
    for i, out in enumerate(outs):
        cols = out.shape[2]
        out[...] = got[:, :, i * cols : (i + 1) * cols]


def merge_ff_kernel(nctx, *refs):
    out = refs[nctx]
    me_c = lax.axis_index("ctx")
    for k in range(nctx):
        quarter = refs[k].shape[1]
        out[:, pl.ds(pl.multiple_of((me_c ^ k) * quarter, quarter), quarter)] = refs[k][...]


def attention_kernel(sizes, *refs):
    nctx, ntp, ndp, main, width, rows, padded = sizes
    t_in, (own, got, own_oth, got_oth_a, got_oth_b), refs = refs[:nctx], refs[nctx : nctx + 5], refs[nctx + 5 :]
    x_out, mid_out, n1_out, n2_out, qkv, ctx, ctx_full, lse, wqkv, wot, vec, ub, cot, stage, stage_oth = refs
    body = nctx * main
    total = body + EXTRA
    half = got_oth_a.shape[2]
    place_rows(stage, own, got, rows)
    place_rows(stage_oth.at[:, :half], own_oth.at[:, :, :half], got_oth_a, rows)
    place_rows(stage_oth.at[:, half:], own_oth.at[:, :, half:], got_oth_b, rows)
    tiles, outs = assemble(stage[...].astype(F32), stage_oth[...].astype(F32))
    for i, v in enumerate(tiles):
        wqkv[:, i * TILE : (i + 1) * TILE] = v.astype(BF)
    for i, v in enumerate(outs):
        wot[:, i * TILE : (i + 1) * TILE] = v.astype(BF)
    extra = own[0, padded:, :].astype(F32)
    extra_oth = own_oth[0, padded:, :].astype(F32)
    tiles, _ = assemble(extra, extra_oth)
    bias = jnp.concatenate([v[0:1] for v in tiles], axis=1)
    vec_sum = jnp.zeros((EXTRA, width), F32)
    for i in range(own.shape[0]):
        vec_sum += own[i, padded:, :width].astype(F32) + got[i, padded:, :width].astype(F32)
    vec[...] = vec_sum
    ub[...] = jnp.broadcast_to(jnp.concatenate([extra[7:8], extra_oth[7:8]], axis=1), ub.shape)
    extra = jnp.zeros((EXTRA, width), F32)
    for k in range(nctx):
        x_out[k * main : (k + 1) * main, :] = t_in[k][0:main, :].astype(F32)
        cot[k * main : (k + 1) * main, :] = t_in[k][main + EXTRA :, :]
        extra += t_in[k][main : main + EXTRA, :].astype(F32)
    x_out[body:, :] = jnp.where(row_is((EXTRA, width), 0), extra, 0.0)
    cot[body:, :] = jnp.where(row_is((EXTRA, width), 0), extra[1:2, :], 0.0).astype(BF)
    x = x_out[...]
    xhat, _ = norm_stats(x)
    n1 = (xhat * vec_sum[1:2, :] + vec_sum[2:3, :]).astype(BF)
    n1_out[...] = n1
    proj = nn(n1, wqkv[...]) + bias
    qkv[0:total, 0:width] = (proj[:, 0:width].astype(BF).astype(F32) * SCALE).astype(BF)
    qkv[0:total, width:] = proj[:, width:].astype(BF)
    keys = qkv.shape[0]
    qkv[total:, :] = jnp.zeros((keys - total, qkv.shape[1]), BF)
    off = jnp.where(lax.broadcasted_iota(jnp.int32, (1, keys), 1) > body, FLOOR, 0.0)
    low = low_lanes((total, TILE))
    lane = lax.broadcasted_iota(jnp.int32, (total, TILE), 1)
    all_lse = jnp.zeros((total, TILE), F32)
    for p in range(3):
        qp = qkv[0:total, p * TILE : (p + 1) * TILE]
        kp = qkv[:, width + p * TILE : width + (p + 1) * TILE]
        vp = qkv[:, 2 * width + p * TILE : 2 * width + (p + 1) * TILE]
        parts = []
        for a in range(2):
            qa = jnp.where(low if a == 0 else ~low, qp, jnp.zeros_like(qp))
            s = nt(qa, kp) + off
            m = jnp.max(s, axis=-1, keepdims=True)
            e = jnp.exp(s - m)
            l = jnp.sum(e, axis=-1, keepdims=True)
            parts.append(nn(e.astype(BF), vp) * (1.0 / l))
            all_lse = jnp.where(lane == 2 * p + a, m + jnp.log(l), all_lse)
        ctx_full[:, p * TILE : (p + 1) * TILE] = jnp.where(low, parts[0], parts[1])
    ctx[...] = ctx_full[...].astype(BF)
    lse[...] = all_lse
    attended = nt(ctx[...], wot[...]) + vec_sum[5:6, :]
    valid = lax.broadcasted_iota(jnp.int32, (total, 1), 0) <= body
    middle = x_out[...] + jnp.where(valid, attended, 0.0)
    mid_out[...] = middle
    xhat2, _ = norm_stats(middle)
    n2_out[...] = (xhat2 * vec_sum[3:4, :] + vec_sum[4:5, :]).astype(BF)


def mlp_half_kernel(sizes, side, n2, cot, w, ub, hid, hgr, ubgrad, grads):
    nctx, ntp, ndp, main, width, rows, padded = sizes
    half = w.shape[1] // 2
    n2v, dcot = n2[...], cot[...]
    act, slope = gelu_pair(nn(n2v, w[:, :half]) + ub[0:1, side * half : (side + 1) * half])
    h = act.astype(BF)
    hg = (nn(dcot, w[:, half:]) * slope).astype(BF)
    hid[...] = h
    hgr[...] = hg
    ubgrad[...] = jnp.broadcast_to(jnp.sum(hg.astype(F32), axis=0, keepdims=True), ubgrad.shape)
    cols = grads.shape[3]
    for part, g in ((0, tn(n2v, hg).astype(BF)), (1, tn(dcot, h).astype(BF))):
        for d in range(ndp):
            for c in range(half // cols):
                grads[2 * part + c, d, 0:rows, :] = g[d * rows : (d + 1) * rows, c * cols : (c + 1) * cols]


def mlp_sums_kernel(sizes, mid, ctx, wot, vec, cot, w_own, w_oth, hgr_own, hgr_oth, dmid, dctx, g_out, vgrad):
    nctx, ntp, ndp, main, width, rows, padded = sizes
    body = nctx * main
    total = body + EXTRA
    half = w_own.shape[1] // 2
    dcot = cot[...]
    middle = mid[...]
    valid = lax.broadcasted_iota(jnp.int32, (total, 1), 0) <= body
    n2g = nt(hgr_own[...], w_own[:, :half]) + nt(hgr_oth[...], w_oth[:, :half])
    xhat, r = norm_stats(middle)
    back = norm_back(n2g * vec[3:4, :], xhat, r)
    middle_grad = dcot.astype(F32) + back
    dmid[...] = middle_grad
    agrad = jnp.where(valid, middle_grad, 0.0).astype(BF)
    dctx[...] = nn(agrad, wot[...]).astype(BF)
    g_out[...] = tn(agrad, ctx[...])
    shape = vgrad.shape
    v = jnp.where(row_is(shape, 2), jnp.sum(n2g * xhat, axis=0, keepdims=True), 0.0)
    v = jnp.where(row_is(shape, 3), jnp.sum(n2g, axis=0, keepdims=True), v)
    v = jnp.where(row_is(shape, 4), jnp.sum(agrad.astype(F32), axis=0, keepdims=True), v)
    v = jnp.where(row_is(shape, 5), jnp.sum(dcot.astype(F32), axis=0, keepdims=True), v)
    vgrad[...] = v


def results_kernel(sizes, mid, vec, w_own, w_oth, hid_own, hid_oth, x, dmid, n1_grad, bo, ig):
    nctx, ntp, ndp, main, width, rows, padded = sizes
    body = nctx * main
    half = w_own.shape[1] // 2
    valid = lax.broadcasted_iota(jnp.int32, (body + EXTRA, 1), 0) <= body
    mlp_out = nt(hid_own[...], w_own[:, half:]) + nt(hid_oth[...], w_oth[:, half:]) + vec[6:7, :]
    bo[...] = (mid[...] + jnp.where(valid, mlp_out, 0.0)).astype(BF)
    xhat, r = norm_stats(x[...])
    ig[...] = (dmid[...] + norm_back(n1_grad[...] * vec[1:2, :], xhat, r)).astype(BF)


def pair_back(p, width, total, body, qkv, dctx, lse, ctx):
    keys = qkv.shape[0]
    off = jnp.where(lax.broadcasted_iota(jnp.int32, (1, keys), 1) > body, FLOOR, 0.0)
    low = low_lanes((total, TILE))
    at = slice(p * TILE, (p + 1) * TILE)
    qp = qkv[0:total, at]
    kp = qkv[:, width + p * TILE : width + (p + 1) * TILE]
    vp = qkv[:, 2 * width + p * TILE : 2 * width + (p + 1) * TILE]
    dp = dctx[:, at]
    both = dp.astype(F32) * ctx[:, at]
    qt = jnp.transpose(qp.astype(F32)).astype(BF)
    dt = jnp.transpose(dp.astype(F32)).astype(BF)
    dk, dv = [], []
    zero = jnp.zeros_like(qp)
    qs = jnp.concatenate([jnp.where(low, qp, zero), jnp.where(low, zero, qp)], axis=0)
    ds_ = jnp.concatenate([jnp.where(low, dp, zero), jnp.where(low, zero, dp)], axis=0)
    bs = jnp.concatenate([jnp.where(low, both, 0.0), jnp.where(low, 0.0, both)], axis=0)
    inner = jnp.sum(bs, axis=-1, keepdims=True)
    ls = jnp.concatenate([lse[:, 2 * p : 2 * p + 1], lse[:, 2 * p + 1 : 2 * p + 2]], axis=0)
    prob = jnp.exp(nt(qs, kp) + off - ls)
    ds = (prob * (nt(ds_, vp) - inner)).astype(BF)
    w = prob.astype(BF)
    dq = nn(ds, kp)
    dq = jnp.where(low, dq[0:total], dq[total:]) * SCALE
    for a in range(2):
        dk.append(nn(qt[a * HD : (a + 1) * HD], ds[a * total : (a + 1) * total]))
        dv.append(nn(dt[a * HD : (a + 1) * HD], w[a * total : (a + 1) * total]))
    dk, dv = (jnp.transpose(jnp.concatenate(v, axis=0))[0:total] for v in (dk, dv))
    return dq.astype(BF), dk.astype(BF), dv.astype(BF)


def attention_back_kernel(sizes, *refs):
    nctx, ntp, ndp, main, width, rows, padded = sizes
    qkv, dctx, lse, ctx, n1, x_in, wqkv, g_out, vgrad, ub_own, ub_oth = refs[:11]
    n1_grad, g_own, g_oth, dqkv = refs[11:]
    body = nctx * main
    total = body + EXTRA
    for p in range(3):
        for i, v in enumerate(pair_back(p, width, total, body, qkv, dctx, lse, ctx)):
            dqkv[:, i * width + p * TILE : i * width + (p + 1) * TILE] = v
    d = dqkv[...]
    bias = jnp.sum(d.astype(F32), axis=0, keepdims=True)
    g = tn(n1[...], d)
    go = g_out[...]
    own, oth = disassemble([tile(g, i) for i in range(9)], [tile(go, i) for i in range(3)])
    half = padded // 2
    for to, tiles in ((g_own, own), (g_oth, oth)):
        for j in range(4):
            lo = j % 2 * half
            for e in range(ndp):
                to[j, e, 0:rows, :] = tiles[j][e * rows : (e + 1) * rows].astype(BF)
                shared = tiles[4 + j // 2][e * rows + lo : e * rows + min(rows, lo + half)]
                to[j, e, padded : padded + shared.shape[0], :] = shared.astype(BF)
    dn1 = nt(d, wqkv[...])
    n1_grad[...] = dn1
    xhat, _ = norm_stats(x_in[...])
    gains = jnp.sum(dn1 * xhat, axis=0, keepdims=True)
    shifts = jnp.sum(dn1, axis=0, keepdims=True)
    vecs = [gains, shifts] + [vgrad[i : i + 1, :] for i in range(2, 6)]
    zero = [jnp.zeros((1, TILE), F32)] * 3
    bias_own, bias_oth = disassemble([tile(bias, i) for i in range(9)], zero)
    for to, tiles, ub in ((g_own, bias_own, ub_own), (g_oth, bias_oth, ub_oth)):
        rows_ = [tile(v, i) for v in vecs for i in range(3)] + tiles
        rows_ += [ub[0:1, i * TILE : (i + 1) * TILE] for i in range(6)]
        for j in range(4):
            block = jnp.zeros((EXTRA, TILE), F32)
            for i, v in enumerate(rows_[8 * j : 8 * (j + 1)]):
                block = jnp.where(row_is(block.shape, i), v, block)
            for e in range(ndp):
                to[j, e, padded + half :, :] = block.astype(BF)


def sum_core_kernel(n, own, oth, *outs):
    me = lax.axis_index("ctx")
    for k in range(n):
        outs[k][...] = own[me ^ k] + oth[me ^ k]


def sum_ctx_kernel(n, ndp, *refs):
    me = lax.axis_index("dp")
    for k in range(ndp):
        v = refs[0][me ^ k].astype(F32)
        for i in range(1, n):
            v = v + refs[i][me ^ k].astype(F32)
        refs[n + k][...] = v.astype(BF)


def halve(stride, item, keep, send):
    bit = lax.rem(lax.div(lax.axis_index("dp"), stride), 2)
    for j in range(keep.shape[0]):
        keep[j] = item(2 * j + bit).astype(BF)
        send[j] = item(2 * j + 1 - bit).astype(BF)


def ctx_bits():
    me = lax.axis_index("ctx")
    return lax.rem(me, 2), lax.div(me, 2)


def sum_core_ff_kernel(own, oth, keep_a, send_a, keep_b, send_b):
    low, high = ctx_bits()
    half = own.shape[1] // 2

    def put(to, i, quarter, blocks):
        to[i] = own[quarter, blocks] + oth[quarter, blocks]

    for i in range(2):
        first, second = slice(0, half), slice(half, 2 * half)
        put(keep_a, i, 2 * i + low, first)
        put(send_a, i, 2 * i + 1 - low, first)
        put(keep_b, i, 2 * high + i, second)
        put(send_b, i, 2 * (1 - high) + i, second)


def sum_ctx_first_kernel(own_a, got_a, own_b, got_b, keep_a, send_a, keep_b, send_b):
    low, high = ctx_bits()
    for own, got, keep, send, bit in (
        (own_a, got_a, keep_a, send_a, high),
        (own_b, got_b, keep_b, send_b, low),
    ):
        keep[...] = own[bit] + got[bit]
        send[...] = own[1 - bit] + got[1 - bit]


def sum_ctx_second_kernel(own_a, got_a, own_b, got_b, keep, send):
    bit = lax.rem(lax.axis_index("dp"), 2)
    half = own_a.shape[0]
    for j in range(keep.shape[0]):
        own, got, at = (own_a, got_a, 2 * j) if 2 * j < half else (own_b, got_b, 2 * j - half)
        for to, i in ((keep, at + bit), (send, at + 1 - bit)):
            to[j] = own[i] + got[i]


def add_halves_kernel(stride, own, got, keep, send):
    halve(stride, lambda i: own[i].astype(F32) + got[i].astype(F32), keep, send)


def sum_dp_kernel(n, own, got, *refs):
    out = refs[n]
    rows = own.shape[1]
    out[:rows, :] = (own[0].astype(F32) + got[0, 0:rows, :].astype(F32)).astype(BF)
    v = refs[0][...].astype(F32)
    for r in refs[1:n]:
        v = v + r[...].astype(F32)
    span = out.shape[0] - rows
    out[rows:, :] = jnp.zeros((span, out.shape[1]), BF)
    for i in range(out.shape[1] // TILE):
        part = v[i * span : (i + 1) * span].astype(BF)
        if part.shape[0]:
            out[rows : rows + part.shape[0], i * TILE : (i + 1) * TILE] = part


def returns_kernel(sizes, bo, ig, out):
    nctx, ntp, ndp, main, width, rows, padded = sizes
    me = lax.axis_index("ctx")
    body = nctx * main
    shape = (EXTRA, width)
    extra = jnp.where(
        row_is(shape, 0),
        bo[body:, :].astype(F32),
        jnp.where(row_is(shape, 1), ig[body:, :].astype(F32)[0:1, :], 0.0),
    ).astype(BF)
    for k in range(nctx):
        at = slice(k * main, (k + 1) * main)
        out[me ^ k, 0:main, :] = bo[at, :]
        out[me ^ k, main : main + EXTRA, :] = extra
        out[me ^ k, main + EXTRA :, :] = ig[at, :]


def hand_on_kernel(held, out):
    out[...] = held[...]


def grads_kernel(sizes, *refs):
    nctx, ntp, ndp, main, width, rows, padded = sizes
    parts, refs = refs[:nctx], refs[nctx:]
    gq, gk, gv, gqb, gvb, go, gu, gub, gd = refs[:9]
    gvec, f, f2 = refs[9:15], refs[15], refs[16]
    me, me_d = lax.axis_index("ctx"), lax.axis_index("dp")
    span = parts[0].shape[0] - padded
    for k in range(nctx):
        f2[me ^ k] = parts[k][0:padded, :].astype(F32)
        for i in range(f2.shape[2] // TILE):
            n = min(span, f.shape[1] - i * span)
            if n > 0:
                f[me ^ k, i * span : i * span + n, :] = parts[k][
                    padded : padded + n, i * TILE : (i + 1) * TILE
                ].astype(F32)
    half = f2.shape[2]
    for j in range(2):
        gu[:, j * half : (j + 1) * half] = f2[j, 0:rows, :]
        gd[:, j * half : (j + 1) * half] = f2[2 + j, 0:rows, :]
    q01, k01, v01, o01 = (f[j, 0:rows, :] for j in range(4))
    low, high = slice(padded, padded + padded // 2), slice(padded, padded + rows - padded // 2)
    qk2 = jnp.concatenate([f[0, low, :], f[1, high, :]], axis=0)
    vo2 = jnp.concatenate([f[2, low, :], f[3, high, :]], axis=0)
    gq[:, 0:TILE] = q01
    gq[:, TILE:] = qk2[:, 0:HD]
    gk[:, 0:TILE] = k01
    gk[:, TILE:] = swap(qk2)[:, 0:HD]
    gv[:, 0:TILE] = v01
    gv[:, TILE:] = vo2[:, 0:HD]
    go[0:TILE, :] = jnp.transpose(o01)
    go[TILE:, :] = jnp.transpose(vo2)[HD:, :]

    def line(i):
        at = padded + padded // 2 + i % 8
        return f[i // 8, at : at + 1, :]

    for i in range(6):
        v = jnp.concatenate([line(3 * i), line(3 * i + 1), line(3 * i + 2)], axis=1)
        v = jnp.broadcast_to(v, (8, width))
        v = pltpu.roll(v, lax.rem(width - me_d * rows, width), axis=1)
        gvec[i][...] = v[0, 0:rows]
    b = [line(18 + i) for i in range(6)]
    gqb[...] = jnp.concatenate([b[0], b[4][:, 0:HD]], axis=1)[0]
    gvb[...] = jnp.concatenate([b[2], b[5][:, 0:HD]], axis=1)[0]
    gub[...] = jnp.concatenate([line(24 + i) for i in range(6)], axis=1)[0]


def unpack_kernel(sizes, own, oth, tails, mask, *refs):
    nctx, ntp, ndp, main, width, rows, padded = sizes
    outs, done, valid, sem = refs[:2], refs[2], refs[3], refs[4]
    images = nctx * ntp
    me_t = lax.axis_index("tp")
    where = [j * ntp + t for t in (me_t, 1 - me_t) for j in range(nctx)]
    sources = [v.at[j] for v in (own, oth) for j in range(nctx)]
    get_valid = pltpu.make_async_copy(mask, valid, sem.at[0])
    get_valid.start()

    def hit(r, c):
        img = where[-1]
        for j in range(images - 1):
            img = jnp.where(c // BLOCK == j, where[j], img)
        return r == (c % BLOCK) * images + img

    put = one_hot((images * BLOCK, images * BLOCK), hit)
    for i in range(2):
        for b in range(main // BLOCK):
            lo = i * (main + EXTRA) + b * BLOCK
            got = jnp.concatenate([src[lo : lo + BLOCK, :] for src in sources], axis=0)
            outs[i][b * BLOCK * images : (b + 1) * BLOCK * images, :] = nn(put, got)
    get_valid.wait()
    for i in range(2):
        for src, img in zip(sources, where):
            got = src[main : main + EXTRA, :].astype(F32)[i : i + 1, :]
            outs[i][pl.ds(main * images + img, 1), :] = jnp.where(
                valid[img, main] > 0, got, tails[i, pl.ds(img, 1), :]
            )
    done[...] = jnp.zeros_like(done)


def xor(n, k):
    return [(i, i ^ k) for i in range(n)]


def over(axis, n, items):
    return [items[0]] + [lax.ppermute(items[k], axis, xor(n, k)) for k in range(1, n)]


def body(nctx, ntp, ndp, *args):
    (tokens, valid_mask, cotangent, w_query, w_key, w_value, query_bias, value_bias, w_out, w_up, up_bias, w_down) = args[:12]
    vecs = args[12:]
    images, slots, width = tokens.shape
    main = slots - 1
    rows = w_query.shape[0]
    padded = -(-rows // EXTRA) * EXTRA
    ff = w_up.shape[1]
    p1_cols = 4 * w_query.shape[1]
    sizes = (nctx, ntp, ndp, main, width, rows, padded)
    total = nctx * main + EXTRA
    keys = -(-total // TILE) * TILE
    stage = BF if rows % 16 == 0 else F32
    flip = xor(ntp, 1)
    tok = jnp.transpose(tokens, (1, 0, 2)).reshape(slots * images, width)
    cot = jnp.transpose(cotangent, (1, 0, 2)).reshape(slots * images, width)

    def one(f):
        return functools.partial(f, sizes)

    def other(v):
        return lax.ppermute(v, "tp", flip)

    def held(arrays):
        return [
            (pltpu.SMEM if v.dtype == jnp.int32 else pltpu.VMEM)(v.shape, v.dtype) for v in arrays
        ] + [pltpu.SemaphoreType.DMA((len(arrays),))]

    def gather_dp(name, piece, after):
        v = piece[None]
        stride = ndp // 2
        while stride > 1:
            v = call(
                name,
                functools.partial(join_kernel, "dp", stride),
                sds((2 * v.shape[0],) + v.shape[1:], v.dtype),
                after=after,
            )(v, lax.ppermute(v, "dp", xor(ndp, stride)))
            stride //= 2
        return v, lax.ppermute(v, "dp", xor(ndp, 1))

    sources = [w_query, w_key, w_value, w_out, w_up, jnp.transpose(w_down), query_bias, value_bias, up_bias, *vecs]
    p1, p2q = call(
        "pack_weights",
        functools.partial(pack_weights_kernel, sizes, len(sources)),
        [sds((padded + EXTRA, p1_cols), BF), sds((padded, ff // 2), BF)],
        scratch=held(sources),
        mib=56,
        raw=range(len(sources)),
    )(*sources)
    *sent, tails = call(
        "pack_slots",
        one(pack_slots_kernel),
        [sds((2 * main + EXTRA, width), BF)] * nctx + [sds((2, images, width), F32)],
        scratch=[pltpu.SMEM(valid_mask.shape, valid_mask.dtype), pltpu.SemaphoreType.DMA((1,))],
        mib=48,
        raw=(2,),
    )(tok, cot, valid_mask)
    t_in = over("ctx", nctx, sent)
    w2q = gather_dp("join_quarter", p2q, [])
    w1, w1_got = gather_dp("join_attn", p1, [])
    w2q, w1_early = call(
        "merge_quarter",
        one(merge_quarter_kernel),
        [sds((width, ff // 2), BF), sds(w1.shape, BF)],
        scratch=[pltpu.VMEM((width, ff // 2), stage)],
        after=t_in[1:],
    )(w1, *w2q)
    w1_oth = other(w1_early)
    w2q = over("ctx", nctx, [w2q] * nctx)
    late = call(
        "split_attn",
        split_kernel,
        [sds(w1.shape[:2] + (p1_cols // 2,), BF)] * 2,
        after=[w1_oth, w2q[0]],
    )(w1_got)
    w1 = [w1, w1_got, w1_oth, *[other(v) for v in late]]
    x, mid, n1, n2, qkv, ctx, ctx_full, lse, wqkv, wot, vec, ub, cot_in = call(
        "attention",
        one(attention_kernel),
        [
            sds((total, width), F32), sds((total, width), F32), sds((total, width), BF), sds((total, width), BF),
            sds((keys, 3 * width), BF), sds((total, width), BF), sds((total, width), F32), sds((total, TILE), F32),
            sds((width, 3 * width), BF), sds((width, width), BF), sds((EXTRA, width), F32), sds((8, 2 * ff), F32),
            sds((total, width), BF),
        ],
        scratch=[pltpu.VMEM((width, p1_cols), stage)] * 2,
        mib=32,
    )(*t_in, *w1)
    w2_own = call(
        "merge_ff", functools.partial(merge_ff_kernel, nctx), sds((width, 2 * ff), BF), after=[vec]
    )(*w2q)
    w2_oth = other(w2_own)
    ff_grads = sds((4, ndp, padded, ff // 2), BF)

    def mlp_half(name, side, w, after=()):
        return call(
            name,
            functools.partial(mlp_half_kernel, sizes, side),
            [sds((total, ff), BF), sds((total, ff), BF), sds((8, ff), F32), ff_grads],
            mib=32,
            after=after,
        )(n2, cot_in, w, ub)

    hid_own, hgr_own, ub_own, g2_own = mlp_half("mlp_own", 0, w2_own)
    hid_oth, hgr_oth, ub_oth, g2_oth = mlp_half("mlp_oth", 1, w2_oth, [ub_own])
    dmid, dctx, g_out, vgrad = call(
        "mlp_sums",
        one(mlp_sums_kernel),
        [
            sds((total, width), F32), sds((total, width), BF), sds((width, width), F32), sds((EXTRA, width), F32),
        ],
        mib=32,
    )(mid, ctx, wot, vec, cot_in, w2_own, w2_oth, hgr_own, hgr_oth)

    def core_sums(name, own, oth, after=()):
        outs = [sds(own.shape[1:], BF)] * nctx
        return call(name, functools.partial(sum_core_kernel, nctx), outs, after=after)(own, other(oth))

    def by_image(v):
        return jnp.transpose(v.reshape(slots, images, width), (1, 0, 2))

    pairs = sds((2, ndp // 2, padded, ff // 2), BF)
    keep_a, send_a, keep_b, send_b = call("sum_core_ff", sum_core_ff_kernel, [pairs] * 4, after=[vgrad])(
        g2_own, other(g2_oth)
    )
    got_a, got_b = lax.ppermute(send_a, "ctx", xor(nctx, 1)), lax.ppermute(send_b, "ctx", xor(nctx, 2))
    n1_grad, g1_own, g1_oth = call(
        "attention_back",
        one(attention_back_kernel),
        [sds((total, width), F32)] + [sds((4, ndp, padded + padded // 2 + EXTRA, TILE), BF)] * 2,
        scratch=[pltpu.VMEM((total, 3 * width), BF)],
        mib=32,
        after=[keep_a],
    )(qkv, dctx, lse, ctx_full, n1, x, wqkv, g_out, vgrad, ub_own, ub_oth)
    one_quarter = sds(pairs.shape[1:], BF)
    keep_a, send_a, keep_b, send_b = call(
        "sum_ctx_first", sum_ctx_first_kernel, [one_quarter] * 4, after=[g1_own]
    )(keep_a, got_a, keep_b, got_b)
    got_a, got_b = lax.ppermute(send_a, "ctx", xor(nctx, 2)), lax.ppermute(send_b, "ctx", xor(nctx, 1))
    s1_send = core_sums("sum_core_attn", g1_own, g1_oth, after=[keep_a])
    s1 = over("ctx", nctx, s1_send)
    bo, ig = call(
        "results", one(results_kernel), [sds((total, width), BF)] * 2, mib=16, after=[s1_send[0]]
    )(mid, vec, w2_own, w2_oth, hid_own, hid_oth, x, dmid, n1_grad)
    keep, send = call("sum_ctx_second", sum_ctx_second_kernel, [one_quarter] * 2, after=[bo])(
        keep_a, got_a, keep_b, got_b
    )
    back = call(
        "returns",
        one(returns_kernel),
        sds((nctx, 2 * main + EXTRA, width), BF),
        after=[keep],
    )(bo, ig)
    returned = lax.all_to_all(back, "ctx", 0, 0)
    u1_send = call(
        "sum_ctx_attn",
        functools.partial(sum_ctx_kernel, nctx, ndp),
        [sds(s1[0].shape[1:], BF)] * ndp,
        after=[back],
    )(*s1)
    u1 = over("dp", ndp, u1_send)
    stride = 2
    while stride < ndp:
        half = sds((keep.shape[0] // 2,) + keep.shape[1:], BF)
        keep, send = call(
            "add_dp_ff", functools.partial(add_halves_kernel, stride), [half, half], after=[u1_send[0]]
        )(keep, lax.ppermute(send, "dp", xor(ndp, stride // 2)))
        stride *= 2
    summed = call(
        "sum_dp", functools.partial(sum_dp_kernel, ndp), sds((padded + -(-s1[0].shape[1] // (3 * EXTRA)) * EXTRA, ff // 2), BF)
    )(keep, lax.ppermute(send, "dp", xor(ndp, ndp // 2)), *u1)
    shares = over("ctx", nctx, [summed] * nctx)
    back = call("hand_on", hand_on_kernel, sds(returned.shape, BF), after=[summed])(returned)
    block_out, input_grad, placed = call(
        "place_slots",
        one(unpack_kernel),
        [sds(tok.shape, F32)] * 2 + [sds((8, TILE), F32)],
        scratch=[pltpu.SMEM(valid_mask.shape, valid_mask.dtype), pltpu.SemaphoreType.DMA((1,))],
        raw=(3,),
        mib=16,
    )(back, other(back), tails, valid_mask)
    gq, gk, gv, gqb, gvb, go, gu, gub, gd, *gvec = call(
        "place_grads",
        one(grads_kernel),
        [
            sds(w_query.shape, F32), sds(w_key.shape, F32), sds(w_value.shape, F32),
            sds(query_bias.shape, F32), sds(value_bias.shape, F32), sds(w_out.shape, F32),
            sds(w_up.shape, F32), sds(up_bias.shape, F32), sds((rows, ff), F32),
        ]
        + [sds((rows,), F32)] * 6,
        scratch=[
            pltpu.VMEM((nctx,) + s1[0].shape[1:], F32),
            pltpu.VMEM((nctx, padded, ff // 2), F32),
        ],
        after=[placed],
    )(*shares)
    return (by_image(block_out), by_image(input_grad), gq, gk, gv, gqb, gvb, go, gu, gub, jnp.transpose(gd), *gvec)


def solution(mesh):
    rows, cols, tp, dp = P("dp", "tp"), P("tp", "dp"), P("tp"), P("dp")
    act = P("dp", "ctx", None)
    return jax.shard_map(
        functools.partial(body, mesh.shape["ctx"], mesh.shape["tp"], mesh.shape["dp"]),
        mesh=mesh,
        in_specs=(act, P("dp", "ctx"), act, rows, rows, rows, tp, tp, cols, rows, tp, cols) + (dp,) * 6,
        out_specs=(act, act, rows, rows, rows, tp, tp, cols, rows, tp, cols) + (dp,) * 6,
        check_vma=False,
    )
```
